32 devices in a mesh: ctx: 8 (over y, x, core), ch: 4 (over z).
Axes of the slice: x: 2, y: 2, z: 4, core: 2. Of those that a mesh axis runs over, the one named last changes fastest.
Arguments:
- tokens: float32 [1024, 3072], P('ctx', 'ch'), may hold values from -6 to 6
- gate_input: float32 [1024, 3072], P('ctx', 'ch'), may hold values from -6 to 6
- cotangent: float32 [1024, 3072], P('ctx', 'ch'), may hold values from -6 to 6
- conv_weight: float32 [2, 4, 3072], P(None, None, 'ch'), may hold values from -3 to 3
- conv_bias: float32 [2, 3072], P(None, 'ch'), may hold values from -3 to 3
- select_weight: float32 [2, 3072, 128], P(None, 'ch'), may hold values from -0.109375 to 0.109375
- step_weight: float32 [2, 96, 3072], P(None, None, 'ch'), may hold values from -0.625 to 0.625
- step_bias: float32 [2, 3072], P(None, 'ch'), may hold values from -6 to -2.5
- decay_log: float32 [2, 16, 3072], P(None, None, 'ch'), may hold values from -12 to 2.75
- skip_gain: float32 [2, 3072], P(None, 'ch'), may hold values from 0.5 to 1.5
Outputs:
- block_out: float32 [1024, 3072], P('ctx', 'ch')
- tokens_grad: float32 [1024, 3072], P('ctx', 'ch')
- gate_grad: float32 [1024, 3072], P('ctx', 'ch')
- select_grad: float32 [2, 3072, 128], P(None, 'ch')
- step_grad: float32 [2, 96, 3072], P(None, None, 'ch')
The draws below stay inside these ranges and needn't reach their ends.
All inputs are finite; a program needn't handle non-finite values.
Results may differ from the reference program's by a relative error of at most 0.0003.
Values sent between devices are 32-bit elements; how exact they have to be, the bound alone decides.
No kernel may reach another device: no remote copies, remote signals or barrier semaphores. Data moves between devices by JAX's collectives and lax.ppermute only.
A program may use at most 64 MiB of HBM per device.

```python
import jax
import jax.numpy as jnp
from jax import lax

E = 3072
N = 16
K = 4
R = 96
TOKENS = 1024
PROJ = 128


def block_levels(stream_key, shape, shards, smallest, top_value):
    gain, own = 1.0, jax.random.fold_in(stream_key, 6)
    for position, shards_of in shards:
        draws = jnp.exp(jax.random.uniform(jax.random.fold_in(own, position), (shards_of,), jnp.float32, smallest / len(shards), top_value / len(shards)))
        gain = gain * jnp.repeat(draws, shape[position] // shards_of).reshape([-1 if axis == position else 1 for axis in range(len(shape))])
    return gain


def scatter_about(own_key, shape, scale, reach, cuts=(), dtype=jnp.bfloat16):
    values = scale * jax.random.normal(own_key, shape, jnp.float32)
    if cuts:
        values = values * block_levels(own_key, shape, cuts, -0.22, 0.18)
    return jnp.clip(values, -reach, reach).astype(dtype)


def setup_inputs(seed: int = 0) -> dict:
    keys = jax.random.split(jax.random.key(seed), 11)
    tokens = scatter_about(keys[0], (TOKENS, E), 1.0, 6.0, ((0, 8), (1, 4)), jnp.float32)
    gate_input = scatter_about(keys[1], (TOKENS, E), 1.0, 6.0, ((0, 8), (1, 4)), jnp.float32)
    cotangent = scatter_about(keys[2], (TOKENS, E), 1.0, 6.0, ((0, 8), (1, 4)), jnp.float32)
    conv_weight = scatter_about(keys[3], (2, K, E), K ** -0.5, 3.0, ((2, 4),), jnp.float32)
    conv_bias = scatter_about(keys[4], (2, E), 0.5, 3.0, ((1, 4),), jnp.float32)
    select_weight = scatter_about(keys[5], (2, E, PROJ), E ** -0.5, 0.109375, ((1, 4),), jnp.float32)
    step_weight = scatter_about(keys[6], (2, R, E), R ** -0.5, 0.625, ((2, 4),), jnp.float32)
    step_bias = jnp.clip(-6.0 + 3.5 * jax.random.uniform(keys[7], (2, E), jnp.float32) ** block_levels(keys[7], (2, E), ((1, 4),), -0.2, 0.2), -6.0, -2.5)
    decay_log = jnp.clip(-12.0 + 14.75 * jax.random.uniform(keys[8], (2, N, E), jnp.float32) ** block_levels(keys[8], (2, N, E), ((2, 4),), -0.2, 0.2), -12.0, 2.75)
    skip_gain = jnp.clip(0.5 + 1.0 * jax.random.uniform(keys[9], (2, E), jnp.float32) ** block_levels(keys[9], (2, E), ((1, 4),), -0.2, 0.2), 0.5, 1.5)
    return dict(tokens=tokens, gate_input=gate_input, cotangent=cotangent, conv_weight=conv_weight, conv_bias=conv_bias, select_weight=select_weight, step_weight=step_weight, step_bias=step_bias, decay_log=decay_log, skip_gain=skip_gain)


def link(earlier, later):
    return (earlier[0] * later[0], later[0] * earlier[1] + later[1])

def selective(step, activated, in_basis, out_basis, rates):
    length, width = step.shape
    block = 256 if width % 256 == 0 else width
    count = width // block
    step_blocks = step.reshape(length, count, block).transpose(1, 0, 2)
    act_blocks = activated.reshape(length, count, block).transpose(1, 0, 2)
    rate_blocks = rates.reshape(rates.shape[0], count, block).transpose(1, 0, 2)

    def one_block(items):
        step_part, act_part, rate_part = items

        def advance(state, row):
            step_row, act_row, in_row, out_row = row
            state = jnp.exp(step_row[None, :] * rate_part) * state + in_row[:, None] * (step_row * act_row)[None, :]
            return (state, lax.optimization_barrier(jnp.sum(out_row[:, None] * state, axis=0)))
        start = jnp.zeros(rate_part.shape, jnp.float32)
        _, outputs = lax.scan(advance, start, (step_part, act_part, in_basis, out_basis))
        return outputs
    outputs = lax.map(jax.checkpoint(one_block), (step_blocks, act_blocks, rate_blocks))
    return outputs.transpose(1, 0, 2).reshape(length, width)

def branch(sequence, taps_weight, taps_bias, select_side, step_side, bias_side, decay_side, skip_side):
    length = sequence.shape[0]
    taps = taps_weight.shape[0]
    padded = jnp.concatenate([jnp.zeros((taps - 1, sequence.shape[1]), jnp.float32), sequence], 0)
    conv_pre = taps_bias[None, :]
    for lag in range(taps):
        conv_pre = conv_pre + taps_weight[lag][None, :] * padded[lag:lag + length]
    activated = jax.nn.silu(conv_pre)
    projection = jnp.dot(activated, select_side, precision=lax.Precision.HIGHEST, preferred_element_type=jnp.float32)
    low_rank = projection[:, :R]
    in_basis = projection[:, R:R + N]
    out_basis = projection[:, R + N:]
    step = jax.nn.softplus(jnp.dot(low_rank, step_side, precision=lax.Precision.HIGHEST, preferred_element_type=jnp.float32) + bias_side[None, :])
    rates = -jnp.exp(decay_side)
    return selective(step, activated, in_basis, out_basis, rates) + skip_side[None, :] * activated

def reference(tokens, gate_input, cotangent, conv_weight, conv_bias, select_weight, step_weight, step_bias, decay_log, skip_gain):

    def block(sequence, gate_values, select_all, step_all):
        forward_out = branch(sequence, conv_weight[0], conv_bias[0], select_all[0], step_all[0], step_bias[0], decay_log[0], skip_gain[0])
        backward_out = branch(jnp.flip(sequence, 0), conv_weight[1], conv_bias[1], select_all[1], step_all[1], step_bias[1], decay_log[1], skip_gain[1])
        return (forward_out + jnp.flip(backward_out, 0)) * jax.nn.silu(gate_values)
    block_out, pullback = jax.vjp(block, tokens, gate_input, select_weight, step_weight)
    tokens_grad, gate_grad, select_grad, step_grad = pullback(cotangent)
    return (block_out, tokens_grad, gate_grad, select_grad, step_grad)
```

```python
import functools

import jax
import jax.numpy as jnp
from jax import lax
from jax.experimental import pallas as pl
from jax.experimental.pallas import tpu as pltpu
from jax.sharding import PartitionSpec as P

FULL_PRECISION = lax.Precision.HIGHEST
LANES = 128
CHAINS = 8
HALO = 8
LOG2E = 1.4426950408889634
LN2 = 0.6931471805599453
MIB = 1024 * 1024


def params(mib):
    return pltpu.CompilerParams(vmem_limit_bytes=mib * MIB)


def shape_of(*dims):
    return jax.ShapeDtypeStruct(dims, jnp.float32)


def dot(a, b, contract):
    return lax.dot_general(
        a, b, ((contract[:1], contract[1:]), ((), ())), precision=FULL_PRECISION,
        preferred_element_type=jnp.float32,
    )


def silu_grad(values):
    sigmoid_values = jax.nn.sigmoid(values)
    return sigmoid_values * (1.0 + values * (1.0 - sigmoid_values))


def lane_tile(t):
    return slice(t * LANES, (t + 1) * LANES)


def full_width(ref, *lead):
    tiles = ref.shape[len(lead)]
    return jnp.concatenate([ref[(*lead, t)] for t in range(tiles)], axis=1)


def entry_kernel(tokens, before, after, conv_weight, conv_bias, select, partial, act, pre, ext):
    length, width = tokens.shape
    taps = conv_weight.shape[1]
    margin = taps - 1
    ext[:HALO] = before[...]
    ext[HALO : HALO + length] = tokens[...]
    ext[HALO + length :] = after[...]
    for side in range(2):
        for t in range(width // LANES):
            lanes = lane_tile(t)
            conv = jnp.broadcast_to(conv_bias[side : side + 1, lanes], (length, LANES))
            for k in range(taps):
                at = HALO - margin + k if side == 0 else HALO + margin - k
                conv = conv + conv_weight[side, k : k + 1, lanes] * ext[at : at + length, lanes]
            pre[side, t] = conv
            act[side, t] = conv * jax.nn.sigmoid(conv)
        partial[side] = dot(full_width(act, side), select[side], (1, 0))


def spread(projection, side, j, states, basis_b, basis_c):
    length = basis_b.shape[0]
    count = length // CHAINS
    rows = projection[side, pl.ds(j, CHAINS, stride=count), :]
    ranks = LANES - 2 * states
    at = pl.ds(pl.multiple_of(j * CHAINS, CHAINS), CHAINS)
    for n in range(states):
        b = rows[:, ranks + n : ranks + n + 1]
        c = rows[:, ranks + states + n : ranks + states + n + 1]
        basis_b[at, lane_tile(n)] = jnp.broadcast_to(b, (CHAINS, LANES))
        basis_c[at, lane_tile(n)] = jnp.broadcast_to(c, (CHAINS, LANES))


def fill_bases(projection, side, states, basis_b, basis_c):
    def body(j, carry):
        spread(projection, side, j, states, basis_b, basis_c)
        return carry

    lax.fori_loop(0, basis_b.shape[0] // CHAINS, body, 0)


def fill_rates(decay_log, rates):
    for side in range(rates.shape[0]):
        for t in range(rates.shape[1]):
            rates[side, t] = -LOG2E * jnp.exp(decay_log[side, :, lane_tile(t)])


def sublane():
    return lax.broadcasted_iota(jnp.int32, (CHAINS, LANES), 0)


def shifted(value, by, up):
    rolled = pltpu.roll(value, by if up else CHAINS - by, 0)
    place = sublane()
    keep = place >= by if up else place < CHAINS - by
    return jnp.where(keep, rolled, 0.0)


def over_chains(decays, ends, up):
    by = 1
    while by < CHAINS:
        ends = [d * shifted(f, by, up) + f for d, f in zip(decays, ends)]
        if 2 * by < CHAINS:
            turn = by if up else CHAINS - by
            decays = [d * pltpu.roll(d, turn, 0) for d in decays]
        by *= 2
    return ends


def order(i, count, up):
    return i if up else count - 1 - i


def local_kernel(
    gathered, step_weight, step_bias, decay_log, act, gate, cot,
    projection, step, step_pre, grad_gated, entering, carry,
    rates, basis_b, basis_c, rate_rows, decays,
):
    sides, tiles, length, _ = act.shape
    states = decay_log.shape[1]
    ranks = step_weight.shape[1]
    count = length // CHAINS
    total = gathered[0]
    for part in range(1, gathered.shape[0]):
        total = total + gathered[part]
    projection[...] = total
    for t in range(tiles):
        lanes = lane_tile(t)
        values = gate[:, lanes]
        grad_gated[t] = cot[:, lanes] * values * jax.nn.sigmoid(values)
    fill_rates(decay_log, rates)
    for side in range(2):
        wide = dot(projection[side][:, :ranks], step_weight[side], (1, 0))
        wide = wide + step_bias[side : side + 1]
        for t in range(tiles):
            part = wide[:, lane_tile(t)]
            step_pre[side, t] = part
            step[side, t] = jnp.maximum(part, 0.0) + jnp.log1p(jnp.exp(-jnp.abs(part)))
    zero = jnp.zeros((CHAINS, LANES), jnp.float32)
    carry[...] = jnp.zeros_like(carry)
    for side in range(2):
        up = side == 0
        fill_bases(projection, side, states, basis_b, basis_c)

        def one_tile(t, keep):
            for n in range(states):
                rate_rows[n] = jnp.broadcast_to(rates[side, t, n : n + 1], (CHAINS, LANES))

            def forward(i, current):
                state, summed = current
                j = order(i, count, up)
                rows = pl.ds(j, CHAINS, stride=count)
                at = pl.ds(pl.multiple_of(j * CHAINS, CHAINS), CHAINS)
                step_rows = step[side, t, rows, :]
                drive = step_rows * act[side, t, rows, :]
                new = []
                for n in range(states):
                    decay = jnp.exp2(step_rows * rate_rows[n])
                    decays[at, lane_tile(n)] = decay
                    new.append(decay * state[n] + basis_b[at, lane_tile(n)] * drive)
                return (tuple(new), summed + step_rows)

            state, summed = lax.fori_loop(0, count, forward, ((zero,) * states, zero))

            def retreat(i, state):
                j = order(i, count, not up)
                rows = pl.ds(j, CHAINS, stride=count)
                at = pl.ds(pl.multiple_of(j * CHAINS, CHAINS), CHAINS)
                grad_rows = grad_gated[t, rows, :]
                return tuple(
                    decays[at, lane_tile(n)]
                    * (state[n] + basis_c[at, lane_tile(n)] * grad_rows)
                    for n in range(states)
                )

            sent = lax.fori_loop(0, count, retreat, (zero,) * states)
            across = [jnp.exp2(summed * rate_rows[n]) for n in range(states)]
            for kind, ends, upward in ((0, state, up), (1, sent, not up)):
                slot = 2 * side + kind
                ends = over_chains(across, list(ends), upward)
                last = CHAINS - 1 if upward else 0
                for n in range(states):
                    entering[slot, t, n] = shifted(ends[n], 1, upward)
                    at = slot * states + n
                    carry[t, at : at + 1] = ends[n][last : last + 1]
            whole = jnp.sum(summed, axis=0, keepdims=True)
            carry[t, 4 * states + side : 4 * states + side + 1] = whole
            return keep

        lax.fori_loop(0, tiles, one_tile, 0)


def scan_kernel(
    place, carries, projection, step_weight, decay_log, skip_gain, act, step, step_pre,
    grad_gated, entering, gate, cot,
    block_out, gate_grad, partial, step_part, grad_act,
    rates, basis_b, basis_c, rate_rows, decays, history, incoming, summed_out,
    grad_in, grad_out, grad_pre, weights, packed,
):
    sides, tiles, length, _ = act.shape
    states = decay_log.shape[1]
    ranks = step_weight.shape[1]
    count = length // CHAINS
    shards = carries.shape[0]
    me = place[0]
    fill_rates(decay_log, rates)
    zero = jnp.zeros((CHAINS, LANES), jnp.float32)
    for side in range(2):
        for kind in range(2):
            slot = 2 * side + kind
            upward = (side == 0) == (kind == 0)

            def chain(i, current):
                k = order(i, shards, upward)
                at = 4 * states + side
                decay = jnp.exp2(rates[side] * carries[k, :, at : at + 1, :])
                return decay * current + carries[k, :, slot * states : (slot + 1) * states, :]

            turns = me if upward else shards - 1 - me
            start = jnp.zeros((tiles, states, LANES), jnp.float32)
            incoming[slot] = lax.fori_loop(0, turns, chain, start)
    for side in range(2):
        up = side == 0
        fill_bases(projection, side, states, basis_b, basis_c)
        grad_in[...] = jnp.zeros_like(grad_in)
        grad_out[...] = jnp.zeros_like(grad_out)

        def one_tile(t, keep):
            for n in range(states):
                rate_rows[n] = jnp.broadcast_to(rates[side, t, n : n + 1], (CHAINS, LANES))
            skip = skip_gain[side, t]
            summed = step[side, t, pl.ds(0, CHAINS, stride=count), :]
            for j in range(1, count):
                summed = summed + step[side, t, pl.ds(j, CHAINS, stride=count), :]

            def start(kind, upward):
                slot = 2 * side + kind
                span = shifted(summed, 1, upward)
                by = 1
                while by < CHAINS:
                    span = span + shifted(span, by, upward)
                    by *= 2
                return tuple(
                    entering[slot, t, n]
                    + jnp.exp2(span * rate_rows[n]) * incoming[slot, t, n : n + 1, :]
                    for n in range(states)
                )

            def forward(i, state):
                j = order(i, count, up)
                rows = pl.ds(j, CHAINS, stride=count)
                at = pl.ds(pl.multiple_of(j * CHAINS, CHAINS), CHAINS)
                step_rows = step[side, t, rows, :]
                act_rows = act[side, t, rows, :]
                drive = step_rows * act_rows
                out = skip * act_rows
                new = []
                for n in range(states):
                    decay = jnp.exp2(step_rows * rate_rows[n])
                    decays[at, lane_tile(n)] = decay
                    history[i, n] = state[n]
                    current = decay * state[n] + basis_b[at, lane_tile(n)] * drive
                    out = out + basis_c[at, lane_tile(n)] * current
                    new.append(current)
                if side == 0:
                    summed_out[t, rows, :] = out
                else:
                    summed_out[t, rows, :] = summed_out[t, rows, :] + out
                return tuple(new)

            final = lax.fori_loop(0, count, forward, start(0, up))
            for n in range(states):
                history[count, n] = final[n]

            def retreat(i, state):
                back = count - 1 - i
                j = order(back, count, up)
                rows = pl.ds(j, CHAINS, stride=count)
                at = pl.ds(pl.multiple_of(j * CHAINS, CHAINS), CHAINS)
                step_rows = step[side, t, rows, :]
                act_rows = act[side, t, rows, :]
                drive = step_rows * act_rows
                grad_rows = grad_gated[t, rows, :]
                step_term = zero
                drive_grad = zero
                new = []
                for n in range(states):
                    lanes = lane_tile(n)
                    adjoint = state[n] + basis_c[at, lanes] * grad_rows
                    carried = decays[at, lanes] * adjoint
                    new.append(carried)
                    step_term = step_term + carried * history[back, n] * rate_rows[n]
                    drive_grad = drive_grad + adjoint * basis_b[at, lanes]
                    grad_in[at, lanes] = grad_in[at, lanes] + adjoint * drive
                    grad_out[at, lanes] = grad_out[at, lanes] + history[back + 1, n] * grad_rows
                grad_step = step_term * LN2 + drive_grad * act_rows
                grad_act[side, t, rows, :] = grad_rows * skip + drive_grad * step_rows
                pre = step_pre[side, t, rows, :]
                grad_pre[t, rows, :] = grad_step * jax.nn.sigmoid(pre)
                return tuple(new)

            lax.fori_loop(0, count, retreat, start(1, not up))
            return keep

        lax.fori_loop(0, tiles, one_tile, 0)
        wide = full_width(grad_pre)
        weights[...] = jnp.zeros_like(weights)
        weights[:ranks] = step_weight[side]
        step_part[side] = dot(projection[side], wide, (0, 0))[:ranks]
        result = dot(wide, weights[...], (1, 1))
        sums = None
        for values, first in ((grad_in, ranks), (grad_out, ranks + states)):
            whole = values[...]
            row = lax.broadcasted_iota(jnp.int32, (states * LANES, LANES), 0)
            column = lax.broadcasted_iota(jnp.int32, (states * LANES, LANES), 1)
            pick = lax.shift_right_logical(row, 7) + first == column
            pick = jnp.where(pick, 1.0, 0.0).astype(jnp.bfloat16)
            for _ in range(3):
                short = whole.astype(jnp.bfloat16)
                whole = whole - short.astype(jnp.float32)
                term = jnp.dot(short, pick, preferred_element_type=jnp.float32)
                sums = term if sums is None else sums + term
        for j in range(count):
            packed[pl.ds(j, CHAINS, stride=count), :] = sums[j * CHAINS : (j + 1) * CHAINS]
        partial[side] = result + packed[...]
    for t in range(tiles):
        lanes = lane_tile(t)
        values = gate[:, lanes]
        block_out[:, lanes] = summed_out[t] * values * jax.nn.sigmoid(values)
        gate_grad[:, lanes] = cot[:, lanes] * summed_out[t] * silu_grad(values)


def weight_kernel(grad, act, pre, grad_act, select, select_part, conv_grad):
    sides, tiles, length, _ = act.shape
    for side in range(2):
        select_part[side] = dot(full_width(act, side), grad[side], (0, 0))
        wide = dot(grad[side], select[side], (1, 1))
        for t in range(tiles):
            lanes = lane_tile(t)
            total = grad_act[side, t] + wide[:, lanes]
            conv_grad[side, :, lanes] = total * silu_grad(pre[side, t])


def exit_kernel(conv_grad, before, after, conv_weight, tokens_grad, up, down):
    _, length, width = conv_grad.shape
    taps = conv_weight.shape[1]
    margin = taps - 1
    up[:length] = conv_grad[0]
    up[length:] = after[...]
    down[:HALO] = before[...]
    down[HALO:] = conv_grad[1]
    for t in range(width // LANES):
        lanes = lane_tile(t)
        total = jnp.zeros((length, LANES), jnp.float32)
        for k in range(taps):
            at = margin - k
            total = total + conv_weight[0, k : k + 1, lanes] * up[at : at + length, lanes]
            at = HALO - margin + k
            total = total + conv_weight[1, k : k + 1, lanes] * down[at : at + length, lanes]
        tokens_grad[:, lanes] = total


def from_before(value, axis):
    count = lax.axis_size(axis)
    return lax.ppermute(value, axis, [(i, i + 1) for i in range(count - 1)])


def from_after(value, axis):
    count = lax.axis_size(axis)
    return lax.ppermute(value, axis, [(i + 1, i) for i in range(count - 1)])


def summed_over(value, axis):
    count = lax.axis_size(axis)
    if count & (count - 1):
        return lax.psum(value, axis)
    by = 1
    while by < count:
        value = value + lax.ppermute(value, axis, [(i, i ^ by) for i in range(count)])
        by *= 2
    return value


def summed_in_shares(value, axis):
    count = lax.axis_size(axis)
    flat = value.reshape(count, -1, value.shape[-1])
    mine = lax.all_to_all(flat, axis, 0, 0)
    return lax.all_gather(jnp.sum(mine, axis=0), axis).reshape(value.shape)


def on_device(
    tokens, gate_input, cotangent, conv_weight, conv_bias, select_weight, step_weight,
    step_bias, decay_log, skip_gain,
):
    length, width = tokens.shape
    tiles = width // LANES
    states = decay_log.shape[1]
    ranks = step_weight.shape[1]
    count = length // CHAINS
    rows = 4 * states + 8
    narrow = shape_of(2, length, LANES)
    pair = shape_of(2, tiles, length, LANES)
    scratch = functools.partial(pltpu.VMEM, dtype=jnp.float32)
    bases = scratch((length, states * LANES))
    rate_scratch = scratch((2, tiles, states, LANES))
    row_scratch = scratch((states, CHAINS, LANES))

    before = from_before(tokens[length - HALO :], "ctx")
    after = from_after(tokens[:HALO], "ctx")
    partial, act, pre = pl.pallas_call(
        entry_kernel,
        out_shape=(narrow, pair, pair),
        scratch_shapes=[scratch((length + 2 * HALO, width))],
        compiler_params=params(32),
        name="entry",
    )(tokens, before, after, conv_weight, conv_bias, select_weight)
    gathered = lax.all_gather(partial, "ch")
    projection, step, step_pre, grad_gated, entering, carry = pl.pallas_call(
        local_kernel,
        out_shape=(
            narrow, pair, pair, shape_of(tiles, length, LANES),
            shape_of(4, tiles, states, CHAINS, LANES), shape_of(tiles, rows, LANES),
        ),
        scratch_shapes=[rate_scratch, bases, bases, row_scratch, bases],
        compiler_params=params(40),
        name="local",
    )(gathered, step_weight, step_bias, decay_log, act, gate_input, cotangent)
    carries = lax.all_gather(carry, "ctx")
    place = lax.axis_index("ctx").astype(jnp.int32).reshape(1)
    vmem = pl.BlockSpec(memory_space=pltpu.VMEM)
    block_out, gate_grad, partial_grad, step_part, grad_act = pl.pallas_call(
        scan_kernel,
        in_specs=[pl.BlockSpec(memory_space=pltpu.SMEM)] + [vmem] * 12,
        out_shape=(
            shape_of(length, width), shape_of(length, width), narrow,
            shape_of(2, ranks, width), pair,
        ),
        scratch_shapes=[
            rate_scratch, bases, bases, row_scratch, bases,
            scratch((count + 1, states, CHAINS, LANES)),
            scratch((4, tiles, states, LANES)),
            scratch((tiles, length, LANES)),
            bases, bases,
            scratch((tiles, length, LANES)),
            scratch((LANES, width)),
            scratch((length, LANES)),
        ],
        compiler_params=params(56),
        name="scan",
    )(
        place, carries, projection, step_weight, decay_log,
        skip_gain.reshape(2, tiles, 1, LANES), act, step, step_pre, grad_gated, entering,
        gate_input, cotangent,
    )
    step_grad = lax.psum(step_part, "ctx")
    grad_projection = summed_over(partial_grad, "ch")
    select_part, conv_grad = pl.pallas_call(
        weight_kernel,
        out_shape=(shape_of(2, width, LANES), shape_of(2, length, width)),
        compiler_params=params(32),
        name="weights",
    )(grad_projection, act, pre, grad_act, select_weight)
    before = from_before(conv_grad[1, length - HALO :], "ctx")
    after = from_after(conv_grad[0, :HALO], "ctx")
    tokens_grad = pl.pallas_call(
        exit_kernel,
        out_shape=shape_of(length, width),
        scratch_shapes=[scratch((length + HALO, width)), scratch((length + HALO, width))],
        compiler_params=params(32),
        name="exit",
    )(conv_grad, before, after, conv_weight)
    select_grad = summed_in_shares(select_part, "ctx")
    return (block_out, tokens_grad, gate_grad, select_grad, step_grad)


def solution(mesh):
    return jax.shard_map(
        on_device,
        mesh=mesh,
        in_specs=(
            P("ctx", "ch"),
            P("ctx", "ch"),
            P("ctx", "ch"),
            P(None, None, "ch"),
            P(None, "ch"),
            P(None, "ch", None),
            P(None, None, "ch"),
            P(None, "ch"),
            P(None, None, "ch"),
            P(None, "ch"),
        ),
        out_specs=(
            P("ctx", "ch"),
            P("ctx", "ch"),
            P("ctx", "ch"),
            P(None, "ch", None),
            P(None, None, "ch"),
        ),
        check_vma=False,
    )
```

```python
import functools

import jax
import jax.numpy as jnp
from jax import lax
from jax.experimental import pallas as pl
from jax.experimental.pallas import tpu as pltpu
from jax.sharding import PartitionSpec as P

FULL_PRECISION = lax.Precision.HIGHEST
LANES = 128
CHAINS = 8
HALO = 8
LOG2E = 1.4426950408889634
LN2 = 0.6931471805599453
MIB = 1024 * 1024


def params(mib):
    return pltpu.CompilerParams(vmem_limit_bytes=mib * MIB)


def shape_of(*dims):
    return jax.ShapeDtypeStruct(dims, jnp.float32)


def dot(a, b, contract):
    return lax.dot_general(
        a, b, ((contract[:1], contract[1:]), ((), ())), precision=FULL_PRECISION,
        preferred_element_type=jnp.float32,
    )


def silu_grad(values):
    sigmoid_values = jax.nn.sigmoid(values)
    return sigmoid_values * (1.0 + values * (1.0 - sigmoid_values))


def lane_tile(t):
    return slice(t * LANES, (t + 1) * LANES)


def full_width(ref, *lead):
    tiles = ref.shape[len(lead)]
    return jnp.concatenate([ref[(*lead, t)] for t in range(tiles)], axis=1)


def convolved(ext, at_row, side, lanes, rows, conv_weight, conv_bias):
    taps = conv_weight.shape[1]
    margin = taps - 1
    conv = jnp.broadcast_to(conv_bias[side : side + 1, lanes], (rows, LANES))
    for k in range(taps):
        at = at_row + (k - margin if side == 0 else margin - k)
        conv = conv + conv_weight[side, k : k + 1, lanes] * ext[at : at + rows, lanes]
    return conv


def entry_kernel(tokens, conv_weight, conv_bias, select, partial, act, pre, ext):
    length, width = tokens.shape
    shards, _, share, _ = partial.shape
    ext[:HALO] = jnp.zeros((HALO, width), jnp.float32)
    ext[HALO : HALO + length] = tokens[...]
    ext[HALO + length :] = jnp.zeros((HALO, width), jnp.float32)
    for side in range(2):
        for t in range(width // LANES):
            conv = convolved(ext, HALO, side, lane_tile(t), length, conv_weight, conv_bias)
            pre[side, t] = conv
            act[side, t] = conv * jax.nn.sigmoid(conv)
        whole = dot(full_width(act, side), select[side], (1, 0))
        for k in range(shards):
            partial[k, side] = whole[k * share : (k + 1) * share]


def edge_kernel(
    tokens, before, after, conv_weight, conv_bias, select, partial, act, pre,
    partial_new, edge_act, edge_pre, ext, rows,
):
    length, width = tokens.shape
    shards, _, share, _ = partial.shape
    partial_new[...] = partial[...]
    for side in range(2):
        if side == 0:
            ext[:HALO] = before[...]
            ext[HALO:] = tokens[:HALO]
        else:
            ext[:HALO] = tokens[length - HALO :]
            ext[HALO:] = after[...]
        at = HALO if side == 0 else 0
        for t in range(width // LANES):
            lanes = lane_tile(t)
            conv = convolved(ext, at, side, lanes, HALO, conv_weight, conv_bias)
            edge_pre[side, t] = conv
            value = conv * jax.nn.sigmoid(conv)
            edge_act[side, t] = value
            rows[:, lanes] = value
        new = dot(rows[...], select[side], (1, 0))
        if side == 0:
            partial_new[0, side, :HALO] = new
        else:
            partial_new[shards - 1, side, share - HALO :] = new


def with_edges(whole, edges, length):
    whole[0, :, :HALO, :] = edges[0]
    whole[1, :, length - HALO :, :] = edges[1]


def share_kernel(parts, out):
    total = parts[0]
    for k in range(1, parts.shape[0]):
        total = total + parts[k]
    for k in range(out.shape[0]):
        out[k] = total


def spread(projection, side, j, states, basis_b, basis_c):
    length = basis_b.shape[0]
    count = length // CHAINS
    rows = projection[side, pl.ds(j, CHAINS, stride=count), :]
    ranks = LANES - 2 * states
    at = pl.ds(pl.multiple_of(j * CHAINS, CHAINS), CHAINS)
    for n in range(states):
        b = rows[:, ranks + n : ranks + n + 1]
        c = rows[:, ranks + states + n : ranks + states + n + 1]
        basis_b[at, lane_tile(n)] = jnp.broadcast_to(b, (CHAINS, LANES))
        basis_c[at, lane_tile(n)] = jnp.broadcast_to(c, (CHAINS, LANES))


def fill_bases(projection, side, states, basis_b, basis_c):
    def body(j, carry):
        spread(projection, side, j, states, basis_b, basis_c)
        return carry

    lax.fori_loop(0, basis_b.shape[0] // CHAINS, body, 0)


def fill_rates(decay_log, rates):
    for side in range(rates.shape[0]):
        for t in range(rates.shape[1]):
            rates[side, t] = -LOG2E * jnp.exp(decay_log[side, :, lane_tile(t)])


def sublane():
    return lax.broadcasted_iota(jnp.int32, (CHAINS, LANES), 0)


def shifted(value, by, up):
    rolled = pltpu.roll(value, by if up else CHAINS - by, 0)
    place = sublane()
    keep = place >= by if up else place < CHAINS - by
    return jnp.where(keep, rolled, 0.0)


def over_chains(decays, ends, up):
    by = 1
    while by < CHAINS:
        ends = [d * shifted(f, by, up) + f for d, f in zip(decays, ends)]
        if 2 * by < CHAINS:
            turn = by if up else CHAINS - by
            decays = [d * pltpu.roll(d, turn, 0) for d in decays]
        by *= 2
    return ends


def order(i, count, up):
    return i if up else count - 1 - i


def tile_group(tiles):
    return 2 if tiles % 2 == 0 else 1


def unrolled(count, body, start):
    times = 2 if count % 2 == 0 else 1

    def several(i, state):
        for k in range(times):
            state = body(i * times + k, state)
        return state

    return lax.fori_loop(0, count // times, several, start)


def fill_rate_rows(rates, side, tiles, rate_rows):
    for g, t in enumerate(tiles):
        for n in range(rate_rows.shape[1]):
            rate_rows[g, n] = jnp.broadcast_to(rates[side, t, n : n + 1], (CHAINS, LANES))


def token_rows(j, count):
    return pl.ds(j, CHAINS, stride=count)


def cell_rows(j):
    return pl.ds(pl.multiple_of(j * CHAINS, CHAINS), CHAINS)


def local_kernel(
    gathered, step_weight, step_bias, decay_log, act_in, edge_act, gate, cot,
    projection, act, step, step_pre, grad_gated, entering, carry,
    rates, basis_b, basis_c, rate_rows, decays,
):
    sides, tiles, length, _ = act.shape
    states = decay_log.shape[1]
    ranks = step_weight.shape[1]
    count = length // CHAINS
    shards, _, share, _ = gathered.shape
    groups = carry.shape[0]
    each = states // groups
    group = tile_group(tiles)
    for k in range(shards):
        projection[:, k * share : (k + 1) * share] = gathered[k]
    act[...] = act_in[...]
    with_edges(act, edge_act, length)
    for t in range(tiles):
        lanes = lane_tile(t)
        values = gate[:, lanes]
        grad_gated[t] = cot[:, lanes] * values * jax.nn.sigmoid(values)
    fill_rates(decay_log, rates)
    for side in range(2):
        wide = dot(projection[side][:, :ranks], step_weight[side], (1, 0))
        wide = wide + step_bias[side : side + 1]
        for t in range(tiles):
            part = wide[:, lane_tile(t)]
            step_pre[side, t] = part
            step[side, t] = jnp.maximum(part, 0.0) + jnp.log1p(jnp.exp(-jnp.abs(part)))
    zero = jnp.zeros((CHAINS, LANES), jnp.float32)
    carry[...] = jnp.zeros_like(carry)
    for side in range(2):
        up = side == 0
        fill_bases(projection, side, states, basis_b, basis_c)

        def some_tiles(first, keep):
            at_tiles = [first * group + g for g in range(group)]
            fill_rate_rows(rates, side, at_tiles, rate_rows)

            def forward(i, current):
                state, summed = current
                j = order(i, count, up)
                rows, at = token_rows(j, count), cell_rows(j)
                steps = [step[side, t, rows, :] for t in at_tiles]
                drives = [v * act[side, t, rows, :] for v, t in zip(steps, at_tiles)]
                new = []
                for n in range(states):
                    lanes = lane_tile(n)
                    b = basis_b[at, lanes]
                    for g in range(group):
                        decay = jnp.exp2(steps[g] * rate_rows[g, n])
                        decays[g, at, lanes] = decay
                        new.append(decay * state[n * group + g] + b * drives[g])
                return (tuple(new), tuple(a + v for a, v in zip(summed, steps)))

            start = ((zero,) * (states * group), (zero,) * group)
            state, summed = unrolled(count, forward, start)

            def retreat(i, state):
                j = order(i, count, not up)
                rows, at = token_rows(j, count), cell_rows(j)
                grads = [grad_gated[t, rows, :] for t in at_tiles]
                new = []
                for n in range(states):
                    lanes = lane_tile(n)
                    c = basis_c[at, lanes]
                    for g in range(group):
                        adjoint = state[n * group + g] + c * grads[g]
                        new.append(decays[g, at, lanes] * adjoint)
                return tuple(new)

            sent = unrolled(count, retreat, (zero,) * (states * group))
            for g, t in enumerate(at_tiles):
                across = [jnp.exp2(summed[g] * rate_rows[g, n]) for n in range(states)]
                for kind, ends, upward in ((0, state, up), (1, sent, not up)):
                    slot = 2 * side + kind
                    ends = over_chains(across, list(ends[g::group]), upward)
                    last = CHAINS - 1 if upward else 0
                    for n in range(states):
                        entering[slot, t, n] = shifted(ends[n], 1, upward)
                        at = slot * each + n % each
                        carry[n // each, t, at : at + 1] = ends[n][last : last + 1]
                whole = jnp.sum(summed[g], axis=0, keepdims=True)
                at = 4 * each + side
                for k in range(groups):
                    carry[k, t, at : at + 1] = whole
            return keep

        lax.fori_loop(0, tiles // group, some_tiles, 0)


def chain_kernel(carries, decay_rows, out, rates):
    shards, tiles, _, _ = carries.shape
    rows = out.shape[2]
    each = rows // 4
    for t in range(tiles):
        rates[t] = -LOG2E * jnp.exp(decay_rows[:, lane_tile(t)])
    row = lax.broadcasted_iota(jnp.int32, (tiles, rows, LANES), 1)
    upward = (row < each) | (row >= 3 * each)

    def turn(i, state, up):
        k = order(i, shards, up)
        if up:
            out[k] = state
        else:
            out[k] = jnp.where(upward, out[k], state)
        first_sum = carries[k, :, rows : rows + 1, :]
        second_sum = carries[k, :, rows + 1 : rows + 2, :]
        decay = jnp.exp2(rates[...] * jnp.where(row < 2 * each, first_sum, second_sum))
        return decay * state + carries[k, :, :rows, :]

    for up in (True, False):
        state = jnp.zeros((tiles, rows, LANES), jnp.float32)
        if shards <= 8:
            for i in range(shards):
                state = turn(i, state, up)
        else:
            lax.fori_loop(0, shards, functools.partial(turn, up=up), state)


def scan_kernel(
    incoming, projection, step_weight, decay_log, skip_gain, act, step, step_pre,
    grad_gated, entering, gate, cot,
    block_out, gate_grad, partial, step_part, grad_act,
    rates, basis_b, basis_c, rate_rows, decays, history, summed_out,
    grad_in, grad_out, grad_pre, weights, packed,
):
    sides, tiles, length, _ = act.shape
    states = decay_log.shape[1]
    ranks = step_weight.shape[1]
    count = length // CHAINS
    each = states // incoming.shape[0]
    shards, _, share, _ = partial.shape
    group = tile_group(tiles)
    fill_rates(decay_log, rates)
    zero = jnp.zeros((CHAINS, LANES), jnp.float32)
    column = lax.broadcasted_iota(jnp.int32, (CHAINS, LANES), 1)
    for side in range(2):
        up = side == 0
        fill_bases(projection, side, states, basis_b, basis_c)
        grad_in[...] = jnp.zeros_like(grad_in)
        grad_out[...] = jnp.zeros_like(grad_out)

        def some_tiles(first, keep):
            at_tiles = [first * group + g for g in range(group)]
            fill_rate_rows(rates, side, at_tiles, rate_rows)
            skips = [skip_gain[side, t] for t in at_tiles]
            sums = []
            for t in at_tiles:
                summed = step[side, t, token_rows(0, count), :]
                for j in range(1, count):
                    summed = summed + step[side, t, token_rows(j, count), :]
                sums.append(summed)

            def start(kind, upward):
                slot = 2 * side + kind
                spans = []
                for g in range(group):
                    span = shifted(sums[g], 1, upward)
                    by = 1
                    while by < CHAINS:
                        span = span + shifted(span, by, upward)
                        by *= 2
                    spans.append(span)
                first = []
                for n in range(states):
                    at = slot * each + n % each
                    for g, t in enumerate(at_tiles):
                        decay = jnp.exp2(spans[g] * rate_rows[g, n])
                        value = incoming[n // each, t, at : at + 1, :]
                        first.append(entering[slot, t, n] + decay * value)
                return tuple(first)

            def forward(i, state):
                j = order(i, count, up)
                rows, at = token_rows(j, count), cell_rows(j)
                steps = [step[side, t, rows, :] for t in at_tiles]
                acts = [act[side, t, rows, :] for t in at_tiles]
                grads = [grad_gated[t, rows, :] for t in at_tiles]
                drives = [v * a for v, a in zip(steps, acts)]
                outs = [v * a for v, a in zip(skips, acts)]
                new = []
                for n in range(states):
                    lanes = lane_tile(n)
                    b, c = basis_b[at, lanes], basis_c[at, lanes]
                    read = grad_out[at, lanes]
                    for g in range(group):
                        before = state[n * group + g]
                        decay = jnp.exp2(steps[g] * rate_rows[g, n])
                        decays[g, at, lanes] = decay
                        history[g, at, lanes] = before
                        current = decay * before + b * drives[g]
                        outs[g] = outs[g] + c * current
                        read = read + current * grads[g]
                        new.append(current)
                    grad_out[at, lanes] = read
                for g, t in enumerate(at_tiles):
                    if side == 0:
                        summed_out[t, rows, :] = outs[g]
                    else:
                        summed_out[t, rows, :] = summed_out[t, rows, :] + outs[g]
                return tuple(new)

            unrolled(count, forward, start(0, up))

            def retreat(i, state):
                j = order(i, count, not up)
                rows, at = token_rows(j, count), cell_rows(j)
                steps = [step[side, t, rows, :] for t in at_tiles]
                acts = [act[side, t, rows, :] for t in at_tiles]
                grads = [grad_gated[t, rows, :] for t in at_tiles]
                drives = [v * a for v, a in zip(steps, acts)]
                step_terms = [zero] * group
                drive_grads = [zero] * group
                new = []
                for n in range(states):
                    lanes = lane_tile(n)
                    b, c = basis_b[at, lanes], basis_c[at, lanes]
                    put = grad_in[at, lanes]
                    for g in range(group):
                        adjoint = state[n * group + g] + c * grads[g]
                        carried = decays[g, at, lanes] * adjoint
                        new.append(carried)
                        term = carried * history[g, at, lanes] * rate_rows[g, n]
                        step_terms[g] = step_terms[g] + term
                        drive_grads[g] = drive_grads[g] + adjoint * b
                        put = put + adjoint * drives[g]
                    grad_in[at, lanes] = put
                for g, t in enumerate(at_tiles):
                    grad_step = step_terms[g] * LN2 + drive_grads[g] * acts[g]
                    grad_act[side, t, rows, :] = grads[g] * skips[g] + drive_grads[g] * steps[g]
                    pre = step_pre[side, t, rows, :]
                    grad_pre[t, rows, :] = grad_step * jax.nn.sigmoid(pre)
                return tuple(new)

            unrolled(count, retreat, start(1, not up))
            return keep

        lax.fori_loop(0, tiles // group, some_tiles, 0)
        wide = full_width(grad_pre)
        weights[...] = jnp.zeros_like(weights)
        weights[:ranks] = step_weight[side]
        step_part[side] = dot(projection[side], wide, (0, 0))[:ranks]
        packed[...] = dot(wide, weights[...], (1, 1))

        def pack(j, keep):
            rows, at = token_rows(j, count), cell_rows(j)
            line = packed[rows, :]
            for values, start_at in ((grad_in, ranks), (grad_out, ranks + states)):
                for n in range(states):
                    total = jnp.sum(values[at, lane_tile(n)], axis=1, keepdims=True)
                    line = jnp.where(column == start_at + n, total, line)
            packed[rows, :] = line
            return keep

        lax.fori_loop(0, count, pack, 0)
        for k in range(shards):
            partial[k, side] = packed[k * share : (k + 1) * share]
    for t in range(tiles):
        lanes = lane_tile(t)
        values = gate[:, lanes]
        block_out[:, lanes] = summed_out[t] * values * jax.nn.sigmoid(values)
        gate_grad[:, lanes] = cot[:, lanes] * summed_out[t] * silu_grad(values)


def weight_kernel(
    gathered, act, pre_in, edge_pre, grad_act, select, select_part, conv_grad, grad, pre,
):
    sides, tiles, length, _ = act.shape
    shards, _, share, _ = gathered.shape
    for k in range(shards):
        grad[:, k * share : (k + 1) * share] = gathered[k]
    pre[...] = pre_in[...]
    with_edges(pre, edge_pre, length)
    for side in range(2):
        select_part[side] = dot(full_width(act, side), grad[side], (0, 0))
        wide = dot(grad[side], select[side], (1, 1))
        for t in range(tiles):
            lanes = lane_tile(t)
            total = grad_act[side, t] + wide[:, lanes]
            conv_grad[side, :, lanes] = total * silu_grad(pre[side, t])


def exit_kernel(conv_grad, before, after, conv_weight, tokens_grad, up, down):
    _, length, width = conv_grad.shape
    taps = conv_weight.shape[1]
    margin = taps - 1
    up[:length] = conv_grad[0]
    up[length:] = after[...]
    down[:HALO] = before[...]
    down[HALO:] = conv_grad[1]
    for t in range(width // LANES):
        lanes = lane_tile(t)
        total = jnp.zeros((length, LANES), jnp.float32)
        for k in range(taps):
            at = margin - k
            total = total + conv_weight[0, k : k + 1, lanes] * up[at : at + length, lanes]
            at = HALO - margin + k
            total = total + conv_weight[1, k : k + 1, lanes] * down[at : at + length, lanes]
        tokens_grad[:, lanes] = total


def from_before(value, axis):
    count = lax.axis_size(axis)
    return lax.ppermute(value, axis, [(i, i + 1) for i in range(count - 1)])


def from_after(value, axis):
    count = lax.axis_size(axis)
    return lax.ppermute(value, axis, [(i + 1, i) for i in range(count - 1)])


def exchanged(parts, axis):
    return lax.all_to_all(parts, axis, 0, 0)


def share_sum(parts, copies, name):
    return pl.pallas_call(
        share_kernel,
        out_shape=shape_of(copies, *parts.shape[1:]),
        compiler_params=params(8),
        name=name,
    )(parts)


def on_device(
    tokens, gate_input, cotangent, conv_weight, conv_bias, select_weight, step_weight,
    step_bias, decay_log, skip_gain,
):
    length, width = tokens.shape
    tiles = width // LANES
    states = decay_log.shape[1]
    ranks = step_weight.shape[1]
    columns = lax.axis_size("ch")
    places = lax.axis_size("ctx")
    place = lax.axis_index("ctx").astype(jnp.int32)
    group = tile_group(tiles)
    groups = places if states % places == 0 else 1
    each = states // groups
    carry_rows = -(-(4 * each + 2) // 8) * 8
    shared = shape_of(columns, 2, length // columns, LANES)
    narrow = shape_of(2, length, LANES)
    pair = shape_of(2, tiles, length, LANES)
    edge = shape_of(2, tiles, HALO, LANES)
    scratch = functools.partial(pltpu.VMEM, dtype=jnp.float32)
    bases = scratch((length, states * LANES))
    grouped = scratch((group, length, states * LANES))
    rate_scratch = scratch((2, tiles, states, LANES))
    row_scratch = scratch((group, states, CHAINS, LANES))

    first = place * each if groups > 1 else 0
    decay_rows = lax.dynamic_slice_in_dim(decay_log, first, each, 1)
    decay_rows = jnp.repeat(decay_rows, 2, axis=0).reshape(4 * each, width)
    before = from_before(tokens[length - HALO :], "ctx")
    after = from_after(tokens[:HALO], "ctx")
    partial, act, pre = pl.pallas_call(
        entry_kernel,
        out_shape=(shared, pair, pair),
        scratch_shapes=[scratch((length + 2 * HALO, width))],
        compiler_params=params(12),
        cost_estimate=pl.CostEstimate(flops=2**28, bytes_accessed=2**22, transcendentals=2**18),
        name="entry",
    )(tokens, conv_weight, conv_bias, select_weight)
    partial, edge_act, edge_pre = pl.pallas_call(
        edge_kernel,
        out_shape=(shared, edge, edge),
        scratch_shapes=[scratch((2 * HALO, width)), scratch((HALO, width))],
        compiler_params=params(10),
        name="edges",
    )(tokens, before, after, conv_weight, conv_bias, select_weight, partial, act, pre)
    gathered = exchanged(share_sum(exchanged(partial, "ch"), columns, "projected"), "ch")
    projection, act, step, step_pre, grad_gated, entering, carry = pl.pallas_call(
        local_kernel,
        out_shape=(
            narrow, pair, pair, pair, shape_of(tiles, length, LANES),
            shape_of(4, tiles, states, CHAINS, LANES),
            shape_of(groups, tiles, carry_rows, LANES),
        ),
        scratch_shapes=[rate_scratch, bases, bases, row_scratch, grouped],
        compiler_params=params(20),
        name="local",
    )(gathered, step_weight, step_bias, decay_log, act, edge_act, gate_input, cotangent)
    if groups > 1:
        carries = exchanged(carry, "ctx")
    else:
        carries = lax.all_gather(carry[0], "ctx")
    incoming = pl.pallas_call(
        chain_kernel,
        out_shape=shape_of(places, tiles, 4 * each, LANES),
        scratch_shapes=[scratch((tiles, 4 * each, LANES))],
        compiler_params=params(8 if groups > 1 else 48),
        name="chain",
    )(carries, decay_rows)
    if groups > 1:
        incoming = exchanged(incoming, "ctx")
    else:
        incoming = lax.dynamic_slice_in_dim(incoming, place, 1, 0)
    block_out, gate_grad, partial_grad, step_part, grad_act = pl.pallas_call(
        scan_kernel,
        out_shape=(
            shape_of(length, width), shape_of(length, width), shared,
            shape_of(2, ranks, width), pair,
        ),
        scratch_shapes=[
            rate_scratch, bases, bases, row_scratch, grouped, grouped,
            scratch((tiles, length, LANES)),
            bases, bases,
            scratch((tiles, length, LANES)),
            scratch((LANES, width)),
            scratch((length, LANES)),
        ],
        compiler_params=params(28),
        name="scan",
    )(
        incoming, projection, step_weight, decay_log, skip_gain.reshape(2, tiles, 1, LANES),
        act, step, step_pre, grad_gated, entering, gate_input, cotangent,
    )
    if (2 * ranks) % (8 * places) == 0:
        step_shares = step_part.reshape(places, -1, width)
        step_sum = share_sum(exchanged(step_shares, "ctx"), places, "step_sum")
        step_grad = exchanged(step_sum, "ctx").reshape(2, ranks, width)
    else:
        step_grad = lax.psum(step_part, "ctx")
    grad_sum = share_sum(exchanged(partial_grad, "ch"), 1, "grad_sum")
    gathered_grad = lax.all_gather(grad_sum[0], "ch")
    select_part, conv_grad = pl.pallas_call(
        weight_kernel,
        out_shape=(shape_of(2, width, LANES), shape_of(2, length, width)),
        scratch_shapes=[scratch(narrow.shape), scratch(pair.shape)],
        compiler_params=params(14),
        name="weights",
    )(gathered_grad, act, pre, edge_pre, grad_act, select_weight)
    before = from_before(conv_grad[1, length - HALO :], "ctx")
    after = from_after(conv_grad[0, :HALO], "ctx")
    select_shares = exchanged(select_part.reshape(places, -1, LANES), "ctx")
    tokens_grad = pl.pallas_call(
        exit_kernel,
        out_shape=shape_of(length, width),
        scratch_shapes=[scratch((length + HALO, width)), scratch((length + HALO, width))],
        compiler_params=params(8),
        name="exit",
    )(conv_grad, before, after, conv_weight)
    select_sum = share_sum(select_shares, 1, "select_sum")
    select_grad = lax.all_gather(select_sum[0], "ctx").reshape(2, width, LANES)
    return (block_out, tokens_grad, gate_grad, select_grad, step_grad)


def solution(mesh):
    return jax.shard_map(
        on_device,
        mesh=mesh,
        in_specs=(
            P("ctx", "ch"),
            P("ctx", "ch"),
            P("ctx", "ch"),
            P(None, None, "ch"),
            P(None, "ch"),
            P(None, "ch", None),
            P(None, None, "ch"),
            P(None, "ch"),
            P(None, None, "ch"),
            P(None, "ch"),
        ),
        out_specs=(
            P("ctx", "ch"),
            P("ctx", "ch"),
            P("ctx", "ch"),
            P(None, "ch", None),
            P(None, None, "ch"),
        ),
        check_vma=False,
    )
```

```python
import functools

import jax
import jax.numpy as jnp
from jax import lax
from jax.experimental import pallas as pl
from jax.experimental.pallas import tpu as pltpu
from jax.sharding import PartitionSpec as P

FULL_PRECISION = lax.Precision.HIGHEST
LANES = 128
CHAINS = 8
HALO = 8
MIB = 1024 * 1024


def params(mib):
    return pltpu.CompilerParams(vmem_limit_bytes=mib * MIB)


def shape_of(*dims):
    return jax.ShapeDtypeStruct(dims, jnp.float32)


def dot(a, b, contract):
    return lax.dot_general(
        a, b, ((contract[:1], contract[1:]), ((), ())), precision=FULL_PRECISION,
        preferred_element_type=jnp.float32,
    )


def silu_grad(values):
    sigmoid_values = jax.nn.sigmoid(values)
    return sigmoid_values * (1.0 + values * (1.0 - sigmoid_values))


def lane_tile(t):
    return slice(t * LANES, (t + 1) * LANES)


def full_width(ref, *lead):
    tiles = ref.shape[len(lead)]
    return jnp.concatenate([ref[(*lead, t)] for t in range(tiles)], axis=1)


def convolved(ext, at_row, side, lanes, rows, conv_weight, conv_bias):
    taps = conv_weight.shape[1]
    margin = taps - 1
    conv = jnp.broadcast_to(conv_bias[side : side + 1, lanes], (rows, LANES))
    for k in range(taps):
        at = at_row + (k - margin if side == 0 else margin - k)
        conv = conv + conv_weight[side, k : k + 1, lanes] * ext[at : at + rows, lanes]
    return conv


def copies_of(pairs, sems):
    copies = [pltpu.make_async_copy(a, b, sems.at[i]) for i, (a, b) in enumerate(pairs)]
    for copy in copies:
        copy.start()
    return copies


def finish_all(copies):
    for copy in copies:
        copy.wait()


def entry_kernel(
    before, after, tokens, conv_weight_in, conv_bias_in, select_in,
    partial, act_out, pre_out,
    ext, conv_weight, conv_bias, select, act, pre, sems,
):
    length, width = tokens.shape
    loads = copies_of(
        [
            (tokens, ext.at[pl.ds(HALO, length)]), (conv_weight_in, conv_weight),
            (conv_bias_in, conv_bias), (select_in, select),
        ],
        sems,
    )
    ext[:HALO] = before[...]
    ext[HALO + length :] = after[...]
    finish_all(loads[:3])
    for side in range(2):
        for t in range(width // LANES):
            conv = convolved(ext, HALO, side, lane_tile(t), length, conv_weight, conv_bias)
            pre[side, t] = conv
            act[side, t] = conv * jax.nn.sigmoid(conv)
    stores = copies_of([(pre, pre_out), (act, act_out)], sems.at[pl.ds(4, 2)])
    loads[3].wait()
    for side in range(2):
        partial[side] = dot(full_width(act, side), select[side], (1, 0))
    finish_all(stores)


def spread(projection, side, j, states, basis_b, basis_c):
    length = basis_b.shape[0]
    count = length // CHAINS
    rows = projection[side, pl.ds(j, CHAINS, stride=count), :]
    ranks = LANES - 2 * states
    at = pl.ds(pl.multiple_of(j * CHAINS, CHAINS), CHAINS)
    for n in range(states):
        b = rows[:, ranks + n : ranks + n + 1]
        c = rows[:, ranks + states + n : ranks + states + n + 1]
        basis_b[at, lane_tile(n)] = jnp.broadcast_to(b, (CHAINS, LANES))
        basis_c[at, lane_tile(n)] = jnp.broadcast_to(c, (CHAINS, LANES))


def fill_bases(projection, side, states, basis_b, basis_c):
    def body(j, carry):
        spread(projection, side, j, states, basis_b, basis_c)
        return carry

    lax.fori_loop(0, basis_b.shape[0] // CHAINS, body, 0)


def fill_rates(decay_log, rates):
    for side in range(rates.shape[0]):
        for t in range(rates.shape[1]):
            rates[side, t] = -jnp.exp(decay_log[side, :, lane_tile(t)])


def sublane():
    return lax.broadcasted_iota(jnp.int32, (CHAINS, LANES), 0)


def shifted(value, by, up):
    rolled = pltpu.roll(value, by if up else CHAINS - by, 0)
    place = sublane()
    keep = place >= by if up else place < CHAINS - by
    return jnp.where(keep, rolled, 0.0)


def over_chains(decays, ends, up):
    by = 1
    while by < CHAINS:
        ends = [d * shifted(f, by, up) + f for d, f in zip(decays, ends)]
        if 2 * by < CHAINS:
            turn = by if up else CHAINS - by
            decays = [d * pltpu.roll(d, turn, 0) for d in decays]
        by *= 2
    return ends


def order(i, count, up):
    return i if up else count - 1 - i


def tile_group(tiles):
    return 2 if tiles % 2 == 0 else 1


def unrolled(count, body, start):
    times = 2 if count % 2 == 0 else 1

    def several(i, state):
        for k in range(times):
            state = body(i * times + k, state)
        return state

    return lax.fori_loop(0, count // times, several, start)


def fill_rate_rows(rates, side, tiles, rate_rows):
    for g, t in enumerate(tiles):
        for n in range(rate_rows.shape[1]):
            rate_rows[g, n] = jnp.broadcast_to(rates[side, t, n : n + 1], (CHAINS, LANES))


def token_rows(j, count):
    return pl.ds(j, CHAINS, stride=count)


def cell_rows(j):
    return pl.ds(pl.multiple_of(j * CHAINS, CHAINS), CHAINS)


def local_kernel(
    own, first, second, third, step_weight_in, step_bias_in, decay_log_in, act_in, gate_in, cot_in,
    projection_out, step_out, step_pre_out, grad_gated_out, entering_out, carry,
    projection, act, step, step_pre, grad_gated, entering, step_weight, step_bias, decay_log,
    gate, cot, rates, basis_b, basis_c, rate_rows, decays, sems,
):
    sides, tiles, length, _ = act.shape
    states = decay_log.shape[1]
    ranks = step_weight.shape[1]
    count = length // CHAINS
    group = tile_group(tiles)
    loads = copies_of(
        [
            (step_weight_in, step_weight), (step_bias_in, step_bias), (decay_log_in, decay_log),
            (gate_in, gate), (cot_in, cot), (act_in, act),
        ],
        sems,
    )
    projection[...] = (own[...] + first[...]) + (second[...] + third[...])
    finish_all(loads)
    for t in range(tiles):
        lanes = lane_tile(t)
        values = gate[:, lanes]
        grad_gated[t] = cot[:, lanes] * values * jax.nn.sigmoid(values)
    fill_rates(decay_log, rates)
    for side in range(2):
        wide = dot(projection[side][:, :ranks], step_weight[side], (1, 0))
        wide = wide + step_bias[side : side + 1]
        for t in range(tiles):
            part = wide[:, lane_tile(t)]
            step_pre[side, t] = part
            step[side, t] = jnp.maximum(part, 0.0) + jnp.log1p(jnp.exp(-jnp.abs(part)))
    stores = copies_of(
        [
            (projection, projection_out), (step, step_out), (step_pre, step_pre_out),
            (grad_gated, grad_gated_out),
        ],
        sems,
    )
    zero = jnp.zeros((CHAINS, LANES), jnp.float32)
    carry[...] = jnp.zeros_like(carry)
    for side in range(2):
        up = side == 0
        fill_bases(projection, side, states, basis_b, basis_c)

        def some_tiles(first, keep):
            at_tiles = [first * group + g for g in range(group)]
            fill_rate_rows(rates, side, at_tiles, rate_rows)

            def forward(i, current):
                state, summed = current
                j = order(i, count, up)
                rows, at = token_rows(j, count), cell_rows(j)
                steps = [step[side, t, rows, :] for t in at_tiles]
                drives = [v * act[side, t, rows, :] for v, t in zip(steps, at_tiles)]
                new = []
                for n in range(states):
                    lanes = lane_tile(n)
                    b = basis_b[at, lanes]
                    for g in range(group):
                        decay = jnp.exp(steps[g] * rate_rows[g, n])
                        decays[g, at, lanes] = decay
                        new.append(decay * state[n * group + g] + b * drives[g])
                return (tuple(new), tuple(a + v for a, v in zip(summed, steps)))

            start = ((zero,) * (states * group), (zero,) * group)
            state, summed = unrolled(count, forward, start)

            def retreat(i, state):
                j = order(i, count, not up)
                rows, at = token_rows(j, count), cell_rows(j)
                grads = [grad_gated[t, rows, :] for t in at_tiles]
                new = []
                for n in range(states):
                    lanes = lane_tile(n)
                    c = basis_c[at, lanes]
                    for g in range(group):
                        adjoint = state[n * group + g] + c * grads[g]
                        new.append(decays[g, at, lanes] * adjoint)
                return tuple(new)

            sent = unrolled(count, retreat, (zero,) * (states * group))
            for g, t in enumerate(at_tiles):
                across = [jnp.exp(summed[g] * rate_rows[g, n]) for n in range(states)]
                for kind, ends, upward in ((0, state, up), (1, sent, not up)):
                    slot = 2 * side + kind
                    ends = over_chains(across, list(ends[g::group]), upward)
                    last = CHAINS - 1 if upward else 0
                    for n in range(states):
                        entering[slot, t, n] = shifted(ends[n], 1, upward)
                        at = side * states + n
                        carry[0 if upward else 1, t, at : at + 1] = ends[n][last : last + 1]
                whole = jnp.sum(summed[g], axis=0, keepdims=True)
                at = 2 * states + side
                for k in range(2):
                    carry[k, t, at : at + 1] = whole
            return keep

        lax.fori_loop(0, tiles // group, some_tiles, 0)
    stores = stores + copies_of([(entering, entering_out)], sems.at[pl.ds(4, 1)])
    finish_all(stores)


def fill_row_rates(decay_log, rates):
    for side in range(2):
        states = decay_log.shape[1]
        for t in range(rates.shape[0]):
            value = -jnp.exp(decay_log[side, :, lane_tile(t)])
            rates[t, side * states : (side + 1) * states] = value


def tile_decay(part, rates):
    rows = rates.shape[1]
    row = lax.broadcasted_iota(jnp.int32, rates.shape, 1)
    sums = jnp.where(row < rows // 2, part[:, rows : rows + 1], part[:, rows + 1 : rows + 2])
    return jnp.exp(rates * sums)


def pair_kernel(place, mine, other, decay_log, *refs):
    outs, (rates, total) = refs[:-2], refs[-2:]
    rows = rates.shape[1]
    fill_row_rates(decay_log, rates)
    core, chip = lax.rem(place[0], 2), lax.div(place[0], 2)
    low = jnp.where(core == 0, mine[...], other[...])
    high = jnp.where(core == 0, other[...], mine[...])
    spread_rates = rates[...]
    decay_low = tile_decay(low[0], spread_rates)
    decay_high = tile_decay(high[0], spread_rates)
    total[...] = low + high
    total[0, :, :rows] = decay_high * low[0][:, :rows] + high[0][:, :rows]
    total[1, :, :rows] = decay_low * high[1][:, :rows] + low[1][:, :rows]
    for s, out in enumerate(outs, 1):
        below = lax.convert_element_type((chip ^ s) < chip, jnp.int32)
        out[...] = total[below]


def chain_kernel(place, other, decay_log, *refs):
    gathered, (out, rates, parts) = refs[:-3], refs[-3:]
    rows = rates.shape[1]
    chips = parts.shape[0]
    fill_row_rates(decay_log, rates)
    core, chip = lax.rem(place[0], 2), lax.div(place[0], 2)
    parts[chip] = jnp.zeros(parts.shape[1:], jnp.float32)
    for s, part in enumerate(gathered, 1):
        parts[chip ^ s] = part[...]
    spread_rates = rates[...]
    for kind in range(2):
        state = jnp.zeros(rates.shape, jnp.float32)
        for k in range(chips) if kind == 0 else reversed(range(chips)):
            part = parts[k]
            new = tile_decay(part, spread_rates) * state + part[:, :rows]
            state = jnp.where(k < chip if kind == 0 else k > chip, new, state)
        part = other[kind]
        new = tile_decay(part, spread_rates) * state + part[:, :rows]
        out[kind] = jnp.where(core == 1 - kind, new, state)


def long_chain_kernel(place, gathered, decay_log, out, rates):
    rows = rates.shape[1]
    shards = gathered.shape[0]
    fill_row_rates(decay_log, rates)
    for kind in range(2):

        def turn(i, state):
            part = gathered[order(i, shards, kind == 0), kind]
            return tile_decay(part, rates[...]) * state + part[:, :rows]

        turns = place[0] if kind == 0 else shards - 1 - place[0]
        out[kind] = lax.fori_loop(0, turns, turn, jnp.zeros(rates.shape, jnp.float32))


def scan_kernel(
    incoming, projection_in, step_weight_in, decay_log_in, skip_gain_in, act_in, step_in,
    step_pre_in, grad_gated_in, entering_in,
    partial, grad_act_out, grad_pre_out, summed_outs,
    projection, step_weight, decay_log, skip_gain, act, step, step_pre, grad_gated, entering,
    grad_act, grad_pre, summed_out, rates, basis_b, basis_c, rate_rows, history,
    grad_in, grad_out, weights, packed, sems,
):
    sides, tiles, length, _ = act.shape
    states = decay_log.shape[1]
    ranks = step_weight.shape[1]
    count = length // CHAINS
    group = tile_group(tiles)
    loads = copies_of(
        [
            (projection_in, projection), (decay_log_in, decay_log), (step_in, step),
            (act_in, act), (grad_gated_in, grad_gated), (entering_in, entering),
            (skip_gain_in, skip_gain), (step_pre_in, step_pre), (step_weight_in, step_weight),
        ],
        sems,
    )
    stores = []
    finish_all(loads[:2])
    fill_rates(decay_log, rates)
    zero = jnp.zeros((CHAINS, LANES), jnp.float32)
    column = lax.broadcasted_iota(jnp.int32, (CHAINS, LANES), 1)
    for side in range(2):
        up = side == 0
        fill_bases(projection, side, states, basis_b, basis_c)
        grad_in[...] = jnp.zeros_like(grad_in)
        grad_out[...] = jnp.zeros_like(grad_out)
        if side == 0:
            finish_all(loads[2:])

        def some_tiles(first, keep):
            at_tiles = [first * group + g for g in range(group)]
            fill_rate_rows(rates, side, at_tiles, rate_rows)
            skips = [skip_gain[side, t] for t in at_tiles]
            sums = []
            for t in at_tiles:
                summed = step[side, t, token_rows(0, count), :]
                for j in range(1, count):
                    summed = summed + step[side, t, token_rows(j, count), :]
                sums.append(summed)

            def start(kind, upward):
                slot = 2 * side + kind
                spans = []
                for g in range(group):
                    span = shifted(sums[g], 1, upward)
                    by = 1
                    while by < CHAINS:
                        span = span + shifted(span, by, upward)
                        by *= 2
                    spans.append(span)
                first = []
                for n in range(states):
                    at = side * states + n
                    for g, t in enumerate(at_tiles):
                        decay = jnp.exp(spans[g] * rate_rows[g, n])
                        value = incoming[0 if upward else 1, t, at : at + 1, :]
                        first.append(entering[slot, t, n] + decay * value)
                return tuple(first)

            def forward(i, state):
                j = order(i, count, up)
                rows, at = token_rows(j, count), cell_rows(j)
                steps = [step[side, t, rows, :] for t in at_tiles]
                acts = [act[side, t, rows, :] for t in at_tiles]
                grads = [grad_gated[t, rows, :] for t in at_tiles]
                drives = [v * a for v, a in zip(steps, acts)]
                outs = [v * a for v, a in zip(skips, acts)]
                new = []
                for n in range(states):
                    lanes = lane_tile(n)
                    b, c = basis_b[at, lanes], basis_c[at, lanes]
                    read = grad_out[at, lanes]
                    for g in range(group):
                        before = state[n * group + g]
                        decay = jnp.exp(steps[g] * rate_rows[g, n])
                        history[g, at, lanes] = before
                        current = decay * before + b * drives[g]
                        outs[g] = outs[g] + c * current
                        read = read + current * grads[g]
                        new.append(current)
                    grad_out[at, lanes] = read
                for g, t in enumerate(at_tiles):
                    if side == 0:
                        summed_out[t, rows, :] = outs[g]
                    else:
                        summed_out[t, rows, :] = summed_out[t, rows, :] + outs[g]
                return tuple(new)

            unrolled(count, forward, start(0, up))

            def retreat(i, state):
                j = order(i, count, not up)
                rows, at = token_rows(j, count), cell_rows(j)
                steps = [step[side, t, rows, :] for t in at_tiles]
                acts = [act[side, t, rows, :] for t in at_tiles]
                grads = [grad_gated[t, rows, :] for t in at_tiles]
                drives = [v * a for v, a in zip(steps, acts)]
                step_terms = [zero] * group
                drive_grads = [zero] * group
                new = []
                for n in range(states):
                    lanes = lane_tile(n)
                    b, c = basis_b[at, lanes], basis_c[at, lanes]
                    put = grad_in[at, lanes]
                    for g in range(group):
                        adjoint = state[n * group + g] + c * grads[g]
                        rate = rate_rows[g, n]
                        carried = jnp.exp(steps[g] * rate) * adjoint
                        new.append(carried)
                        term = carried * history[g, at, lanes] * rate
                        step_terms[g] = step_terms[g] + term
                        drive_grads[g] = drive_grads[g] + adjoint * b
                        put = put + adjoint * drives[g]
                    grad_in[at, lanes] = put
                for g, t in enumerate(at_tiles):
                    grad_step = step_terms[g] + drive_grads[g] * acts[g]
                    grad_act[side, t, rows, :] = grads[g] * skips[g] + drive_grads[g] * steps[g]
                    pre = step_pre[side, t, rows, :]
                    grad_pre[side, t, rows, :] = grad_step * jax.nn.sigmoid(pre)
                return tuple(new)

            unrolled(count, retreat, start(1, not up))
            return keep

        lax.fori_loop(0, tiles // group, some_tiles, 0)
        pairs = [
            (grad_act.at[side], grad_act_out.at[side]), (grad_pre.at[side], grad_pre_out.at[side]),
        ]
        if side == 1:
            pairs.append((summed_out, summed_outs))
        stores = stores + copies_of(pairs, sems.at[pl.ds(2 * side, 3)])
        wide = full_width(grad_pre, side)
        weights[...] = jnp.zeros_like(weights)
        weights[:ranks] = step_weight[side]
        packed[...] = dot(wide, weights[...], (1, 1))

        def pack(j, keep):
            rows, at = token_rows(j, count), cell_rows(j)
            line = packed[rows, :]
            for values, start_at in ((grad_in, ranks), (grad_out, ranks + states)):
                for n in range(states):
                    total = jnp.sum(values[at, lane_tile(n)], axis=1, keepdims=True)
                    line = jnp.where(column == start_at + n, total, line)
            packed[rows, :] = line
            return keep

        lax.fori_loop(0, count, pack, 0)
        partial[side] = packed[...]
    finish_all(stores)


def outer_kernel(
    summed_in, gate_in, cot_in, grad_pre_in, projection_in, block_out, gate_grad, step_part,
    summed, gate, cot, grad_pre, projection, sems,
):
    tiles = summed.shape[0]
    ranks = step_part.shape[2]
    loads = copies_of(
        [
            (summed_in, summed), (gate_in, gate), (cot_in, cot), (grad_pre_in, grad_pre),
            (projection_in, projection),
        ],
        sems,
    )
    finish_all(loads)
    for t in range(tiles):
        lanes = lane_tile(t)
        values = gate[:, lanes]
        block_out[:, lanes] = summed[t] * values * jax.nn.sigmoid(values)
        gate_grad[:, lanes] = cot[:, lanes] * summed[t] * silu_grad(values)
    for side in range(2):
        wide = dot(projection[side], full_width(grad_pre, side), (0, 0))
        for t in range(tiles):
            step_part[side, t] = wide[:ranks, lane_tile(t)]


def weight_kernel(
    place, own, first, second, third, act_in, pre_in, grad_act_in, select_in, step_part,
    keep, send, conv_grad_out, head, tail,
    act, pre, grad_act, select, grad, both, conv_grad, sems,
):
    sides, tiles, length, _ = act.shape
    width = tiles * LANES
    half = both.shape[1]
    loads = copies_of(
        [
            (act_in, act), (select_in, select), (grad_act_in, grad_act), (pre_in, pre),
        ],
        sems,
    )
    grad[...] = (own[...] + first[...]) + (second[...] + third[...])
    loads[0].wait()
    place_rows(both, 2 * width, step_part[...].reshape(-1, LANES))
    for side in range(2):
        part = dot(full_width(act, side), grad[side], (0, 0))
        place_rows(both, side * width, part)
    core = lax.rem(place[0], 2)
    stores = copies_of(
        [(both.at[core], keep), (both.at[1 - core], send)], sems.at[pl.ds(4, 2)]
    )
    finish_all(loads[1:])
    for side in range(2):
        wide = dot(grad[side], select[side], (1, 1))
        for t in range(tiles):
            lanes = lane_tile(t)
            total = grad_act[side, t] + wide[:, lanes]
            conv_grad[side, :, lanes] = total * silu_grad(pre[side, t])
    head[...] = conv_grad[0, :HALO]
    tail[...] = conv_grad[1, length - HALO :]
    stores = stores + copies_of([(conv_grad, conv_grad_out)], sems.at[pl.ds(0, 1)])
    finish_all(stores)


def place_rows(both, first, value):
    half = both.shape[1]
    rows = value.shape[0]
    for k in range(2):
        low, high = max(first, k * half), min(first + rows, (k + 1) * half)
        if low < high:
            both[k, low - k * half : high - k * half] = value[low - first : high - first]


def halves_kernel(place, keep, got, mine, *refs):
    outs, (total,) = refs[:-1], refs[-1:]
    share = mine.shape[0]
    chips = len(outs) + 1
    for k in range(chips):
        at = slice(k * share, (k + 1) * share)
        total[k] = keep[at] + got[at]
    chip = lax.div(place[0], 2)
    mine[...] = total[chip]
    for s, out in enumerate(outs, 1):
        out[...] = total[chip ^ s]


def add_kernel(*refs):
    total = refs[0][...]
    for ref in refs[1:-1]:
        total = total + ref[...]
    refs[-1][...] = total


def join_kernel(place, mine, *refs):
    parts, out = refs[:-1], refs[-1]
    chip = lax.div(place[0], 2)
    out[chip] = mine[...]
    for s, part in enumerate(parts, 1):
        out[chip ^ s] = part[...]


def outputs_kernel(place, mine, other, select_grad, step_grad, both):
    sides, width, _ = select_grad.shape
    ranks = step_grad.shape[1]
    core = lax.rem(place[0], 2)
    half = both.shape[0] // 2
    size = mine.shape[1]
    for k in range(mine.shape[0]):
        low = jnp.where(core == 0, mine[k], other[k])
        high = jnp.where(core == 0, other[k], mine[k])
        both[k * size : (k + 1) * size] = low
        both[half + k * size : half + (k + 1) * size] = high
    for side in range(sides):
        select_grad[side] = both[side * width : (side + 1) * width]
        for t in range(width // LANES):
            at = 2 * width + (side * (width // LANES) + t) * ranks
            step_grad[side, :, lane_tile(t)] = both[at : at + ranks]


def exit_kernel(
    before, after, conv_grad, conv_weight_in, tokens_grad, up, down, conv_weight, sems
):
    _, length, width = conv_grad.shape
    taps = conv_weight.shape[1]
    margin = taps - 1
    loads = copies_of(
        [
            (conv_grad.at[0], up.at[pl.ds(0, length)]),
            (conv_grad.at[1], down.at[pl.ds(HALO, length)]),
            (conv_weight_in, conv_weight),
        ],
        sems,
    )
    up[length:] = after[...]
    down[:HALO] = before[...]
    finish_all(loads)
    for t in range(width // LANES):
        lanes = lane_tile(t)
        total = jnp.zeros((length, LANES), jnp.float32)
        for k in range(taps):
            at = margin - k
            total = total + conv_weight[0, k : k + 1, lanes] * up[at : at + length, lanes]
            at = HALO - margin + k
            total = total + conv_weight[1, k : k + 1, lanes] * down[at : at + length, lanes]
        tokens_grad[:, lanes] = total


def from_before(value, axis):
    count = lax.axis_size(axis)
    return lax.ppermute(value, axis, [(i, i + 1) for i in range(count - 1)])


def from_after(value, axis):
    count = lax.axis_size(axis)
    return lax.ppermute(value, axis, [(i + 1, i) for i in range(count - 1)])


def swapped(value, axis, by):
    count = lax.axis_size(axis)
    return lax.ppermute(value, axis, [(i, i ^ by) for i in range(count)])


def call(kernel, name, out_shape, scratch, mib, args, kinds, outs=None):
    spaces = {
        "v": pl.BlockSpec(memory_space=pltpu.VMEM),
        "h": pl.BlockSpec(memory_space=pltpu.HBM),
        "s": pl.BlockSpec(memory_space=pltpu.SMEM),
    }
    single = isinstance(out_shape, jax.ShapeDtypeStruct)
    outs = outs or "v" * (1 if single else len(out_shape))
    out_specs = [spaces[k] for k in outs]
    return pl.pallas_call(
        kernel,
        in_specs=[spaces[k] for k in kinds],
        out_specs=out_specs[0] if single else out_specs,
        out_shape=out_shape,
        scratch_shapes=scratch,
        compiler_params=params(mib),
        cost_estimate=pl.CostEstimate(flops=2**28, bytes_accessed=2**22, transcendentals=2**18),
        name=name,
    )(*args)


def summed_parts(partial):
    count = lax.axis_size("ch")
    if count == 4:
        return (partial, *(swapped(partial, "ch", s) for s in range(1, 4)))
    zero = jnp.zeros_like(partial)
    return (lax.psum(partial, "ch"), zero, zero, zero)


def on_device(
    tokens, gate_input, cotangent, conv_weight, conv_bias, select_weight, step_weight,
    step_bias, decay_log, skip_gain,
):
    length, width = tokens.shape
    tiles = width // LANES
    states = decay_log.shape[1]
    ranks = step_weight.shape[1]
    places = lax.axis_size("ctx")
    place = lax.axis_index("ctx").astype(jnp.int32).reshape(1)
    group = tile_group(tiles)
    chips = places // 2
    near = places == 8
    narrow = (2, length, LANES)
    one = (tiles, length, LANES)
    pair = (2, *one)
    chain_ends = (4, tiles, states, CHAINS, LANES)
    carry = (2, tiles, 2 * states + 8, LANES)
    vmem = functools.partial(pltpu.VMEM, dtype=jnp.float32)
    dma = lambda n: pltpu.SemaphoreType.DMA((n,))
    bases = vmem((length, states * LANES))
    grouped = vmem((group, length, states * LANES))
    rate_scratch = vmem((2, tiles, states, LANES))
    row_scratch = vmem((group, states, CHAINS, LANES))
    row_rates = vmem((tiles, 2 * states, LANES))
    skip = skip_gain.reshape(2, tiles, 1, LANES)

    before = from_before(tokens[length - HALO :], "ctx")
    after = from_after(tokens[:HALO], "ctx")
    partial, act, pre = call(
        entry_kernel, "entry", (shape_of(*narrow), shape_of(*pair), shape_of(*pair)),
        [
            vmem((length + 2 * HALO, width)), vmem(conv_weight.shape), vmem(conv_bias.shape),
            vmem(select_weight.shape), vmem(pair), vmem(pair), dma(6),
        ],
        12, (before, after, tokens, conv_weight, conv_bias, select_weight), "vvhhhh", "vhh",
    )
    projection, step, step_pre, grad_gated, entering, carried = call(
        local_kernel, "local",
        (
            shape_of(*narrow), shape_of(*pair), shape_of(*pair), shape_of(*one),
            shape_of(*chain_ends), shape_of(*carry),
        ),
        [
            vmem(narrow), vmem(pair), vmem(pair), vmem(pair), vmem(one), vmem(chain_ends),
            vmem(step_weight.shape), vmem(step_bias.shape), vmem(decay_log.shape),
            vmem((length, width)), vmem((length, width)),
            rate_scratch, bases, bases, row_scratch, grouped, dma(6),
        ],
        24,
        (*summed_parts(partial), step_weight, step_bias, decay_log, act, gate_input, cotangent),
        "vvvvhhhhhh", "hhhhhv",
    )
    if near:
        other = swapped(carried, "ctx", 1)
        sent = call(
            pair_kernel, "pair", (shape_of(*carry[1:]),) * (chips - 1),
            [row_rates, vmem(carry)], 8, (place, carried, other, decay_log), "svvv",
        )
        got = [swapped(part, "ctx", 2 * s) for s, part in enumerate(sent, 1)]
        incoming = call(
            chain_kernel, "chain", shape_of(2, tiles, 2 * states, LANES),
            [row_rates, vmem((chips, *carry[1:]))],
            8, (place, other, decay_log, *got), "svv" + "v" * len(got),
        )
    else:
        gathered = lax.all_gather(carried, "ctx")
        incoming = call(
            long_chain_kernel, "chain", shape_of(2, tiles, 2 * states, LANES), [row_rates],
            48, (place, gathered, decay_log), "svv",
        )
    partial_grad, grad_act, grad_pre, summed = call(
        scan_kernel, "scan",
        (shape_of(*narrow), shape_of(*pair), shape_of(*pair), shape_of(*one)),
        [
            vmem(narrow), vmem(step_weight.shape), vmem(decay_log.shape), vmem(skip.shape),
            vmem(pair), vmem(pair), vmem(pair), vmem(one), vmem(chain_ends),
            vmem(pair), vmem(pair), vmem(one), rate_scratch, bases, bases, row_scratch, grouped,
            bases, bases, vmem((LANES, width)), vmem((length, LANES)), dma(9),
        ],
        28,
        (
            incoming, projection, step_weight, decay_log, skip, act, step, step_pre, grad_gated,
            entering,
        ),
        "vhhhhhhhhh", "vhhh",
    )
    grad_parts = summed_parts(partial_grad)
    block_out, gate_grad, step_part = call(
        outer_kernel, "outer",
        (
            shape_of(length, width), shape_of(length, width),
            shape_of(2, tiles, ranks, LANES),
        ),
        [
            vmem(one), vmem((length, width)), vmem((length, width)), vmem(pair), vmem(narrow),
            dma(5),
        ],
        12, (summed, gate_input, cotangent, grad_pre, projection), "hhhhh",
    )
    half = width + tiles * ranks
    keep, send, conv_grad, head, tail = call(
        weight_kernel, "weights",
        (
            shape_of(half, LANES), shape_of(half, LANES), shape_of(2, length, width),
            shape_of(HALO, width), shape_of(HALO, width),
        ),
        [
            vmem(pair), vmem(pair), vmem(pair), vmem(select_weight.shape), vmem(narrow),
            vmem((2, half, LANES)), vmem((2, length, width)), dma(6),
        ],
        16,
        (place, *grad_parts, act, pre, grad_act, select_weight, step_part),
        "svvvvhhhhv", "hhhvv",
    )
    before = from_before(tail, "ctx")
    after = from_after(head, "ctx")
    if near:
        share = half // chips
        mine, *sent = call(
            halves_kernel, "halves", (shape_of(share, LANES),) * chips,
            [vmem((chips, share, LANES))],
            8, (place, keep, swapped(send, "ctx", 1)), "svv",
        )
        got = [swapped(part, "ctx", 2 * s) for s, part in enumerate(sent, 1)]
        mine = call(
            add_kernel, "share_sum", shape_of(share, LANES), [], 4, (mine, *got), "v" * chips
        )
        got = [swapped(mine, "ctx", 2 * s) for s in range(1, chips)]
        joined = call(
            join_kernel, "joined", shape_of(chips, share, LANES), [],
            8, (place, mine, *got), "s" + "v" * chips,
        )
        select_grad, step_grad = call(
            outputs_kernel, "weight_grads",
            (shape_of(2, width, LANES), shape_of(2, ranks, width)),
            [vmem((2 * half, LANES))],
            12, (place, joined, swapped(joined, "ctx", 1)), "svv",
        )
    else:
        core = lax.rem(place[0], 2) == 0
        both = jnp.where(core, jnp.stack([keep, send]), jnp.stack([send, keep]))
        both = lax.psum(both, "ctx").reshape(2 * half, LANES)
        select_grad = both[: 2 * width].reshape(2, width, LANES)
        step_grad = both[2 * width :].reshape(2, tiles, ranks, LANES)
        step_grad = step_grad.transpose(0, 2, 1, 3).reshape(2, ranks, width)
    tokens_grad = call(
        exit_kernel, "exit", shape_of(length, width),
        [
            vmem((length + HALO, width)), vmem((length + HALO, width)), vmem(conv_weight.shape),
            dma(3),
        ],
        8, (before, after, conv_grad, conv_weight), "vvhh",
    )
    return (block_out, tokens_grad, gate_grad, select_grad, step_grad)


def solution(mesh):
    return jax.shard_map(
        on_device,
        mesh=mesh,
        in_specs=(
            P("ctx", "ch"),
            P("ctx", "ch"),
            P("ctx", "ch"),
            P(None, None, "ch"),
            P(None, "ch"),
            P(None, "ch", None),
            P(None, None, "ch"),
            P(None, "ch"),
            P(None, None, "ch"),
            P(None, "ch"),
        ),
        out_specs=(
            P("ctx", "ch"),
            P("ctx", "ch"),
            P("ctx", "ch"),
            P(None, "ch", None),
            P(None, None, "ch"),
        ),
        check_vma=False,
    )
```

```python
import functools

import jax
import jax.numpy as jnp
from jax import lax
from jax.experimental import pallas as pl
from jax.experimental.pallas import tpu as pltpu
from jax.sharding import PartitionSpec as P

FULL_PRECISION = lax.Precision.HIGHEST
LANES = 128
CHAINS = 8
HALO = 8
LOG2E = 1.4426950408889634
LN2 = 0.6931471805599453
MIB = 1024 * 1024


def params(mib):
    return pltpu.CompilerParams(vmem_limit_bytes=mib * MIB)


def shape_of(*dims):
    return jax.ShapeDtypeStruct(dims, jnp.float32)


def dot(a, b, contract):
    return lax.dot_general(
        a, b, ((contract[:1], contract[1:]), ((), ())), precision=FULL_PRECISION,
        preferred_element_type=jnp.float32,
    )


def silu_grad(values):
    sigmoid_values = jax.nn.sigmoid(values)
    return sigmoid_values * (1.0 + values * (1.0 - sigmoid_values))


def lane_tile(t):
    return slice(t * LANES, (t + 1) * LANES)


def full_width(ref, *lead):
    tiles = ref.shape[len(lead)]
    return jnp.concatenate([ref[(*lead, t)] for t in range(tiles)], axis=1)


def convolved(ext, at_row, side, lanes, rows, conv_weight, conv_bias):
    taps = conv_weight.shape[1]
    margin = taps - 1
    conv = jnp.broadcast_to(conv_bias[side : side + 1, lanes], (rows, LANES))
    for k in range(taps):
        at = at_row + (k - margin if side == 0 else margin - k)
        conv = conv + conv_weight[side, k : k + 1, lanes] * ext[at : at + rows, lanes]
    return conv


def copies_of(pairs, sems):
    copies = [pltpu.make_async_copy(a, b, sems.at[i]) for i, (a, b) in enumerate(pairs)]
    for copy in copies:
        copy.start()
    return copies


def finish_all(copies):
    for copy in copies:
        copy.wait()


def entry_kernel(
    place, before, after, tokens, conv_weight_in, conv_bias_in, select_in,
    *refs,
):
    outs, refs = refs[:-9], refs[-9:]
    act_out, pre_out, ext, conv_weight, conv_bias, select, act, pre, sems = refs

    length, width = tokens.shape
    loads = copies_of(
        [
            (tokens, ext.at[pl.ds(HALO, length)]), (conv_weight_in, conv_weight),
            (conv_bias_in, conv_bias), (select_in, select),
        ],
        sems,
    )
    ext[:HALO] = before[...]
    ext[HALO + length :] = after[...]
    finish_all(loads[:3])
    for side in range(2):
        for t in range(width // LANES):
            conv = convolved(ext, HALO, side, lane_tile(t), length, conv_weight, conv_bias)
            pre[side, t] = conv
            act[side, t] = conv * jax.nn.sigmoid(conv)
    stores = copies_of([(pre, pre_out), (act, act_out)], sems.at[pl.ds(4, 2)])
    loads[3].wait()
    for side in range(2):
        deal(place, outs, side, dot(full_width(act, side), select[side], (1, 0)))
    finish_all(stores)


def deal(place, outs, side, rows):
    share = outs[0].shape[1]
    for k in range(len(outs)):
        for mine in range(len(outs)):

            @pl.when(place[0] == mine)
            def _():
                at = (mine ^ k) * share
                outs[k][side] = rows[at : at + share]


def collect(place, parts, out):
    share = parts[0].shape[1]
    for k in range(len(parts)):
        at = pl.multiple_of((place[0] ^ k) * share, share)
        out[:, pl.ds(at, share), :] = parts[k][...]


def spread(projection, side, j, states, basis_b, basis_c):
    length = basis_b.shape[0]
    count = length // CHAINS
    rows = projection[side, pl.ds(j, CHAINS, stride=count), :]
    ranks = LANES - 2 * states
    at = pl.ds(pl.multiple_of(j * CHAINS, CHAINS), CHAINS)
    for n in range(states):
        b = rows[:, ranks + n : ranks + n + 1]
        c = rows[:, ranks + states + n : ranks + states + n + 1]
        basis_b[at, lane_tile(n)] = jnp.broadcast_to(b, (CHAINS, LANES))
        basis_c[at, lane_tile(n)] = jnp.broadcast_to(c, (CHAINS, LANES))


def fill_bases(projection, side, states, basis_b, basis_c):
    def body(j, carry):
        spread(projection, side, j, states, basis_b, basis_c)
        return carry

    lax.fori_loop(0, basis_b.shape[0] // CHAINS, body, 0)


def fill_rates(decay_log, rates):
    for side in range(rates.shape[0]):
        for t in range(rates.shape[1]):
            rates[side, t] = -LOG2E * jnp.exp(decay_log[side, :, lane_tile(t)])


def sublane():
    return lax.broadcasted_iota(jnp.int32, (CHAINS, LANES), 0)


def shifted(value, by, up):
    rolled = pltpu.roll(value, by if up else CHAINS - by, 0)
    place = sublane()
    keep = place >= by if up else place < CHAINS - by
    return jnp.where(keep, rolled, 0.0)


def over_chains(decays, ends, up):
    by = 1
    while by < CHAINS:
        ends = [d * shifted(f, by, up) + f for d, f in zip(decays, ends)]
        if 2 * by < CHAINS:
            turn = by if up else CHAINS - by
            decays = [d * pltpu.roll(d, turn, 0) for d in decays]
        by *= 2
    return ends


def order(i, count, up):
    return i if up else count - 1 - i


def tile_group(tiles):
    return 2 if tiles % 2 == 0 else 1


def unrolled(count, body, start):
    times = 2 if count % 2 == 0 else 1

    def several(i, state):
        for k in range(times):
            state = body(i * times + k, state)
        return state

    return lax.fori_loop(0, count // times, several, start)


def fill_rate_rows(rates, side, tiles, rate_rows):
    for g, t in enumerate(tiles):
        for n in range(rate_rows.shape[1]):
            rate_rows[g, n] = jnp.broadcast_to(rates[side, t, n : n + 1], (CHAINS, LANES))


def token_rows(j, count):
    return pl.ds(j, CHAINS, stride=count)


def cell_rows(j):
    return pl.ds(pl.multiple_of(j * CHAINS, CHAINS), CHAINS)


def local_kernel(
    place, own, first, second, third,
    step_weight_in, step_bias_in, decay_log_in, act_in, gate_in, cot_in,
    projection_out, step_out, step_pre_out, grad_gated_out, entering_out, carry, row_rates,
    projection, act, step, step_pre, grad_gated, entering, step_weight, step_bias, decay_log,
    gate, cot, rates, basis_b, basis_c, rate_rows, decays, sems,
):
    sides, tiles, length, _ = act.shape
    states = decay_log.shape[1]
    ranks = step_weight.shape[1]
    count = length // CHAINS
    group = tile_group(tiles)
    loads = copies_of(
        [
            (step_weight_in, step_weight), (step_bias_in, step_bias), (decay_log_in, decay_log),
            (gate_in, gate), (cot_in, cot), (act_in, act),
        ],
        sems,
    )
    collect(place, (own, first, second, third), projection)
    finish_all(loads)
    for t in range(tiles):
        lanes = lane_tile(t)
        values = gate[:, lanes]
        grad_gated[t] = cot[:, lanes] * values * jax.nn.sigmoid(values)
    fill_rates(decay_log, rates)
    for side in range(2):
        wide = dot(projection[side][:, :ranks], step_weight[side], (1, 0))
        wide = wide + step_bias[side : side + 1]
        for t in range(tiles):
            part = wide[:, lane_tile(t)]
            step_pre[side, t] = part
            step[side, t] = jnp.maximum(part, 0.0) + jnp.log1p(jnp.exp(-jnp.abs(part)))
    stores = copies_of(
        [
            (projection, projection_out), (step, step_out), (step_pre, step_pre_out),
            (grad_gated, grad_gated_out),
        ],
        sems,
    )
    zero = jnp.zeros((CHAINS, LANES), jnp.float32)
    carry[...] = jnp.zeros_like(carry)
    for side in range(2):
        up = side == 0
        fill_bases(projection, side, states, basis_b, basis_c)

        def some_tiles(first, keep):
            at_tiles = [first * group + g for g in range(group)]
            fill_rate_rows(rates, side, at_tiles, rate_rows)

            def forward(i, current):
                state, summed = current
                j = order(i, count, up)
                rows, at = token_rows(j, count), cell_rows(j)
                steps = [step[side, t, rows, :] for t in at_tiles]
                drives = [v * act[side, t, rows, :] for v, t in zip(steps, at_tiles)]
                new = []
                for n in range(states):
                    lanes = lane_tile(n)
                    b = basis_b[at, lanes]
                    for g in range(group):
                        decay = jnp.exp2(steps[g] * rate_rows[g, n])
                        decays[g, at, lanes] = decay
                        new.append(decay * state[n * group + g] + b * drives[g])
                return (tuple(new), tuple(a + v for a, v in zip(summed, steps)))

            start = ((zero,) * (states * group), (zero,) * group)
            state, summed = unrolled(count, forward, start)

            def retreat(i, state):
                j = order(i, count, not up)
                rows, at = token_rows(j, count), cell_rows(j)
                grads = [grad_gated[t, rows, :] for t in at_tiles]
                new = []
                for n in range(states):
                    lanes = lane_tile(n)
                    c = basis_c[at, lanes]
                    for g in range(group):
                        adjoint = state[n * group + g] + c * grads[g]
                        new.append(decays[g, at, lanes] * adjoint)
                return tuple(new)

            sent = unrolled(count, retreat, (zero,) * (states * group))
            for g, t in enumerate(at_tiles):
                across = [jnp.exp2(summed[g] * rate_rows[g, n]) for n in range(states)]
                for kind, ends, upward in ((0, state, up), (1, sent, not up)):
                    slot = 2 * side + kind
                    ends = over_chains(across, list(ends[g::group]), upward)
                    last = CHAINS - 1 if upward else 0
                    for n in range(states):
                        entering[slot, t, n] = shifted(ends[n], 1, upward)
                        at = side * states + n
                        carry[0 if upward else 1, t, at : at + 1] = ends[n][last : last + 1]
                whole = jnp.sum(summed[g], axis=0, keepdims=True)
                at = 2 * states + side
                for k in range(2):
                    carry[k, t, at : at + 1] = whole
            return keep

        lax.fori_loop(0, tiles // group, some_tiles, 0)
    stores = stores + copies_of([(entering, entering_out)], sems.at[pl.ds(4, 1)])
    for side in range(2):
        row_rates[:, side * states : (side + 1) * states] = rates[side]
    finish_all(stores)


def tile_decay(part, rates):
    rows = rates.shape[1]
    row = lax.broadcasted_iota(jnp.int32, rates.shape, 1)
    sums = jnp.where(row < rows // 2, part[:, rows : rows + 1], part[:, rows + 1 : rows + 2])
    return jnp.exp2(rates * sums)


def pair_kernel(place, mine, other, rates, *refs):
    outs, total = refs[:-1], refs[-1]
    rows = rates.shape[1]
    core, chip = lax.rem(place[0], 2), lax.div(place[0], 2)
    low = jnp.where(core == 0, mine[...], other[...])
    high = jnp.where(core == 0, other[...], mine[...])
    spread_rates = rates[...]
    decay_low = tile_decay(low[0], spread_rates)
    decay_high = tile_decay(high[0], spread_rates)
    total[...] = low + high
    total[0, :, :rows] = decay_high * low[0][:, :rows] + high[0][:, :rows]
    total[1, :, :rows] = decay_low * high[1][:, :rows] + low[1][:, :rows]
    for s, out in enumerate(outs, 1):
        below = lax.convert_element_type((chip ^ s) < chip, jnp.int32)
        out[...] = total[below]


def chain_kernel(place, other, rates, *refs):
    gathered, (out, parts) = refs[:-2], refs[-2:]
    rows = rates.shape[1]
    chips = parts.shape[0]
    core, chip = lax.rem(place[0], 2), lax.div(place[0], 2)
    parts[chip] = jnp.zeros(parts.shape[1:], jnp.float32)
    for s, part in enumerate(gathered, 1):
        parts[chip ^ s] = part[...]
    spread_rates = rates[...]
    for kind in range(2):
        state = jnp.zeros(rates.shape, jnp.float32)
        for k in range(chips) if kind == 0 else reversed(range(chips)):
            part = parts[k]
            new = tile_decay(part, spread_rates) * state + part[:, :rows]
            state = jnp.where(k < chip if kind == 0 else k > chip, new, state)
        part = other[kind]
        new = tile_decay(part, spread_rates) * state + part[:, :rows]
        out[kind] = jnp.where(core == 1 - kind, new, state)


def long_chain_kernel(place, gathered, rates, out):
    rows = rates.shape[1]
    shards = gathered.shape[0]
    for kind in range(2):

        def turn(i, state):
            part = gathered[order(i, shards, kind == 0), kind]
            return tile_decay(part, rates[...]) * state + part[:, :rows]

        turns = place[0] if kind == 0 else shards - 1 - place[0]
        out[kind] = lax.fori_loop(0, turns, turn, jnp.zeros(rates.shape, jnp.float32))


def scan_kernel(
    place, incoming, projection_in, step_weight_in, decay_log_in, skip_gain_in, act_in, step_in,
    step_pre_in, grad_gated_in, entering_in,
    mine, first_out, second_out, third_out, grad_act_out, grad_pre_out, summed_outs,
    projection, step_weight, decay_log, skip_gain, act, step, step_pre, grad_gated, entering,
    grad_act, grad_pre, summed_out, rates, basis_b, basis_c, rate_rows, decays, history,
    grad_in, grad_out, weights, packed, skip_rows, sems,
):
    sides, tiles, length, _ = act.shape
    states = decay_log.shape[1]
    ranks = step_weight.shape[1]
    count = length // CHAINS
    group = tile_group(tiles)
    loads = copies_of(
        [
            (projection_in, projection), (decay_log_in, decay_log), (step_in, step),
            (act_in, act), (grad_gated_in, grad_gated), (entering_in, entering),
            (skip_gain_in, skip_gain), (step_pre_in, step_pre), (step_weight_in, step_weight),
        ],
        sems,
    )
    stores = []
    finish_all(loads[:2])
    fill_rates(decay_log, rates)
    zero = jnp.zeros((CHAINS, LANES), jnp.float32)
    column = lax.broadcasted_iota(jnp.int32, (CHAINS, LANES), 1)
    for side in range(2):
        up = side == 0
        fill_bases(projection, side, states, basis_b, basis_c)
        grad_in[...] = jnp.zeros_like(grad_in)
        grad_out[...] = jnp.zeros_like(grad_out)
        if side == 0:
            finish_all(loads[2:])
            for k in range(2):
                for t in range(tiles):
                    skip_rows[k, t] = skip_gain[k : k + 1, lane_tile(t)]

        def some_tiles(first, keep):
            at_tiles = [first * group + g for g in range(group)]
            fill_rate_rows(rates, side, at_tiles, rate_rows)
            skips = [skip_rows[side, t] for t in at_tiles]
            sums = []
            for t in at_tiles:
                summed = step[side, t, token_rows(0, count), :]
                for j in range(1, count):
                    summed = summed + step[side, t, token_rows(j, count), :]
                sums.append(summed)

            def start(kind, upward):
                slot = 2 * side + kind
                spans = []
                for g in range(group):
                    span = shifted(sums[g], 1, upward)
                    by = 1
                    while by < CHAINS:
                        span = span + shifted(span, by, upward)
                        by *= 2
                    spans.append(span)
                first = []
                for n in range(states):
                    at = side * states + n
                    for g, t in enumerate(at_tiles):
                        decay = jnp.exp2(spans[g] * rate_rows[g, n])
                        value = incoming[0 if upward else 1, t, at : at + 1, :]
                        first.append(entering[slot, t, n] + decay * value)
                return tuple(first)

            def forward(i, state):
                j = order(i, count, up)
                rows, at = token_rows(j, count), cell_rows(j)
                steps = [step[side, t, rows, :] for t in at_tiles]
                acts = [act[side, t, rows, :] for t in at_tiles]
                grads = [grad_gated[t, rows, :] for t in at_tiles]
                drives = [v * a for v, a in zip(steps, acts)]
                outs = [v * a for v, a in zip(skips, acts)]
                new = []
                for n in range(states):
                    lanes = lane_tile(n)
                    b, c = basis_b[at, lanes], basis_c[at, lanes]
                    read = grad_out[at, lanes]
                    for g in range(group):
                        before = state[n * group + g]
                        decay = jnp.exp2(steps[g] * rate_rows[g, n])
                        decays[g, at, lanes] = decay
                        history[g, at, lanes] = before
                        current = decay * before + b * drives[g]
                        outs[g] = outs[g] + c * current
                        read = read + current * grads[g]
                        new.append(current)
                    grad_out[at, lanes] = read
                for g, t in enumerate(at_tiles):
                    if side == 0:
                        summed_out[t, rows, :] = outs[g]
                    else:
                        summed_out[t, rows, :] = summed_out[t, rows, :] + outs[g]
                return tuple(new)

            unrolled(count, forward, start(0, up))

            def retreat(i, state):
                j = order(i, count, not up)
                rows, at = token_rows(j, count), cell_rows(j)
                steps = [step[side, t, rows, :] for t in at_tiles]
                acts = [act[side, t, rows, :] for t in at_tiles]
                grads = [grad_gated[t, rows, :] for t in at_tiles]
                drives = [v * a for v, a in zip(steps, acts)]
                step_terms = [zero] * group
                drive_grads = [zero] * group
                new = []
                for n in range(states):
                    lanes = lane_tile(n)
                    b, c = basis_b[at, lanes], basis_c[at, lanes]
                    put = grad_in[at, lanes]
                    for g in range(group):
                        adjoint = state[n * group + g] + c * grads[g]
                        carried = decays[g, at, lanes] * adjoint
                        new.append(carried)
                        term = carried * history[g, at, lanes] * rate_rows[g, n]
                        step_terms[g] = step_terms[g] + term
                        drive_grads[g] = drive_grads[g] + adjoint * b
                        put = put + adjoint * drives[g]
                    grad_in[at, lanes] = put
                for g, t in enumerate(at_tiles):
                    grad_step = step_terms[g] * LN2 + drive_grads[g] * acts[g]
                    grad_act[side, t, rows, :] = grads[g] * skips[g] + drive_grads[g] * steps[g]
                    pre = step_pre[side, t, rows, :]
                    grad_pre[side, t, rows, :] = grad_step * jax.nn.sigmoid(pre)
                return tuple(new)

            unrolled(count, retreat, start(1, not up))
            return keep

        lax.fori_loop(0, tiles // group, some_tiles, 0)
        pairs = [
            (grad_act.at[side], grad_act_out.at[side]), (grad_pre.at[side], grad_pre_out.at[side]),
        ]
        if side == 1:
            pairs.append((summed_out, summed_outs))
        stores = stores + copies_of(pairs, sems.at[pl.ds(2 * side, 3)])
        wide = full_width(grad_pre, side)
        weights[...] = jnp.zeros_like(weights)
        weights[:ranks] = step_weight[side]
        packed[...] = dot(wide, weights[...], (1, 1))

        def pack(j, keep):
            rows, at = token_rows(j, count), cell_rows(j)
            line = packed[rows, :]
            for values, start_at in ((grad_in, ranks), (grad_out, ranks + states)):
                for n in range(states):
                    total = jnp.sum(values[at, lane_tile(n)], axis=1, keepdims=True)
                    line = jnp.where(column == start_at + n, total, line)
            packed[rows, :] = line
            return keep

        lax.fori_loop(0, count, pack, 0)
        deal(place, (mine, first_out, second_out, third_out), side, packed)
    finish_all(stores)


def outer_kernel(
    place, summed_in, gate_in, cot_in, grad_pre_in, projection_in, block_out, gate_grad, keep, send,
    summed, gate, cot, grad_pre, projection, sems,
):
    tiles = summed.shape[0]
    ranks = keep.shape[1]
    loads = copies_of(
        [
            (summed_in, summed), (gate_in, gate), (cot_in, cot), (grad_pre_in, grad_pre),
            (projection_in, projection),
        ],
        sems,
    )
    finish_all(loads)
    for t in range(tiles):
        lanes = lane_tile(t)
        values = gate[:, lanes]
        block_out[:, lanes] = summed[t] * values * jax.nn.sigmoid(values)
        gate_grad[:, lanes] = cot[:, lanes] * summed[t] * silu_grad(values)
    for side in range(2):
        wide = dot(projection[side], full_width(grad_pre, side), (0, 0))
        for out, core in ((keep, side), (send, 1 - side)):

            @pl.when(lax.rem(place[0], 2) == core)
            def _():
                for t in range(tiles):
                    out[t] = wide[:ranks, lane_tile(t)]


def weight_kernel(
    place, column, own, first, second, third, act_in, pre_in, grad_act_in, select_in, after_this,
    keep, send, conv_grad_out, head, tail,
    act, pre, grad_act, select, grad, both, conv_grad, sems,
):
    sides, tiles, length, _ = act.shape
    loads = copies_of(
        [
            (act_in, act), (select_in, select), (grad_act_in, grad_act), (pre_in, pre),
        ],
        sems,
    )
    collect(column, (own, first, second, third), grad)
    loads[0].wait()
    for side in range(2):
        both[side] = dot(full_width(act, side), grad[side], (0, 0))
    core = lax.rem(place[0], 2)
    stores = copies_of(
        [(both.at[core], keep), (both.at[1 - core], send)], sems.at[pl.ds(4, 2)]
    )
    finish_all(loads[1:])
    for side in range(2):
        wide = dot(grad[side], select[side], (1, 1))
        for t in range(tiles):
            lanes = lane_tile(t)
            total = grad_act[side, t] + wide[:, lanes]
            conv_grad[side, :, lanes] = total * silu_grad(pre[side, t])
    head[...] = conv_grad[0, :HALO]
    tail[...] = conv_grad[1, length - HALO :]
    stores = stores + copies_of([(conv_grad, conv_grad_out)], sems.at[pl.ds(0, 1)])
    finish_all(stores)


def halves_kernel(place, keep, got, mine, *refs):
    outs, (total,) = refs[:-1], refs[-1:]
    share = mine.shape[0]
    chips = len(outs) + 1
    for k in range(chips):
        at = slice(k * share, (k + 1) * share)
        total[k] = keep[at] + got[at]
    chip = lax.div(place[0], 2)
    mine[...] = total[chip]
    for s, out in enumerate(outs, 1):
        out[...] = total[chip ^ s]


def add_kernel(*refs):
    total = refs[0][...]
    for ref in refs[1:-1]:
        total = total + ref[...]
    refs[-1][...] = total


def add_both_kernel(*refs):
    parts, out = refs[:-1], refs[-1]
    count = len(parts) // 2
    at = 0
    for some in (parts[:count], parts[count:]):
        total = some[0][...]
        for ref in some[1:]:
            total = total + ref[...]
        out[at : at + total.shape[0]] = total
        at += total.shape[0]


def join_kernel(place, after_this, mine, *refs):
    parts, out = refs[:-1], refs[-1]
    chip = lax.div(place[0], 2)
    out[chip] = mine[...]
    for s, part in enumerate(parts, 1):
        out[chip ^ s] = part[...]


def outputs_kernel(place, mine, other, select_grad, step_grad, both):
    sides, width, _ = select_grad.shape
    ranks = step_grad.shape[1]
    chips = mine.shape[0]
    core = lax.rem(place[0], 2)
    part = width // chips
    flat = both.shape[1] // chips
    for side in range(2):
        for k in range(chips):
            rows = jnp.where(core == side, mine[k], other[k])
            select_grad[side, k * part : (k + 1) * part] = rows[:part]
            both[side, k * flat : (k + 1) * flat] = rows[part:]
        for t in range(width // LANES):
            step_grad[side, :, lane_tile(t)] = both[side, t * ranks : (t + 1) * ranks]


def exit_kernel(
    before, after, conv_grad, conv_weight_in, tokens_grad, up, down, conv_weight, sems
):
    _, length, width = conv_grad.shape
    taps = conv_weight.shape[1]
    margin = taps - 1
    loads = copies_of(
        [
            (conv_grad.at[0], up.at[pl.ds(0, length)]),
            (conv_grad.at[1], down.at[pl.ds(HALO, length)]),
            (conv_weight_in, conv_weight),
        ],
        sems,
    )
    up[length:] = after[...]
    down[:HALO] = before[...]
    finish_all(loads)
    for t in range(width // LANES):
        lanes = lane_tile(t)
        total = jnp.zeros((length, LANES), jnp.float32)
        for k in range(taps):
            at = margin - k
            total = total + conv_weight[0, k : k + 1, lanes] * up[at : at + length, lanes]
            at = HALO - margin + k
            total = total + conv_weight[1, k : k + 1, lanes] * down[at : at + length, lanes]
        tokens_grad[:, lanes] = total


def from_before(value, axis):
    count = lax.axis_size(axis)
    return lax.ppermute(value, axis, [(i, i + 1) for i in range(count - 1)])


def from_after(value, axis):
    count = lax.axis_size(axis)
    return lax.ppermute(value, axis, [(i + 1, i) for i in range(count - 1)])


def swapped(value, axis, by):
    count = lax.axis_size(axis)
    return lax.ppermute(value, axis, [(i, i ^ by) for i in range(count)])


def call(kernel, name, out_shape, scratch, mib, args, kinds, outs=None):
    spaces = {
        "v": pl.BlockSpec(memory_space=pltpu.VMEM),
        "h": pl.BlockSpec(memory_space=pltpu.HBM),
        "s": pl.BlockSpec(memory_space=pltpu.SMEM),
    }
    outs = outs or "v" * len(out_shape)
    args = [
        pltpu.with_memory_space_constraint(a, pltpu.HBM) if k == "h" else a
        for a, k in zip(args, kinds, strict=True)
    ]
    results = [
        pltpu.HBM(shape, jnp.float32) if k == "h" else shape_of(*shape)
        for shape, k in zip(out_shape, outs, strict=True)
    ]
    return pl.pallas_call(
        kernel,
        in_specs=[spaces[k] for k in kinds],
        out_specs=[spaces[k] for k in outs],
        out_shape=results,
        scratch_shapes=scratch,
        compiler_params=params(mib),
        cost_estimate=pl.CostEstimate(flops=2**28, bytes_accessed=2**22, transcendentals=2**18),
        name=name,
    )(*args)


def summed_shares(parts, name):
    count = len(parts)
    if count == 1:
        return (lax.psum(parts[0], "ch"),)
    got = [swapped(part, "ch", s) for s, part in enumerate(parts[1:], 1)]
    (mine,) = call(add_kernel, name, (parts[0].shape,), [], 4, (parts[0], *got), "v" * count)
    return (mine, *(swapped(mine, "ch", s) for s in range(1, count)))


def halved(place, keep, send, rows, chips, name):
    got = swapped(send, "ctx", 1)
    share = rows // chips
    mine, *sent = call(
        halves_kernel, name, ((share, LANES),) * chips, [pltpu.VMEM((chips, share, LANES), jnp.float32)],
        8, (place, keep.reshape(rows, LANES), got.reshape(rows, LANES)), "svv",
    )
    return (mine, *(swapped(part, "ctx", 2 * s) for s, part in enumerate(sent, 1)))


def on_device(
    tokens, gate_input, cotangent, conv_weight, conv_bias, select_weight, step_weight,
    step_bias, decay_log, skip_gain,
):
    length, width = tokens.shape
    tiles = width // LANES
    states = decay_log.shape[1]
    ranks = step_weight.shape[1]
    places = lax.axis_size("ctx")
    columns = lax.axis_size("ch")
    place = lax.axis_index("ctx").astype(jnp.int32).reshape(1)
    column = lax.axis_index("ch").astype(jnp.int32).reshape(1)
    group = tile_group(tiles)
    chips = places // 2
    near = places == 8
    narrow = (2, length, LANES)
    shared = (2, length // columns, LANES)
    one = (tiles, length, LANES)
    pair = (2, *one)
    flat = (length, width)
    chain_ends = (4, tiles, states, CHAINS, LANES)
    carry = (2, tiles, 2 * states + 8, LANES)
    row_rates = (tiles, 2 * states, LANES)
    vmem = functools.partial(pltpu.VMEM, dtype=jnp.float32)
    dma = lambda n: pltpu.SemaphoreType.DMA((n,))
    bases = vmem((length, states * LANES))
    grouped = vmem((group, length, states * LANES))
    rate_scratch = vmem((2, tiles, states, LANES))
    row_scratch = vmem((group, states, CHAINS, LANES))

    before = from_before(tokens[length - HALO :], "ctx")
    after = from_after(tokens[:HALO], "ctx")
    *parts, act, pre = call(
        entry_kernel, "entry", (*(shared,) * columns, pair, pair),
        [
            vmem((length + 2 * HALO, width)), vmem(conv_weight.shape), vmem(conv_bias.shape),
            vmem(select_weight.shape), vmem(pair), vmem(pair), dma(6),
        ],
        12, (column, before, after, tokens, conv_weight, conv_bias, select_weight), "svvhhhh",
        "v" * columns + "hh",
    )
    projection, step, step_pre, grad_gated, entering, carried, rates = call(
        local_kernel, "local", (narrow, pair, pair, one, chain_ends, carry, row_rates),
        [
            vmem(narrow), vmem(pair), vmem(pair), vmem(pair), vmem(one), vmem(chain_ends),
            vmem(step_weight.shape), vmem(step_bias.shape), vmem(decay_log.shape),
            vmem(flat), vmem(flat),
            rate_scratch, bases, bases, row_scratch, grouped, dma(6),
        ],
        24,
        (
            column, *summed_shares(parts, "projection"), step_weight, step_bias, decay_log, act,
            gate_input, cotangent,
        ),
        "svvvvhhhhhh", "hhhhhvv",
    )
    if near:
        other = swapped(carried, "ctx", 1)
        sent = call(
            pair_kernel, "pair", (carry[1:],) * (chips - 1),
            [vmem(carry)], 8, (place, carried, other, rates), "svvv",
        )
        got = [swapped(part, "ctx", 2 * s) for s, part in enumerate(sent, 1)]
        (incoming,) = call(
            chain_kernel, "chain", ((2, *row_rates),), [vmem((chips, *carry[1:]))],
            8, (place, other, rates, *got), "svv" + "v" * len(got),
        )
    else:
        gathered = lax.all_gather(carried, "ctx")
        (incoming,) = call(
            long_chain_kernel, "chain", ((2, *row_rates),), [],
            48, (place, gathered, rates), "svv",
        )
    *grad_parts, grad_act, grad_pre, summed = call(
        scan_kernel, "scan", (*(shared,) * columns, pair, pair, one),
        [
            vmem(narrow), vmem(step_weight.shape), vmem(decay_log.shape), vmem(skip_gain.shape),
            vmem(pair), vmem(pair), vmem(pair), vmem(one), vmem(chain_ends),
            vmem(pair), vmem(pair), vmem(one), rate_scratch, bases, bases, row_scratch, grouped,
            grouped, bases, bases, vmem((LANES, width)), vmem((length, LANES)),
            vmem((2, tiles, 1, LANES)), dma(9),
        ],
        28,
        (
            column, incoming, projection, step_weight, decay_log, skip_gain, act, step, step_pre,
            grad_gated, entering,
        ),
        "svhhhhhhhhh", "v" * columns + "hhh",
    )
    grad_shares = summed_shares(grad_parts, "grad_projection")
    block_out, gate_grad, step_keep, step_send = call(
        outer_kernel, "outer", (flat, flat, (tiles, ranks, LANES), (tiles, ranks, LANES)),
        [vmem(one), vmem(flat), vmem(flat), vmem(pair), vmem(narrow), dma(5)],
        12, (place, summed, gate_input, cotangent, grad_pre, projection), "shhhhh",
    )
    if near:
        step_shares = halved(place, step_keep, step_send, tiles * ranks, chips, "step_halves")
        ahead = step_shares[0]
    else:
        ahead = step_keep
    keep, send, conv_grad, head, tail = call(
        weight_kernel, "weights",
        ((width, LANES), (width, LANES), (2, *flat), (HALO, width), (HALO, width)),
        [
            vmem(pair), vmem(pair), vmem(pair), vmem(select_weight.shape), vmem(narrow),
            vmem(select_weight.shape), vmem((2, *flat)), dma(6),
        ],
        16,
        (place, column, *grad_shares, act, pre, grad_act, select_weight, ahead),
        "ssvvvvhhhhv", "vvhvv",
    )
    before = from_before(tail, "ctx")
    after = from_after(head, "ctx")
    (tokens_grad,) = call(
        exit_kernel, "exit", (flat,),
        [
            vmem((length + HALO, width)), vmem((length + HALO, width)), vmem(conv_weight.shape),
            dma(3),
        ],
        8, (before, after, conv_grad, conv_weight), "vvhh",
    )
    if near:
        shares = halved(place, keep, send, width, chips, "select_halves")
        rows = width // chips + tiles * ranks // chips
        (mine,) = call(
            add_both_kernel, "share_sum", ((rows, LANES),), [], 4, (*shares, *step_shares),
            "v" * (2 * chips),
        )
        got = [swapped(mine, "ctx", 2 * s) for s in range(1, chips)]
        (joined,) = call(
            join_kernel, "joined", ((chips, rows, LANES),), [],
            8, (place, tokens_grad, mine, *got), "sh" + "v" * chips,
        )
        select_grad, step_grad = call(
            outputs_kernel, "weight_grads", ((2, width, LANES), (2, ranks, width)),
            [vmem((2, tiles * ranks, LANES))],
            12, (place, joined, swapped(joined, "ctx", 1)), "svv",
        )
    else:
        first = lax.rem(place[0], 2) == 0
        order_of = lambda a, b: jnp.where(first, jnp.stack([a, b]), jnp.stack([b, a]))
        sums = lax.psum((order_of(keep, send), order_of(step_keep, step_send)), "ctx")
        select_grad = sums[0]
        step_grad = sums[1].transpose(0, 2, 1, 3).reshape(2, ranks, width)
    return (block_out, tokens_grad, gate_grad, select_grad, step_grad)


def solution(mesh):
    return jax.shard_map(
        on_device,
        mesh=mesh,
        in_specs=(
            P("ctx", "ch"),
            P("ctx", "ch"),
            P("ctx", "ch"),
            P(None, None, "ch"),
            P(None, "ch"),
            P(None, "ch", None),
            P(None, None, "ch"),
            P(None, "ch"),
            P(None, None, "ch"),
            P(None, "ch"),
        ),
        out_specs=(
            P("ctx", "ch"),
            P("ctx", "ch"),
            P("ctx", "ch"),
            P(None, "ch", None),
            P(None, None, "ch"),
        ),
        check_vma=False,
    )
```

```python
import functools

import jax
import jax.numpy as jnp
from jax import lax
from jax.experimental import pallas as pl
from jax.experimental.pallas import tpu as pltpu
from jax.sharding import PartitionSpec as P

FULL_PRECISION = lax.Precision.HIGHEST
LANES = 128
CHAINS = 8
HALO = 8
LOG2E = 1.4426950408889634
LN2 = 0.6931471805599453
MIB = 1024 * 1024


def params(mib):
    return pltpu.CompilerParams(vmem_limit_bytes=mib * MIB)


def shape_of(*dims):
    return jax.ShapeDtypeStruct(dims, jnp.float32)


def dot(a, b, contract):
    return lax.dot_general(
        a, b, ((contract[:1], contract[1:]), ((), ())), precision=FULL_PRECISION,
        preferred_element_type=jnp.float32,
    )


def silu_grad(values):
    sigmoid_values = jax.nn.sigmoid(values)
    return sigmoid_values * (1.0 + values * (1.0 - sigmoid_values))


def lane_tile(t):
    return slice(t * LANES, (t + 1) * LANES)


def full_width(ref, *lead):
    tiles = ref.shape[len(lead)]
    return jnp.concatenate([ref[(*lead, t)] for t in range(tiles)], axis=1)


def convolved(ext, at_row, side, lanes, rows, conv_weight, conv_bias):
    taps = conv_weight.shape[1]
    margin = taps - 1
    conv = jnp.broadcast_to(conv_bias[side : side + 1, lanes], (rows, LANES))
    for k in range(taps):
        at = at_row + (k - margin if side == 0 else margin - k)
        conv = conv + conv_weight[side, k : k + 1, lanes] * ext[at : at + rows, lanes]
    return conv


def copies_of(pairs, sems):
    copies = [pltpu.make_async_copy(a, b, sems.at[i]) for i, (a, b) in enumerate(pairs)]
    for copy in copies:
        copy.start()
    return copies


def to_cells(tokens, cells):
    count = tokens.shape[0] // CHAINS
    for j in range(count):
        cells[j * CHAINS : (j + 1) * CHAINS] = tokens[pl.ds(j, CHAINS, stride=count), :]


def to_tokens(cells, tokens):
    count = tokens.shape[0] // CHAINS
    for j in range(count):
        tokens[pl.ds(j, CHAINS, stride=count), :] = cells[j * CHAINS : (j + 1) * CHAINS]


def finish_all(copies):
    for copy in copies:
        copy.wait()


def entry_kernel(
    place, before, after, tokens, conv_weight_in, conv_bias_in, select_in,
    *refs,
):
    outs, refs = refs[:-10], refs[-10:]
    act_out, pre_out, ext, conv_weight, conv_bias, select, act, pre, plain, sems = refs

    length, width = tokens.shape
    loads = copies_of(
        [
            (tokens, ext.at[pl.ds(HALO, length)]), (conv_weight_in, conv_weight),
            (conv_bias_in, conv_bias), (select_in, select),
        ],
        sems,
    )
    ext[:HALO] = before[...]
    ext[HALO + length :] = after[...]
    finish_all(loads[:3])
    for side in range(2):
        for t in range(width // LANES):
            conv = convolved(ext, HALO, side, lane_tile(t), length, conv_weight, conv_bias)
            pre[side, t] = conv
            plain[...] = conv * jax.nn.sigmoid(conv)
            to_cells(plain, act.at[side, t])
    stores = copies_of([(pre, pre_out), (act, act_out)], sems.at[pl.ds(4, 2)])
    loads[3].wait()
    for side in range(2):
        deal(place, outs, side, dot(full_width(act, side), select[side], (1, 0)))
    finish_all(stores)


def deal(place, outs, side, rows):
    share = outs[0].shape[1]
    for k in range(len(outs)):
        for mine in range(len(outs)):

            @pl.when(place[0] == mine)
            def _():
                at = (mine ^ k) * share
                outs[k][side] = rows[at : at + share]


def collect(place, parts, out):
    share = parts[0].shape[1]
    for k in range(len(parts)):
        at = pl.multiple_of((place[0] ^ k) * share, share)
        out[:, pl.ds(at, share), :] = parts[k][...]


def spread(projection, side, j, states, basis_b, basis_c):
    ranks = LANES - 2 * states
    at = pl.ds(pl.multiple_of(j * CHAINS, CHAINS), CHAINS)
    rows = projection[side, at, :]
    for n in range(states):
        b = rows[:, ranks + n : ranks + n + 1]
        c = rows[:, ranks + states + n : ranks + states + n + 1]
        basis_b[at, lane_tile(n)] = jnp.broadcast_to(b, (CHAINS, LANES))
        basis_c[at, lane_tile(n)] = jnp.broadcast_to(c, (CHAINS, LANES))


def fill_bases(projection, side, states, basis_b, basis_c):
    def body(j, carry):
        spread(projection, side, j, states, basis_b, basis_c)
        return carry

    lax.fori_loop(0, basis_b.shape[0] // CHAINS, body, 0)


def fill_rates(decay_log, rates):
    for side in range(rates.shape[0]):
        for t in range(rates.shape[1]):
            rates[side, t] = -LOG2E * jnp.exp(decay_log[side, :, lane_tile(t)])


def sublane():
    return lax.broadcasted_iota(jnp.int32, (CHAINS, LANES), 0)


def shifted(value, by, up):
    rolled = pltpu.roll(value, by if up else CHAINS - by, 0)
    place = sublane()
    keep = place >= by if up else place < CHAINS - by
    return jnp.where(keep, rolled, 0.0)


def over_chains(decays, ends, up):
    by = 1
    while by < CHAINS:
        ends = [d * shifted(f, by, up) + f for d, f in zip(decays, ends)]
        if 2 * by < CHAINS:
            turn = by if up else CHAINS - by
            decays = [d * pltpu.roll(d, turn, 0) for d in decays]
        by *= 2
    return ends


def order(i, count, up):
    return i if up else count - 1 - i


def tile_group(tiles):
    return 2 if tiles % 2 == 0 else 1


def unrolled(count, times, body, start):
    times = times if count % times == 0 else 1

    def several(i, state):
        for k in range(times):
            state = body(i * times + k, state)
        return state

    return lax.fori_loop(0, count // times, several, start)


def fill_rate_rows(rates, side, tiles, rate_rows):
    for g, t in enumerate(tiles):
        for n in range(rate_rows.shape[1]):
            rate_rows[g, n] = jnp.broadcast_to(rates[side, t, n : n + 1], (CHAINS, LANES))


def cell_rows(j):
    return pl.ds(pl.multiple_of(j * CHAINS, CHAINS), CHAINS)


def local_kernel(
    place, own, first, second, third,
    step_weight_in, step_bias_in, decay_log_in, act_in, gate_in, cot_in,
    projection_out, step_out, step_pre_out, grad_gated_out, entering_out, carry, row_rates,
    projection, act, step, step_pre, grad_gated, entering, step_weight, step_bias, decay_log,
    gate, cot, plain, rates, basis_b, basis_c, rate_rows, decays, sems,
):
    sides, tiles, length, _ = act.shape
    states = decay_log.shape[1]
    ranks = step_weight.shape[1]
    count = length // CHAINS
    group = tile_group(tiles)
    loads = copies_of(
        [
            (step_weight_in, step_weight), (step_bias_in, step_bias), (decay_log_in, decay_log),
            (gate_in, gate), (cot_in, cot), (act_in, act),
        ],
        sems,
    )
    collect(place, (own, first, second, third), projection)
    finish_all(loads)
    for t in range(tiles):
        lanes = lane_tile(t)
        values = gate[:, lanes]
        plain[...] = cot[:, lanes] * values * jax.nn.sigmoid(values)
        to_cells(plain, grad_gated.at[t])
    fill_rates(decay_log, rates)
    for side in range(2):
        wide = dot(projection[side][:, :ranks], step_weight[side], (1, 0))
        wide = wide + step_bias[side : side + 1]
        for t in range(tiles):
            part = wide[:, lane_tile(t)]
            step_pre[side, t] = part
            step[side, t] = jnp.maximum(part, 0.0) + jnp.log1p(jnp.exp(-jnp.abs(part)))
    stores = copies_of(
        [
            (projection, projection_out), (step, step_out), (step_pre, step_pre_out),
            (grad_gated, grad_gated_out),
        ],
        sems,
    )
    zero = jnp.zeros((CHAINS, LANES), jnp.float32)
    carry[...] = jnp.zeros_like(carry)
    for side in range(2):
        up = side == 0
        fill_bases(projection, side, states, basis_b, basis_c)

        def some_tiles(first, keep):
            at_tiles = [first * group + g for g in range(group)]
            fill_rate_rows(rates, side, at_tiles, rate_rows)

            def forward(i, current):
                state, summed = current
                j = order(i, count, up)
                at = cell_rows(j)
                steps = [step[side, t, at, :] for t in at_tiles]
                drives = [v * act[side, t, at, :] for v, t in zip(steps, at_tiles)]
                new = []
                for n in range(states):
                    lanes = lane_tile(n)
                    b = basis_b[at, lanes]
                    for g in range(group):
                        decay = jnp.exp2(steps[g] * rate_rows[g, n])
                        decays[g, at, lanes] = decay
                        new.append(decay * state[n * group + g] + b * drives[g])
                return (tuple(new), tuple(a + v for a, v in zip(summed, steps)))

            start = ((zero,) * (states * group), (zero,) * group)
            state, summed = unrolled(count, 4, forward, start)

            def retreat(i, state):
                j = order(i, count, not up)
                at = cell_rows(j)
                grads = [grad_gated[t, at, :] for t in at_tiles]
                new = []
                for n in range(states):
                    lanes = lane_tile(n)
                    c = basis_c[at, lanes]
                    for g in range(group):
                        adjoint = state[n * group + g] + c * grads[g]
                        new.append(decays[g, at, lanes] * adjoint)
                return tuple(new)

            sent = unrolled(count, 4, retreat, (zero,) * (states * group))
            for g, t in enumerate(at_tiles):
                across = [jnp.exp2(summed[g] * rate_rows[g, n]) for n in range(states)]
                for kind, ends, upward in ((0, state, up), (1, sent, not up)):
                    slot = 2 * side + kind
                    ends = over_chains(across, list(ends[g::group]), upward)
                    last = CHAINS - 1 if upward else 0
                    for n in range(states):
                        entering[slot, t, n] = shifted(ends[n], 1, upward)
                        at = side * states + n
                        carry[0 if upward else 1, t, at : at + 1] = ends[n][last : last + 1]
                whole = jnp.sum(summed[g], axis=0, keepdims=True)
                at = 2 * states + side
                for k in range(2):
                    carry[k, t, at : at + 1] = whole
            return keep

        lax.fori_loop(0, tiles // group, some_tiles, 0)
    stores = stores + copies_of([(entering, entering_out)], sems.at[pl.ds(4, 1)])
    for side in range(2):
        row_rates[:, side * states : (side + 1) * states] = rates[side]
    finish_all(stores)


def tile_decay(part, rates):
    rows = rates.shape[1]
    row = lax.broadcasted_iota(jnp.int32, rates.shape, 1)
    sums = jnp.where(row < rows // 2, part[:, rows : rows + 1], part[:, rows + 1 : rows + 2])
    return jnp.exp2(rates * sums)


def pair_kernel(place, mine, other, rates, *refs):
    outs, total = refs[:-1], refs[-1]
    rows = rates.shape[1]
    core, chip = lax.rem(place[0], 2), lax.div(place[0], 2)
    low = jnp.where(core == 0, mine[...], other[...])
    high = jnp.where(core == 0, other[...], mine[...])
    spread_rates = rates[...]
    decay_low = tile_decay(low[0], spread_rates)
    decay_high = tile_decay(high[0], spread_rates)
    total[...] = low + high
    total[0, :, :rows] = decay_high * low[0][:, :rows] + high[0][:, :rows]
    total[1, :, :rows] = decay_low * high[1][:, :rows] + low[1][:, :rows]
    for s, out in enumerate(outs, 1):
        below = lax.convert_element_type((chip ^ s) < chip, jnp.int32)
        out[...] = total[below]


def chain_kernel(place, other, rates, *refs):
    gathered, (out, parts) = refs[:-2], refs[-2:]
    rows = rates.shape[1]
    chips = parts.shape[0]
    core, chip = lax.rem(place[0], 2), lax.div(place[0], 2)
    parts[chip] = jnp.zeros(parts.shape[1:], jnp.float32)
    for s, part in enumerate(gathered, 1):
        parts[chip ^ s] = part[...]
    spread_rates = rates[...]
    for kind in range(2):
        state = jnp.zeros(rates.shape, jnp.float32)
        for k in range(chips) if kind == 0 else reversed(range(chips)):
            part = parts[k]
            new = tile_decay(part, spread_rates) * state + part[:, :rows]
            state = jnp.where(k < chip if kind == 0 else k > chip, new, state)
        part = other[kind]
        new = tile_decay(part, spread_rates) * state + part[:, :rows]
        out[kind] = jnp.where(core == 1 - kind, new, state)


def long_chain_kernel(place, gathered, rates, out):
    rows = rates.shape[1]
    shards = gathered.shape[0]
    for kind in range(2):

        def turn(i, state):
            part = gathered[order(i, shards, kind == 0), kind]
            return tile_decay(part, rates[...]) * state + part[:, :rows]

        turns = place[0] if kind == 0 else shards - 1 - place[0]
        out[kind] = lax.fori_loop(0, turns, turn, jnp.zeros(rates.shape, jnp.float32))


def scan_kernel(
    place, incoming, projection_in, step_weight_in, decay_log_in, skip_gain_in, act_in, step_in,
    step_pre_in, grad_gated_in, entering_in,
    mine, first_out, second_out, third_out, grad_act_out, grad_pre_out, summed_outs,
    projection, step_weight, decay_log, skip_gain, act, step, step_pre, grad_gated, entering,
    grad_act, grad_pre, summed_out, rates, basis_b, basis_c, rate_rows, decays, history,
    grad_in, grad_out, weights, packed, skip_rows, sems,
):
    sides, tiles, length, _ = act.shape
    states = decay_log.shape[1]
    ranks = step_weight.shape[1]
    count = length // CHAINS
    group = tile_group(tiles)
    loads = copies_of(
        [
            (projection_in, projection), (decay_log_in, decay_log), (step_in, step),
            (act_in, act), (grad_gated_in, grad_gated), (entering_in, entering),
            (skip_gain_in, skip_gain), (step_pre_in, step_pre), (step_weight_in, step_weight),
        ],
        sems,
    )
    stores = []
    finish_all(loads[:2])
    fill_rates(decay_log, rates)
    zero = jnp.zeros((CHAINS, LANES), jnp.float32)
    column = lax.broadcasted_iota(jnp.int32, (CHAINS, LANES), 1)
    for side in range(2):
        up = side == 0
        fill_bases(projection, side, states, basis_b, basis_c)
        grad_in[...] = jnp.zeros_like(grad_in)
        grad_out[...] = jnp.zeros_like(grad_out)
        if side == 0:
            finish_all(loads[2:])
            for k in range(2):
                for t in range(tiles):
                    skip_rows[k, t] = skip_gain[k : k + 1, lane_tile(t)]

        def some_tiles(first, keep):
            at_tiles = [first * group + g for g in range(group)]
            fill_rate_rows(rates, side, at_tiles, rate_rows)
            skips = [skip_rows[side, t] for t in at_tiles]
            sums = []
            for t in at_tiles:
                summed = step[side, t, cell_rows(0), :]
                for j in range(1, count):
                    summed = summed + step[side, t, cell_rows(j), :]
                sums.append(summed)

            def start(kind, upward):
                slot = 2 * side + kind
                spans = []
                for g in range(group):
                    span = shifted(sums[g], 1, upward)
                    by = 1
                    while by < CHAINS:
                        span = span + shifted(span, by, upward)
                        by *= 2
                    spans.append(span)
                first = []
                for n in range(states):
                    at = side * states + n
                    for g, t in enumerate(at_tiles):
                        decay = jnp.exp2(spans[g] * rate_rows[g, n])
                        value = incoming[0 if upward else 1, t, at : at + 1, :]
                        first.append(entering[slot, t, n] + decay * value)
                return tuple(first)

            def forward(i, state):
                j = order(i, count, up)
                at = cell_rows(j)
                steps = [step[side, t, at, :] for t in at_tiles]
                acts = [act[side, t, at, :] for t in at_tiles]
                grads = [grad_gated[t, at, :] for t in at_tiles]
                drives = [v * a for v, a in zip(steps, acts)]
                outs = [v * a for v, a in zip(skips, acts)]
                new = []
                for n in range(states):
                    lanes = lane_tile(n)
                    b, c = basis_b[at, lanes], basis_c[at, lanes]
                    read = grad_out[at, lanes]
                    for g in range(group):
                        before = state[n * group + g]
                        decay = jnp.exp2(steps[g] * rate_rows[g, n])
                        decays[g, at, lanes] = decay
                        history[g, at, lanes] = before
                        current = decay * before + b * drives[g]
                        outs[g] = outs[g] + c * current
                        read = read + current * grads[g]
                        new.append(current)
                    grad_out[at, lanes] = read
                for g, t in enumerate(at_tiles):
                    if side == 0:
                        summed_out[t, at, :] = outs[g]
                    else:
                        summed_out[t, at, :] = summed_out[t, at, :] + outs[g]
                return tuple(new)

            unrolled(count, 2, forward, start(0, up))

            def retreat(i, state):
                j = order(i, count, not up)
                at = cell_rows(j)
                steps = [step[side, t, at, :] for t in at_tiles]
                acts = [act[side, t, at, :] for t in at_tiles]
                grads = [grad_gated[t, at, :] for t in at_tiles]
                drives = [v * a for v, a in zip(steps, acts)]
                step_terms = [zero] * group
                drive_grads = [zero] * group
                new = []
                for n in range(states):
                    lanes = lane_tile(n)
                    b, c = basis_b[at, lanes], basis_c[at, lanes]
                    put = grad_in[at, lanes]
                    for g in range(group):
                        adjoint = state[n * group + g] + c * grads[g]
                        carried = decays[g, at, lanes] * adjoint
                        new.append(carried)
                        term = carried * history[g, at, lanes] * rate_rows[g, n]
                        step_terms[g] = step_terms[g] + term
                        drive_grads[g] = drive_grads[g] + adjoint * b
                        put = put + adjoint * drives[g]
                    grad_in[at, lanes] = put
                for g, t in enumerate(at_tiles):
                    grad_step = step_terms[g] * LN2 + drive_grads[g] * acts[g]
                    grad_act[side, t, at, :] = grads[g] * skips[g] + drive_grads[g] * steps[g]
                    pre = step_pre[side, t, at, :]
                    grad_pre[side, t, at, :] = grad_step * jax.nn.sigmoid(pre)
                return tuple(new)

            unrolled(count, 2, retreat, start(1, not up))
            return keep

        lax.fori_loop(0, tiles // group, some_tiles, 0)
        pairs = [
            (grad_act.at[side], grad_act_out.at[side]), (grad_pre.at[side], grad_pre_out.at[side]),
        ]
        if side == 1:
            pairs.append((summed_out, summed_outs))
        stores = stores + copies_of(pairs, sems.at[pl.ds(2 * side, 3)])
        wide = full_width(grad_pre, side)
        weights[...] = jnp.zeros_like(weights)
        weights[:ranks] = step_weight[side]
        packed[...] = dot(wide, weights[...], (1, 1))

        def pack(j, keep):
            at = cell_rows(j)
            line = packed[at, :]
            for values, start_at in ((grad_in, ranks), (grad_out, ranks + states)):
                for n in range(states):
                    total = jnp.sum(values[at, lane_tile(n)], axis=1, keepdims=True)
                    line = jnp.where(column == start_at + n, total, line)
            packed[at, :] = line
            return keep

        lax.fori_loop(0, count, pack, 0)
        deal(place, (mine, first_out, second_out, third_out), side, packed)
    finish_all(stores)


def step_kernel(grad_pre_in, projection_in, after_this, step_part, grad_pre, projection, sems):
    _, tiles, ranks, _ = step_part.shape
    finish_all(copies_of([(grad_pre_in, grad_pre), (projection_in, projection)], sems))
    for side in range(2):
        wide = dot(projection[side], full_width(grad_pre, side), (0, 0))
        for t in range(tiles):
            step_part[side, t] = wide[:ranks, lane_tile(t)]


def gate_kernel(
    summed_in, gate_in, cot_in, after_this, block_out, gate_grad, summed, gate, cot, plain, sems
):
    finish_all(copies_of([(summed_in, summed), (gate_in, gate), (cot_in, cot)], sems))
    for t in range(summed.shape[0]):
        lanes = lane_tile(t)
        values = gate[:, lanes]
        to_tokens(summed.at[t], plain)
        both = plain[...]
        block_out[:, lanes] = both * values * jax.nn.sigmoid(values)
        gate_grad[:, lanes] = cot[:, lanes] * both * silu_grad(values)


def weight_kernel(
    place, column, own, first, second, third, act_in, pre_in, grad_act_in, select_in, step_part,
    keep, send, conv_grad_out, head, tail,
    act, pre, grad_act, select, grad, both, conv_grad, plain, sems,
):
    sides, tiles, length, _ = act.shape
    loads = copies_of(
        [
            (act_in, act), (select_in, select), (grad_act_in, grad_act), (pre_in, pre),
        ],
        sems,
    )
    collect(column, (own, first, second, third), grad)
    loads[0].wait()
    for side in range(2):
        both[side, : tiles * LANES] = dot(full_width(act, side), grad[side], (0, 0))
        both[side, tiles * LANES :] = step_part[side].reshape(-1, LANES)
    core = lax.rem(place[0], 2)
    stores = copies_of(
        [(both.at[core], keep), (both.at[1 - core], send)], sems.at[pl.ds(4, 2)]
    )
    finish_all(loads[1:])
    for side in range(2):
        wide = dot(grad[side], select[side], (1, 1))
        for t in range(tiles):
            lanes = lane_tile(t)
            grad_act[side, t] = grad_act[side, t] + wide[:, lanes]
            to_tokens(grad_act.at[side, t], plain)
            conv_grad[side, :, lanes] = plain[...] * silu_grad(pre[side, t])
    head[...] = conv_grad[0, :HALO]
    tail[...] = conv_grad[1, length - HALO :]
    stores = stores + copies_of([(conv_grad, conv_grad_out)], sems.at[pl.ds(0, 1)])
    finish_all(stores)


def halves_kernel(place, keep, got, mine, *refs):
    outs, (total,) = refs[:-1], refs[-1:]
    share = mine.shape[0]
    chips = len(outs) + 1
    for k in range(chips):
        at = slice(k * share, (k + 1) * share)
        total[k] = keep[at] + got[at]
    chip = lax.div(place[0], 2)
    mine[...] = total[chip]
    for s, out in enumerate(outs, 1):
        out[...] = total[chip ^ s]


def add_after_kernel(after_this, *refs):
    add_kernel(*refs)


def add_kernel(*refs):
    total = refs[0][...]
    for ref in refs[1:-1]:
        total = total + ref[...]
    refs[-1][...] = total


def join_kernel(place, after_this, mine, *refs):
    parts, out = refs[:-1], refs[-1]
    chip = lax.div(place[0], 2)
    out[chip] = mine[...]
    for s, part in enumerate(parts, 1):
        out[chip ^ s] = part[...]


def outputs_kernel(place, mine, other, select_grad, step_grad, both):
    sides, width, _ = select_grad.shape
    ranks = step_grad.shape[1]
    chips = mine.shape[0]
    core = lax.rem(place[0], 2)
    size = mine.shape[1]
    for side in range(2):
        for k in range(chips):
            both[side, k * size : (k + 1) * size] = jnp.where(core == side, mine[k], other[k])
        select_grad[side] = both[side, :width]
        for t in range(width // LANES):
            at = width + t * ranks
            step_grad[side, :, lane_tile(t)] = both[side, at : at + ranks]


def exit_kernel(
    before, after, conv_grad, conv_weight_in, after_this, tokens_grad, up, down, conv_weight, sems
):
    _, length, width = conv_grad.shape
    taps = conv_weight.shape[1]
    margin = taps - 1
    loads = copies_of(
        [
            (conv_grad.at[0], up.at[pl.ds(0, length)]),
            (conv_grad.at[1], down.at[pl.ds(HALO, length)]),
            (conv_weight_in, conv_weight),
        ],
        sems,
    )
    up[length:] = after[...]
    down[:HALO] = before[...]
    finish_all(loads)
    for t in range(width // LANES):
        lanes = lane_tile(t)
        total = jnp.zeros((length, LANES), jnp.float32)
        for k in range(taps):
            at = margin - k
            total = total + conv_weight[0, k : k + 1, lanes] * up[at : at + length, lanes]
            at = HALO - margin + k
            total = total + conv_weight[1, k : k + 1, lanes] * down[at : at + length, lanes]
        tokens_grad[:, lanes] = total


def from_before(value, axis):
    count = lax.axis_size(axis)
    return lax.ppermute(value, axis, [(i, i + 1) for i in range(count - 1)])


def from_after(value, axis):
    count = lax.axis_size(axis)
    return lax.ppermute(value, axis, [(i + 1, i) for i in range(count - 1)])


def swapped(value, axis, by):
    count = lax.axis_size(axis)
    return lax.ppermute(value, axis, [(i, i ^ by) for i in range(count)])


def call(kernel, name, out_shape, scratch, mib, args, kinds, outs=None):
    spaces = {
        "v": pl.BlockSpec(memory_space=pltpu.VMEM),
        "h": pl.BlockSpec(memory_space=pltpu.HBM),
        "s": pl.BlockSpec(memory_space=pltpu.SMEM),
    }
    outs = outs or "v" * len(out_shape)
    args = [
        pltpu.with_memory_space_constraint(a, pltpu.HBM) if k == "h" else a
        for a, k in zip(args, kinds, strict=True)
    ]
    results = [
        pltpu.HBM(shape, jnp.float32) if k == "h" else shape_of(*shape)
        for shape, k in zip(out_shape, outs, strict=True)
    ]
    return pl.pallas_call(
        kernel,
        in_specs=[spaces[k] for k in kinds],
        out_specs=[spaces[k] for k in outs],
        out_shape=results,
        scratch_shapes=scratch,
        compiler_params=params(mib),
        cost_estimate=pl.CostEstimate(flops=2**28, bytes_accessed=2**22, transcendentals=2**18),
        name=name,
    )(*args)


def summed_shares(parts, name):
    count = len(parts)
    if count == 1:
        return (lax.psum(parts[0], "ch"),), parts[0]
    got = [swapped(part, "ch", s) for s, part in enumerate(parts[1:], 1)]
    (mine,) = call(add_kernel, name, (parts[0].shape,), [], 4, (parts[0], *got), "v" * count)
    return (mine, *(swapped(mine, "ch", s) for s in range(1, count))), got[0]


def halved(place, keep, send, rows, chips, name):
    got = swapped(send, "ctx", 1)
    share = rows // chips
    mine, *sent = call(
        halves_kernel, name, ((share, LANES),) * chips, [pltpu.VMEM((chips, share, LANES), jnp.float32)],
        8, (place, keep, got), "svv",
    )
    return (mine, *(swapped(part, "ctx", 2 * s) for s, part in enumerate(sent, 1)))


def on_device(
    tokens, gate_input, cotangent, conv_weight, conv_bias, select_weight, step_weight,
    step_bias, decay_log, skip_gain,
):
    length, width = tokens.shape
    tiles = width // LANES
    states = decay_log.shape[1]
    ranks = step_weight.shape[1]
    places = lax.axis_size("ctx")
    columns = lax.axis_size("ch")
    place = lax.axis_index("ctx").astype(jnp.int32).reshape(1)
    column = lax.axis_index("ch").astype(jnp.int32).reshape(1)
    group = tile_group(tiles)
    chips = places // 2
    near = places == 8
    narrow = (2, length, LANES)
    shared = (2, length // columns, LANES)
    one = (tiles, length, LANES)
    pair = (2, *one)
    flat = (length, width)
    chain_ends = (4, tiles, states, CHAINS, LANES)
    carry = (2, tiles, 2 * states + 8, LANES)
    row_rates = (tiles, 2 * states, LANES)
    vmem = functools.partial(pltpu.VMEM, dtype=jnp.float32)
    dma = lambda n: pltpu.SemaphoreType.DMA((n,))
    bases = vmem((length, states * LANES))
    grouped = vmem((group, length, states * LANES))
    rate_scratch = vmem((2, tiles, states, LANES))
    row_scratch = vmem((group, states, CHAINS, LANES))

    before = from_before(tokens[length - HALO :], "ctx")
    after = from_after(tokens[:HALO], "ctx")
    *parts, act, pre = call(
        entry_kernel, "entry", (*(shared,) * columns, pair, pair),
        [
            vmem((length + 2 * HALO, width)), vmem(conv_weight.shape), vmem(conv_bias.shape),
            vmem(select_weight.shape), vmem(pair), vmem(pair), vmem(one[1:]), dma(6),
        ],
        12, (column, before, after, tokens, conv_weight, conv_bias, select_weight), "svvhhhh",
        "v" * columns + "hh",
    )
    projection, step, step_pre, grad_gated, entering, carried, rates = call(
        local_kernel, "local", (narrow, pair, pair, one, chain_ends, carry, row_rates),
        [
            vmem(narrow), vmem(pair), vmem(pair), vmem(pair), vmem(one), vmem(chain_ends),
            vmem(step_weight.shape), vmem(step_bias.shape), vmem(decay_log.shape),
            vmem(flat), vmem(flat), vmem(one[1:]),
            rate_scratch, bases, bases, row_scratch, grouped, dma(6),
        ],
        24,
        (
            column, *summed_shares(parts, "projection")[0], step_weight, step_bias, decay_log, act,
            gate_input, cotangent,
        ),
        "svvvvhhhhhh", "hhhhhvv",
    )
    if near:
        other = swapped(carried, "ctx", 1)
        sent = call(
            pair_kernel, "pair", (carry[1:],) * (chips - 1),
            [vmem(carry)], 8, (place, carried, other, rates), "svvv",
        )
        got = [swapped(part, "ctx", 2 * s) for s, part in enumerate(sent, 1)]
        (incoming,) = call(
            chain_kernel, "chain", ((2, *row_rates),), [vmem((chips, *carry[1:]))],
            8, (place, other, rates, *got), "svv" + "v" * len(got),
        )
    else:
        gathered = lax.all_gather(carried, "ctx")
        (incoming,) = call(
            long_chain_kernel, "chain", ((2, *row_rates),), [],
            48, (place, gathered, rates), "svv",
        )
    *grad_parts, grad_act, grad_pre, summed = call(
        scan_kernel, "scan", (*(shared,) * columns, pair, pair, one),
        [
            vmem(narrow), vmem(step_weight.shape), vmem(decay_log.shape), vmem(skip_gain.shape),
            vmem(pair), vmem(pair), vmem(pair), vmem(one), vmem(chain_ends),
            vmem(pair), vmem(pair), vmem(one), rate_scratch, bases, bases, row_scratch, grouped,
            grouped, bases, bases, vmem((LANES, width)), vmem((length, LANES)),
            vmem((2, tiles, 1, LANES)), dma(9),
        ],
        28,
        (
            column, incoming, projection, step_weight, decay_log, skip_gain, act, step, step_pre,
            grad_gated, entering,
        ),
        "svhhhhhhhhh", "v" * columns + "hhh",
    )
    grad_shares, arrived = summed_shares(grad_parts, "grad_projection")
    (step_part,) = call(
        step_kernel, "step_grad", ((2, tiles, ranks, LANES),), [vmem(pair), vmem(narrow), dma(2)],
        8, (grad_pre, projection, arrived), "hhv",
    )
    half = width + tiles * ranks
    keep, send, conv_grad, head, tail = call(
        weight_kernel, "weights",
        ((half, LANES), (half, LANES), (2, *flat), (HALO, width), (HALO, width)),
        [
            vmem(pair), vmem(pair), vmem(pair), vmem(select_weight.shape), vmem(narrow),
            vmem((2, half, LANES)), vmem((2, *flat)), vmem(one[1:]), dma(6),
        ],
        16,
        (place, column, *grad_shares, act, pre, grad_act, select_weight, step_part),
        "ssvvvvhhhhv", "vvhvv",
    )
    before = from_before(tail, "ctx")
    after = from_after(head, "ctx")
    if near:
        shares = halved(place, keep, send, half, chips, "halves")
        ahead = shares[0]
    else:
        ahead = head
    (tokens_grad,) = call(
        exit_kernel, "exit", (flat,),
        [
            vmem((length + HALO, width)), vmem((length + HALO, width)), vmem(conv_weight.shape),
            dma(3),
        ],
        8, (before, after, conv_grad, conv_weight, ahead), "vvhhv",
    )
    if near:
        rows = half // chips
        (mine,) = call(
            add_after_kernel, "share_sum", ((rows, LANES),), [], 4, (tokens_grad, *shares),
            "h" + "v" * chips,
        )
        ahead = mine
    block_out, gate_grad = call(
        gate_kernel, "gate", (flat, flat),
        [vmem(one), vmem(flat), vmem(flat), vmem(one[1:]), dma(3)],
        8, (summed, gate_input, cotangent, ahead), "hhhv",
    )
    if near:
        got = [swapped(mine, "ctx", 2 * s) for s in range(1, chips)]
        (joined,) = call(
            join_kernel, "joined", ((chips, rows, LANES),), [],
            8, (place, block_out, mine, *got), "sh" + "v" * chips,
        )
        select_grad, step_grad = call(
            outputs_kernel, "weight_grads", ((2, width, LANES), (2, ranks, width)),
            [vmem((2, half, LANES))],
            12, (place, joined, swapped(joined, "ctx", 1)), "svv",
        )
    else:
        first = lax.rem(place[0], 2) == 0
        both = jnp.where(first, jnp.stack([keep, send]), jnp.stack([send, keep]))
        both = lax.psum(both, "ctx")
        select_grad = both[:, :width]
        step_grad = both[:, width:].reshape(2, tiles, ranks, LANES)
        step_grad = step_grad.transpose(0, 2, 1, 3).reshape(2, ranks, width)
    return (block_out, tokens_grad, gate_grad, select_grad, step_grad)


def solution(mesh):
    return jax.shard_map(
        on_device,
        mesh=mesh,
        in_specs=(
            P("ctx", "ch"),
            P("ctx", "ch"),
            P("ctx", "ch"),
            P(None, None, "ch"),
            P(None, "ch"),
            P(None, "ch", None),
            P(None, None, "ch"),
            P(None, "ch"),
            P(None, None, "ch"),
            P(None, "ch"),
        ),
        out_specs=(
            P("ctx", "ch"),
            P("ctx", "ch"),
            P("ctx", "ch"),
            P(None, "ch", None),
            P(None, None, "ch"),
        ),
        check_vma=False,
    )
```

```python
import functools

import jax
import jax.numpy as jnp
from jax import lax
from jax.experimental import pallas as pl
from jax.experimental.pallas import tpu as pltpu
from jax.sharding import PartitionSpec as P

FULL_PRECISION = lax.Precision.HIGHEST
LANES = 128
CHAINS = 8
HALO = 8
LOG2E = 1.4426950408889634
LN2 = 0.6931471805599453
MIB = 1024 * 1024


def params(mib):
    return pltpu.CompilerParams(vmem_limit_bytes=mib * MIB)


def shape_of(*dims):
    return jax.ShapeDtypeStruct(dims, jnp.float32)


def dot(a, b, contract):
    return lax.dot_general(
        a, b, ((contract[:1], contract[1:]), ((), ())), precision=FULL_PRECISION,
        preferred_element_type=jnp.float32,
    )


def silu_grad(values):
    sigmoid_values = jax.nn.sigmoid(values)
    return sigmoid_values * (1.0 + values * (1.0 - sigmoid_values))


def lane_tile(t):
    return slice(t * LANES, (t + 1) * LANES)


def full_width(ref, *lead):
    tiles = ref.shape[len(lead)]
    return jnp.concatenate([ref[(*lead, t)] for t in range(tiles)], axis=1)


def convolved(ext, at_row, side, lanes, rows, conv_weight, conv_bias):
    taps = conv_weight.shape[1]
    margin = taps - 1
    conv = jnp.broadcast_to(conv_bias[side : side + 1, lanes], (rows, LANES))
    for k in range(taps):
        at = at_row + (k - margin if side == 0 else margin - k)
        conv = conv + conv_weight[side, k : k + 1, lanes] * ext[at : at + rows, lanes]
    return conv


def copies_of(pairs, sems):
    copies = [pltpu.make_async_copy(a, b, sems.at[i]) for i, (a, b) in enumerate(pairs)]
    for copy in copies:
        copy.start()
    return copies


def to_cells(tokens, cells):
    count = tokens.shape[0] // CHAINS
    for j in range(count):
        cells[j * CHAINS : (j + 1) * CHAINS] = tokens[pl.ds(j, CHAINS, stride=count), :]


def to_tokens(cells, tokens):
    count = tokens.shape[0] // CHAINS
    for j in range(count):
        tokens[pl.ds(j, CHAINS, stride=count), :] = cells[j * CHAINS : (j + 1) * CHAINS]


def finish_all(copies):
    for copy in copies:
        copy.wait()


def entry_kernel(
    place, before, after, tokens, conv_weight_in, conv_bias_in, select_in,
    *refs,
):
    outs, refs = refs[:-11], refs[-11:]
    act_out, pre_out, ext, conv_weight, conv_bias, select, act, pre, plain, rows, sems = refs

    length, width = tokens.shape
    loads = copies_of(
        [
            (tokens, ext.at[pl.ds(HALO, length)]), (conv_weight_in, conv_weight),
            (conv_bias_in, conv_bias), (select_in, select),
        ],
        sems,
    )
    ext[:HALO] = before[...]
    ext[HALO + length :] = after[...]
    finish_all(loads[:3])
    for side in range(2):
        for t in range(width // LANES):
            conv = convolved(ext, HALO, side, lane_tile(t), length, conv_weight, conv_bias)
            pre[side, t] = conv
            plain[...] = conv * jax.nn.sigmoid(conv)
            to_cells(plain, act.at[side, t])
    stores = copies_of([(pre, pre_out), (act, act_out)], sems.at[pl.ds(4, 2)])
    loads[3].wait()
    for side in range(2):
        rows[...] = dot(full_width(act, side), select[side], (1, 0))
        deal(place, outs, side, rows)
    finish_all(stores)


def turned(k, by, count):
    return lax.rem(k - 1 + by, count - 1) + 1


def deal(place, outs, side, rows):
    share = outs[0].shape[1]
    for k in range(len(outs)):
        to = place[1] ^ turned(k, place[0], len(outs)) if k else place[1]
        at = pl.multiple_of(to * share, share)
        outs[k][side] = rows[pl.ds(at, share), :]


def collect(place, parts, out):
    share = parts[0].shape[1]
    for k in range(len(parts)):
        source = place[1] ^ turned(k, place[0], len(parts)) if k else place[1]
        at = pl.multiple_of(source * share, share)
        out[:, pl.ds(at, share), :] = parts[k][...]


def spread(projection, side, j, states, basis_b, basis_c):
    ranks = LANES - 2 * states
    at = pl.ds(pl.multiple_of(j * CHAINS, CHAINS), CHAINS)
    rows = projection[side, at, :]
    for n in range(states):
        b = rows[:, ranks + n : ranks + n + 1]
        c = rows[:, ranks + states + n : ranks + states + n + 1]
        basis_b[at, lane_tile(n)] = jnp.broadcast_to(b, (CHAINS, LANES))
        basis_c[at, lane_tile(n)] = jnp.broadcast_to(c, (CHAINS, LANES))


def fill_bases(projection, side, states, basis_b, basis_c):
    def body(j, carry):
        spread(projection, side, j, states, basis_b, basis_c)
        return carry

    lax.fori_loop(0, basis_b.shape[0] // CHAINS, body, 0)


def fill_rates(decay_log, rates):
    for side in range(rates.shape[0]):
        for t in range(rates.shape[1]):
            rates[side, t] = -LOG2E * jnp.exp(decay_log[side, :, lane_tile(t)])


def sublane():
    return lax.broadcasted_iota(jnp.int32, (CHAINS, LANES), 0)


def shifted(value, by, up):
    rolled = pltpu.roll(value, by if up else CHAINS - by, 0)
    place = sublane()
    keep = place >= by if up else place < CHAINS - by
    return jnp.where(keep, rolled, 0.0)


def over_chains(decays, ends, up):
    by = 1
    while by < CHAINS:
        ends = [d * shifted(f, by, up) + f for d, f in zip(decays, ends)]
        if 2 * by < CHAINS:
            turn = by if up else CHAINS - by
            decays = [d * pltpu.roll(d, turn, 0) for d in decays]
        by *= 2
    return ends


def order(i, count, up):
    return i if up else count - 1 - i


def tile_group(tiles):
    return 2 if tiles % 2 == 0 else 1


def unrolled(count, times, body, start):
    times = times if count % times == 0 else 1

    def several(i, state):
        for k in range(times):
            state = body(i * times + k, state)
        return state

    return lax.fori_loop(0, count // times, several, start)


def plus(total, term):
    return term if total is None else total + term


def fill_rate_rows(rates, side, tiles, rate_rows):
    for g, t in enumerate(tiles):
        for n in range(rate_rows.shape[1]):
            rate_rows[g, n] = jnp.broadcast_to(rates[side, t, n : n + 1], (CHAINS, LANES))


def cell_rows(j):
    return pl.ds(pl.multiple_of(j * CHAINS, CHAINS), CHAINS)


def local_kernel(
    place, own, first, second, third,
    step_weight_in, step_bias_in, decay_log_in, act_in, gate_in, cot_in,
    projection_out, step_out, step_pre_out, grad_gated_out, entering_out, carry, row_rates,
    projection, act, step, step_pre, grad_gated, entering, step_weight, step_bias, decay_log,
    gate, cot, plain, rates, basis_b, basis_c, rate_rows, decays, sems,
):
    sides, tiles, length, _ = act.shape
    states = decay_log.shape[1]
    ranks = step_weight.shape[1]
    count = length // CHAINS
    group = tile_group(tiles)
    loads = copies_of(
        [
            (step_weight_in, step_weight), (step_bias_in, step_bias), (decay_log_in, decay_log),
            (gate_in, gate), (cot_in, cot), (act_in, act),
        ],
        sems,
    )
    collect(place, (own, first, second, third), projection)
    finish_all(loads)
    for t in range(tiles):
        lanes = lane_tile(t)
        values = gate[:, lanes]
        plain[...] = cot[:, lanes] * values * jax.nn.sigmoid(values)
        to_cells(plain, grad_gated.at[t])
    fill_rates(decay_log, rates)
    for side in range(2):
        wide = dot(projection[side][:, :ranks], step_weight[side], (1, 0))
        wide = wide + step_bias[side : side + 1]
        for t in range(tiles):
            part = wide[:, lane_tile(t)]
            step_pre[side, t] = part
            step[side, t] = jnp.maximum(part, 0.0) + jnp.log1p(jnp.exp(-jnp.abs(part)))
    stores = copies_of(
        [
            (projection, projection_out), (step, step_out), (step_pre, step_pre_out),
            (grad_gated, grad_gated_out),
        ],
        sems,
    )
    zero = jnp.zeros((CHAINS, LANES), jnp.float32)
    carry[...] = jnp.zeros_like(carry)
    for side in range(2):
        up = side == 0
        fill_bases(projection, side, states, basis_b, basis_c)

        def some_tiles(first, keep):
            at_tiles = [first * group + g for g in range(group)]
            fill_rate_rows(rates, side, at_tiles, rate_rows)

            def forward(i, current):
                state, summed = current
                j = order(i, count, up)
                at = cell_rows(j)
                steps = [step[side, t, at, :] for t in at_tiles]
                drives = [v * act[side, t, at, :] for v, t in zip(steps, at_tiles)]
                new = []
                for n in range(states):
                    lanes = lane_tile(n)
                    b = basis_b[at, lanes]
                    for g in range(group):
                        decay = jnp.exp2(steps[g] * rate_rows[g, n])
                        decays[g, at, lanes] = decay
                        new.append(decay * state[n * group + g] + b * drives[g])
                return (tuple(new), tuple(a + v for a, v in zip(summed, steps)))

            start = ((zero,) * (states * group), (zero,) * group)
            state, summed = unrolled(count, 8, forward, start)

            def retreat(i, state):
                j = order(i, count, not up)
                at = cell_rows(j)
                grads = [grad_gated[t, at, :] for t in at_tiles]
                new = []
                for n in range(states):
                    lanes = lane_tile(n)
                    c = basis_c[at, lanes]
                    for g in range(group):
                        adjoint = state[n * group + g] + c * grads[g]
                        new.append(decays[g, at, lanes] * adjoint)
                return tuple(new)

            sent = unrolled(count, 8, retreat, (zero,) * (states * group))
            for g, t in enumerate(at_tiles):
                across = [jnp.exp2(summed[g] * rate_rows[g, n]) for n in range(states)]
                for kind, ends, upward in ((0, state, up), (1, sent, not up)):
                    slot = 2 * side + kind
                    ends = over_chains(across, list(ends[g::group]), upward)
                    last = CHAINS - 1 if upward else 0
                    for n in range(states):
                        entering[slot, t, n] = shifted(ends[n], 1, upward)
                        at = side * states + n
                        carry[0 if upward else 1, t, at : at + 1] = ends[n][last : last + 1]
                whole = jnp.sum(summed[g], axis=0, keepdims=True)
                at = 2 * states + side
                for k in range(2):
                    carry[k, t, at : at + 1] = whole
            return keep

        lax.fori_loop(0, tiles // group, some_tiles, 0)
    stores = stores + copies_of([(entering, entering_out)], sems.at[pl.ds(4, 1)])
    for side in range(2):
        row_rates[:, side * states : (side + 1) * states] = rates[side]
    finish_all(stores)


def tile_decay(part, rates):
    rows = rates.shape[1]
    row = lax.broadcasted_iota(jnp.int32, rates.shape, 1)
    sums = jnp.where(row < rows // 2, part[:, rows : rows + 1], part[:, rows + 1 : rows + 2])
    return jnp.exp2(rates * sums)


def prep_kernel(
    projection_in, act_in, pre_in, after_this, bases_out, turned_act_out, slope_out, done,
    projection, act, pre, bases, turned_act, sems,
):
    sides, tiles, length, _ = act.shape
    states = bases.shape[3] // LANES
    loads = copies_of([(projection_in, projection), (act_in, act), (pre_in, pre)], sems)
    loads[0].wait()
    stores = []
    for side in range(sides):
        fill_bases(projection, side, states, bases.at[side, 0], bases.at[side, 1])
        stores += copies_of([(bases.at[side], bases_out.at[side])], sems.at[pl.ds(3 + side, 1)])
    finish_all(loads[1:])
    for side in range(sides):
        for t in range(tiles):
            turned_act[side, lane_tile(t)] = act[side, t].T
            pre[side, t] = silu_grad(pre[side, t])
    stores += copies_of(
        [(turned_act, turned_act_out), (pre, slope_out)], sems.at[pl.ds(5, 2)]
    )
    done[...] = jnp.zeros_like(done)
    finish_all(stores)


def pair_kernel(place, mine, other, rates, *refs):
    outs, total = refs[:-1], refs[-1]
    rows = rates.shape[1]
    core, chip = lax.rem(place[0], 2), lax.div(place[0], 2)
    low = jnp.where(core == 0, mine[...], other[...])
    high = jnp.where(core == 0, other[...], mine[...])
    spread_rates = rates[...]
    decay_low = tile_decay(low[0], spread_rates)
    decay_high = tile_decay(high[0], spread_rates)
    total[...] = low + high
    total[0, :, :rows] = decay_high * low[0][:, :rows] + high[0][:, :rows]
    total[1, :, :rows] = decay_low * high[1][:, :rows] + low[1][:, :rows]
    tiles = rates.shape[0]
    for k, out in enumerate(outs, 1):
        to = chip ^ turned(k, core, len(outs) + 1)
        below = lax.convert_element_type(to < chip, jnp.int32)
        for t in range(tiles):
            out[t * rows : (t + 1) * rows] = total[below, t, :rows]
            for side in range(2):
                at = tiles * rows + side * tiles + t
                out[at : at + 1] = total[0, t, rows + side : rows + side + 1]


def chain_kernel(place, other, rates, after_this, *refs):
    gathered, (out, parts) = refs[:-2], refs[-2:]
    rows = rates.shape[1]
    chips = parts.shape[0]
    core, chip = lax.rem(place[0], 2), lax.div(place[0], 2)
    parts[chip] = jnp.zeros(parts.shape[1:], jnp.float32)
    tiles = rates.shape[0]
    for k, part in enumerate(gathered, 1):
        source = chip ^ turned(k, core, chips)
        for t in range(tiles):
            parts[source, t, :rows] = part[t * rows : (t + 1) * rows]
            for side in range(2):
                at = tiles * rows + side * tiles + t
                parts[source, t, rows + side : rows + side + 1] = part[at : at + 1]
    spread_rates = rates[...]
    for kind in range(2):
        state = jnp.zeros(rates.shape, jnp.float32)
        for k in range(chips) if kind == 0 else reversed(range(chips)):
            part = parts[k]
            new = tile_decay(part, spread_rates) * state + part[:, :rows]
            state = jnp.where(k < chip if kind == 0 else k > chip, new, state)
        part = other[kind]
        new = tile_decay(part, spread_rates) * state + part[:, :rows]
        out[kind] = jnp.where(core == 1 - kind, new, state)


def long_chain_kernel(place, gathered, rates, out):
    rows = rates.shape[1]
    shards = gathered.shape[0]
    for kind in range(2):

        def turn(i, state):
            part = gathered[order(i, shards, kind == 0), kind]
            return tile_decay(part, rates[...]) * state + part[:, :rows]

        turns = place[0] if kind == 0 else shards - 1 - place[0]
        out[kind] = lax.fori_loop(0, turns, turn, jnp.zeros(rates.shape, jnp.float32))


def scan_kernel(
    place, incoming, bases_in, step_weight_in, decay_log_in, skip_gain_in, act_in, step_in,
    step_pre_in, grad_gated_in, entering_in,
    mine, first_out, second_out, third_out, grad_act_out, grad_pre_out, summed_outs,
    bases, step_weight, decay_log, skip_gain, act, step, step_pre, grad_gated, entering,
    grad_act, grad_pre, summed_out, rates, rate_rows, decays, history,
    grad_in, grad_out, weights, packed, skip_rows, sems,
):
    sides, tiles, length, _ = act.shape
    states = decay_log.shape[1]
    ranks = step_weight.shape[1]
    count = length // CHAINS
    group = tile_group(tiles)
    loads = copies_of(
        [
            (decay_log_in, decay_log), (skip_gain_in, skip_gain), (step_in, step),
            (act_in, act), (bases_in.at[0], bases.at[0]), (grad_gated_in, grad_gated),
            (entering_in, entering), (step_pre_in, step_pre), (bases_in.at[1], bases.at[1]),
            (step_weight_in, step_weight),
        ],
        sems,
    )
    stores = []
    finish_all(loads[:2])
    fill_rates(decay_log, rates)
    column = lax.broadcasted_iota(jnp.int32, (CHAINS, LANES), 1)
    for side in range(2):
        up = side == 0
        basis_b, basis_c = bases.at[side, 0], bases.at[side, 1]
        grad_in[...] = jnp.zeros_like(grad_in)
        grad_out[...] = jnp.zeros_like(grad_out)
        if side == 0:
            for k in range(2):
                for t in range(tiles):
                    skip_rows[k, t] = skip_gain[k : k + 1, lane_tile(t)]
            finish_all(loads[2:-2])
        else:
            loads[-2].wait()

        def some_tiles(first, keep):
            at_tiles = [first * group + g for g in range(group)]
            fill_rate_rows(rates, side, at_tiles, rate_rows)
            skips = [skip_rows[side, t] for t in at_tiles]
            sums = []
            for t in at_tiles:
                summed = step[side, t, cell_rows(0), :]
                for j in range(1, count):
                    summed = summed + step[side, t, cell_rows(j), :]
                sums.append(summed)

            def start(kind, upward):
                slot = 2 * side + kind
                spans = []
                for g in range(group):
                    span = shifted(sums[g], 1, upward)
                    by = 1
                    while by < CHAINS:
                        span = span + shifted(span, by, upward)
                        by *= 2
                    spans.append(span)
                first = []
                for n in range(states):
                    at = side * states + n
                    for g, t in enumerate(at_tiles):
                        decay = jnp.exp2(spans[g] * rate_rows[g, n])
                        value = incoming[0 if upward else 1, t, at : at + 1, :]
                        first.append(entering[slot, t, n] + decay * value)
                return tuple(first)

            def forward(i, state):
                j = order(i, count, up)
                at = cell_rows(j)
                steps = [step[side, t, at, :] for t in at_tiles]
                acts = [act[side, t, at, :] for t in at_tiles]
                grads = [grad_gated[t, at, :] for t in at_tiles]
                drives = [v * a for v, a in zip(steps, acts)]
                outs = [[v * a, None] for v, a in zip(skips, acts)]
                new = []
                for n in range(states):
                    lanes = lane_tile(n)
                    b, c = basis_b[at, lanes], basis_c[at, lanes]
                    read = grad_out[at, lanes]
                    for g in range(group):
                        before = state[n * group + g]
                        decay = jnp.exp2(steps[g] * rate_rows[g, n])
                        decays[g, at, lanes] = decay
                        history[g, at, lanes] = before
                        current = decay * before + b * drives[g]
                        outs[g][n % 2] = plus(outs[g][n % 2], c * current)
                        read = read + current * grads[g]
                        new.append(current)
                    grad_out[at, lanes] = read
                for g, t in enumerate(at_tiles):
                    out = outs[g][0] + outs[g][1]
                    if side == 0:
                        summed_out[t, at, :] = out
                    else:
                        summed_out[t, at, :] = summed_out[t, at, :] + out
                return tuple(new)

            unrolled(count, 4, forward, start(0, up))

            def retreat(i, state):
                j = order(i, count, not up)
                at = cell_rows(j)
                steps = [step[side, t, at, :] for t in at_tiles]
                acts = [act[side, t, at, :] for t in at_tiles]
                grads = [grad_gated[t, at, :] for t in at_tiles]
                drives = [v * a for v, a in zip(steps, acts)]
                step_terms = [[None, None] for _ in range(group)]
                drive_grads = [[None, None] for _ in range(group)]
                new = []
                for n in range(states):
                    lanes = lane_tile(n)
                    b, c = basis_b[at, lanes], basis_c[at, lanes]
                    put = grad_in[at, lanes]
                    for g in range(group):
                        adjoint = state[n * group + g] + c * grads[g]
                        carried = decays[g, at, lanes] * adjoint
                        new.append(carried)
                        term = carried * history[g, at, lanes] * rate_rows[g, n]
                        step_terms[g][n % 2] = plus(step_terms[g][n % 2], term)
                        drive_grads[g][n % 2] = plus(drive_grads[g][n % 2], adjoint * b)
                        put = put + adjoint * drives[g]
                    grad_in[at, lanes] = put
                for g, t in enumerate(at_tiles):
                    drive_grad = drive_grads[g][0] + drive_grads[g][1]
                    step_term = step_terms[g][0] + step_terms[g][1]
                    grad_step = step_term * LN2 + drive_grad * acts[g]
                    grad_act[side, t, at, :] = grads[g] * skips[g] + drive_grad * steps[g]
                    pre = step_pre[side, t, at, :]
                    grad_pre[side, t, at, :] = grad_step * jax.nn.sigmoid(pre)
                return tuple(new)

            unrolled(count, 4, retreat, start(1, not up))
            return keep

        lax.fori_loop(0, tiles // group, some_tiles, 0)
        pairs = [
            (grad_act.at[side], grad_act_out.at[side]), (grad_pre.at[side], grad_pre_out.at[side]),
        ]
        if side == 1:
            pairs.append((summed_out, summed_outs))
        stores = stores + copies_of(pairs, sems.at[pl.ds(2 * side, 3)])
        wide = full_width(grad_pre, side)
        weights[...] = jnp.zeros_like(weights)
        if side == 0:
            loads[-1].wait()
        weights[:ranks] = step_weight[side]
        packed[...] = dot(wide, weights[...], (1, 1))

        def pack(j, keep):
            at = cell_rows(j)
            line = packed[at, :]
            for values, start_at in ((grad_in, ranks), (grad_out, ranks + states)):
                for n in range(states):
                    total = jnp.sum(values[at, lane_tile(n)], axis=1, keepdims=True)
                    line = jnp.where(column == start_at + n, total, line)
            packed[at, :] = line
            return keep

        lax.fori_loop(0, count, pack, 0)
        deal(place, (mine, first_out, second_out, third_out), side, packed)
    finish_all(stores)


def step_kernel(grad_pre_in, projection_in, after_this, step_part, grad_pre, projection, sems):
    _, tiles, ranks, _ = step_part.shape
    finish_all(copies_of([(grad_pre_in, grad_pre), (projection_in, projection)], sems))
    for side in range(2):
        wide = dot(projection[side], full_width(grad_pre, side), (0, 0))
        for t in range(tiles):
            step_part[side, t] = wide[:ranks, lane_tile(t)]


def gate_kernel(
    summed_in, gate_in, cot_in, after_this, block_out, gate_grad, summed, gate, cot, plain, sems
):
    finish_all(copies_of([(summed_in, summed), (gate_in, gate), (cot_in, cot)], sems))
    for t in range(summed.shape[0]):
        lanes = lane_tile(t)
        values = gate[:, lanes]
        to_tokens(summed.at[t], plain)
        both = plain[...]
        block_out[:, lanes] = both * values * jax.nn.sigmoid(values)
        gate_grad[:, lanes] = cot[:, lanes] * both * silu_grad(values)


def weight_kernel(
    place, own, first, second, third, turned_act_in, slope_in, grad_act_in, select_in, step_part,
    keep, send, conv_grad_out, head, tail,
    turned_act, slope, grad_act, select, grad, conv_grad, plain, sems,
):
    sides, tiles, length, _ = slope.shape
    loads = copies_of(
        [
            (turned_act_in, turned_act), (select_in, select), (grad_act_in, grad_act),
            (slope_in, slope),
        ],
        sems,
    )
    collect(place, (own, first, second, third), grad)
    loads[0].wait()
    for side in range(2):
        part = dot(turned_act[side], grad[side], (1, 0))
        for out, core in ((keep, side), (send, 1 - side)):

            @pl.when(lax.rem(place[0], 2) == core)
            def _():
                out[: tiles * LANES] = part
                out[tiles * LANES :] = step_part[side].reshape(-1, LANES)
    finish_all(loads[1:])
    for side in range(2):
        wide = dot(grad[side], select[side], (1, 1))
        for t in range(tiles):
            lanes = lane_tile(t)
            grad_act[side, t] = grad_act[side, t] + wide[:, lanes]
            to_tokens(grad_act.at[side, t], plain)
            conv_grad[side, :, lanes] = plain[...] * slope[side, t]
    head[...] = conv_grad[0, :HALO]
    tail[...] = conv_grad[1, length - HALO :]
    stores = copies_of([(conv_grad, conv_grad_out)], sems.at[pl.ds(4, 1)])
    finish_all(stores)


def halves_kernel(place, keep, got, mine, *refs):
    outs, (total,) = refs[:-1], refs[-1:]
    share = mine.shape[0]
    chips = len(outs) + 1
    for k in range(chips):
        at = slice(k * share, (k + 1) * share)
        total[k] = keep[at] + got[at]
    core, chip = lax.rem(place[0], 2), lax.div(place[0], 2)
    mine[...] = total[chip]
    for k, out in enumerate(outs, 1):
        out[...] = total[chip ^ turned(k, core, chips)]


def add_after_kernel(after_this, *refs):
    add_kernel(*refs)


def add_kernel(*refs):
    total = refs[0][...]
    for ref in refs[1:-1]:
        total = total + ref[...]
    refs[-1][...] = total


def join_kernel(place, after_this, mine, *refs):
    parts, out = refs[:-1], refs[-1]
    core, chip = lax.rem(place[0], 2), lax.div(place[0], 2)
    out[chip] = mine[...]
    for k, part in enumerate(parts, 1):
        out[chip ^ turned(k, core, len(parts) + 1)] = part[...]


def outputs_kernel(place, mine, other, select_grad, step_grad, both):
    sides, width, _ = select_grad.shape
    ranks = step_grad.shape[1]
    chips = mine.shape[0]
    core = lax.rem(place[0], 2)
    size = mine.shape[1]
    for side in range(2):
        for k in range(chips):
            both[side, k * size : (k + 1) * size] = jnp.where(core == side, mine[k], other[k])
        select_grad[side] = both[side, :width]
        for t in range(width // LANES):
            at = width + t * ranks
            step_grad[side, :, lane_tile(t)] = both[side, at : at + ranks]


def exit_kernel(
    before, after, conv_grad, conv_weight_in, after_this, tokens_grad, up, down, conv_weight, sems
):
    _, length, width = conv_grad.shape
    taps = conv_weight.shape[1]
    margin = taps - 1
    loads = copies_of(
        [
            (conv_grad.at[0], up.at[pl.ds(0, length)]),
            (conv_grad.at[1], down.at[pl.ds(HALO, length)]),
            (conv_weight_in, conv_weight),
        ],
        sems,
    )
    up[length:] = after[...]
    down[:HALO] = before[...]
    finish_all(loads)
    for t in range(width // LANES):
        lanes = lane_tile(t)
        total = jnp.zeros((length, LANES), jnp.float32)
        for k in range(taps):
            at = margin - k
            total = total + conv_weight[0, k : k + 1, lanes] * up[at : at + length, lanes]
            at = HALO - margin + k
            total = total + conv_weight[1, k : k + 1, lanes] * down[at : at + length, lanes]
        tokens_grad[:, lanes] = total


def from_before(value, axis):
    count = lax.axis_size(axis)
    return lax.ppermute(value, axis, [(i, i + 1) for i in range(count - 1)])


def from_after(value, axis):
    count = lax.axis_size(axis)
    return lax.ppermute(value, axis, [(i + 1, i) for i in range(count - 1)])


def swapped(value, axis, by):
    count = lax.axis_size(axis)
    return lax.ppermute(value, axis, [(i, i ^ by) for i in range(count)])


def swapped_shares(value, k):
    places, columns = lax.axis_size("ctx"), lax.axis_size("ch")
    pairs = [
        (i * columns + j, i * columns + (j ^ ((k - 1 + i) % (columns - 1) + 1)))
        for i in range(places)
        for j in range(columns)
    ]
    return lax.ppermute(value, ("ctx", "ch"), pairs)


def swapped_chips(value, k):
    places = lax.axis_size("ctx")
    chips = places // 2
    pairs = [(i, i ^ (2 * ((k - 1 + i % 2) % (chips - 1) + 1))) for i in range(places)]
    return lax.ppermute(value, "ctx", pairs)


def call(kernel, name, out_shape, scratch, mib, args, kinds, outs=None):
    spaces = {
        "v": pl.BlockSpec(memory_space=pltpu.VMEM),
        "h": pl.BlockSpec(memory_space=pltpu.HBM),
        "s": pl.BlockSpec(memory_space=pltpu.SMEM),
    }
    outs = outs or "v" * len(out_shape)
    args = [
        pltpu.with_memory_space_constraint(a, pltpu.HBM) if k == "h" else a
        for a, k in zip(args, kinds, strict=True)
    ]
    results = [
        pltpu.HBM(shape, jnp.float32) if k == "h" else shape_of(*shape)
        for shape, k in zip(out_shape, outs, strict=True)
    ]
    return pl.pallas_call(
        kernel,
        in_specs=[spaces[k] for k in kinds],
        out_specs=[spaces[k] for k in outs],
        out_shape=results,
        scratch_shapes=scratch,
        compiler_params=params(mib),
        cost_estimate=pl.CostEstimate(flops=2**28, bytes_accessed=2**22, transcendentals=2**18),
        name=name,
    )(*args)


def summed_shares(parts, name):
    count = len(parts)
    if count == 1:
        return (lax.psum(parts[0], "ch"),), parts[0]
    got = [swapped_shares(part, k) for k, part in enumerate(parts[1:], 1)]
    (mine,) = call(add_kernel, name, (parts[0].shape,), [], 4, (parts[0], *got), "v" * count)
    return (mine, *(swapped_shares(mine, k) for k in range(1, count))), got[0]


def halved(place, keep, send, rows, chips, name):
    got = swapped(send, "ctx", 1)
    share = rows // chips
    mine, *sent = call(
        halves_kernel, name, ((share, LANES),) * chips, [pltpu.VMEM((chips, share, LANES), jnp.float32)],
        8, (place, keep, got), "svv",
    )
    return (mine, *(swapped_chips(part, k) for k, part in enumerate(sent, 1)))


def on_device(
    tokens, gate_input, cotangent, conv_weight, conv_bias, select_weight, step_weight,
    step_bias, decay_log, skip_gain,
):
    length, width = tokens.shape
    tiles = width // LANES
    states = decay_log.shape[1]
    ranks = step_weight.shape[1]
    places = lax.axis_size("ctx")
    columns = lax.axis_size("ch")
    place = jnp.stack([lax.axis_index("ctx"), lax.axis_index("ch")]).astype(jnp.int32)
    group = tile_group(tiles)
    chips = places // 2
    near = places == 8
    narrow = (2, length, LANES)
    shared = (2, length // columns, LANES)
    one = (tiles, length, LANES)
    pair = (2, *one)
    flat = (length, width)
    chain_ends = (4, tiles, states, CHAINS, LANES)
    carry = (2, tiles, 2 * states + 8, LANES)
    row_rates = (tiles, 2 * states, LANES)
    packed = (tiles * 2 * states + -(-2 * tiles // 8) * 8, LANES)
    vmem = functools.partial(pltpu.VMEM, dtype=jnp.float32)
    dma = lambda n: pltpu.SemaphoreType.DMA((n,))
    bases = vmem((length, states * LANES))
    grouped = vmem((group, length, states * LANES))
    rate_scratch = vmem((2, tiles, states, LANES))
    row_scratch = vmem((group, states, CHAINS, LANES))

    before = from_before(tokens[length - HALO :], "ctx")
    after = from_after(tokens[:HALO], "ctx")
    *parts, act, pre = call(
        entry_kernel, "entry", (*(shared,) * columns, pair, pair),
        [
            vmem((length + 2 * HALO, width)), vmem(conv_weight.shape), vmem(conv_bias.shape),
            vmem(select_weight.shape), vmem(pair), vmem(pair), vmem(one[1:]), vmem(one[1:]), dma(6),
        ],
        12, (place, before, after, tokens, conv_weight, conv_bias, select_weight), "svvhhhh",
        "v" * columns + "hh",
    )
    projection, step, step_pre, grad_gated, entering, carried, rates = call(
        local_kernel, "local", (narrow, pair, pair, one, chain_ends, carry, row_rates),
        [
            vmem(narrow), vmem(pair), vmem(pair), vmem(pair), vmem(one), vmem(chain_ends),
            vmem(step_weight.shape), vmem(step_bias.shape), vmem(decay_log.shape),
            vmem(flat), vmem(flat), vmem(one[1:]),
            rate_scratch, bases, bases, row_scratch, grouped, dma(6),
        ],
        24,
        (
            place, *summed_shares(parts, "projection")[0], step_weight, step_bias, decay_log, act,
            gate_input, cotangent,
        ),
        "svvvvhhhhhh", "hhhhhvv",
    )
    if near:
        other = swapped(carried, "ctx", 1)
        sent = call(
            pair_kernel, "pair", (packed,) * (chips - 1),
            [vmem(carry)], 8, (place, carried, other, rates), "svvv",
        )
        got = [swapped_chips(part, k) for k, part in enumerate(sent, 1)]
        ahead = sent[0]
    else:
        gathered = lax.all_gather(carried, "ctx")
        ahead = rates
    spread_bases, turned_act, slope, done = call(
        prep_kernel, "prep",
        ((2, 2, length, states * LANES), (2, width, length), pair, (HALO, LANES)),
        [
            vmem(narrow), vmem(pair), vmem(pair), vmem((2, 2, length, states * LANES)),
            vmem((2, width, length)), dma(7),
        ],
        14, (projection, act, pre, ahead), "hhhv", "hhhv",
    )
    if near:
        (incoming,) = call(
            chain_kernel, "chain", ((2, *row_rates),), [vmem((chips, *carry[1:]))],
            8, (place, other, rates, done, *got), "svvv" + "v" * len(got),
        )
    else:
        (incoming,) = call(
            long_chain_kernel, "chain", ((2, *row_rates),), [],
            48, (place, gathered, rates), "svv",
        )
    *grad_parts, grad_act, grad_pre, summed = call(
        scan_kernel, "scan", (*(shared,) * columns, pair, pair, one),
        [
            vmem(spread_bases.shape), vmem(step_weight.shape), vmem(decay_log.shape),
            vmem(skip_gain.shape),
            vmem(pair), vmem(pair), vmem(pair), vmem(one), vmem(chain_ends),
            vmem(pair), vmem(pair), vmem(one), rate_scratch, row_scratch, grouped,
            grouped, bases, bases, vmem((LANES, width)), vmem((length, LANES)),
            vmem((2, tiles, 1, LANES)), dma(10),
        ],
        28,
        (
            place, incoming, spread_bases, step_weight, decay_log, skip_gain, act, step, step_pre,
            grad_gated, entering,
        ),
        "svhhhhhhhhh", "v" * columns + "hhh",
    )
    grad_shares, arrived = summed_shares(grad_parts, "grad_projection")
    (step_part,) = call(
        step_kernel, "step_grad", ((2, tiles, ranks, LANES),), [vmem(pair), vmem(narrow), dma(2)],
        8, (grad_pre, projection, arrived), "hhv",
    )
    half = width + tiles * ranks
    keep, send, conv_grad, head, tail = call(
        weight_kernel, "weights",
        ((half, LANES), (half, LANES), (2, *flat), (HALO, width), (HALO, width)),
        [
            vmem((2, width, length)), vmem(pair), vmem(pair), vmem(select_weight.shape),
            vmem(narrow), vmem((2, *flat)), vmem(one[1:]), dma(5),
        ],
        16,
        (place, *grad_shares, turned_act, slope, grad_act, select_weight, step_part),
        "svvvvhhhhv", "vvhvv",
    )
    before = from_before(tail, "ctx")
    after = from_after(head, "ctx")
    if near:
        shares = halved(place, keep, send, half, chips, "halves")
        ahead = shares[0]
    else:
        ahead = head
    (tokens_grad,) = call(
        exit_kernel, "exit", (flat,),
        [
            vmem((length + HALO, width)), vmem((length + HALO, width)), vmem(conv_weight.shape),
            dma(3),
        ],
        8, (before, after, conv_grad, conv_weight, ahead), "vvhhv",
    )
    if near:
        rows = half // chips
        (mine,) = call(
            add_after_kernel, "share_sum", ((rows, LANES),), [], 4, (tokens_grad, *shares),
            "h" + "v" * chips,
        )
        ahead = mine
    block_out, gate_grad = call(
        gate_kernel, "gate", (flat, flat),
        [vmem(one), vmem(flat), vmem(flat), vmem(one[1:]), dma(3)],
        8, (summed, gate_input, cotangent, ahead), "hhhv",
    )
    if near:
        got = [swapped_chips(mine, k) for k in range(1, chips)]
        (joined,) = call(
            join_kernel, "joined", ((chips, rows, LANES),), [],
            8, (place, block_out, mine, *got), "sh" + "v" * chips,
        )
        select_grad, step_grad = call(
            outputs_kernel, "weight_grads", ((2, width, LANES), (2, ranks, width)),
            [vmem((2, half, LANES))],
            12, (place, joined, swapped(joined, "ctx", 1)), "svv",
        )
    else:
        first = lax.rem(place[0], 2) == 0
        both = jnp.where(first, jnp.stack([keep, send]), jnp.stack([send, keep]))
        both = lax.psum(both, "ctx")
        select_grad = both[:, :width]
        step_grad = both[:, width:].reshape(2, tiles, ranks, LANES)
        step_grad = step_grad.transpose(0, 2, 1, 3).reshape(2, ranks, width)
    return (block_out, tokens_grad, gate_grad, select_grad, step_grad)


def solution(mesh):
    return jax.shard_map(
        on_device,
        mesh=mesh,
        in_specs=(
            P("ctx", "ch"),
            P("ctx", "ch"),
            P("ctx", "ch"),
            P(None, None, "ch"),
            P(None, "ch"),
            P(None, "ch", None),
            P(None, None, "ch"),
            P(None, "ch"),
            P(None, None, "ch"),
            P(None, "ch"),
        ),
        out_specs=(
            P("ctx", "ch"),
            P("ctx", "ch"),
            P("ctx", "ch"),
            P(None, "ch", None),
            P(None, None, "ch"),
        ),
        check_vma=False,
    )
```

```python
import functools

import jax
import jax.numpy as jnp
from jax import lax
from jax.experimental import pallas as pl
from jax.experimental.pallas import tpu as pltpu
from jax.sharding import PartitionSpec as P

FULL_PRECISION = lax.Precision.HIGHEST
LANES = 128
CHAINS = 8
HALO = 8
LOG2E = 1.4426950408889634
LN2 = 0.6931471805599453
MIB = 1024 * 1024


def params(mib):
    return pltpu.CompilerParams(vmem_limit_bytes=mib * MIB)


def shape_of(*dims):
    return jax.ShapeDtypeStruct(dims, jnp.float32)


def dot(a, b, contract):
    return lax.dot_general(
        a, b, ((contract[:1], contract[1:]), ((), ())), precision=FULL_PRECISION,
        preferred_element_type=jnp.float32,
    )


def silu_grad(values):
    sigmoid_values = jax.nn.sigmoid(values)
    return sigmoid_values * (1.0 + values * (1.0 - sigmoid_values))


def lane_tile(t):
    return slice(t * LANES, (t + 1) * LANES)


def full_width(ref, *lead):
    tiles = ref.shape[len(lead)]
    return jnp.concatenate([ref[(*lead, t)] for t in range(tiles)], axis=1)


def convolved(ext, at_row, side, lanes, rows, conv_weight, conv_bias):
    taps = conv_weight.shape[1]
    margin = taps - 1
    conv = jnp.broadcast_to(conv_bias[side : side + 1, lanes], (rows, LANES))
    for k in range(taps):
        at = at_row + (k - margin if side == 0 else margin - k)
        conv = conv + conv_weight[side, k : k + 1, lanes] * ext[at : at + rows, lanes]
    return conv


def copies_of(pairs, sems):
    copies = [pltpu.make_async_copy(a, b, sems.at[i]) for i, (a, b) in enumerate(pairs)]
    for copy in copies:
        copy.start()
    return copies


def to_cells(tokens, cells):
    count = tokens.shape[0] // CHAINS
    for j in range(count):
        cells[j * CHAINS : (j + 1) * CHAINS] = tokens[pl.ds(j, CHAINS, stride=count), :]


def to_tokens(cells, tokens):
    count = tokens.shape[0] // CHAINS
    for j in range(count):
        tokens[pl.ds(j, CHAINS, stride=count), :] = cells[j * CHAINS : (j + 1) * CHAINS]


def finish_all(copies):
    for copy in copies:
        copy.wait()


def entry_kernel(
    place, column, before, after, tokens, conv_weight_in, conv_bias_in, select_in,
    *refs,
):
    outs, refs = refs[:-9], refs[-9:]
    act, pre, ext, conv_weight, conv_bias, select, plain, rows, sems = refs

    length, width = tokens.shape
    loads = copies_of(
        [
            (tokens, ext.at[pl.ds(HALO, length)]), (conv_weight_in, conv_weight),
            (conv_bias_in, conv_bias), (select_in, select),
        ],
        sems,
    )
    ext[:HALO] = before[...]
    ext[HALO + length :] = after[...]
    finish_all(loads[:3])
    for side in range(2):
        for t in range(width // LANES):
            conv = convolved(ext, HALO, side, lane_tile(t), length, conv_weight, conv_bias)
            pre[side, t] = conv
            plain[...] = conv * jax.nn.sigmoid(conv)
            to_cells(plain, act.at[side, t])
    loads[3].wait()
    for side in range(2):
        rows[...] = dot(full_width(act, side), select[side], (1, 0))
        deal(place, column, outs, side, rows)


def turned(k, by, count):
    return lax.rem(k - 1 + by, count - 1) + 1


def deal(place, column, outs, side, rows):
    share = outs[0].shape[1]
    for k in range(len(outs)):
        to = column[0] ^ turned(k, place[0], len(outs)) if k else column[0]
        at = pl.multiple_of(to * share, share)
        outs[k][side] = rows[pl.ds(at, share), :]


def collect(place, column, parts, out):
    share = parts[0].shape[1]
    for k in range(len(parts)):
        source = column[0] ^ turned(k, place[0], len(parts)) if k else column[0]
        at = pl.multiple_of(source * share, share)
        out[:, pl.ds(at, share), :] = parts[k][...]


def spread(projection, side, j, states, basis_b, basis_c):
    ranks = LANES - 2 * states
    at = pl.ds(pl.multiple_of(j * CHAINS, CHAINS), CHAINS)
    rows = projection[side, at, :]
    for n in range(states):
        b = rows[:, ranks + n : ranks + n + 1]
        c = rows[:, ranks + states + n : ranks + states + n + 1]
        basis_b[at, lane_tile(n)] = jnp.broadcast_to(b, (CHAINS, LANES))
        basis_c[at, lane_tile(n)] = jnp.broadcast_to(c, (CHAINS, LANES))


def fill_bases(projection, side, states, basis_b, basis_c):
    def body(j, carry):
        spread(projection, side, j, states, basis_b, basis_c)
        return carry

    lax.fori_loop(0, basis_b.shape[0] // CHAINS, body, 0)


def fill_rates(decay_log, rates):
    for side in range(rates.shape[0]):
        for t in range(rates.shape[1]):
            rates[side, t] = -LOG2E * jnp.exp(decay_log[side, :, lane_tile(t)])


def sublane():
    return lax.broadcasted_iota(jnp.int32, (CHAINS, LANES), 0)


def shifted(value, by, up):
    rolled = pltpu.roll(value, by if up else CHAINS - by, 0)
    place = sublane()
    keep = place >= by if up else place < CHAINS - by
    return jnp.where(keep, rolled, 0.0)


def over_chains(decays, ends, up):
    by = 1
    while by < CHAINS:
        ends = [d * shifted(f, by, up) + f for d, f in zip(decays, ends)]
        if 2 * by < CHAINS:
            turn = by if up else CHAINS - by
            decays = [d * pltpu.roll(d, turn, 0) for d in decays]
        by *= 2
    return ends


def order(i, count, up):
    return i if up else count - 1 - i


def tile_group(tiles):
    return 2 if tiles % 2 == 0 else 1


def unrolled(count, times, body, start):
    times = times if count % times == 0 else 1

    def several(i, state):
        for k in range(times):
            state = body(i * times + k, state)
        return state

    return lax.fori_loop(0, count // times, several, start)


def plus(total, term):
    return term if total is None else total + term


def fill_rate_rows(rates, side, tiles, rate_rows):
    for g, t in enumerate(tiles):
        for n in range(rate_rows.shape[1]):
            rate_rows[g, n] = jnp.broadcast_to(rates[side, t, n : n + 1], (CHAINS, LANES))


def cell_rows(j):
    return pl.ds(pl.multiple_of(j * CHAINS, CHAINS), CHAINS)


def local_kernel(
    place, column, own, first, second, third, act,
    step_weight_in, step_bias_in, decay_log_in, gate_in, cot_in,
    projection, step, step_pre, grad_gated, entering, decays, carry, row_rates,
    step_weight, step_bias, decay_log, gate, cot, plain, rates, basis_b, basis_c, rate_rows, sems,
):
    sides, tiles, length, _ = act.shape
    states = decay_log.shape[1]
    ranks = step_weight.shape[1]
    count = length // CHAINS
    group = tile_group(tiles)
    loads = copies_of(
        [
            (step_weight_in, step_weight), (step_bias_in, step_bias), (decay_log_in, decay_log),
            (gate_in, gate), (cot_in, cot),
        ],
        sems,
    )
    collect(place, column, (own, first, second, third), projection)
    finish_all(loads)
    for t in range(tiles):
        lanes = lane_tile(t)
        values = gate[:, lanes]
        plain[...] = cot[:, lanes] * values * jax.nn.sigmoid(values)
        to_cells(plain, grad_gated.at[t])
    fill_rates(decay_log, rates)
    for side in range(2):
        wide = dot(projection[side][:, :ranks], step_weight[side], (1, 0))
        wide = wide + step_bias[side : side + 1]
        for t in range(tiles):
            part = wide[:, lane_tile(t)]
            step_pre[side, t] = part
            step[side, t] = jnp.maximum(part, 0.0) + jnp.log1p(jnp.exp(-jnp.abs(part)))
    zero = jnp.zeros((CHAINS, LANES), jnp.float32)
    carry[...] = jnp.zeros_like(carry)
    for side in range(2):
        up = side == 0
        fill_bases(projection, side, states, basis_b, basis_c)

        def some_tiles(first, keep):
            at_tiles = [first * group + g for g in range(group)]
            fill_rate_rows(rates, side, at_tiles, rate_rows)

            def forward(i, current):
                state, summed = current
                j = order(i, count, up)
                at = cell_rows(j)
                steps = [step[side, t, at, :] for t in at_tiles]
                drives = [v * act[side, t, at, :] for v, t in zip(steps, at_tiles)]
                new = []
                for n in range(states):
                    lanes = lane_tile(n)
                    b = basis_b[at, lanes]
                    for g in range(group):
                        decay = jnp.exp2(steps[g] * rate_rows[g, n])
                        decays[side, at_tiles[g], at, lanes] = decay
                        new.append(decay * state[n * group + g] + b * drives[g])
                return (tuple(new), tuple(a + v for a, v in zip(summed, steps)))

            start = ((zero,) * (states * group), (zero,) * group)
            state, summed = unrolled(count, 4, forward, start)

            def retreat(i, state):
                j = order(i, count, not up)
                at = cell_rows(j)
                grads = [grad_gated[t, at, :] for t in at_tiles]
                new = []
                for n in range(states):
                    lanes = lane_tile(n)
                    c = basis_c[at, lanes]
                    for g in range(group):
                        adjoint = state[n * group + g] + c * grads[g]
                        new.append(decays[side, at_tiles[g], at, lanes] * adjoint)
                return tuple(new)

            sent = unrolled(count, 4, retreat, (zero,) * (states * group))
            for g, t in enumerate(at_tiles):
                across = [jnp.exp2(summed[g] * rate_rows[g, n]) for n in range(states)]
                for kind, ends, upward in ((0, state, up), (1, sent, not up)):
                    slot = 2 * side + kind
                    ends = over_chains(across, list(ends[g::group]), upward)
                    last = CHAINS - 1 if upward else 0
                    for n in range(states):
                        entering[slot, t, n] = shifted(ends[n], 1, upward)
                        at = side * states + n
                        carry[0 if upward else 1, t, at : at + 1] = ends[n][last : last + 1]
                whole = jnp.sum(summed[g], axis=0, keepdims=True)
                at = 2 * states + side
                for k in range(2):
                    carry[k, t, at : at + 1] = whole
            return keep

        lax.fori_loop(0, tiles // group, some_tiles, 0)
    for side in range(2):
        row_rates[:, side * states : (side + 1) * states] = rates[side]


def tile_decay(part, rates):
    rows = rates.shape[1]
    row = lax.broadcasted_iota(jnp.int32, rates.shape, 1)
    sums = jnp.where(row < rows // 2, part[:, rows : rows + 1], part[:, rows + 1 : rows + 2])
    return jnp.exp2(rates * sums)


def prep_kernel(projection, after_this, bases, done):
    for side in range(bases.shape[0]):
        states = bases.shape[3] // LANES
        fill_bases(projection, side, states, bases.at[side, 0], bases.at[side, 1])
    done[...] = jnp.zeros_like(done)


def pair_kernel(place, mine, other, rates, *refs):
    outs, total = refs[:-1], refs[-1]
    rows = rates.shape[1]
    core, chip = lax.rem(place[0], 2), lax.div(place[0], 2)
    low = jnp.where(core == 0, mine[...], other[...])
    high = jnp.where(core == 0, other[...], mine[...])
    spread_rates = rates[...]
    decay_low = tile_decay(low[0], spread_rates)
    decay_high = tile_decay(high[0], spread_rates)
    total[...] = low + high
    total[0, :, :rows] = decay_high * low[0][:, :rows] + high[0][:, :rows]
    total[1, :, :rows] = decay_low * high[1][:, :rows] + low[1][:, :rows]
    tiles = rates.shape[0]
    for k, out in enumerate(outs, 1):
        to = chip ^ turned(k, core, len(outs) + 1)
        below = lax.convert_element_type(to < chip, jnp.int32)
        for t in range(tiles):
            out[t * rows : (t + 1) * rows] = total[below, t, :rows]
            for side in range(2):
                at = tiles * rows + side * tiles + t
                out[at : at + 1] = total[0, t, rows + side : rows + side + 1]


def chain_kernel(place, other, rates, after_this, *refs):
    gathered, (out, parts) = refs[:-2], refs[-2:]
    rows = rates.shape[1]
    chips = parts.shape[0]
    core, chip = lax.rem(place[0], 2), lax.div(place[0], 2)
    parts[chip] = jnp.zeros(parts.shape[1:], jnp.float32)
    tiles = rates.shape[0]
    for k, part in enumerate(gathered, 1):
        source = chip ^ turned(k, core, chips)
        for t in range(tiles):
            parts[source, t, :rows] = part[t * rows : (t + 1) * rows]
            for side in range(2):
                at = tiles * rows + side * tiles + t
                parts[source, t, rows + side : rows + side + 1] = part[at : at + 1]
    spread_rates = rates[...]
    for kind in range(2):
        state = jnp.zeros(rates.shape, jnp.float32)
        for k in range(chips) if kind == 0 else reversed(range(chips)):
            part = parts[k]
            new = tile_decay(part, spread_rates) * state + part[:, :rows]
            state = jnp.where(k < chip if kind == 0 else k > chip, new, state)
        part = other[kind]
        new = tile_decay(part, spread_rates) * state + part[:, :rows]
        out[kind] = jnp.where(core == 1 - kind, new, state)


def long_chain_kernel(place, gathered, rates, out):
    rows = rates.shape[1]
    shards = gathered.shape[0]
    for kind in range(2):

        def turn(i, state):
            part = gathered[order(i, shards, kind == 0), kind]
            return tile_decay(part, rates[...]) * state + part[:, :rows]

        turns = place[0] if kind == 0 else shards - 1 - place[0]
        out[kind] = lax.fori_loop(0, turns, turn, jnp.zeros(rates.shape, jnp.float32))


def scan_kernel(
    place, column, incoming, bases, act, step, step_pre, grad_gated, entering, decays,
    step_weight_in, decay_log_in, skip_gain_in,
    mine, first_out, second_out, third_out, grad_act, grad_pre, summed_out,
    step_weight, decay_log, skip_gain, rates, rate_rows, history,
    grad_in, grad_out, weights, packed, skip_rows, sems,
):
    sides, tiles, length, _ = act.shape
    states = decay_log.shape[1]
    ranks = step_weight.shape[1]
    count = length // CHAINS
    group = tile_group(tiles)
    loads = copies_of(
        [
            (decay_log_in, decay_log), (skip_gain_in, skip_gain), (step_weight_in, step_weight),
        ],
        sems,
    )
    finish_all(loads)
    fill_rates(decay_log, rates)
    lane = lax.broadcasted_iota(jnp.int32, (CHAINS, LANES), 1)
    for side in range(2):
        up = side == 0
        basis_b, basis_c = bases.at[side, 0], bases.at[side, 1]
        grad_in[...] = jnp.zeros_like(grad_in)
        grad_out[...] = jnp.zeros_like(grad_out)
        if side == 0:
            for k in range(2):
                for t in range(tiles):
                    skip_rows[k, t] = skip_gain[k : k + 1, lane_tile(t)]

        def some_tiles(first, keep):
            at_tiles = [first * group + g for g in range(group)]
            fill_rate_rows(rates, side, at_tiles, rate_rows)
            skips = [skip_rows[side, t] for t in at_tiles]
            sums = []
            for t in at_tiles:
                summed = step[side, t, cell_rows(0), :]
                for j in range(1, count):
                    summed = summed + step[side, t, cell_rows(j), :]
                sums.append(summed)

            def start(kind, upward):
                slot = 2 * side + kind
                spans = []
                for g in range(group):
                    span = shifted(sums[g], 1, upward)
                    by = 1
                    while by < CHAINS:
                        span = span + shifted(span, by, upward)
                        by *= 2
                    spans.append(span)
                first = []
                for n in range(states):
                    at = side * states + n
                    for g, t in enumerate(at_tiles):
                        decay = jnp.exp2(spans[g] * rate_rows[g, n])
                        value = incoming[0 if upward else 1, t, at : at + 1, :]
                        first.append(entering[slot, t, n] + decay * value)
                return tuple(first)

            def forward(i, state):
                j = order(i, count, up)
                at = cell_rows(j)
                acts = [act[side, t, at, :] for t in at_tiles]
                grads = [grad_gated[t, at, :] for t in at_tiles]
                drives = [step[side, t, at, :] * a for t, a in zip(at_tiles, acts)]
                outs = [[v * a, None] for v, a in zip(skips, acts)]
                new = []
                for n in range(states):
                    lanes = lane_tile(n)
                    b, c = basis_b[at, lanes], basis_c[at, lanes]
                    read = grad_out[at, lanes]
                    for g in range(group):
                        before = state[n * group + g]
                        decay = decays[side, at_tiles[g], at, lanes]
                        history[g, at, lanes] = before
                        current = decay * before + b * drives[g]
                        outs[g][n % 2] = plus(outs[g][n % 2], c * current)
                        read = read + current * grads[g]
                        new.append(current)
                    grad_out[at, lanes] = read
                for g, t in enumerate(at_tiles):
                    out = outs[g][0] + outs[g][1]
                    if side == 0:
                        summed_out[t, at, :] = out
                    else:
                        summed_out[t, at, :] = summed_out[t, at, :] + out
                return tuple(new)

            unrolled(count, 4, forward, start(0, up))

            def retreat(i, state):
                j = order(i, count, not up)
                at = cell_rows(j)
                steps = [step[side, t, at, :] for t in at_tiles]
                acts = [act[side, t, at, :] for t in at_tiles]
                grads = [grad_gated[t, at, :] for t in at_tiles]
                drives = [v * a for v, a in zip(steps, acts)]
                step_terms = [[None, None] for _ in range(group)]
                drive_grads = [[None, None] for _ in range(group)]
                new = []
                for n in range(states):
                    lanes = lane_tile(n)
                    b, c = basis_b[at, lanes], basis_c[at, lanes]
                    put = grad_in[at, lanes]
                    for g in range(group):
                        adjoint = state[n * group + g] + c * grads[g]
                        carried = decays[side, at_tiles[g], at, lanes] * adjoint
                        new.append(carried)
                        term = carried * history[g, at, lanes] * rate_rows[g, n]
                        step_terms[g][n % 2] = plus(step_terms[g][n % 2], term)
                        drive_grads[g][n % 2] = plus(drive_grads[g][n % 2], adjoint * b)
                        put = put + adjoint * drives[g]
                    grad_in[at, lanes] = put
                for g, t in enumerate(at_tiles):
                    drive_grad = drive_grads[g][0] + drive_grads[g][1]
                    step_term = step_terms[g][0] + step_terms[g][1]
                    grad_step = step_term * LN2 + drive_grad * acts[g]
                    grad_act[side, t, at, :] = grads[g] * skips[g] + drive_grad * steps[g]
                    pre = step_pre[side, t, at, :]
                    grad_pre[side, t, at, :] = grad_step * jax.nn.sigmoid(pre)
                return tuple(new)

            unrolled(count, 4, retreat, start(1, not up))
            return keep

        lax.fori_loop(0, tiles // group, some_tiles, 0)
        wide = full_width(grad_pre, side)
        weights[...] = jnp.zeros_like(weights)
        weights[:ranks] = step_weight[side]
        packed[...] = dot(wide, weights[...], (1, 1))

        def pack(j, keep):
            at = cell_rows(j)
            line = packed[at, :]
            for values, start_at in ((grad_in, ranks), (grad_out, ranks + states)):
                for n in range(states):
                    total = jnp.sum(values[at, lane_tile(n)], axis=1, keepdims=True)
                    line = jnp.where(lane == start_at + n, total, line)
            packed[at, :] = line
            return keep

        lax.fori_loop(0, count, pack, 0)
        deal(place, column, (mine, first_out, second_out, third_out), side, packed)


def step_kernel(grad_pre, projection, after_this, step_part):
    _, tiles, ranks, _ = step_part.shape
    for side in range(2):
        wide = dot(projection[side], full_width(grad_pre, side), (0, 0))
        for t in range(tiles):
            step_part[side, t] = wide[:ranks, lane_tile(t)]


def gate_kernel(
    summed, gate_in, cot_in, after_this, block_out, gate_grad, gate, cot, plain, sems
):
    finish_all(copies_of([(gate_in, gate), (cot_in, cot)], sems))
    for t in range(summed.shape[0]):
        lanes = lane_tile(t)
        values = gate[:, lanes]
        to_tokens(summed.at[t], plain)
        both = plain[...]
        block_out[:, lanes] = both * values * jax.nn.sigmoid(values)
        gate_grad[:, lanes] = cot[:, lanes] * both * silu_grad(values)


def weight_kernel(
    place, column, own, first, second, third, act, pre, grad_act, step_part, select_in,
    keep, send, conv_grad, head, tail, select, grad, plain, cells, sems,
):
    sides, tiles, length, _ = act.shape
    loads = copies_of([(select_in, select)], sems)
    collect(place, column, (own, first, second, third), grad)
    for side in range(2):
        part = dot(full_width(act, side), grad[side], (0, 0))
        for out, core in ((keep, side), (send, 1 - side)):

            @pl.when(lax.rem(place[0], 2) == core)
            def _():
                out[: tiles * LANES] = part
                out[tiles * LANES :] = step_part[side].reshape(-1, LANES)
    finish_all(loads)
    for side in range(2):
        wide = dot(grad[side], select[side], (1, 1))
        for t in range(tiles):
            lanes = lane_tile(t)
            cells[...] = grad_act[side, t] + wide[:, lanes]
            to_tokens(cells, plain)
            conv_grad[side, :, lanes] = plain[...] * silu_grad(pre[side, t])
    head[...] = conv_grad[0, :HALO]
    tail[...] = conv_grad[1, length - HALO :]


def halves_kernel(place, keep, got, mine, *refs):
    outs, (total,) = refs[:-1], refs[-1:]
    share = mine.shape[0]
    chips = len(outs) + 1
    for k in range(chips):
        at = slice(k * share, (k + 1) * share)
        total[k] = keep[at] + got[at]
    core, chip = lax.rem(place[0], 2), lax.div(place[0], 2)
    mine[...] = total[chip]
    for k, out in enumerate(outs, 1):
        out[...] = total[chip ^ turned(k, core, chips)]


def add_after_kernel(after_this, *refs):
    add_kernel(*refs)


def add_kernel(*refs):
    total = refs[0][...]
    for ref in refs[1:-1]:
        total = total + ref[...]
    refs[-1][...] = total


def join_kernel(place, after_this, mine, *refs):
    parts, out = refs[:-1], refs[-1]
    core, chip = lax.rem(place[0], 2), lax.div(place[0], 2)
    out[chip] = mine[...]
    for k, part in enumerate(parts, 1):
        out[chip ^ turned(k, core, len(parts) + 1)] = part[...]


def outputs_kernel(place, mine, other, select_grad, step_grad, both):
    sides, width, _ = select_grad.shape
    ranks = step_grad.shape[1]
    chips = mine.shape[0]
    core = lax.rem(place[0], 2)
    size = mine.shape[1]
    for side in range(2):
        for k in range(chips):
            both[side, k * size : (k + 1) * size] = jnp.where(core == side, mine[k], other[k])
        select_grad[side] = both[side, :width]
        for t in range(width // LANES):
            at = width + t * ranks
            step_grad[side, :, lane_tile(t)] = both[side, at : at + ranks]


def exit_kernel(
    before, after, conv_grad, conv_weight_in, after_this, tokens_grad, up, down, conv_weight, sems
):
    _, length, width = conv_grad.shape
    taps = conv_weight.shape[1]
    margin = taps - 1
    loads = copies_of(
        [
            (conv_weight_in, conv_weight),
        ],
        sems,
    )
    up[:length] = conv_grad[0]
    up[length:] = after[...]
    down[:HALO] = before[...]
    down[HALO:] = conv_grad[1]
    finish_all(loads)
    for t in range(width // LANES):
        lanes = lane_tile(t)
        total = jnp.zeros((length, LANES), jnp.float32)
        for k in range(taps):
            at = margin - k
            total = total + conv_weight[0, k : k + 1, lanes] * up[at : at + length, lanes]
            at = HALO - margin + k
            total = total + conv_weight[1, k : k + 1, lanes] * down[at : at + length, lanes]
        tokens_grad[:, lanes] = total


def from_before(value, axis):
    count = lax.axis_size(axis)
    return lax.ppermute(value, axis, [(i, i + 1) for i in range(count - 1)])


def from_after(value, axis):
    count = lax.axis_size(axis)
    return lax.ppermute(value, axis, [(i + 1, i) for i in range(count - 1)])


def swapped(value, axis, by):
    count = lax.axis_size(axis)
    return lax.ppermute(value, axis, [(i, i ^ by) for i in range(count)])


def swapped_shares(value, k):
    places, columns = lax.axis_size("ctx"), lax.axis_size("ch")
    pairs = [
        (i * columns + j, i * columns + (j ^ ((k - 1 + i) % (columns - 1) + 1)))
        for i in range(places)
        for j in range(columns)
    ]
    return lax.ppermute(value, ("ctx", "ch"), pairs)


def swapped_chips(value, k):
    places = lax.axis_size("ctx")
    chips = places // 2
    pairs = [(i, i ^ (2 * ((k - 1 + i % 2) % (chips - 1) + 1))) for i in range(places)]
    return lax.ppermute(value, "ctx", pairs)


def call(kernel, name, out_shape, scratch, mib, args, kinds, outs=None):
    spaces = {
        "v": pl.BlockSpec(memory_space=pltpu.VMEM),
        "m": pl.BlockSpec(memory_space=pltpu.VMEM),
        "h": pl.BlockSpec(memory_space=pltpu.HBM),
        "s": pl.BlockSpec(memory_space=pltpu.SMEM),
    }
    outs = outs or "v" * len(out_shape)
    pinned = {"m": pltpu.VMEM, "h": pltpu.HBM}
    args = [
        pltpu.with_memory_space_constraint(a, pinned[k]) if k in pinned else a
        for a, k in zip(args, kinds, strict=True)
    ]
    results = [
        pinned[k](shape, jnp.float32) if k in pinned else shape_of(*shape)
        for shape, k in zip(out_shape, outs, strict=True)
    ]
    return pl.pallas_call(
        kernel,
        in_specs=[spaces[k] for k in kinds],
        out_specs=[spaces[k] for k in outs],
        out_shape=results,
        scratch_shapes=scratch,
        compiler_params=params(mib),
        cost_estimate=pl.CostEstimate(flops=2**28, bytes_accessed=2**22, transcendentals=2**18),
        name=name,
    )(*args)


def summed_shares(parts, name):
    count = len(parts)
    if count == 1:
        return (lax.psum(parts[0], "ch"),), parts[0]
    got = [swapped_shares(part, k) for k, part in enumerate(parts[1:], 1)]
    (mine,) = call(add_kernel, name, (parts[0].shape,), [], 4, (parts[0], *got), "v" * count)
    return (mine, *(swapped_shares(mine, k) for k in range(1, count))), got[0]


def halved(place, keep, send, rows, chips, name):
    got = swapped(send, "ctx", 1)
    share = rows // chips
    mine, *sent = call(
        halves_kernel, name, ((share, LANES),) * chips, [pltpu.VMEM((chips, share, LANES), jnp.float32)],
        8, (place, keep, got), "svv",
    )
    return (mine, *(swapped_chips(part, k) for k, part in enumerate(sent, 1)))


def on_device(
    tokens, gate_input, cotangent, conv_weight, conv_bias, select_weight, step_weight,
    step_bias, decay_log, skip_gain,
):
    length, width = tokens.shape
    tiles = width // LANES
    states = decay_log.shape[1]
    ranks = step_weight.shape[1]
    places = lax.axis_size("ctx")
    columns = lax.axis_size("ch")
    place = lax.axis_index("ctx").astype(jnp.int32).reshape(1)
    column = lax.axis_index("ch").astype(jnp.int32).reshape(1)
    group = tile_group(tiles)
    chips = places // 2
    near = places == 8
    narrow = (2, length, LANES)
    shared = (2, length // columns, LANES)
    one = (tiles, length, LANES)
    pair = (2, *one)
    flat = (length, width)
    chain_ends = (4, tiles, states, CHAINS, LANES)
    carry = (2, tiles, 2 * states + 8, LANES)
    row_rates = (tiles, 2 * states, LANES)
    packed = (tiles * 2 * states + -(-2 * tiles // 8) * 8, LANES)
    vmem = functools.partial(pltpu.VMEM, dtype=jnp.float32)
    dma = lambda n: pltpu.SemaphoreType.DMA((n,))
    bases = vmem((length, states * LANES))
    grouped = vmem((group, length, states * LANES))
    rate_scratch = vmem((2, tiles, states, LANES))
    row_scratch = vmem((group, states, CHAINS, LANES))

    before = from_before(tokens[length - HALO :], "ctx")
    after = from_after(tokens[:HALO], "ctx")
    *parts, act, pre = call(
        entry_kernel, "entry", (*(shared,) * columns, pair, pair),
        [
            vmem((length + 2 * HALO, width)), vmem(conv_weight.shape), vmem(conv_bias.shape),
            vmem(select_weight.shape), vmem(one[1:]), vmem(one[1:]), dma(4),
        ],
        12, (place, column, before, after, tokens, conv_weight, conv_bias, select_weight), "ssvvhhhh",
        "v" * columns + "mm",
    )
    projection, step, step_pre, grad_gated, entering, decays, carried, rates = call(
        local_kernel, "local",
        (narrow, pair, pair, one, chain_ends, (*pair[:-1], states * LANES), carry, row_rates),
        [
            vmem(step_weight.shape), vmem(step_bias.shape), vmem(decay_log.shape),
            vmem(flat), vmem(flat), vmem(one[1:]),
            rate_scratch, bases, bases, row_scratch, dma(5),
        ],
        12,
        (
            place, column, *summed_shares(parts, "projection")[0], act, step_weight, step_bias,
            decay_log, gate_input, cotangent,
        ),
        "ssvvvvmhhhhh", "mmmmmmvv",
    )
    if near:
        other = swapped(carried, "ctx", 1)
        sent = call(
            pair_kernel, "pair", (packed,) * (chips - 1),
            [vmem(carry)], 8, (place, carried, other, rates), "svvv",
        )
        got = [swapped_chips(part, k) for k, part in enumerate(sent, 1)]
        ahead = sent[0]
    else:
        gathered = lax.all_gather(carried, "ctx")
        ahead = rates
    spread_bases, done = call(
        prep_kernel, "prep", ((2, 2, length, states * LANES), (HALO, LANES)), [],
        6, (projection, ahead), "mv", "mv",
    )
    if near:
        (incoming,) = call(
            chain_kernel, "chain", ((2, *row_rates),), [vmem((chips, *carry[1:]))],
            8, (place, other, rates, done, *got), "svvv" + "v" * len(got),
        )
    else:
        (incoming,) = call(
            long_chain_kernel, "chain", ((2, *row_rates),), [],
            48, (place, gathered, rates), "svv",
        )
    *grad_parts, grad_act, grad_pre, summed = call(
        scan_kernel, "scan", (*(shared,) * columns, pair, pair, one),
        [
            vmem(step_weight.shape), vmem(decay_log.shape), vmem(skip_gain.shape),
            rate_scratch, row_scratch, grouped, bases, bases, vmem((LANES, width)),
            vmem((length, LANES)), vmem((2, tiles, 1, LANES)), dma(3),
        ],
        12,
        (
            place, column, incoming, spread_bases, act, step, step_pre, grad_gated, entering,
            decays, step_weight, decay_log, skip_gain,
        ),
        "ssvmmmmmmmhhh", "v" * columns + "mmm",
    )
    grad_shares, arrived = summed_shares(grad_parts, "grad_projection")
    (step_part,) = call(
        step_kernel, "step_grad", ((2, tiles, ranks, LANES),), [],
        8, (grad_pre, projection, arrived), "mmv",
    )
    half = width + tiles * ranks
    keep, send, conv_grad, head, tail = call(
        weight_kernel, "weights",
        ((half, LANES), (half, LANES), (2, *flat), (HALO, width), (HALO, width)),
        [
            vmem(select_weight.shape), vmem(narrow), vmem(one[1:]), vmem(one[1:]), dma(1),
        ],
        12,
        (place, column, *grad_shares, act, pre, grad_act, step_part, select_weight),
        "ssvvvvmmmvh", "vvmvv",
    )
    before = from_before(tail, "ctx")
    after = from_after(head, "ctx")
    if near:
        shares = halved(place, keep, send, half, chips, "halves")
        ahead = shares[0]
    else:
        ahead = head
    (tokens_grad,) = call(
        exit_kernel, "exit", (flat,),
        [
            vmem((length + HALO, width)), vmem((length + HALO, width)), vmem(conv_weight.shape),
            dma(1),
        ],
        8, (before, after, conv_grad, conv_weight, ahead), "vvmhv",
    )
    if near:
        rows = half // chips
        (mine,) = call(
            add_after_kernel, "share_sum", ((rows, LANES),), [], 4, (tokens_grad, *shares),
            "h" + "v" * chips,
        )
        ahead = mine
    block_out, gate_grad = call(
        gate_kernel, "gate", (flat, flat),
        [vmem(flat), vmem(flat), vmem(one[1:]), dma(2)],
        8, (summed, gate_input, cotangent, ahead), "mhhv",
    )
    if near:
        got = [swapped_chips(mine, k) for k in range(1, chips)]
        (joined,) = call(
            join_kernel, "joined", ((chips, rows, LANES),), [],
            8, (place, block_out, mine, *got), "sh" + "v" * chips,
        )
        select_grad, step_grad = call(
            outputs_kernel, "weight_grads", ((2, width, LANES), (2, ranks, width)),
            [vmem((2, half, LANES))],
            12, (place, joined, swapped(joined, "ctx", 1)), "svv",
        )
    else:
        first = lax.rem(place[0], 2) == 0
        both = jnp.where(first, jnp.stack([keep, send]), jnp.stack([send, keep]))
        both = lax.psum(both, "ctx")
        select_grad = both[:, :width]
        step_grad = both[:, width:].reshape(2, tiles, ranks, LANES)
        step_grad = step_grad.transpose(0, 2, 1, 3).reshape(2, ranks, width)
    return (block_out, tokens_grad, gate_grad, select_grad, step_grad)


def solution(mesh):
    return jax.shard_map(
        on_device,
        mesh=mesh,
        in_specs=(
            P("ctx", "ch"),
            P("ctx", "ch"),
            P("ctx", "ch"),
            P(None, None, "ch"),
            P(None, "ch"),
            P(None, "ch", None),
            P(None, None, "ch"),
            P(None, "ch"),
            P(None, None, "ch"),
            P(None, "ch"),
        ),
        out_specs=(
            P("ctx", "ch"),
            P("ctx", "ch"),
            P("ctx", "ch"),
            P(None, "ch", None),
            P(None, None, "ch"),
        ),
        check_vma=False,
    )
```

```python
import functools

import jax
import jax.numpy as jnp
from jax import lax
from jax.experimental import pallas as pl
from jax.experimental.pallas import tpu as pltpu
from jax.sharding import PartitionSpec as P

FULL_PRECISION = lax.Precision.HIGHEST
LANES = 128
CHAINS = 8
HALO = 8
LOG2E = 1.4426950408889634
LN2 = 0.6931471805599453
MIB = 1024 * 1024


def params(mib):
    return pltpu.CompilerParams(vmem_limit_bytes=mib * MIB)


def shape_of(*dims):
    return jax.ShapeDtypeStruct(dims, jnp.float32)


def dot(a, b, contract):
    return lax.dot_general(
        a, b, ((contract[:1], contract[1:]), ((), ())), precision=FULL_PRECISION,
        preferred_element_type=jnp.float32,
    )


def silu_grad(values):
    sigmoid_values = jax.nn.sigmoid(values)
    return sigmoid_values * (1.0 + values * (1.0 - sigmoid_values))


def lane_tile(t):
    return slice(t * LANES, (t + 1) * LANES)


def full_width(ref, *lead):
    tiles = ref.shape[len(lead)]
    return jnp.concatenate([ref[(*lead, t)] for t in range(tiles)], axis=1)


def convolved(ext, at_row, side, lanes, rows, conv_weight, conv_bias):
    taps = conv_weight.shape[1]
    margin = taps - 1
    conv = jnp.broadcast_to(conv_bias[side : side + 1, lanes], (rows, LANES))
    for k in range(taps):
        at = at_row + (k - margin if side == 0 else margin - k)
        conv = conv + conv_weight[side, k : k + 1, lanes] * ext[at : at + rows, lanes]
    return conv


def copies_of(pairs, sems):
    copies = [pltpu.make_async_copy(a, b, sems.at[i]) for i, (a, b) in enumerate(pairs)]
    for copy in copies:
        copy.start()
    return copies


def to_cells(tokens, cells):
    count = tokens.shape[0] // CHAINS
    for j in range(count):
        cells[j * CHAINS : (j + 1) * CHAINS] = tokens[pl.ds(j, CHAINS, stride=count), :]


def to_tokens(cells, tokens):
    count = tokens.shape[0] // CHAINS
    for j in range(count):
        tokens[pl.ds(j, CHAINS, stride=count), :] = cells[j * CHAINS : (j + 1) * CHAINS]


def finish_all(copies):
    for copy in copies:
        copy.wait()


def entry_kernel(
    place, near, far, tokens, conv_weight_in, conv_bias_in, select_in,
    partial, act, pre, ext, conv_weight, conv_bias, select, plain, sems,
):
    length, width = tokens.shape
    loads = copies_of(
        [
            (tokens, ext.at[pl.ds(HALO, length)]), (conv_weight_in, conv_weight),
            (conv_bias_in, conv_bias), (select_in.at[0], select),
        ],
        sems,
    )
    core = lax.rem(place[0], 2)
    ext[:HALO] = jnp.where(core == 0, far[...], near[...])
    ext[HALO + length :] = jnp.where(core == 0, near[...], far[...])
    finish_all(loads[:3])
    enter(0, ext, conv_weight, conv_bias, select, loads[3], partial, act, pre, plain)


def second_entry_kernel(
    ext, conv_weight_in, conv_bias_in, select_in, gate_in, cot_in,
    partial, act, pre, grad_gated, spreader,
    conv_weight, conv_bias, select, plain, gate, cot, sems,
):
    loads = copies_of(
        [
            (conv_weight_in, conv_weight), (conv_bias_in, conv_bias), (select_in.at[1], select),
            (gate_in, gate), (cot_in, cot),
        ],
        sems,
    )
    fill_spreader(spreader)
    finish_all(loads[:2])
    enter(1, ext, conv_weight, conv_bias, select, loads[2], partial, act, pre, plain)
    finish_all(loads[3:])
    for t in range(grad_gated.shape[0]):
        lanes = lane_tile(t)
        values = gate[:, lanes]
        plain[...] = cot[:, lanes] * values * jax.nn.sigmoid(values)
        to_cells(plain, grad_gated.at[t])


def enter(side, ext, conv_weight, conv_bias, select, load, partial, act, pre, plain):
    tiles, length, _ = act.shape
    for t in range(tiles):
        conv = convolved(ext, HALO, side, lane_tile(t), length, conv_weight, conv_bias)
        pre[t] = conv
        plain[...] = conv * jax.nn.sigmoid(conv)
        to_cells(plain, act.at[t])
    load.wait()
    partial[...] = dot(full_width(act), select[...], (1, 0))


def turned(k, by, count):
    return lax.rem(k - 1 + by, count - 1) + 1


def fill_spreader(spreader):
    rows, columns = spreader.shape
    bases = columns // LANES
    row = lax.broadcasted_iota(jnp.int32, (rows, LANES), 0)
    kind = jnp.where(row >= rows - 3 * bases, lax.rem(row + bases - rows % bases, bases), -1)
    for n in range(bases):
        spreader[:, lane_tile(n)] = jnp.where(kind == n, 1.0, 0.0).astype(jnp.bfloat16)


def fill_bases(projection, spreader, bases):
    states = bases.shape[2] // LANES
    first = LANES - 2 * states
    lane = lax.broadcasted_iota(jnp.int32, projection.shape, 1)
    rest = jnp.where(lane >= first, projection[...], 0.0)
    joined = jnp.zeros_like(rest)
    for k in range(3):
        part = rest.astype(jnp.bfloat16).astype(jnp.float32)
        rest = rest - part
        joined = joined + (pltpu.roll(part, LANES - 2 * states * k, 1) if k else part)
    joined = joined.astype(jnp.bfloat16)
    width = 4 * LANES
    for at in range(0, 2 * states * LANES, width):
        value = jnp.dot(
            joined, spreader[:, at : at + width], preferred_element_type=jnp.float32
        )
        kind, lanes = at // (states * LANES), at % (states * LANES)
        bases[kind, :, lanes : lanes + width] = value


def fill_rates(decay_log, rates):
    for t in range(rates.shape[0]):
        rates[t] = -LOG2E * jnp.exp(decay_log[:, lane_tile(t)])


def sublane():
    return lax.broadcasted_iota(jnp.int32, (CHAINS, LANES), 0)


def shifted(value, by, up):
    rolled = pltpu.roll(value, by if up else CHAINS - by, 0)
    place = sublane()
    keep = place >= by if up else place < CHAINS - by
    return jnp.where(keep, rolled, 0.0)


def over_chains(decays, ends, up):
    by = 1
    while by < CHAINS:
        ends = [d * shifted(f, by, up) + f for d, f in zip(decays, ends)]
        if 2 * by < CHAINS:
            turn = by if up else CHAINS - by
            decays = [d * pltpu.roll(d, turn, 0) for d in decays]
        by *= 2
    return ends


def order(i, count, up):
    return i if up else count - 1 - i


def tile_group(tiles):
    return 2 if tiles % 2 == 0 else 1


def unrolled(count, times, body, start):
    times = times if count % times == 0 else 1

    def several(i, state):
        for k in range(times):
            state = body(i * times + k, state)
        return state

    return lax.fori_loop(0, count // times, several, start)


def plus(total, term):
    return term if total is None else total + term


def fill_rate_rows(rates, tiles, rate_rows):
    for g, t in enumerate(tiles):
        for n in range(rate_rows.shape[1]):
            rate_rows[g, n] = jnp.broadcast_to(rates[t, n : n + 1], (CHAINS, LANES))


def cell_rows(j):
    return pl.ds(pl.multiple_of(j * CHAINS, CHAINS), CHAINS)


def local_kernel(side, *refs):
    own, first, second, third, act, grad_gated, spreader = refs[:7]
    earlier, refs = refs[7 : 7 + 2 * side], refs[7 + 2 * side :]
    step_weight_in, step_bias_in, decay_log_in, *refs = refs
    projection, step, step_pre, entering, decays, bases, carry, row_rates, *refs = refs
    step_weight, step_bias, decay_log, rates, rate_rows, sems = refs
    tiles, length, _ = act.shape
    states = decay_log.shape[0]
    ranks = step_weight.shape[0]
    count = length // CHAINS
    group = tile_group(tiles)
    loads = copies_of(
        [
            (step_weight_in.at[side], step_weight), (decay_log_in.at[side], decay_log),
            (step_bias_in, step_bias),
        ],
        sems,
    )
    projection[...] = (own[...] + first[...]) + (second[...] + third[...])
    fill_bases(projection, spreader, bases)
    finish_all(loads)
    fill_rates(decay_log, rates)
    wide = dot(projection[:, :ranks], step_weight[...], (1, 0)) + step_bias[side : side + 1]
    for t in range(tiles):
        part = wide[:, lane_tile(t)]
        step_pre[t] = part
        step[t] = jnp.maximum(part, 0.0) + jnp.log1p(jnp.exp(-jnp.abs(part)))
    zero = jnp.zeros((CHAINS, LANES), jnp.float32)
    if side:
        carry[...] = earlier[0][...]
        row_rates[...] = earlier[1][...]
    else:
        carry[...] = jnp.zeros_like(carry)
        row_rates[...] = jnp.zeros_like(row_rates)
    up = side == 0
    basis_b, basis_c = bases.at[0], bases.at[1]

    def some_tiles(first, keep):
        at_tiles = [first * group + g for g in range(group)]
        fill_rate_rows(rates, at_tiles, rate_rows)

        def forward(i, current):
            state, summed = current
            j = order(i, count, up)
            at = cell_rows(j)
            steps = [step[t, at, :] for t in at_tiles]
            drives = [v * act[t, at, :] for v, t in zip(steps, at_tiles)]
            new = []
            for n in range(states):
                lanes = lane_tile(n)
                b = basis_b[at, lanes]
                for g in range(group):
                    decay = jnp.exp2(steps[g] * rate_rows[g, n])
                    decays[at_tiles[g], at, lanes] = decay
                    new.append(decay * state[n * group + g] + b * drives[g])
            return (tuple(new), tuple(a + v for a, v in zip(summed, steps)))

        start = ((zero,) * (states * group), (zero,) * group)
        state, summed = unrolled(count, 4, forward, start)

        def retreat(i, state):
            j = order(i, count, not up)
            at = cell_rows(j)
            grads = [grad_gated[t, at, :] for t in at_tiles]
            new = []
            for n in range(states):
                lanes = lane_tile(n)
                c = basis_c[at, lanes]
                for g in range(group):
                    adjoint = state[n * group + g] + c * grads[g]
                    new.append(decays[at_tiles[g], at, lanes] * adjoint)
            return tuple(new)

        sent = unrolled(count, 4, retreat, (zero,) * (states * group))
        for g, t in enumerate(at_tiles):
            across = [jnp.exp2(summed[g] * rate_rows[g, n]) for n in range(states)]
            for kind, ends, upward in ((0, state, up), (1, sent, not up)):
                ends = over_chains(across, list(ends[g::group]), upward)
                last = CHAINS - 1 if upward else 0
                for n in range(states):
                    entering[kind, t, n] = shifted(ends[n], 1, upward)
                    at = side * states + n
                    carry[0 if upward else 1, t, at : at + 1] = ends[n][last : last + 1]
            whole = jnp.sum(summed[g], axis=0, keepdims=True)
            at = 2 * states + side
            for k in range(2):
                carry[k, t, at : at + 1] = whole
        return keep

    lax.fori_loop(0, tiles // group, some_tiles, 0)
    row_rates[:, side * states : (side + 1) * states] = rates[...]


def tile_decay(part, rates):
    rows = rates.shape[1]
    row = lax.broadcasted_iota(jnp.int32, rates.shape, 1)
    sums = jnp.where(row < rows // 2, part[:, rows : rows + 1], part[:, rows + 1 : rows + 2])
    return jnp.exp2(rates * sums)


def pair_kernel(place, mine, other, rates, *refs):
    outs, total = refs[:-1], refs[-1]
    rows = rates.shape[1]
    core, chip = lax.rem(place[0], 2), lax.div(place[0], 2)
    low = jnp.where(core == 0, mine[...], other[...])
    high = jnp.where(core == 0, other[...], mine[...])
    spread_rates = rates[...]
    decay_low = tile_decay(low[0], spread_rates)
    decay_high = tile_decay(high[0], spread_rates)
    total[...] = low + high
    total[0, :, :rows] = decay_high * low[0][:, :rows] + high[0][:, :rows]
    total[1, :, :rows] = decay_low * high[1][:, :rows] + low[1][:, :rows]
    tiles = rates.shape[0]
    for k, out in enumerate(outs, 1):
        to = chip ^ turned(k, core, len(outs) + 1)
        below = lax.convert_element_type(to < chip, jnp.int32)
        for t in range(tiles):
            out[t * rows : (t + 1) * rows] = total[below, t, :rows]
            for side in range(2):
                at = tiles * rows + side * tiles + t
                out[at : at + 1] = total[0, t, rows + side : rows + side + 1]


def chain_kernel(place, other, rates, *refs):
    gathered, (out, parts) = refs[:-2], refs[-2:]
    rows = rates.shape[1]
    chips = parts.shape[0]
    core, chip = lax.rem(place[0], 2), lax.div(place[0], 2)
    parts[chip] = jnp.zeros(parts.shape[1:], jnp.float32)
    tiles = rates.shape[0]
    for k, part in enumerate(gathered, 1):
        source = chip ^ turned(k, core, chips)
        for t in range(tiles):
            parts[source, t, :rows] = part[t * rows : (t + 1) * rows]
            for side in range(2):
                at = tiles * rows + side * tiles + t
                parts[source, t, rows + side : rows + side + 1] = part[at : at + 1]
    spread_rates = rates[...]
    for kind in range(2):
        state = jnp.zeros(rates.shape, jnp.float32)
        for k in range(chips) if kind == 0 else reversed(range(chips)):
            part = parts[k]
            new = tile_decay(part, spread_rates) * state + part[:, :rows]
            state = jnp.where(k < chip if kind == 0 else k > chip, new, state)
        part = other[kind]
        new = tile_decay(part, spread_rates) * state + part[:, :rows]
        out[kind] = jnp.where(core == 1 - kind, new, state)


def long_chain_kernel(place, gathered, rates, out):
    rows = rates.shape[1]
    shards = gathered.shape[0]
    for kind in range(2):

        def turn(i, state):
            part = gathered[order(i, shards, kind == 0), kind]
            return tile_decay(part, rates[...]) * state + part[:, :rows]

        turns = place[0] if kind == 0 else shards - 1 - place[0]
        out[kind] = lax.fori_loop(0, turns, turn, jnp.zeros(rates.shape, jnp.float32))


def scan_kernel(side, *refs):
    incoming, bases, act, step, step_pre, grad_gated, entering, decays, spreader = refs[:9]
    earlier, refs = refs[9 : 9 + side], refs[9 + side :]
    step_weight_in, decay_log_in, skip_gain_in, *refs = refs
    partial, grad_act, grad_pre, summed_out, *refs = refs
    step_weight, decay_log, skip_gain, rates, rate_rows, history, *refs = refs
    grad_in, grad_out, weights, skip_rows, sems = refs
    tiles, length, _ = act.shape
    states = decay_log.shape[0]
    ranks = step_weight.shape[0]
    count = length // CHAINS
    group = tile_group(tiles)
    loads = copies_of(
        [
            (decay_log_in.at[side], decay_log), (skip_gain_in, skip_gain),
            (step_weight_in.at[side], step_weight),
        ],
        sems,
    )
    grad_in[...] = jnp.zeros_like(grad_in)
    grad_out[...] = jnp.zeros_like(grad_out)
    finish_all(loads)
    fill_rates(decay_log, rates)
    for t in range(tiles):
        skip_rows[t] = skip_gain[side : side + 1, lane_tile(t)]
    up = side == 0
    basis_b, basis_c = bases.at[0], bases.at[1]

    def some_tiles(first, keep):
        at_tiles = [first * group + g for g in range(group)]
        fill_rate_rows(rates, at_tiles, rate_rows)
        skips = [skip_rows[t] for t in at_tiles]
        sums = []
        for t in at_tiles:
            summed = step[t, cell_rows(0), :]
            for j in range(1, count):
                summed = summed + step[t, cell_rows(j), :]
            sums.append(summed)

        def start(kind, upward):
            spans = []
            for g in range(group):
                span = shifted(sums[g], 1, upward)
                by = 1
                while by < CHAINS:
                    span = span + shifted(span, by, upward)
                    by *= 2
                spans.append(span)
            first = []
            for n in range(states):
                at = side * states + n
                for g, t in enumerate(at_tiles):
                    decay = jnp.exp2(spans[g] * rate_rows[g, n])
                    value = incoming[0 if upward else 1, t, at : at + 1, :]
                    first.append(entering[kind, t, n] + decay * value)
            return tuple(first)

        def forward(i, state):
            j = order(i, count, up)
            at = cell_rows(j)
            acts = [act[t, at, :] for t in at_tiles]
            grads = [grad_gated[t, at, :] for t in at_tiles]
            drives = [step[t, at, :] * a for t, a in zip(at_tiles, acts)]
            outs = [[v * a, None] for v, a in zip(skips, acts)]
            new = []
            for n in range(states):
                lanes = lane_tile(n)
                b, c = basis_b[at, lanes], basis_c[at, lanes]
                read = grad_out[at, lanes]
                for g in range(group):
                    before = state[n * group + g]
                    decay = decays[at_tiles[g], at, lanes]
                    history[g, at, lanes] = before
                    current = decay * before + b * drives[g]
                    outs[g][n % 2] = plus(outs[g][n % 2], c * current)
                    read = read + current * grads[g]
                    new.append(current)
                grad_out[at, lanes] = read
            for g, t in enumerate(at_tiles):
                out = outs[g][0] + outs[g][1]
                if side == 0:
                    summed_out[t, at, :] = out
                else:
                    summed_out[t, at, :] = earlier[0][t, at, :] + out
            return tuple(new)

        unrolled(count, 4, forward, start(0, up))

        def retreat(i, state):
            j = order(i, count, not up)
            at = cell_rows(j)
            steps = [step[t, at, :] for t in at_tiles]
            acts = [act[t, at, :] for t in at_tiles]
            grads = [grad_gated[t, at, :] for t in at_tiles]
            drives = [v * a for v, a in zip(steps, acts)]
            step_terms = [[None, None] for _ in range(group)]
            drive_grads = [[None, None] for _ in range(group)]
            new = []
            for n in range(states):
                lanes = lane_tile(n)
                b, c = basis_b[at, lanes], basis_c[at, lanes]
                put = grad_in[at, lanes]
                for g in range(group):
                    adjoint = state[n * group + g] + c * grads[g]
                    carried = decays[at_tiles[g], at, lanes] * adjoint
                    new.append(carried)
                    term = carried * history[g, at, lanes] * rate_rows[g, n]
                    step_terms[g][n % 2] = plus(step_terms[g][n % 2], term)
                    drive_grads[g][n % 2] = plus(drive_grads[g][n % 2], adjoint * b)
                    put = put + adjoint * drives[g]
                grad_in[at, lanes] = put
            for g, t in enumerate(at_tiles):
                drive_grad = drive_grads[g][0] + drive_grads[g][1]
                step_term = step_terms[g][0] + step_terms[g][1]
                grad_step = step_term * LN2 + drive_grad * acts[g]
                grad_act[t, at, :] = grads[g] * skips[g] + drive_grad * steps[g]
                pre = step_pre[t, at, :]
                grad_pre[t, at, :] = grad_step * jax.nn.sigmoid(pre)
            return tuple(new)

        unrolled(count, 4, retreat, start(1, not up))
        return keep

    lax.fori_loop(0, tiles // group, some_tiles, 0)
    wide = full_width(grad_pre)
    weights[...] = jnp.zeros_like(weights)
    weights[:ranks] = step_weight[...]
    sums = jnp.zeros((length, LANES), jnp.float32)
    step_lanes = 4 * LANES
    for k, values in enumerate((grad_in, grad_out)):
        for at in range(0, states * LANES, step_lanes):
            rest = values[:, at : at + step_lanes]
            from_lane = k * states * LANES + at
            pick = spreader[:, from_lane : from_lane + step_lanes]
            for _ in range(2):
                piece = rest.astype(jnp.bfloat16)
                rest = rest - piece.astype(jnp.float32)
                sums = sums + lax.dot_general(
                    piece, pick, (((1,), (1,)), ((), ())), preferred_element_type=jnp.float32
                )
    lane = lax.broadcasted_iota(jnp.int32, (length, LANES), 1)
    partial[...] = dot(wide, weights[...], (1, 1)) + jnp.where(lane >= ranks, sums, 0.0)


def step_kernel(first_pre, second_pre, first, second, after_this, step_part):
    _, tiles, ranks, _ = step_part.shape
    for side, (grad_pre, projection) in enumerate(((first_pre, first), (second_pre, second))):
        wide = dot(projection[...], full_width(grad_pre), (0, 0))
        for t in range(tiles):
            step_part[side, t] = wide[:ranks, lane_tile(t)]


def gate_kernel(
    summed, gate_in, cot_in, after_this, block_out, gate_grad, gate, cot, plain, sems
):
    finish_all(copies_of([(gate_in, gate), (cot_in, cot)], sems))
    for t in range(summed.shape[0]):
        lanes = lane_tile(t)
        values = gate[:, lanes]
        to_tokens(summed.at[t], plain)
        both = plain[...]
        block_out[:, lanes] = both * values * jax.nn.sigmoid(values)
        gate_grad[:, lanes] = cot[:, lanes] * both * silu_grad(values)


def weight_kernel(
    total, act, pre, grad_act, select_in, after_this,
    part, conv_grad, select, grad, plain, cells, sems,
):
    weigh(
        0, (total,), act, pre, grad_act, select_in,
        conv_grad, select, grad, plain, cells, sems, part,
    )


def second_weight_kernel(
    place, own, first, second, third, act, pre, grad_act, select_in, part, step_part, other_grad,
    keep, send, conv_grad, near, far, select, grad, plain, cells, mine, sems,
):
    length, width = conv_grad.shape
    weigh(
        1, (own, first, second, third), act, pre, grad_act, select_in,
        conv_grad, select, grad, plain, cells, sems, mine,
    )
    core = lax.rem(place[0], 2)
    for side, value in enumerate((part, mine)):
        for out, whose in ((keep, side), (send, 1 - side)):

            @pl.when(core == whose)
            def _():
                out[:width] = value[...]
                out[width:] = step_part[side].reshape(-1, LANES)
    head, tail = other_grad[:HALO], conv_grad[length - HALO :]
    near[...] = jnp.where(core == 0, tail, head)
    far[...] = jnp.where(core == 0, head, tail)


def weigh(
    side, terms, act, pre, grad_act, select_in, conv_grad, select, grad, plain, cells, sems, part
):
    loads = copies_of([(select_in.at[side], select)], sems)
    total = terms[0][...]
    for term in terms[1:]:
        total = total + term[...]
    grad[...] = total
    part[...] = dot(full_width(act), grad[...], (0, 0))
    finish_all(loads)
    wide = dot(grad[...], select[...], (1, 1))
    for t in range(act.shape[0]):
        lanes = lane_tile(t)
        cells[...] = grad_act[t] + wide[:, lanes]
        to_tokens(cells, plain)
        conv_grad[:, lanes] = plain[...] * silu_grad(pre[t])


def halves_kernel(place, keep, got, mine, *refs):
    outs, (total,) = refs[:-1], refs[-1:]
    share = mine.shape[0]
    chips = len(outs) + 1
    for k in range(chips):
        at = slice(k * share, (k + 1) * share)
        total[k] = keep[at] + got[at]
    core, chip = lax.rem(place[0], 2), lax.div(place[0], 2)
    mine[...] = total[chip]
    for k, out in enumerate(outs, 1):
        out[...] = total[chip ^ turned(k, core, chips)]


def handover_kernel(value, *refs):
    terms, (total, out) = refs[:-2], refs[-2:]
    add_kernel(*terms, total)
    out[...] = value[...]


def add_after_kernel(after_this, *refs):
    add_kernel(*refs)


def add_kernel(*refs):
    total = refs[0][...]
    for ref in refs[1:-1]:
        total = total + ref[...]
    refs[-1][...] = total


def join_kernel(place, after_this, mine, *refs):
    parts, out = refs[:-1], refs[-1]
    core, chip = lax.rem(place[0], 2), lax.div(place[0], 2)
    out[chip] = mine[...]
    for k, part in enumerate(parts, 1):
        out[chip ^ turned(k, core, len(parts) + 1)] = part[...]


def outputs_kernel(place, mine, other, select_grad, step_grad, both):
    sides, width, _ = select_grad.shape
    ranks = step_grad.shape[1]
    chips = mine.shape[0]
    core = lax.rem(place[0], 2)
    size = mine.shape[1]
    for side in range(2):
        for k in range(chips):
            both[side, k * size : (k + 1) * size] = jnp.where(core == side, mine[k], other[k])
        select_grad[side] = both[side, :width]
        for t in range(width // LANES):
            at = width + t * ranks
            step_grad[side, :, lane_tile(t)] = both[side, at : at + ranks]


def exit_kernel(
    place, near, far, first, second, conv_weight_in, after_this, tokens_grad, up, down, conv_weight, sems
):
    length, width = first.shape
    taps = conv_weight.shape[1]
    margin = taps - 1
    loads = copies_of(
        [
            (conv_weight_in, conv_weight),
        ],
        sems,
    )
    core = lax.rem(place[0], 2)
    up[:length] = first[...]
    up[length:] = jnp.where(core == 0, near[...], far[...])
    down[:HALO] = jnp.where(core == 0, far[...], near[...])
    down[HALO:] = second[...]
    finish_all(loads)
    for t in range(width // LANES):
        lanes = lane_tile(t)
        total = jnp.zeros((length, LANES), jnp.float32)
        for k in range(taps):
            at = margin - k
            total = total + conv_weight[0, k : k + 1, lanes] * up[at : at + length, lanes]
            at = HALO - margin + k
            total = total + conv_weight[1, k : k + 1, lanes] * down[at : at + length, lanes]
        tokens_grad[:, lanes] = total


def swapped_edges(near, far, axis):
    count = lax.axis_size(axis)
    pairs = [(i, i + 1) for i in range(1, count - 1, 2)]
    pairs = pairs + [(j, i) for i, j in pairs]
    return swapped(near, axis, 1), lax.ppermute(far, axis, pairs)


def swapped(value, axis, by):
    count = lax.axis_size(axis)
    return lax.ppermute(value, axis, [(i, i ^ by) for i in range(count)])


def swapped_chips(value, k):
    places = lax.axis_size("ctx")
    chips = places // 2
    pairs = [(i, i ^ (2 * ((k - 1 + i % 2) % (chips - 1) + 1))) for i in range(places)]
    return lax.ppermute(value, "ctx", pairs)


def call(kernel, name, out_shape, scratch, mib, args, kinds, outs=None, flops=2**28):
    spaces = {
        "v": pl.BlockSpec(memory_space=pltpu.VMEM),
        "m": pl.BlockSpec(memory_space=pltpu.VMEM),
        "b": pl.BlockSpec(memory_space=pltpu.VMEM),
        "h": pl.BlockSpec(memory_space=pltpu.HBM),
        "s": pl.BlockSpec(memory_space=pltpu.SMEM),
    }
    outs = outs or "v" * len(out_shape)
    pinned = {"m": pltpu.VMEM, "h": pltpu.HBM}
    args = [
        pltpu.with_memory_space_constraint(a, pinned[k]) if k in pinned else a
        for a, k in zip(args, kinds, strict=True)
    ]
    results = [
        pinned[k](shape, jnp.float32) if k in pinned else shape_of(*shape)
        for shape, k in zip(out_shape, outs, strict=True)
        if k != "b"
    ]
    at = outs.find("b")
    if at >= 0:
        results.insert(at, pltpu.VMEM(out_shape[at], jnp.bfloat16))
    return pl.pallas_call(
        kernel,
        in_specs=[spaces[k] for k in kinds],
        out_specs=[spaces[k] for k in outs],
        out_shape=results,
        scratch_shapes=scratch,
        compiler_params=params(mib),
        cost_estimate=pl.CostEstimate(flops=flops, bytes_accessed=flops // 64, transcendentals=0),
        name=name,
    )(*args)


def terms_of(partial):
    count = lax.axis_size("ch")
    if count != 4:
        zero = jnp.zeros_like(partial)
        return (lax.psum(partial, "ch"), zero, zero, zero)
    return (partial, *(swapped(partial, "ch", k) for k in range(1, count)))


def halved(place, keep, send, rows, chips, name):
    got = swapped(send, "ctx", 1)
    share = rows // chips
    mine, *sent = call(
        halves_kernel, name, ((share, LANES),) * chips, [pltpu.VMEM((chips, share, LANES), jnp.float32)],
        8, (place, keep, got), "svv",
    )
    return (mine, *(swapped_chips(part, k) for k, part in enumerate(sent, 1)))


def on_device(
    tokens, gate_input, cotangent, conv_weight, conv_bias, select_weight, step_weight,
    step_bias, decay_log, skip_gain,
):
    length, width = tokens.shape
    tiles = width // LANES
    states = decay_log.shape[1]
    ranks = step_weight.shape[1]
    places = lax.axis_size("ctx")
    place = lax.axis_index("ctx").astype(jnp.int32).reshape(1)
    group = tile_group(tiles)
    chips = places // 2
    near = places == 8
    narrow = (length, LANES)
    one = (tiles, length, LANES)
    flat = (length, width)
    chain_ends = (2, tiles, states, CHAINS, LANES)
    carry = (2, tiles, 2 * states + 8, LANES)
    row_rates = (tiles, 2 * states, LANES)
    packed = (tiles * 2 * states + -(-2 * tiles // 8) * 8, LANES)
    vmem = functools.partial(pltpu.VMEM, dtype=jnp.float32)
    dma = lambda n: pltpu.SemaphoreType.DMA((n,))
    bases = vmem((length, states * LANES))
    grouped = vmem((group, length, states * LANES))
    rate_scratch = vmem((tiles, states, LANES))
    row_scratch = vmem((group, states, CHAINS, LANES))

    core = (place & 1)[:, None] == 0
    head, tail = tokens[:HALO], tokens[length - HALO :]
    edges = swapped_edges(jnp.where(core, tail, head), jnp.where(core, head, tail), "ctx")
    conv_scratch = [
        vmem(conv_weight.shape), vmem(conv_bias.shape), vmem(select_weight.shape[1:]), vmem(narrow),
    ]
    first_partial, first_act, first_pre, extended = call(
        entry_kernel, "entry", (narrow, one, one, (length + 2 * HALO, width)),
        [*conv_scratch, dma(4)],
        8, (place, *edges, tokens, conv_weight, conv_bias, select_weight), "svvhhhh", "vmmm",
    )
    first_terms = terms_of(first_partial)
    partial, act, pre, grad_gated, spreader = call(
        second_entry_kernel, "second_entry",
        (narrow, one, one, one, (LANES, 2 * states * LANES)),
        [*conv_scratch, vmem(flat), vmem(flat), dma(5)],
        10, (extended, conv_weight, conv_bias, select_weight, gate_input, cotangent),
        "mhhhhh", "vmmmb",
    )
    projection_terms = (first_terms, terms_of(partial))
    acts, pres = (first_act, act), (first_pre, pre)
    earlier, locals_ = (), []
    for side in range(2):
        *found, carried, rates = call(
            functools.partial(local_kernel, side), ("first_local", "second_local")[side],
            (
                narrow, one, one, chain_ends, (*one[:-1], states * LANES),
                (2, length, states * LANES), carry, row_rates,
            ),
            [
                vmem(step_weight.shape[1:]), vmem(step_bias.shape), vmem(decay_log.shape[1:]),
                rate_scratch, row_scratch, dma(3),
            ],
            10,
            (
                *projection_terms[side], acts[side], grad_gated, spreader, *earlier, step_weight,
                step_bias, decay_log,
            ),
            "vvvvmmm" + "v" * len(earlier) + "hhh", "mmmmmmvv", 2**32,
        )
        earlier = (carried, rates)
        locals_.append(found)
    if near:
        other = swapped(carried, "ctx", 1)
        sent = call(
            pair_kernel, "pair", (packed,) * (chips - 1),
            [vmem(carry)], 8, (place, carried, other, rates), "svvv",
        )
        got = [swapped_chips(part, k) for k, part in enumerate(sent, 1)]
        (incoming,) = call(
            chain_kernel, "chain", ((2, *row_rates),), [vmem((chips, *carry[1:]))],
            8, (place, other, rates, *got), "svv" + "v" * len(got),
        )
    else:
        gathered = lax.all_gather(carried, "ctx")
        (incoming,) = call(
            long_chain_kernel, "chain", ((2, *row_rates),), [],
            48, (place, gathered, rates), "svv",
        )
    earlier, grad_terms, grad_acts, grad_pres = (), [], [], []
    for side in range(2):
        projection, step, step_pre, entering, decays, spread_bases = locals_[side]
        partial_grad, grad_act, grad_pre, summed = call(
            functools.partial(scan_kernel, side), ("first_scan", "second_scan")[side],
            (narrow, one, one, one),
            [
                vmem(step_weight.shape[1:]), vmem(decay_log.shape[1:]), vmem(skip_gain.shape),
                rate_scratch, row_scratch, grouped, bases, bases, vmem((LANES, width)),
                vmem((tiles, 1, LANES)), dma(3),
            ],
            10,
            (
                incoming, spread_bases, acts[side], step, step_pre, grad_gated, entering, decays,
                spreader, *earlier, step_weight, decay_log, skip_gain,
            ),
            "vmmmmmmmm" + "m" * side + "hhh", "vmmm", 2**33,
        )
        if side == 1:
            first_total, partial_grad = call(
                handover_kernel, "handover", (narrow, narrow), [], 4,
                (partial_grad, *grad_terms[0]), "vvvvv",
            )
        grad_terms.append(terms_of(partial_grad))
        earlier = (summed,)
        grad_acts.append(grad_act)
        grad_pres.append(grad_pre)
    arrived = grad_terms[1][1]
    (step_part,) = call(
        step_kernel, "step_grad", ((2, tiles, ranks, LANES),), [],
        8, (*grad_pres, locals_[0][0], locals_[1][0], arrived), "mmmmv", flops=0,
    )
    weight_scratch = [
        vmem(select_weight.shape[1:]), vmem(narrow), vmem(narrow), vmem(narrow),
    ]
    part, first_grad = call(
        weight_kernel, "first_weights", ((width, LANES), flat), [*weight_scratch, dma(1)],
        8, (first_total, first_act, first_pre, grad_acts[0], select_weight, arrived),
        "vmmmhv", "mm", 0,
    )
    half = width + tiles * ranks
    keep, send, second_grad, *edges = call(
        second_weight_kernel, "weights",
        ((half, LANES), (half, LANES), flat, (HALO, width), (HALO, width)),
        [*weight_scratch, vmem((width, LANES)), dma(1)],
        10,
        (
            place, *grad_terms[1], act, pre, grad_acts[1], select_weight, part, step_part,
            first_grad,
        ),
        "svvvvmmmhmvm", "vvmvv",
    )
    edges = swapped_edges(*edges, "ctx")
    if near:
        shares = halved(place, keep, send, half, chips, "halves")
        ahead = shares[0]
    else:
        ahead = edges[0]
    (tokens_grad,) = call(
        exit_kernel, "exit", (flat,),
        [
            vmem((length + HALO, width)), vmem((length + HALO, width)), vmem(conv_weight.shape),
            dma(1),
        ],
        8, (place, *edges, first_grad, second_grad, conv_weight, ahead), "svvmmhv",
    )
    if near:
        rows = half // chips
        (mine,) = call(
            add_after_kernel, "share_sum", ((rows, LANES),), [], 4, (tokens_grad, *shares),
            "h" + "v" * chips,
        )
        ahead = mine
    block_out, gate_grad = call(
        gate_kernel, "gate", (flat, flat),
        [vmem(flat), vmem(flat), vmem(one[1:]), dma(2)],
        8, (summed, gate_input, cotangent, ahead), "mhhv", flops=0,
    )
    if near:
        got = [swapped_chips(mine, k) for k in range(1, chips)]
        (joined,) = call(
            join_kernel, "joined", ((chips, rows, LANES),), [],
            8, (place, block_out, mine, *got), "sh" + "v" * chips,
        )
        select_grad, step_grad = call(
            outputs_kernel, "weight_grads", ((2, width, LANES), (2, ranks, width)),
            [vmem((2, half, LANES))],
            12, (place, joined, swapped(joined, "ctx", 1)), "svv",
        )
    else:
        first = lax.rem(place[0], 2) == 0
        both = jnp.where(first, jnp.stack([keep, send]), jnp.stack([send, keep]))
        both = lax.psum(both, "ctx")
        select_grad = both[:, :width]
        step_grad = both[:, width:].reshape(2, tiles, ranks, LANES)
        step_grad = step_grad.transpose(0, 2, 1, 3).reshape(2, ranks, width)
    return (block_out, tokens_grad, gate_grad, select_grad, step_grad)


def solution(mesh):
    return jax.shard_map(
        on_device,
        mesh=mesh,
        in_specs=(
            P("ctx", "ch"),
            P("ctx", "ch"),
            P("ctx", "ch"),
            P(None, None, "ch"),
            P(None, "ch"),
            P(None, "ch", None),
            P(None, None, "ch"),
            P(None, "ch"),
            P(None, None, "ch"),
            P(None, "ch"),
        ),
        out_specs=(
            P("ctx", "ch"),
            P("ctx", "ch"),
            P("ctx", "ch"),
            P(None, "ch", None),
            P(None, None, "ch"),
        ),
        check_vma=False,
    )
```

```python
import functools

import jax
import jax.numpy as jnp
from jax import lax
from jax.experimental import pallas as pl
from jax.experimental.pallas import tpu as pltpu
from jax.sharding import PartitionSpec as P

FULL_PRECISION = lax.Precision.HIGHEST
LANES = 128
CHAINS = 8
HALO = 8
LOG2E = 1.4426950408889634
LN2 = 0.6931471805599453
MIB = 1024 * 1024


def params(mib):
    return pltpu.CompilerParams(vmem_limit_bytes=mib * MIB)


def shape_of(*dims):
    return jax.ShapeDtypeStruct(dims, jnp.float32)


def dot(a, b, contract):
    return lax.dot_general(
        a, b, ((contract[:1], contract[1:]), ((), ())), precision=FULL_PRECISION,
        preferred_element_type=jnp.float32,
    )


def silu_grad(values):
    sigmoid_values = jax.nn.sigmoid(values)
    return sigmoid_values * (1.0 + values * (1.0 - sigmoid_values))


def lane_tile(t):
    return slice(t * LANES, (t + 1) * LANES)


def full_width(ref, *lead):
    tiles = ref.shape[len(lead)]
    return jnp.concatenate([ref[(*lead, t)] for t in range(tiles)], axis=1)


def convolved(ext, at_row, side, lanes, rows, conv_weight, conv_bias):
    taps = conv_weight.shape[1]
    margin = taps - 1
    conv = jnp.broadcast_to(conv_bias[side : side + 1, lanes], (rows, LANES))
    for k in range(taps):
        at = at_row + (k - margin if side == 0 else margin - k)
        conv = conv + conv_weight[side, k : k + 1, lanes] * ext[at : at + rows, lanes]
    return conv


def copies_of(pairs, sems):
    copies = [pltpu.make_async_copy(a, b, sems.at[i]) for i, (a, b) in enumerate(pairs)]
    for copy in copies:
        copy.start()
    return copies


def to_cells(tokens, cells):
    count = tokens.shape[0] // CHAINS
    for j in range(count):
        cells[j * CHAINS : (j + 1) * CHAINS] = tokens[pl.ds(j, CHAINS, stride=count), :]


def to_tokens(cells, tokens):
    count = tokens.shape[0] // CHAINS
    for j in range(count):
        tokens[pl.ds(j, CHAINS, stride=count), :] = cells[j * CHAINS : (j + 1) * CHAINS]


def finish_all(copies):
    for copy in copies:
        copy.wait()


def fetch_kernel(*refs):
    count = (len(refs) - 1) // 2
    finish_all(copies_of(list(zip(refs[:count], refs[count : 2 * count])), refs[-1]))


def entry_kernel(
    place, near, far, tokens, conv_weight, conv_bias, select,
    partial, act, pre, ext, plain,
):
    length, width = tokens.shape
    core = lax.rem(place[0], 2)
    ext[:HALO] = jnp.where(core == 0, far[...], near[...])
    ext[HALO : HALO + length] = tokens[...]
    ext[HALO + length :] = jnp.where(core == 0, near[...], far[...])
    enter(0, ext, conv_weight, conv_bias, select, partial, act, pre, plain)


def second_entry_kernel(
    ext, conv_weight, conv_bias, select, gate, cot,
    partial, act, pre, grad_gated, spreader, plain,
):
    fill_spreader(spreader)
    enter(1, ext, conv_weight, conv_bias, select, partial, act, pre, plain)
    for t in range(grad_gated.shape[0]):
        lanes = lane_tile(t)
        values = gate[:, lanes]
        plain[...] = cot[:, lanes] * values * jax.nn.sigmoid(values)
        to_cells(plain, grad_gated.at[t])


def enter(side, ext, conv_weight, conv_bias, select, partial, act, pre, plain):
    tiles, length, _ = act.shape
    for t in range(tiles):
        conv = convolved(ext, HALO, side, lane_tile(t), length, conv_weight, conv_bias)
        pre[t] = conv
        plain[...] = conv * jax.nn.sigmoid(conv)
        to_cells(plain, act.at[t])
    partial[...] = dot(full_width(act), select[side], (1, 0))


def turned(k, by, count):
    return lax.rem(k - 1 + by, count - 1) + 1


def fill_spreader(spreader):
    rows, columns = spreader.shape
    bases = columns // LANES
    row = lax.broadcasted_iota(jnp.int32, (rows, LANES), 0)
    kind = jnp.where(row >= rows - 3 * bases, lax.rem(row + bases - rows % bases, bases), -1)
    for n in range(bases):
        spreader[:, lane_tile(n)] = jnp.where(kind == n, 1.0, 0.0).astype(jnp.bfloat16)


def fill_bases(projection, spreader, bases):
    states = bases.shape[2] // LANES
    first = LANES - 2 * states
    lane = lax.broadcasted_iota(jnp.int32, projection.shape, 1)
    rest = jnp.where(lane >= first, projection[...], 0.0)
    joined = jnp.zeros_like(rest)
    for k in range(3):
        part = rest.astype(jnp.bfloat16).astype(jnp.float32)
        rest = rest - part
        joined = joined + (pltpu.roll(part, LANES - 2 * states * k, 1) if k else part)
    joined = joined.astype(jnp.bfloat16)
    width = 4 * LANES
    for at in range(0, 2 * states * LANES, width):
        value = jnp.dot(
            joined, spreader[:, at : at + width], preferred_element_type=jnp.float32
        )
        kind, lanes = at // (states * LANES), at % (states * LANES)
        bases[kind, :, lanes : lanes + width] = value


def fill_rates(decay_log, rates):
    for t in range(rates.shape[0]):
        rates[t] = -LOG2E * jnp.exp(decay_log[:, lane_tile(t)])


def sublane():
    return lax.broadcasted_iota(jnp.int32, (CHAINS, LANES), 0)


def shifted(value, by, up):
    rolled = pltpu.roll(value, by if up else CHAINS - by, 0)
    place = sublane()
    keep = place >= by if up else place < CHAINS - by
    return jnp.where(keep, rolled, 0.0)


def over_chains(decays, ends, up):
    by = 1
    while by < CHAINS:
        ends = [d * shifted(f, by, up) + f for d, f in zip(decays, ends)]
        if 2 * by < CHAINS:
            turn = by if up else CHAINS - by
            decays = [d * pltpu.roll(d, turn, 0) for d in decays]
        by *= 2
    return ends


def order(i, count, up):
    return i if up else count - 1 - i


def tile_group(tiles):
    return 2 if tiles % 2 == 0 else 1


def unrolled(count, times, body, start):
    times = times if count % times == 0 else 1

    def several(i, state):
        for k in range(times):
            state = body(i * times + k, state)
        return state

    return lax.fori_loop(0, count // times, several, start)


def plus(total, term):
    return term if total is None else total + term


def fill_rate_rows(rates, tiles, rate_rows):
    for g, t in enumerate(tiles):
        for n in range(rate_rows.shape[1]):
            rate_rows[g, n] = jnp.broadcast_to(rates[t, n : n + 1], (CHAINS, LANES))


def cell_rows(j):
    return pl.ds(pl.multiple_of(j * CHAINS, CHAINS), CHAINS)


def local_kernel(side, *refs):
    own, first, second, third, act, grad_gated, spreader = refs[:7]
    earlier, refs = refs[7 : 7 + 2 * side], refs[7 + 2 * side :]
    step_weight_in, step_bias_in, decay_log_in, skip_gain_in, *refs = refs
    projection, step, step_pre, entering, decays, bases, rates, skip_rows, *refs = refs
    carry, row_rates, step_weight, step_bias, decay_log, skip_gain, rate_rows, sems = refs
    tiles, length, _ = act.shape
    states = decay_log.shape[0]
    ranks = step_weight.shape[0]
    count = length // CHAINS
    group = tile_group(tiles)
    loads = copies_of(
        [
            (step_weight_in.at[side], step_weight), (decay_log_in.at[side], decay_log),
            (step_bias_in, step_bias), (skip_gain_in, skip_gain),
        ],
        sems,
    )
    projection[...] = (own[...] + first[...]) + (second[...] + third[...])
    fill_bases(projection, spreader, bases)
    finish_all(loads)
    fill_rates(decay_log, rates)
    for t in range(tiles):
        skip_rows[t] = skip_gain[side : side + 1, lane_tile(t)]
    wide = dot(projection[:, :ranks], step_weight[...], (1, 0)) + step_bias[side : side + 1]
    for t in range(tiles):
        part = wide[:, lane_tile(t)]
        step_pre[t] = part
        step[t] = jnp.maximum(part, 0.0) + jnp.log1p(jnp.exp(-jnp.abs(part)))
    zero = jnp.zeros((CHAINS, LANES), jnp.float32)
    if side:
        carry[...] = earlier[0][...]
        row_rates[...] = earlier[1][...]
    else:
        carry[...] = jnp.zeros_like(carry)
        row_rates[...] = jnp.zeros_like(row_rates)
    up = side == 0
    basis_b, basis_c = bases.at[0], bases.at[1]

    def some_tiles(first, keep):
        at_tiles = [first * group + g for g in range(group)]
        fill_rate_rows(rates, at_tiles, rate_rows)

        def forward(i, current):
            state, summed = current
            j = order(i, count, up)
            at = cell_rows(j)
            steps = [step[t, at, :] for t in at_tiles]
            drives = [v * act[t, at, :] for v, t in zip(steps, at_tiles)]
            new = []
            for n in range(states):
                lanes = lane_tile(n)
                b = basis_b[at, lanes]
                for g in range(group):
                    decay = jnp.exp2(steps[g] * rate_rows[g, n])
                    decays[at_tiles[g], at, lanes] = decay
                    new.append(decay * state[n * group + g] + b * drives[g])
            return (tuple(new), tuple(a + v for a, v in zip(summed, steps)))

        start = ((zero,) * (states * group), (zero,) * group)
        state, summed = unrolled(count, 4, forward, start)

        def retreat(i, state):
            j = order(i, count, not up)
            at = cell_rows(j)
            grads = [grad_gated[t, at, :] for t in at_tiles]
            new = []
            for n in range(states):
                lanes = lane_tile(n)
                c = basis_c[at, lanes]
                for g in range(group):
                    adjoint = state[n * group + g] + c * grads[g]
                    new.append(decays[at_tiles[g], at, lanes] * adjoint)
            return tuple(new)

        sent = unrolled(count, 4, retreat, (zero,) * (states * group))
        for g, t in enumerate(at_tiles):
            across = [jnp.exp2(summed[g] * rate_rows[g, n]) for n in range(states)]
            for kind, ends, upward in ((0, state, up), (1, sent, not up)):
                ends = over_chains(across, list(ends[g::group]), upward)
                last = CHAINS - 1 if upward else 0
                for n in range(states):
                    entering[kind, t, n] = shifted(ends[n], 1, upward)
                    at = side * states + n
                    carry[0 if upward else 1, t, at : at + 1] = ends[n][last : last + 1]
            whole = jnp.sum(summed[g], axis=0, keepdims=True)
            at = 2 * states + side
            for k in range(2):
                carry[k, t, at : at + 1] = whole
        return keep

    lax.fori_loop(0, tiles // group, some_tiles, 0)
    row_rates[:, side * states : (side + 1) * states] = rates[...]


def tile_decay(part, rates):
    rows = rates.shape[1]
    row = lax.broadcasted_iota(jnp.int32, rates.shape, 1)
    sums = jnp.where(row < rows // 2, part[:, rows : rows + 1], part[:, rows + 1 : rows + 2])
    return jnp.exp2(rates * sums)


def pair_kernel(place, mine, other, rates, *refs):
    outs, total = refs[:-1], refs[-1]
    rows = rates.shape[1]
    core, chip = lax.rem(place[0], 2), lax.div(place[0], 2)
    low = jnp.where(core == 0, mine[...], other[...])
    high = jnp.where(core == 0, other[...], mine[...])
    spread_rates = rates[...]
    decay_low = tile_decay(low[0], spread_rates)
    decay_high = tile_decay(high[0], spread_rates)
    total[...] = low + high
    total[0, :, :rows] = decay_high * low[0][:, :rows] + high[0][:, :rows]
    total[1, :, :rows] = decay_low * high[1][:, :rows] + low[1][:, :rows]
    tiles = rates.shape[0]
    for k, out in enumerate(outs, 1):
        to = chip ^ turned(k, core, len(outs) + 1)
        below = lax.convert_element_type(to < chip, jnp.int32)
        for t in range(tiles):
            out[t * rows : (t + 1) * rows] = total[below, t, :rows]
            for side in range(2):
                at = tiles * rows + side * tiles + t
                out[at : at + 1] = total[0, t, rows + side : rows + side + 1]


def chain_kernel(place, other, rates, *refs):
    gathered, (out, parts) = refs[:-2], refs[-2:]
    rows = rates.shape[1]
    chips = parts.shape[0]
    core, chip = lax.rem(place[0], 2), lax.div(place[0], 2)
    parts[chip] = jnp.zeros(parts.shape[1:], jnp.float32)
    tiles = rates.shape[0]
    for k, part in enumerate(gathered, 1):
        source = chip ^ turned(k, core, chips)
        for t in range(tiles):
            parts[source, t, :rows] = part[t * rows : (t + 1) * rows]
            for side in range(2):
                at = tiles * rows + side * tiles + t
                parts[source, t, rows + side : rows + side + 1] = part[at : at + 1]
    spread_rates = rates[...]
    for kind in range(2):
        state = jnp.zeros(rates.shape, jnp.float32)
        for k in range(chips) if kind == 0 else reversed(range(chips)):
            part = parts[k]
            new = tile_decay(part, spread_rates) * state + part[:, :rows]
            state = jnp.where(k < chip if kind == 0 else k > chip, new, state)
        part = other[kind]
        new = tile_decay(part, spread_rates) * state + part[:, :rows]
        out[kind] = jnp.where(core == 1 - kind, new, state)


def long_chain_kernel(place, gathered, rates, out):
    rows = rates.shape[1]
    shards = gathered.shape[0]
    for kind in range(2):

        def turn(i, state):
            part = gathered[order(i, shards, kind == 0), kind]
            return tile_decay(part, rates[...]) * state + part[:, :rows]

        turns = place[0] if kind == 0 else shards - 1 - place[0]
        out[kind] = lax.fori_loop(0, turns, turn, jnp.zeros(rates.shape, jnp.float32))


def scan_kernel(side, *refs):
    incoming, bases, act, step, step_pre, grad_gated, entering, decays, spreader, *refs = refs
    rates, skip_rows, *refs = refs
    earlier, refs = refs[:side], refs[side:]
    step_weight_in, *refs = refs
    partial, grad_act, grad_pre, summed_out, *refs = refs
    step_weight, rate_rows, history, grad_in, grad_out, weights, sems = refs
    tiles, length, _ = act.shape
    states = rates.shape[1]
    ranks = step_weight.shape[0]
    count = length // CHAINS
    group = tile_group(tiles)
    loads = copies_of([(step_weight_in.at[side], step_weight)], sems)
    grad_in[...] = jnp.zeros_like(grad_in)
    grad_out[...] = jnp.zeros_like(grad_out)
    up = side == 0
    basis_b, basis_c = bases.at[0], bases.at[1]

    def some_tiles(first, keep):
        at_tiles = [first * group + g for g in range(group)]
        fill_rate_rows(rates, at_tiles, rate_rows)
        skips = [skip_rows[t] for t in at_tiles]
        sums = []
        for t in at_tiles:
            summed = step[t, cell_rows(0), :]
            for j in range(1, count):
                summed = summed + step[t, cell_rows(j), :]
            sums.append(summed)

        def start(kind, upward):
            spans = []
            for g in range(group):
                span = shifted(sums[g], 1, upward)
                by = 1
                while by < CHAINS:
                    span = span + shifted(span, by, upward)
                    by *= 2
                spans.append(span)
            first = []
            for n in range(states):
                at = side * states + n
                for g, t in enumerate(at_tiles):
                    decay = jnp.exp2(spans[g] * rate_rows[g, n])
                    value = incoming[0 if upward else 1, t, at : at + 1, :]
                    first.append(entering[kind, t, n] + decay * value)
            return tuple(first)

        def forward(i, state):
            j = order(i, count, up)
            at = cell_rows(j)
            acts = [act[t, at, :] for t in at_tiles]
            grads = [grad_gated[t, at, :] for t in at_tiles]
            drives = [step[t, at, :] * a for t, a in zip(at_tiles, acts)]
            outs = [[v * a, None] for v, a in zip(skips, acts)]
            new = []
            for n in range(states):
                lanes = lane_tile(n)
                b, c = basis_b[at, lanes], basis_c[at, lanes]
                read = grad_out[at, lanes]
                for g in range(group):
                    before = state[n * group + g]
                    decay = decays[at_tiles[g], at, lanes]
                    history[g, at, lanes] = before
                    current = decay * before + b * drives[g]
                    outs[g][n % 2] = plus(outs[g][n % 2], c * current)
                    read = read + current * grads[g]
                    new.append(current)
                grad_out[at, lanes] = read
            for g, t in enumerate(at_tiles):
                out = outs[g][0] + outs[g][1]
                if side == 0:
                    summed_out[t, at, :] = out
                else:
                    summed_out[t, at, :] = earlier[0][t, at, :] + out
            return tuple(new)

        unrolled(count, 4, forward, start(0, up))

        def retreat(i, state):
            j = order(i, count, not up)
            at = cell_rows(j)
            steps = [step[t, at, :] for t in at_tiles]
            acts = [act[t, at, :] for t in at_tiles]
            grads = [grad_gated[t, at, :] for t in at_tiles]
            drives = [v * a for v, a in zip(steps, acts)]
            step_terms = [[None, None] for _ in range(group)]
            drive_grads = [[None, None] for _ in range(group)]
            new = []
            for n in range(states):
                lanes = lane_tile(n)
                b, c = basis_b[at, lanes], basis_c[at, lanes]
                put = grad_in[at, lanes]
                for g in range(group):
                    adjoint = state[n * group + g] + c * grads[g]
                    carried = decays[at_tiles[g], at, lanes] * adjoint
                    new.append(carried)
                    term = carried * history[g, at, lanes] * rate_rows[g, n]
                    step_terms[g][n % 2] = plus(step_terms[g][n % 2], term)
                    drive_grads[g][n % 2] = plus(drive_grads[g][n % 2], adjoint * b)
                    put = put + adjoint * drives[g]
                grad_in[at, lanes] = put
            for g, t in enumerate(at_tiles):
                drive_grad = drive_grads[g][0] + drive_grads[g][1]
                step_term = step_terms[g][0] + step_terms[g][1]
                grad_step = step_term * LN2 + drive_grad * acts[g]
                grad_act[t, at, :] = grads[g] * skips[g] + drive_grad * steps[g]
                pre = step_pre[t, at, :]
                grad_pre[t, at, :] = grad_step * jax.nn.sigmoid(pre)
            return tuple(new)

        unrolled(count, 4, retreat, start(1, not up))
        return keep

    lax.fori_loop(0, tiles // group, some_tiles, 0)
    wide = full_width(grad_pre)
    weights[...] = jnp.zeros_like(weights)
    finish_all(loads)
    weights[:ranks] = step_weight[...]
    sums = jnp.zeros((length, LANES), jnp.float32)
    step_lanes = 4 * LANES
    for k, values in enumerate((grad_in, grad_out)):
        for at in range(0, states * LANES, step_lanes):
            rest = values[:, at : at + step_lanes]
            from_lane = k * states * LANES + at
            pick = spreader[:, from_lane : from_lane + step_lanes]
            for _ in range(2):
                piece = rest.astype(jnp.bfloat16)
                rest = rest - piece.astype(jnp.float32)
                sums = sums + lax.dot_general(
                    piece, pick, (((1,), (1,)), ((), ())), preferred_element_type=jnp.float32
                )
    lane = lax.broadcasted_iota(jnp.int32, (length, LANES), 1)
    partial[...] = dot(wide, weights[...], (1, 1)) + jnp.where(lane >= ranks, sums, 0.0)


def step_kernel(first_pre, second_pre, first, second, after_this, step_part):
    _, tiles, ranks, _ = step_part.shape
    for side, (grad_pre, projection) in enumerate(((first_pre, first), (second_pre, second))):
        wide = dot(projection[...], full_width(grad_pre), (0, 0))
        for t in range(tiles):
            step_part[side, t] = wide[:ranks, lane_tile(t)]


def gate_kernel(
    summed, gate, cot, after_this, block_out, gate_grad, plain
):
    for t in range(summed.shape[0]):
        lanes = lane_tile(t)
        values = gate[:, lanes]
        to_tokens(summed.at[t], plain)
        both = plain[...]
        block_out[:, lanes] = both * values * jax.nn.sigmoid(values)
        gate_grad[:, lanes] = cot[:, lanes] * both * silu_grad(values)


def weight_kernel(
    total, act, pre, grad_act, select, after_this, part, conv_grad, grad, plain, cells,
):
    weigh(
        0, (total,), act, pre, grad_act, select, conv_grad, grad, plain, cells, part,
    )


def second_weight_kernel(
    place, own, first, second, third, act, pre, grad_act, select, after_this,
    part, step_part, other_grad,
    keep, send, conv_grad, near, far, grad, plain, cells, mine,
):
    length, width = conv_grad.shape
    weigh(
        1, (own, first, second, third), act, pre, grad_act, select,
        conv_grad, grad, plain, cells, mine,
    )
    core = lax.rem(place[0], 2)
    for side, value in enumerate((part, mine)):
        for out, whose in ((keep, side), (send, 1 - side)):

            @pl.when(core == whose)
            def _():
                out[:width] = value[...]
                out[width:] = step_part[side].reshape(-1, LANES)
    head, tail = other_grad[:HALO], conv_grad[length - HALO :]
    near[...] = jnp.where(core == 0, tail, head)
    far[...] = jnp.where(core == 0, head, tail)


def weigh(side, terms, act, pre, grad_act, select, conv_grad, grad, plain, cells, part):
    total = terms[0][...]
    for term in terms[1:]:
        total = total + term[...]
    grad[...] = total
    part[...] = dot(full_width(act), grad[...], (0, 0))
    wide = dot(grad[...], select[side], (1, 1))
    for t in range(act.shape[0]):
        lanes = lane_tile(t)
        cells[...] = grad_act[t] + wide[:, lanes]
        to_tokens(cells, plain)
        conv_grad[:, lanes] = plain[...] * silu_grad(pre[t])


def halves_kernel(place, keep, got, mine, *refs):
    outs, (total,) = refs[:-1], refs[-1:]
    share = mine.shape[0]
    chips = len(outs) + 1
    for k in range(chips):
        at = slice(k * share, (k + 1) * share)
        total[k] = keep[at] + got[at]
    core, chip = lax.rem(place[0], 2), lax.div(place[0], 2)
    mine[...] = total[chip]
    for k, out in enumerate(outs, 1):
        out[...] = total[chip ^ turned(k, core, chips)]


def handover_kernel(value, *refs):
    terms, (total, out) = refs[:-2], refs[-2:]
    add_kernel(*terms, total)
    out[...] = value[...]


def add_kernel(*refs):
    total = refs[0][...]
    for ref in refs[1:-1]:
        total = total + ref[...]
    refs[-1][...] = total


def join_kernel(place, after_this, mine, *refs):
    parts, out = refs[:-1], refs[-1]
    core, chip = lax.rem(place[0], 2), lax.div(place[0], 2)
    out[chip] = mine[...]
    for k, part in enumerate(parts, 1):
        out[chip ^ turned(k, core, len(parts) + 1)] = part[...]


def outputs_kernel(place, mine, other, select_grad, step_grad, both):
    sides, width, _ = select_grad.shape
    ranks = step_grad.shape[1]
    chips = mine.shape[0]
    core = lax.rem(place[0], 2)
    size = mine.shape[1]
    for side in range(2):
        for k in range(chips):
            both[side, k * size : (k + 1) * size] = jnp.where(core == side, mine[k], other[k])
        select_grad[side] = both[side, :width]
        for t in range(width // LANES):
            at = width + t * ranks
            step_grad[side, :, lane_tile(t)] = both[side, at : at + ranks]


def exit_kernel(
    place, near, far, first, second, conv_weight_in, after_this, tokens_grad, up, down, conv_weight, sems
):
    length, width = first.shape
    taps = conv_weight.shape[1]
    margin = taps - 1
    loads = copies_of(
        [
            (conv_weight_in, conv_weight),
        ],
        sems,
    )
    core = lax.rem(place[0], 2)
    up[:length] = first[...]
    up[length:] = jnp.where(core == 0, near[...], far[...])
    down[:HALO] = jnp.where(core == 0, far[...], near[...])
    down[HALO:] = second[...]
    finish_all(loads)
    for t in range(width // LANES):
        lanes = lane_tile(t)
        total = jnp.zeros((length, LANES), jnp.float32)
        for k in range(taps):
            at = margin - k
            total = total + conv_weight[0, k : k + 1, lanes] * up[at : at + length, lanes]
            at = HALO - margin + k
            total = total + conv_weight[1, k : k + 1, lanes] * down[at : at + length, lanes]
        tokens_grad[:, lanes] = total


def swapped_edges(near, far, axis):
    count = lax.axis_size(axis)
    pairs = [(i, i + 1) for i in range(1, count - 1, 2)]
    pairs = pairs + [(j, i) for i, j in pairs]
    return swapped(near, axis, 1), lax.ppermute(far, axis, pairs)


def swapped(value, axis, by):
    count = lax.axis_size(axis)
    return lax.ppermute(value, axis, [(i, i ^ by) for i in range(count)])


def swapped_chips(value, k):
    places = lax.axis_size("ctx")
    chips = places // 2
    pairs = [(i, i ^ (2 * ((k - 1 + i % 2) % (chips - 1) + 1))) for i in range(places)]
    return lax.ppermute(value, "ctx", pairs)


def call(kernel, name, out_shape, scratch, mib, args, kinds, outs=None, flops=2**28):
    spaces = {
        "v": pl.BlockSpec(memory_space=pltpu.VMEM),
        "m": pl.BlockSpec(memory_space=pltpu.VMEM),
        "b": pl.BlockSpec(memory_space=pltpu.VMEM),
        "h": pl.BlockSpec(memory_space=pltpu.HBM),
        "s": pl.BlockSpec(memory_space=pltpu.SMEM),
    }
    outs = outs or "v" * len(out_shape)
    pinned = {"m": pltpu.VMEM, "h": pltpu.HBM}
    args = [
        pltpu.with_memory_space_constraint(a, pinned[k]) if k in pinned else a
        for a, k in zip(args, kinds, strict=True)
    ]
    results = [
        pinned[k](shape, jnp.float32) if k in pinned else shape_of(*shape)
        for shape, k in zip(out_shape, outs, strict=True)
        if k != "b"
    ]
    at = outs.find("b")
    if at >= 0:
        results.insert(at, pltpu.VMEM(out_shape[at], jnp.bfloat16))
    return pl.pallas_call(
        kernel,
        in_specs=[spaces[k] for k in kinds],
        out_specs=[spaces[k] for k in outs],
        out_shape=results,
        scratch_shapes=scratch,
        compiler_params=params(mib),
        cost_estimate=pl.CostEstimate(flops=flops, bytes_accessed=flops // 64, transcendentals=0),
        name=name,
    )(*args)


def terms_of(partial):
    count = lax.axis_size("ch")
    if count != 4:
        zero = jnp.zeros_like(partial)
        return (lax.psum(partial, "ch"), zero, zero, zero)
    return (partial, *(swapped(partial, "ch", k) for k in range(1, count)))


def halved(place, keep, send, rows, chips, name):
    got = swapped(send, "ctx", 1)
    share = rows // chips
    mine, *sent = call(
        halves_kernel, name, ((share, LANES),) * chips, [pltpu.VMEM((chips, share, LANES), jnp.float32)],
        8, (place, keep, got), "svv",
    )
    return (mine, *(swapped_chips(part, k) for k, part in enumerate(sent, 1)))


def on_device(
    tokens, gate_input, cotangent, conv_weight, conv_bias, select_weight, step_weight,
    step_bias, decay_log, skip_gain,
):
    length, width = tokens.shape
    tiles = width // LANES
    states = decay_log.shape[1]
    ranks = step_weight.shape[1]
    places = lax.axis_size("ctx")
    place = lax.axis_index("ctx").astype(jnp.int32).reshape(1)
    group = tile_group(tiles)
    chips = places // 2
    near = places == 8
    narrow = (length, LANES)
    one = (tiles, length, LANES)
    flat = (length, width)
    chain_ends = (2, tiles, states, CHAINS, LANES)
    carry = (2, tiles, 2 * states + 8, LANES)
    row_rates = (tiles, 2 * states, LANES)
    packed = (tiles * 2 * states + -(-2 * tiles // 8) * 8, LANES)
    vmem = functools.partial(pltpu.VMEM, dtype=jnp.float32)
    dma = lambda n: pltpu.SemaphoreType.DMA((n,))
    bases = vmem((length, states * LANES))
    grouped = vmem((group, length, states * LANES))
    row_scratch = vmem((group, states, CHAINS, LANES))

    core = (place & 1)[:, None] == 0
    head, tail = tokens[:HALO], tokens[length - HALO :]
    edges = swapped_edges(jnp.where(core, tail, head), jnp.where(core, head, tail), "ctx")
    fetched = (tokens, conv_weight, conv_bias, select_weight, gate_input, cotangent)
    held, conv_weight_held, conv_bias_held, select, gate, cot = call(
        fetch_kernel, "fetch", tuple(a.shape for a in fetched), [dma(6)], 4, fetched,
        "hhhhhh", "mmmmmm",
    )
    first_partial, first_act, first_pre, extended = call(
        entry_kernel, "entry", (narrow, one, one, (length + 2 * HALO, width)), [vmem(narrow)],
        6, (place, *edges, held, conv_weight_held, conv_bias_held, select), "svvmmmm", "vmmm",
    )
    first_terms = terms_of(first_partial)
    partial, act, pre, grad_gated, spreader = call(
        second_entry_kernel, "second_entry",
        (narrow, one, one, one, (LANES, 2 * states * LANES)),
        [vmem(narrow)],
        6, (extended, conv_weight_held, conv_bias_held, select, gate, cot), "mmmmmm", "vmmmb",
    )
    projection_terms = (first_terms, terms_of(partial))
    acts, pres = (first_act, act), (first_pre, pre)
    earlier, locals_ = (), []
    for side in range(2):
        *found, carried, every_rate = call(
            functools.partial(local_kernel, side), ("first_local", "second_local")[side],
            (
                narrow, one, one, chain_ends, (*one[:-1], states * LANES),
                (2, length, states * LANES), (tiles, states, LANES), (tiles, 1, LANES),
                carry, row_rates,
            ),
            [
                vmem(step_weight.shape[1:]), vmem(step_bias.shape), vmem(decay_log.shape[1:]),
                vmem(skip_gain.shape), row_scratch, dma(4),
            ],
            10,
            (
                *projection_terms[side], acts[side], grad_gated, spreader, *earlier, step_weight,
                step_bias, decay_log, skip_gain,
            ),
            "vvvvmmm" + "v" * len(earlier) + "hhhh", "mmmmmmmmvv", 2**32,
        )
        earlier = (carried, every_rate)
        locals_.append(found)
    if near:
        other = swapped(carried, "ctx", 1)
        sent = call(
            pair_kernel, "pair", (packed,) * (chips - 1),
            [vmem(carry)], 8, (place, carried, other, every_rate), "svvv",
        )
        got = [swapped_chips(part, k) for k, part in enumerate(sent, 1)]
        (incoming,) = call(
            chain_kernel, "chain", ((2, *row_rates),), [vmem((chips, *carry[1:]))],
            8, (place, other, every_rate, *got), "svv" + "v" * len(got),
        )
    else:
        gathered = lax.all_gather(carried, "ctx")
        (incoming,) = call(
            long_chain_kernel, "chain", ((2, *row_rates),), [],
            48, (place, gathered, every_rate), "svv",
        )
    earlier, grad_terms, grad_acts, grad_pres = (), [], [], []
    for side in range(2):
        _, step, step_pre, entering, decays, spread_bases, rates, skip_rows = locals_[side]
        partial_grad, grad_act, grad_pre, summed = call(
            functools.partial(scan_kernel, side), ("first_scan", "second_scan")[side],
            (narrow, one, one, one),
            [
                vmem(step_weight.shape[1:]), row_scratch, grouped, bases, bases,
                vmem((LANES, width)), dma(1),
            ],
            10,
            (
                incoming, spread_bases, acts[side], step, step_pre, grad_gated, entering, decays,
                spreader, rates, skip_rows, *earlier, step_weight,
            ),
            "vmmmmmmmmmm" + "m" * side + "h", "vmmm", 2**33,
        )
        if side == 1:
            first_total, partial_grad = call(
                handover_kernel, "handover", (narrow, narrow), [], 4,
                (partial_grad, *grad_terms[0]), "vvvvv",
            )
        grad_terms.append(terms_of(partial_grad))
        earlier = (summed,)
        grad_acts.append(grad_act)
        grad_pres.append(grad_pre)
    arrived = grad_terms[1][1]
    (step_part,) = call(
        step_kernel, "step_grad", ((2, tiles, ranks, LANES),), [],
        8, (*grad_pres, locals_[0][0], locals_[1][0], arrived), "mmmmv", flops=0,
    )
    weight_scratch = [vmem(narrow), vmem(narrow), vmem(narrow)]
    part, first_grad = call(
        weight_kernel, "first_weights", ((width, LANES), flat), weight_scratch,
        8, (first_total, first_act, first_pre, grad_acts[0], select, arrived),
        "vmmmmv", "mm", 0,
    )
    block_out, gate_grad = call(
        gate_kernel, "gate", (flat, flat), [vmem(one[1:])],
        6, (summed, gate, cot, arrived), "mmmv", flops=0,
    )
    half = width + tiles * ranks
    keep, send, second_grad, *edges = call(
        second_weight_kernel, "weights",
        ((half, LANES), (half, LANES), flat, (HALO, width), (HALO, width)),
        [*weight_scratch, vmem((width, LANES))],
        10,
        (
            place, *grad_terms[1], act, pre, grad_acts[1], select, block_out, part, step_part,
            first_grad,
        ),
        "svvvvmmmmhmvm", "vvmvv",
    )
    edges = swapped_edges(*edges, "ctx")
    if near:
        shares = halved(place, keep, send, half, chips, "halves")
        rows = half // chips
        (mine,) = call(
            add_kernel, "share_sum", ((rows, LANES),), [], 4, shares, "v" * chips
        )
        ahead = mine
    else:
        ahead = edges[0]
    (tokens_grad,) = call(
        exit_kernel, "exit", (flat,),
        [
            vmem((length + HALO, width)), vmem((length + HALO, width)), vmem(conv_weight.shape),
            dma(1),
        ],
        8, (place, *edges, first_grad, second_grad, conv_weight, ahead), "svvmmhv",
    )
    if near:
        got = [swapped_chips(mine, k) for k in range(1, chips)]
        (joined,) = call(
            join_kernel, "joined", ((chips, rows, LANES),), [],
            8, (place, tokens_grad, mine, *got), "sh" + "v" * chips,
        )
        select_grad, step_grad = call(
            outputs_kernel, "weight_grads", ((2, width, LANES), (2, ranks, width)),
            [vmem((2, half, LANES))],
            12, (place, joined, swapped(joined, "ctx", 1)), "svv",
        )
    else:
        first = lax.rem(place[0], 2) == 0
        both = jnp.where(first, jnp.stack([keep, send]), jnp.stack([send, keep]))
        both = lax.psum(both, "ctx")
        select_grad = both[:, :width]
        step_grad = both[:, width:].reshape(2, tiles, ranks, LANES)
        step_grad = step_grad.transpose(0, 2, 1, 3).reshape(2, ranks, width)
    return (block_out, tokens_grad, gate_grad, select_grad, step_grad)


def solution(mesh):
    return jax.shard_map(
        on_device,
        mesh=mesh,
        in_specs=(
            P("ctx", "ch"),
            P("ctx", "ch"),
            P("ctx", "ch"),
            P(None, None, "ch"),
            P(None, "ch"),
            P(None, "ch", None),
            P(None, None, "ch"),
            P(None, "ch"),
            P(None, None, "ch"),
            P(None, "ch"),
        ),
        out_specs=(
            P("ctx", "ch"),
            P("ctx", "ch"),
            P("ctx", "ch"),
            P(None, "ch", None),
            P(None, None, "ch"),
        ),
        check_vma=False,
    )
```

```python
import functools

import jax
import jax.numpy as jnp
from jax import lax
from jax.experimental import pallas as pl
from jax.experimental.pallas import tpu as pltpu
from jax.sharding import PartitionSpec as P

FULL_PRECISION = lax.Precision.HIGHEST
LANES = 128
CHAINS = 8
HALO = 8
LOG2E = 1.4426950408889634
LN2 = 0.6931471805599453
MIB = 1024 * 1024


def params(mib):
    return pltpu.CompilerParams(vmem_limit_bytes=mib * MIB)


def shape_of(*dims):
    return jax.ShapeDtypeStruct(dims, jnp.float32)


def dot(a, b, contract):
    return lax.dot_general(
        a, b, ((contract[:1], contract[1:]), ((), ())), precision=FULL_PRECISION,
        preferred_element_type=jnp.float32,
    )


def silu_grad(values):
    sigmoid_values = jax.nn.sigmoid(values)
    return sigmoid_values * (1.0 + values * (1.0 - sigmoid_values))


def lane_tile(t):
    return slice(t * LANES, (t + 1) * LANES)


def full_width(ref, *lead):
    tiles = ref.shape[len(lead)]
    return jnp.concatenate([ref[(*lead, t)] for t in range(tiles)], axis=1)


def convolved(ext, at_row, side, lanes, rows, conv_weight, conv_bias):
    taps = conv_weight.shape[1]
    margin = taps - 1
    conv = jnp.broadcast_to(conv_bias[side : side + 1, lanes], (rows, LANES))
    for k in range(taps):
        at = at_row + (k - margin if side == 0 else margin - k)
        conv = conv + conv_weight[side, k : k + 1, lanes] * ext[at : at + rows, lanes]
    return conv


def copies_of(pairs, sems):
    copies = [pltpu.make_async_copy(a, b, sems.at[i]) for i, (a, b) in enumerate(pairs)]
    for copy in copies:
        copy.start()
    return copies


def to_cells(tokens, cells):
    count = tokens.shape[0] // CHAINS
    for j in range(count):
        cells[j * CHAINS : (j + 1) * CHAINS] = tokens[pl.ds(j, CHAINS, stride=count), :]


def to_tokens(cells, tokens):
    count = tokens.shape[0] // CHAINS
    for j in range(count):
        tokens[pl.ds(j, CHAINS, stride=count), :] = cells[j * CHAINS : (j + 1) * CHAINS]


def finish_all(copies):
    for copy in copies:
        copy.wait()


def fetch_kernel(*refs):
    count = (len(refs) - 1) // 2
    finish_all(copies_of(list(zip(refs[:count], refs[count : 2 * count])), refs[-1]))


def entry_kernel(
    place, near, far, tokens, conv_weight, conv_bias, select,
    partial, act, pre, ext, plain,
):
    length, width = tokens.shape
    core = lax.rem(place[0], 2)
    ext[:HALO] = jnp.where(core == 0, far[...], near[...])
    ext[HALO : HALO + length] = tokens[...]
    ext[HALO + length :] = jnp.where(core == 0, near[...], far[...])
    enter(0, ext, conv_weight, conv_bias, select, partial, act, pre, plain)


def second_entry_kernel(
    ext, conv_weight, conv_bias, select, gate, cot,
    partial, act, pre, grad_gated, spreader, plain,
):
    fill_spreader(spreader)
    enter(1, ext, conv_weight, conv_bias, select, partial, act, pre, plain)
    for t in range(grad_gated.shape[0]):
        lanes = lane_tile(t)
        values = gate[:, lanes]
        plain[...] = cot[:, lanes] * values * jax.nn.sigmoid(values)
        to_cells(plain, grad_gated.at[t])


def enter(side, ext, conv_weight, conv_bias, select, partial, act, pre, plain):
    tiles, length, _ = act.shape
    for t in range(tiles):
        conv = convolved(ext, HALO, side, lane_tile(t), length, conv_weight, conv_bias)
        pre[t] = conv
        plain[...] = conv * jax.nn.sigmoid(conv)
        to_cells(plain, act.at[t])
    partial[...] = dot(full_width(act), select[side], (1, 0))


def turned(k, by, count):
    return lax.rem(k - 1 + by, count - 1) + 1


def fill_spreader(spreader):
    rows, columns = spreader.shape
    bases = columns // LANES
    row = lax.broadcasted_iota(jnp.int32, (rows, LANES), 0)
    kind = jnp.where(row >= rows - 3 * bases, lax.rem(row + bases - rows % bases, bases), -1)
    for n in range(bases):
        spreader[:, lane_tile(n)] = jnp.where(kind == n, 1.0, 0.0).astype(jnp.bfloat16)


def fill_bases(projection, spreader, bases):
    states = bases.shape[2] // LANES
    first = LANES - 2 * states
    lane = lax.broadcasted_iota(jnp.int32, projection.shape, 1)
    rest = jnp.where(lane >= first, projection[...], 0.0)
    joined = jnp.zeros_like(rest)
    for k in range(3):
        part = rest.astype(jnp.bfloat16).astype(jnp.float32)
        rest = rest - part
        joined = joined + (pltpu.roll(part, LANES - 2 * states * k, 1) if k else part)
    joined = joined.astype(jnp.bfloat16)
    width = 4 * LANES
    for at in range(0, 2 * states * LANES, width):
        value = jnp.dot(
            joined, spreader[:, at : at + width], preferred_element_type=jnp.float32
        )
        kind, lanes = at // (states * LANES), at % (states * LANES)
        bases[kind, :, lanes : lanes + width] = value


def fill_rates(decay_log, rates):
    for t in range(rates.shape[0]):
        rates[t] = -LOG2E * jnp.exp(decay_log[:, lane_tile(t)])


def sublane():
    return lax.broadcasted_iota(jnp.int32, (CHAINS, LANES), 0)


def shifted(value, by, up):
    rolled = pltpu.roll(value, by if up else CHAINS - by, 0)
    place = sublane()
    keep = place >= by if up else place < CHAINS - by
    return jnp.where(keep, rolled, 0.0)


def over_chains(decays, ends, up):
    by = 1
    while by < CHAINS:
        ends = [d * shifted(f, by, up) + f for d, f in zip(decays, ends)]
        if 2 * by < CHAINS:
            turn = by if up else CHAINS - by
            decays = [d * pltpu.roll(d, turn, 0) for d in decays]
        by *= 2
    return ends


def order(i, count, up):
    return i if up else count - 1 - i


def tile_group(tiles):
    return 2 if tiles % 2 == 0 else 1


def unrolled(count, times, body, start):
    times = times if count % times == 0 else 1

    def several(i, state):
        for k in range(times):
            state = body(i * times + k, state)
        return state

    return lax.fori_loop(0, count // times, several, start)


def plus(total, term):
    return term if total is None else total + term


def fill_rate_rows(rates, tiles, rate_rows):
    for g, t in enumerate(tiles):
        for n in range(rate_rows.shape[1]):
            rate_rows[g, n] = jnp.broadcast_to(rates[t, n : n + 1], (CHAINS, LANES))


def cell_rows(j):
    return pl.ds(pl.multiple_of(j * CHAINS, CHAINS), CHAINS)


def local_kernel(side, *refs):
    own, first, second, third, act, grad_gated, spreader = refs[:7]
    earlier, refs = refs[7 : 7 + 2 * side], refs[7 + 2 * side :]
    step_weight, decay_log, step_bias, skip_gain, *refs = refs
    projection, step, step_pre, entering, decays, bases, rates, skip_rows, *refs = refs
    carry, row_rates, rate_rows = refs
    tiles, length, _ = act.shape
    states = decay_log.shape[1]
    ranks = step_weight.shape[1]
    count = length // CHAINS
    group = tile_group(tiles)
    projection[...] = (own[...] + first[...]) + (second[...] + third[...])
    fill_bases(projection, spreader, bases)
    fill_rates(decay_log.at[side], rates)
    for t in range(tiles):
        skip_rows[t] = skip_gain[side : side + 1, lane_tile(t)]
    wide = dot(projection[:, :ranks], step_weight[side], (1, 0)) + step_bias[side : side + 1]
    for t in range(tiles):
        part = wide[:, lane_tile(t)]
        step_pre[t] = part
        step[t] = jnp.maximum(part, 0.0) + jnp.log1p(jnp.exp(-jnp.abs(part)))
    zero = jnp.zeros((CHAINS, LANES), jnp.float32)
    if side:
        carry[...] = earlier[0][...]
        row_rates[...] = earlier[1][...]
    else:
        carry[...] = jnp.zeros_like(carry)
        row_rates[...] = jnp.zeros_like(row_rates)
    up = side == 0
    basis_b, basis_c = bases.at[0], bases.at[1]

    def some_tiles(first, keep):
        at_tiles = [first * group + g for g in range(group)]
        fill_rate_rows(rates, at_tiles, rate_rows)

        def forward(i, current):
            state, summed = current
            j = order(i, count, up)
            at = cell_rows(j)
            steps = [step[t, at, :] for t in at_tiles]
            drives = [v * act[t, at, :] for v, t in zip(steps, at_tiles)]
            new = []
            for n in range(states):
                lanes = lane_tile(n)
                b = basis_b[at, lanes]
                for g in range(group):
                    decay = jnp.exp2(steps[g] * rate_rows[g, n])
                    decays[at_tiles[g], at, lanes] = decay
                    new.append(decay * state[n * group + g] + b * drives[g])
            return (tuple(new), tuple(a + v for a, v in zip(summed, steps)))

        start = ((zero,) * (states * group), (zero,) * group)
        state, summed = unrolled(count, 4, forward, start)

        def retreat(i, state):
            j = order(i, count, not up)
            at = cell_rows(j)
            grads = [grad_gated[t, at, :] for t in at_tiles]
            new = []
            for n in range(states):
                lanes = lane_tile(n)
                c = basis_c[at, lanes]
                for g in range(group):
                    adjoint = state[n * group + g] + c * grads[g]
                    new.append(decays[at_tiles[g], at, lanes] * adjoint)
            return tuple(new)

        sent = unrolled(count, 4, retreat, (zero,) * (states * group))
        for g, t in enumerate(at_tiles):
            across = [jnp.exp2(summed[g] * rate_rows[g, n]) for n in range(states)]
            for kind, ends, upward in ((0, state, up), (1, sent, not up)):
                ends = over_chains(across, list(ends[g::group]), upward)
                last = CHAINS - 1 if upward else 0
                for n in range(states):
                    entering[kind, t, n] = shifted(ends[n], 1, upward)
                    at = side * states + n
                    carry[0 if upward else 1, t, at : at + 1] = ends[n][last : last + 1]
            whole = jnp.sum(summed[g], axis=0, keepdims=True)
            at = 2 * states + side
            for k in range(2):
                carry[k, t, at : at + 1] = whole
        return keep

    lax.fori_loop(0, tiles // group, some_tiles, 0)
    row_rates[:, side * states : (side + 1) * states] = rates[...]


def tile_decay(part, rates):
    rows = rates.shape[1]
    row = lax.broadcasted_iota(jnp.int32, rates.shape, 1)
    sums = jnp.where(row < rows // 2, part[:, rows : rows + 1], part[:, rows + 1 : rows + 2])
    return jnp.exp2(rates * sums)


def pair_kernel(place, mine, other, rates, *refs):
    outs, total = refs[:-1], refs[-1]
    rows = rates.shape[1]
    core, chip = lax.rem(place[0], 2), lax.div(place[0], 2)
    low = jnp.where(core == 0, mine[...], other[...])
    high = jnp.where(core == 0, other[...], mine[...])
    spread_rates = rates[...]
    decay_low = tile_decay(low[0], spread_rates)
    decay_high = tile_decay(high[0], spread_rates)
    total[...] = low + high
    total[0, :, :rows] = decay_high * low[0][:, :rows] + high[0][:, :rows]
    total[1, :, :rows] = decay_low * high[1][:, :rows] + low[1][:, :rows]
    tiles = rates.shape[0]
    for k, out in enumerate(outs, 1):
        to = chip ^ turned(k, core, len(outs) + 1)
        below = lax.convert_element_type(to < chip, jnp.int32)
        for t in range(tiles):
            out[t * rows : (t + 1) * rows] = total[below, t, :rows]
            for side in range(2):
                at = tiles * rows + side * tiles + t
                out[at : at + 1] = total[0, t, rows + side : rows + side + 1]


def chain_kernel(place, other, rates, *refs):
    gathered, (out, parts) = refs[:-2], refs[-2:]
    rows = rates.shape[1]
    chips = parts.shape[0]
    core, chip = lax.rem(place[0], 2), lax.div(place[0], 2)
    parts[chip] = jnp.zeros(parts.shape[1:], jnp.float32)
    tiles = rates.shape[0]
    for k, part in enumerate(gathered, 1):
        source = chip ^ turned(k, core, chips)
        for t in range(tiles):
            parts[source, t, :rows] = part[t * rows : (t + 1) * rows]
            for side in range(2):
                at = tiles * rows + side * tiles + t
                parts[source, t, rows + side : rows + side + 1] = part[at : at + 1]
    spread_rates = rates[...]
    for kind in range(2):
        state = jnp.zeros(rates.shape, jnp.float32)
        for k in range(chips) if kind == 0 else reversed(range(chips)):
            part = parts[k]
            new = tile_decay(part, spread_rates) * state + part[:, :rows]
            state = jnp.where(k < chip if kind == 0 else k > chip, new, state)
        part = other[kind]
        new = tile_decay(part, spread_rates) * state + part[:, :rows]
        out[kind] = jnp.where(core == 1 - kind, new, state)


def long_chain_kernel(place, gathered, rates, out):
    rows = rates.shape[1]
    shards = gathered.shape[0]
    for kind in range(2):

        def turn(i, state):
            part = gathered[order(i, shards, kind == 0), kind]
            return tile_decay(part, rates[...]) * state + part[:, :rows]

        turns = place[0] if kind == 0 else shards - 1 - place[0]
        out[kind] = lax.fori_loop(0, turns, turn, jnp.zeros(rates.shape, jnp.float32))


def scan_kernel(side, *refs):
    incoming, bases, act, step, step_pre, grad_gated, entering, decays, spreader, *refs = refs
    rates, skip_rows, *refs = refs
    earlier, refs = refs[:side], refs[side:]
    step_weight, *refs = refs
    partial, grad_act, grad_pre, summed_out, *refs = refs
    rate_rows, history, grad_in, grad_out, weights = refs
    tiles, length, _ = act.shape
    states = rates.shape[1]
    ranks = step_weight.shape[1]
    count = length // CHAINS
    group = tile_group(tiles)
    grad_in[...] = jnp.zeros_like(grad_in)
    grad_out[...] = jnp.zeros_like(grad_out)
    up = side == 0
    basis_b, basis_c = bases.at[0], bases.at[1]

    def some_tiles(first, keep):
        at_tiles = [first * group + g for g in range(group)]
        fill_rate_rows(rates, at_tiles, rate_rows)
        skips = [skip_rows[t] for t in at_tiles]
        sums = []
        for t in at_tiles:
            summed = step[t, cell_rows(0), :]
            for j in range(1, count):
                summed = summed + step[t, cell_rows(j), :]
            sums.append(summed)

        def start(kind, upward):
            spans = []
            for g in range(group):
                span = shifted(sums[g], 1, upward)
                by = 1
                while by < CHAINS:
                    span = span + shifted(span, by, upward)
                    by *= 2
                spans.append(span)
            first = []
            for n in range(states):
                at = side * states + n
                for g, t in enumerate(at_tiles):
                    decay = jnp.exp2(spans[g] * rate_rows[g, n])
                    value = incoming[0 if upward else 1, t, at : at + 1, :]
                    first.append(entering[kind, t, n] + decay * value)
            return tuple(first)

        def forward(i, state):
            j = order(i, count, up)
            at = cell_rows(j)
            acts = [act[t, at, :] for t in at_tiles]
            grads = [grad_gated[t, at, :] for t in at_tiles]
            drives = [step[t, at, :] * a for t, a in zip(at_tiles, acts)]
            outs = [[v * a, None] for v, a in zip(skips, acts)]
            new = []
            for n in range(states):
                lanes = lane_tile(n)
                b, c = basis_b[at, lanes], basis_c[at, lanes]
                read = grad_out[at, lanes]
                for g in range(group):
                    before = state[n * group + g]
                    decay = decays[at_tiles[g], at, lanes]
                    history[g, at, lanes] = before
                    current = decay * before + b * drives[g]
                    outs[g][n % 2] = plus(outs[g][n % 2], c * current)
                    read = read + current * grads[g]
                    new.append(current)
                grad_out[at, lanes] = read
            for g, t in enumerate(at_tiles):
                out = outs[g][0] + outs[g][1]
                if side == 0:
                    summed_out[t, at, :] = out
                else:
                    summed_out[t, at, :] = earlier[0][t, at, :] + out
            return tuple(new)

        unrolled(count, 4, forward, start(0, up))

        def retreat(i, state):
            j = order(i, count, not up)
            at = cell_rows(j)
            steps = [step[t, at, :] for t in at_tiles]
            acts = [act[t, at, :] for t in at_tiles]
            grads = [grad_gated[t, at, :] for t in at_tiles]
            drives = [v * a for v, a in zip(steps, acts)]
            step_terms = [[None, None] for _ in range(group)]
            drive_grads = [[None, None] for _ in range(group)]
            new = []
            for n in range(states):
                lanes = lane_tile(n)
                b, c = basis_b[at, lanes], basis_c[at, lanes]
                put = grad_in[at, lanes]
                for g in range(group):
                    adjoint = state[n * group + g] + c * grads[g]
                    carried = decays[at_tiles[g], at, lanes] * adjoint
                    new.append(carried)
                    term = carried * history[g, at, lanes] * rate_rows[g, n]
                    step_terms[g][n % 2] = plus(step_terms[g][n % 2], term)
                    drive_grads[g][n % 2] = plus(drive_grads[g][n % 2], adjoint * b)
                    put = put + adjoint * drives[g]
                grad_in[at, lanes] = put
            for g, t in enumerate(at_tiles):
                drive_grad = drive_grads[g][0] + drive_grads[g][1]
                step_term = step_terms[g][0] + step_terms[g][1]
                grad_step = step_term * LN2 + drive_grad * acts[g]
                grad_act[t, at, :] = grads[g] * skips[g] + drive_grad * steps[g]
                pre = step_pre[t, at, :]
                grad_pre[t, at, :] = grad_step * jax.nn.sigmoid(pre)
            return tuple(new)

        unrolled(count, 4, retreat, start(1, not up))
        return keep

    lax.fori_loop(0, tiles // group, some_tiles, 0)
    wide = full_width(grad_pre)
    weights[...] = jnp.zeros_like(weights)
    weights[:ranks] = step_weight[side]
    sums = jnp.zeros((length, LANES), jnp.float32)
    step_lanes = 4 * LANES
    for k, values in enumerate((grad_in, grad_out)):
        for at in range(0, states * LANES, step_lanes):
            rest = values[:, at : at + step_lanes]
            from_lane = k * states * LANES + at
            pick = spreader[:, from_lane : from_lane + step_lanes]
            for _ in range(2):
                piece = rest.astype(jnp.bfloat16)
                rest = rest - piece.astype(jnp.float32)
                sums = sums + lax.dot_general(
                    piece, pick, (((1,), (1,)), ((), ())), preferred_element_type=jnp.float32
                )
    lane = lax.broadcasted_iota(jnp.int32, (length, LANES), 1)
    partial[...] = dot(wide, weights[...], (1, 1)) + jnp.where(lane >= ranks, sums, 0.0)


def step_kernel(first_pre, second_pre, first, second, after_this, step_part):
    _, tiles, ranks, _ = step_part.shape
    for side, (grad_pre, projection) in enumerate(((first_pre, first), (second_pre, second))):
        wide = dot(projection[...], full_width(grad_pre), (0, 0))
        for t in range(tiles):
            step_part[side, t] = wide[:ranks, lane_tile(t)]


def gate_kernel(
    summed, gate, cot, after_this, block_out, gate_grad, plain
):
    for t in range(summed.shape[0]):
        lanes = lane_tile(t)
        values = gate[:, lanes]
        to_tokens(summed.at[t], plain)
        both = plain[...]
        block_out[:, lanes] = both * values * jax.nn.sigmoid(values)
        gate_grad[:, lanes] = cot[:, lanes] * both * silu_grad(values)


def weight_kernel(
    total, act, pre, grad_act, select, after_this, part, conv_grad, grad, plain, cells,
):
    weigh(
        0, (total,), act, pre, grad_act, select, conv_grad, grad, plain, cells, part,
    )


def second_weight_kernel(
    place, own, first, second, third, act, pre, grad_act, select, after_this,
    part, step_part, other_grad,
    keep, send, conv_grad, near, far, grad, plain, cells, mine,
):
    length, width = conv_grad.shape
    weigh(
        1, (own, first, second, third), act, pre, grad_act, select,
        conv_grad, grad, plain, cells, mine,
    )
    core = lax.rem(place[0], 2)
    for side, value in enumerate((part, mine)):
        for out, whose in ((keep, side), (send, 1 - side)):

            @pl.when(core == whose)
            def _():
                out[:width] = value[...]
                out[width:] = step_part[side].reshape(-1, LANES)
    head, tail = other_grad[:HALO], conv_grad[length - HALO :]
    near[...] = jnp.where(core == 0, tail, head)
    far[...] = jnp.where(core == 0, head, tail)


def weigh(side, terms, act, pre, grad_act, select, conv_grad, grad, plain, cells, part):
    total = terms[0][...]
    for term in terms[1:]:
        total = total + term[...]
    grad[...] = total
    part[...] = dot(full_width(act), grad[...], (0, 0))
    wide = dot(grad[...], select[side], (1, 1))
    for t in range(act.shape[0]):
        lanes = lane_tile(t)
        cells[...] = grad_act[t] + wide[:, lanes]
        to_tokens(cells, plain)
        conv_grad[:, lanes] = plain[...] * silu_grad(pre[t])


def halves_kernel(place, keep, got, mine, *refs):
    outs, (total,) = refs[:-1], refs[-1:]
    share = mine.shape[0]
    chips = len(outs) + 1
    for k in range(chips):
        at = slice(k * share, (k + 1) * share)
        total[k] = keep[at] + got[at]
    core, chip = lax.rem(place[0], 2), lax.div(place[0], 2)
    mine[...] = total[chip]
    for k, out in enumerate(outs, 1):
        out[...] = total[chip ^ turned(k, core, chips)]


def handover_kernel(value, *refs):
    terms, (total, out) = refs[:-2], refs[-2:]
    add_kernel(*terms, total)
    out[...] = value[...]


def add_kernel(*refs):
    total = refs[0][...]
    for ref in refs[1:-1]:
        total = total + ref[...]
    refs[-1][...] = total


def join_kernel(place, after_this, mine, *refs):
    parts, out = refs[:-1], refs[-1]
    core, chip = lax.rem(place[0], 2), lax.div(place[0], 2)
    out[chip] = mine[...]
    for k, part in enumerate(parts, 1):
        out[chip ^ turned(k, core, len(parts) + 1)] = part[...]


def outputs_kernel(place, mine, other, select_grad, step_grad, both):
    sides, width, _ = select_grad.shape
    ranks = step_grad.shape[1]
    chips = mine.shape[0]
    core = lax.rem(place[0], 2)
    size = mine.shape[1]
    for side in range(2):
        for k in range(chips):
            both[side, k * size : (k + 1) * size] = jnp.where(core == side, mine[k], other[k])
        select_grad[side] = both[side, :width]
        for t in range(width // LANES):
            at = width + t * ranks
            step_grad[side, :, lane_tile(t)] = both[side, at : at + ranks]


def exit_kernel(
    place, near, far, first, second, conv_weight, after_this, tokens_grad, up, down
):
    length, width = first.shape
    taps = conv_weight.shape[1]
    margin = taps - 1
    core = lax.rem(place[0], 2)
    up[:length] = first[...]
    up[length:] = jnp.where(core == 0, near[...], far[...])
    down[:HALO] = jnp.where(core == 0, far[...], near[...])
    down[HALO:] = second[...]
    for t in range(width // LANES):
        lanes = lane_tile(t)
        total = jnp.zeros((length, LANES), jnp.float32)
        for k in range(taps):
            at = margin - k
            total = total + conv_weight[0, k : k + 1, lanes] * up[at : at + length, lanes]
            at = HALO - margin + k
            total = total + conv_weight[1, k : k + 1, lanes] * down[at : at + length, lanes]
        tokens_grad[:, lanes] = total


def swapped_edges(near, far, axis):
    count = lax.axis_size(axis)
    pairs = [(i, i + 1) for i in range(1, count - 1, 2)]
    pairs = pairs + [(j, i) for i, j in pairs]
    return swapped(near, axis, 1), lax.ppermute(far, axis, pairs)


def swapped(value, axis, by):
    count = lax.axis_size(axis)
    return lax.ppermute(value, axis, [(i, i ^ by) for i in range(count)])


def swapped_chips(value, k):
    places = lax.axis_size("ctx")
    chips = places // 2
    pairs = [(i, i ^ (2 * ((k - 1 + i % 2) % (chips - 1) + 1))) for i in range(places)]
    return lax.ppermute(value, "ctx", pairs)


def call(kernel, name, out_shape, scratch, mib, args, kinds, outs=None, flops=2**28):
    spaces = {
        "v": pl.BlockSpec(memory_space=pltpu.VMEM),
        "m": pl.BlockSpec(memory_space=pltpu.VMEM),
        "b": pl.BlockSpec(memory_space=pltpu.VMEM),
        "h": pl.BlockSpec(memory_space=pltpu.HBM),
        "s": pl.BlockSpec(memory_space=pltpu.SMEM),
    }
    outs = outs or "v" * len(out_shape)
    pinned = {"m": pltpu.VMEM, "h": pltpu.HBM}
    args = [
        pltpu.with_memory_space_constraint(a, pinned[k]) if k in pinned else a
        for a, k in zip(args, kinds, strict=True)
    ]
    results = [
        pinned[k](shape, jnp.float32) if k in pinned else shape_of(*shape)
        for shape, k in zip(out_shape, outs, strict=True)
        if k != "b"
    ]
    at = outs.find("b")
    if at >= 0:
        results.insert(at, pltpu.VMEM(out_shape[at], jnp.bfloat16))
    return pl.pallas_call(
        kernel,
        in_specs=[spaces[k] for k in kinds],
        out_specs=[spaces[k] for k in outs],
        out_shape=results,
        scratch_shapes=scratch,
        compiler_params=params(mib),
        cost_estimate=pl.CostEstimate(flops=flops, bytes_accessed=flops // 64, transcendentals=0),
        name=name,
    )(*args)


def terms_of(partial):
    count = lax.axis_size("ch")
    if count != 4:
        zero = jnp.zeros_like(partial)
        return (lax.psum(partial, "ch"), zero, zero, zero)
    return (partial, *(swapped(partial, "ch", k) for k in range(1, count)))


def halved(place, keep, send, rows, chips, name):
    got = swapped(send, "ctx", 1)
    share = rows // chips
    mine, *sent = call(
        halves_kernel, name, ((share, LANES),) * chips, [pltpu.VMEM((chips, share, LANES), jnp.float32)],
        8, (place, keep, got), "svv",
    )
    return (mine, *(swapped_chips(part, k) for k, part in enumerate(sent, 1)))


def on_device(
    tokens, gate_input, cotangent, conv_weight, conv_bias, select_weight, step_weight,
    step_bias, decay_log, skip_gain,
):
    length, width = tokens.shape
    tiles = width // LANES
    states = decay_log.shape[1]
    ranks = step_weight.shape[1]
    places = lax.axis_size("ctx")
    place = lax.axis_index("ctx").astype(jnp.int32).reshape(1)
    group = tile_group(tiles)
    chips = places // 2
    near = places == 8
    narrow = (length, LANES)
    one = (tiles, length, LANES)
    flat = (length, width)
    chain_ends = (2, tiles, states, CHAINS, LANES)
    carry = (2, tiles, 2 * states + 8, LANES)
    row_rates = (tiles, 2 * states, LANES)
    packed = (tiles * 2 * states + -(-2 * tiles // 8) * 8, LANES)
    vmem = functools.partial(pltpu.VMEM, dtype=jnp.float32)
    dma = lambda n: pltpu.SemaphoreType.DMA((n,))
    bases = vmem((length, states * LANES))
    grouped = vmem((group, length, states * LANES))
    row_scratch = vmem((group, states, CHAINS, LANES))

    core = (place & 1)[:, None] == 0
    head, tail = tokens[:HALO], tokens[length - HALO :]
    edges = swapped_edges(jnp.where(core, tail, head), jnp.where(core, head, tail), "ctx")
    fetched = (
        tokens, select_weight, conv_weight, conv_bias, gate_input, cotangent, step_weight,
        decay_log, step_bias, skip_gain,
    )
    held, select, taps, taps_bias, gate, cot, *step_held = call(
        fetch_kernel, "fetch", tuple(a.shape for a in fetched), [dma(len(fetched))], 4, fetched,
        "h" * len(fetched), "m" * len(fetched),
    )
    first_partial, first_act, first_pre, extended = call(
        entry_kernel, "entry", (narrow, one, one, (length + 2 * HALO, width)), [vmem(narrow)],
        6, (place, *edges, held, taps, taps_bias, select), "svvmmmm", "vmmm",
    )
    first_terms = terms_of(first_partial)
    partial, act, pre, grad_gated, spreader = call(
        second_entry_kernel, "second_entry",
        (narrow, one, one, one, (LANES, 2 * states * LANES)),
        [vmem(narrow)],
        6, (extended, taps, taps_bias, select, gate, cot), "mmmmmm", "vmmmb",
    )
    projection_terms = (first_terms, terms_of(partial))
    acts, pres = (first_act, act), (first_pre, pre)
    earlier, locals_ = (), []
    for side in range(2):
        *found, carried, every_rate = call(
            functools.partial(local_kernel, side), ("first_local", "second_local")[side],
            (
                narrow, one, one, chain_ends, (*one[:-1], states * LANES),
                (2, length, states * LANES), (tiles, states, LANES), (tiles, 1, LANES),
                carry, row_rates,
            ),
            [row_scratch],
            10,
            (
                *projection_terms[side], acts[side], grad_gated, spreader, *earlier, *step_held,
            ),
            "vvvvmmm" + "v" * len(earlier) + "mmmm", "mmmmmmmmvv", 2**32,
        )
        earlier = (carried, every_rate)
        locals_.append(found)
    if near:
        other = swapped(carried, "ctx", 1)
        sent = call(
            pair_kernel, "pair", (packed,) * (chips - 1),
            [vmem(carry)], 8, (place, carried, other, every_rate), "svvv",
        )
        got = [swapped_chips(part, k) for k, part in enumerate(sent, 1)]
        (incoming,) = call(
            chain_kernel, "chain", ((2, *row_rates),), [vmem((chips, *carry[1:]))],
            8, (place, other, every_rate, *got), "svv" + "v" * len(got),
        )
    else:
        gathered = lax.all_gather(carried, "ctx")
        (incoming,) = call(
            long_chain_kernel, "chain", ((2, *row_rates),), [],
            48, (place, gathered, every_rate), "svv",
        )
    earlier, grad_terms, grad_acts, grad_pres = (), [], [], []
    for side in range(2):
        _, step, step_pre, entering, decays, spread_bases, rates, skip_rows = locals_[side]
        partial_grad, grad_act, grad_pre, summed = call(
            functools.partial(scan_kernel, side), ("first_scan", "second_scan")[side],
            (narrow, one, one, one),
            [
                row_scratch, grouped, bases, bases, vmem((LANES, width)),
            ],
            10,
            (
                incoming, spread_bases, acts[side], step, step_pre, grad_gated, entering, decays,
                spreader, rates, skip_rows, *earlier, step_held[0],
            ),
            "vmmmmmmmmmm" + "m" * side + "m", "vmmm", 2**33,
        )
        if side == 1:
            first_total, partial_grad = call(
                handover_kernel, "handover", (narrow, narrow), [], 4,
                (partial_grad, *grad_terms[0]), "vvvvv",
            )
        grad_terms.append(terms_of(partial_grad))
        earlier = (summed,)
        grad_acts.append(grad_act)
        grad_pres.append(grad_pre)
    arrived = grad_terms[1][1]
    (step_part,) = call(
        step_kernel, "step_grad", ((2, tiles, ranks, LANES),), [],
        8, (*grad_pres, locals_[0][0], locals_[1][0], arrived), "mmmmv", flops=0,
    )
    weight_scratch = [vmem(narrow), vmem(narrow), vmem(narrow)]
    part, first_grad = call(
        weight_kernel, "first_weights", ((width, LANES), flat), weight_scratch,
        8, (first_total, first_act, first_pre, grad_acts[0], select, arrived),
        "vmmmmv", "mm", 0,
    )
    block_out, gate_grad = call(
        gate_kernel, "gate", (flat, flat), [vmem(one[1:])],
        6, (summed, gate, cot, arrived), "mmmv", flops=0,
    )
    half = width + tiles * ranks
    keep, send, second_grad, *edges = call(
        second_weight_kernel, "weights",
        ((half, LANES), (half, LANES), flat, (HALO, width), (HALO, width)),
        [*weight_scratch, vmem((width, LANES))],
        10,
        (
            place, *grad_terms[1], act, pre, grad_acts[1], select, block_out, part, step_part,
            first_grad,
        ),
        "svvvvmmmmhmvm", "vvmvv",
    )
    edges = swapped_edges(*edges, "ctx")
    if near:
        shares = halved(place, keep, send, half, chips, "halves")
        rows = half // chips
        (mine,) = call(
            add_kernel, "share_sum", ((rows, LANES),), [], 4, shares, "v" * chips
        )
        ahead = mine
    else:
        ahead = edges[0]
    (tokens_grad,) = call(
        exit_kernel, "exit", (flat,),
        [
            vmem((length + HALO, width)), vmem((length + HALO, width)),
        ],
        6, (place, *edges, first_grad, second_grad, taps, ahead), "svvmmmv",
    )
    if near:
        got = [swapped_chips(mine, k) for k in range(1, chips)]
        (joined,) = call(
            join_kernel, "joined", ((chips, rows, LANES),), [],
            8, (place, tokens_grad, mine, *got), "sh" + "v" * chips,
        )
        select_grad, step_grad = call(
            outputs_kernel, "weight_grads", ((2, width, LANES), (2, ranks, width)),
            [vmem((2, half, LANES))],
            12, (place, joined, swapped(joined, "ctx", 1)), "svv",
        )
    else:
        first = lax.rem(place[0], 2) == 0
        both = jnp.where(first, jnp.stack([keep, send]), jnp.stack([send, keep]))
        both = lax.psum(both, "ctx")
        select_grad = both[:, :width]
        step_grad = both[:, width:].reshape(2, tiles, ranks, LANES)
        step_grad = step_grad.transpose(0, 2, 1, 3).reshape(2, ranks, width)
    return (block_out, tokens_grad, gate_grad, select_grad, step_grad)


def solution(mesh):
    return jax.shard_map(
        on_device,
        mesh=mesh,
        in_specs=(
            P("ctx", "ch"),
            P("ctx", "ch"),
            P("ctx", "ch"),
            P(None, None, "ch"),
            P(None, "ch"),
            P(None, "ch", None),
            P(None, None, "ch"),
            P(None, "ch"),
            P(None, None, "ch"),
            P(None, "ch"),
        ),
        out_specs=(
            P("ctx", "ch"),
            P("ctx", "ch"),
            P("ctx", "ch"),
            P(None, "ch", None),
            P(None, None, "ch"),
        ),
        check_vma=False,
    )
```

```python
import functools

import jax
import jax.numpy as jnp
from jax import lax
from jax.experimental import pallas as pl
from jax.experimental.pallas import tpu as pltpu
from jax.sharding import PartitionSpec as P

FULL_PRECISION = lax.Precision.HIGHEST
LANES = 128
CHAINS = 8
HALO = 8
LOG2E = 1.4426950408889634
LN2 = 0.6931471805599453
MIB = 1024 * 1024


def params(mib):
    return pltpu.CompilerParams(vmem_limit_bytes=mib * MIB)


def shape_of(*dims):
    return jax.ShapeDtypeStruct(dims, jnp.float32)


def dot(a, b, contract):
    return lax.dot_general(
        a, b, ((contract[:1], contract[1:]), ((), ())), precision=FULL_PRECISION,
        preferred_element_type=jnp.float32,
    )


def silu_grad(values):
    sigmoid_values = jax.nn.sigmoid(values)
    return sigmoid_values * (1.0 + values * (1.0 - sigmoid_values))


def lane_tile(t):
    return slice(t * LANES, (t + 1) * LANES)


def full_width(ref, *lead):
    tiles = ref.shape[len(lead)]
    return jnp.concatenate([ref[(*lead, t)] for t in range(tiles)], axis=1)


def convolved(ext, at_row, side, lanes, rows, conv_weight, conv_bias):
    taps = conv_weight.shape[1]
    margin = taps - 1
    conv = jnp.broadcast_to(conv_bias[side : side + 1, lanes], (rows, LANES))
    for k in range(taps):
        at = at_row + (k - margin if side == 0 else margin - k)
        conv = conv + conv_weight[side, k : k + 1, lanes] * ext[at : at + rows, lanes]
    return conv


def copies_of(pairs, sems):
    copies = [pltpu.make_async_copy(a, b, sems.at[i]) for i, (a, b) in enumerate(pairs)]
    for copy in copies:
        copy.start()
    return copies


def to_cells(tokens, cells):
    count = tokens.shape[0] // CHAINS
    for j in range(count):
        cells[j * CHAINS : (j + 1) * CHAINS] = tokens[pl.ds(j, CHAINS, stride=count), :]


def to_tokens(cells, tokens):
    count = tokens.shape[0] // CHAINS
    for j in range(count):
        tokens[pl.ds(j, CHAINS, stride=count), :] = cells[j * CHAINS : (j + 1) * CHAINS]


def finish_all(copies):
    for copy in copies:
        copy.wait()


def fetch_kernel(*refs):
    count = (len(refs) - 1) // 2
    finish_all(copies_of(list(zip(refs[:count], refs[count : 2 * count])), refs[-1]))


def entry_kernel(
    place, near, far, tokens, conv_weight, conv_bias, select,
    partial, act, pre, ext, plain,
):
    length, width = tokens.shape
    core = lax.rem(place[0], 2)
    ext[:HALO] = jnp.where(core == 0, far[...], near[...])
    ext[HALO : HALO + length] = tokens[...]
    ext[HALO + length :] = jnp.where(core == 0, near[...], far[...])
    enter(0, ext, conv_weight, conv_bias, select, partial, act, pre, plain)


def second_entry_kernel(
    ext, conv_weight, conv_bias, select, gate, cot,
    partial, act, pre, grad_gated, spreader, plain,
):
    fill_spreader(spreader)
    enter(1, ext, conv_weight, conv_bias, select, partial, act, pre, plain)
    for t in range(grad_gated.shape[0]):
        lanes = lane_tile(t)
        values = gate[:, lanes]
        plain[...] = cot[:, lanes] * values * jax.nn.sigmoid(values)
        to_cells(plain, grad_gated.at[t])


def enter(side, ext, conv_weight, conv_bias, select, partial, act, pre, plain):
    tiles, length, _ = act.shape
    for t in range(tiles):
        conv = convolved(ext, HALO, side, lane_tile(t), length, conv_weight, conv_bias)
        pre[t] = conv
        plain[...] = conv * jax.nn.sigmoid(conv)
        to_cells(plain, act.at[t])
    partial[...] = dot(full_width(act), select[side], (1, 0))


def turned(k, by, count):
    return lax.rem(k - 1 + by, count - 1) + 1


def fill_spreader(spreader):
    rows, columns = spreader.shape
    bases = columns // LANES
    row = lax.broadcasted_iota(jnp.int32, (rows, LANES), 0)
    kind = jnp.where(row >= rows - 3 * bases, lax.rem(row + bases - rows % bases, bases), -1)
    for n in range(bases):
        spreader[:, lane_tile(n)] = jnp.where(kind == n, 1.0, 0.0).astype(jnp.bfloat16)


def fill_bases(projection, spreader, bases):
    states = bases.shape[2] // LANES
    first = LANES - 2 * states
    lane = lax.broadcasted_iota(jnp.int32, projection.shape, 1)
    rest = jnp.where(lane >= first, projection[...], 0.0)
    joined = jnp.zeros_like(rest)
    for k in range(3):
        part = rest.astype(jnp.bfloat16).astype(jnp.float32)
        rest = rest - part
        joined = joined + (pltpu.roll(part, LANES - 2 * states * k, 1) if k else part)
    joined = joined.astype(jnp.bfloat16)
    width = 4 * LANES
    for at in range(0, 2 * states * LANES, width):
        value = jnp.dot(
            joined, spreader[:, at : at + width], preferred_element_type=jnp.float32
        )
        kind, lanes = at // (states * LANES), at % (states * LANES)
        bases[kind, :, lanes : lanes + width] = value


def fill_rates(decay_log, rates):
    for t in range(rates.shape[0]):
        rates[t] = -LOG2E * jnp.exp(decay_log[:, lane_tile(t)])


def sublane():
    return lax.broadcasted_iota(jnp.int32, (CHAINS, LANES), 0)


def shifted(value, by, up):
    rolled = pltpu.roll(value, by if up else CHAINS - by, 0)
    place = sublane()
    keep = place >= by if up else place < CHAINS - by
    return jnp.where(keep, rolled, 0.0)


def over_chains(decays, ends, up):
    by = 1
    while by < CHAINS:
        ends = [d * shifted(f, by, up) + f for d, f in zip(decays, ends)]
        if 2 * by < CHAINS:
            turn = by if up else CHAINS - by
            decays = [d * pltpu.roll(d, turn, 0) for d in decays]
        by *= 2
    return ends


def order(i, count, up):
    return i if up else count - 1 - i


def tile_group(tiles):
    return 2 if tiles % 2 == 0 else 1


def unrolled(count, times, body, start):
    times = times if count % times == 0 else 1

    def several(i, state):
        for k in range(times):
            state = body(i * times + k, state)
        return state

    return lax.fori_loop(0, count // times, several, start)


def plus(total, term):
    return term if total is None else total + term


def fill_rate_rows(rates, tiles, rate_rows):
    for g, t in enumerate(tiles):
        for n in range(rate_rows.shape[1]):
            rate_rows[g, n] = jnp.broadcast_to(rates[t, n : n + 1], (CHAINS, LANES))


def cell_rows(j):
    return pl.ds(pl.multiple_of(j * CHAINS, CHAINS), CHAINS)


def local_kernel(side, *refs):
    own, first, second, third, act, grad_gated, spreader = refs[:7]
    earlier, refs = refs[7 : 7 + 2 * side], refs[7 + 2 * side :]
    step_weight, decay_log, step_bias, skip_gain, *refs = refs
    projection, step, step_pre, entering, decays, bases, rates, skip_rows, *refs = refs
    carry, row_rates, rate_rows = refs
    tiles, length, _ = act.shape
    states = decay_log.shape[1]
    ranks = step_weight.shape[1]
    count = length // CHAINS
    group = tile_group(tiles)
    projection[...] = (own[...] + first[...]) + (second[...] + third[...])
    fill_bases(projection, spreader, bases)
    fill_rates(decay_log.at[side], rates)
    for t in range(tiles):
        skip_rows[t] = skip_gain[side : side + 1, lane_tile(t)]
    wide = dot(projection[:, :ranks], step_weight[side], (1, 0)) + step_bias[side : side + 1]
    for t in range(tiles):
        part = wide[:, lane_tile(t)]
        step_pre[t] = part
        step[t] = jnp.maximum(part, 0.0) + jnp.log1p(jnp.exp(-jnp.abs(part)))
    zero = jnp.zeros((CHAINS, LANES), jnp.float32)
    if side:
        carry[...] = earlier[0][...]
        row_rates[...] = earlier[1][...]
    else:
        carry[...] = jnp.zeros_like(carry)
        row_rates[...] = jnp.zeros_like(row_rates)
    up = side == 0
    basis_b, basis_c = bases.at[0], bases.at[1]

    def some_tiles(first, keep):
        at_tiles = [first * group + g for g in range(group)]
        fill_rate_rows(rates, at_tiles, rate_rows)

        def forward(i, current):
            state, summed = current
            j = order(i, count, up)
            at = cell_rows(j)
            steps = [step[t, at, :] for t in at_tiles]
            drives = [v * act[t, at, :] for v, t in zip(steps, at_tiles)]
            new = []
            for n in range(states):
                lanes = lane_tile(n)
                b = basis_b[at, lanes]
                for g in range(group):
                    decay = jnp.exp2(steps[g] * rate_rows[g, n])
                    decays[at_tiles[g], at, lanes] = decay
                    new.append(decay * state[n * group + g] + b * drives[g])
            return (tuple(new), tuple(a + v for a, v in zip(summed, steps)))

        start = ((zero,) * (states * group), (zero,) * group)
        state, summed = unrolled(count, 4, forward, start)

        def retreat(i, state):
            j = order(i, count, not up)
            at = cell_rows(j)
            grads = [grad_gated[t, at, :] for t in at_tiles]
            new = []
            for n in range(states):
                lanes = lane_tile(n)
                c = basis_c[at, lanes]
                for g in range(group):
                    adjoint = state[n * group + g] + c * grads[g]
                    new.append(decays[at_tiles[g], at, lanes] * adjoint)
            return tuple(new)

        sent = unrolled(count, 4, retreat, (zero,) * (states * group))
        for g, t in enumerate(at_tiles):
            across = [jnp.exp2(summed[g] * rate_rows[g, n]) for n in range(states)]
            for kind, ends, upward in ((0, state, up), (1, sent, not up)):
                ends = over_chains(across, list(ends[g::group]), upward)
                last = CHAINS - 1 if upward else 0
                for n in range(states):
                    entering[kind, t, n] = shifted(ends[n], 1, upward)
                    at = side * states + n
                    carry[0 if upward else 1, t, at : at + 1] = ends[n][last : last + 1]
            whole = jnp.sum(summed[g], axis=0, keepdims=True)
            at = 2 * states + side
            for k in range(2):
                carry[k, t, at : at + 1] = whole
        return keep

    lax.fori_loop(0, tiles // group, some_tiles, 0)
    row_rates[:, side * states : (side + 1) * states] = rates[...]


def tile_decay(part, rates):
    rows = rates.shape[1]
    row = lax.broadcasted_iota(jnp.int32, rates.shape, 1)
    sums = jnp.where(row < rows // 2, part[:, rows : rows + 1], part[:, rows + 1 : rows + 2])
    return jnp.exp2(rates * sums)


def pair_kernel(place, mine, other, rates, *refs):
    outs, total = refs[:-1], refs[-1]
    rows = rates.shape[1]
    core, chip = lax.rem(place[0], 2), lax.div(place[0], 2)
    low = jnp.where(core == 0, mine[...], other[...])
    high = jnp.where(core == 0, other[...], mine[...])
    spread_rates = rates[...]
    decay_low = tile_decay(low[0], spread_rates)
    decay_high = tile_decay(high[0], spread_rates)
    total[...] = low + high
    total[0, :, :rows] = decay_high * low[0][:, :rows] + high[0][:, :rows]
    total[1, :, :rows] = decay_low * high[1][:, :rows] + low[1][:, :rows]
    tiles = rates.shape[0]
    for k, out in enumerate(outs, 1):
        to = chip ^ turned(k, core, len(outs) + 1)
        below = lax.convert_element_type(to < chip, jnp.int32)
        for t in range(tiles):
            out[t * rows : (t + 1) * rows] = total[below, t, :rows]
            for side in range(2):
                at = tiles * rows + side * tiles + t
                out[at : at + 1] = total[0, t, rows + side : rows + side + 1]


def chain_kernel(place, other, rates, *refs):
    gathered, (out, parts) = refs[:-2], refs[-2:]
    rows = rates.shape[1]
    chips = parts.shape[0]
    core, chip = lax.rem(place[0], 2), lax.div(place[0], 2)
    parts[chip] = jnp.zeros(parts.shape[1:], jnp.float32)
    tiles = rates.shape[0]
    for k, part in enumerate(gathered, 1):
        source = chip ^ turned(k, core, chips)
        for t in range(tiles):
            parts[source, t, :rows] = part[t * rows : (t + 1) * rows]
            for side in range(2):
                at = tiles * rows + side * tiles + t
                parts[source, t, rows + side : rows + side + 1] = part[at : at + 1]
    spread_rates = rates[...]
    for kind in range(2):
        state = jnp.zeros(rates.shape, jnp.float32)
        for k in range(chips) if kind == 0 else reversed(range(chips)):
            part = parts[k]
            new = tile_decay(part, spread_rates) * state + part[:, :rows]
            state = jnp.where(k < chip if kind == 0 else k > chip, new, state)
        part = other[kind]
        new = tile_decay(part, spread_rates) * state + part[:, :rows]
        out[kind] = jnp.where(core == 1 - kind, new, state)


def long_chain_kernel(place, gathered, rates, out):
    rows = rates.shape[1]
    shards = gathered.shape[0]
    for kind in range(2):

        def turn(i, state):
            part = gathered[order(i, shards, kind == 0), kind]
            return tile_decay(part, rates[...]) * state + part[:, :rows]

        turns = place[0] if kind == 0 else shards - 1 - place[0]
        out[kind] = lax.fori_loop(0, turns, turn, jnp.zeros(rates.shape, jnp.float32))


def scan_kernel(side, *refs):
    incoming, bases, act, step, step_pre, grad_gated, entering, decays, spreader, *refs = refs
    rates, skip_rows, *refs = refs
    earlier, refs = refs[:side], refs[side:]
    step_weight_in, *refs = refs
    partial, grad_act, grad_pre, summed_out, *refs = refs
    step_weight, rate_rows, history, grad_in, grad_out, weights, sems = refs
    tiles, length, _ = act.shape
    states = rates.shape[1]
    ranks = step_weight.shape[0]
    count = length // CHAINS
    group = tile_group(tiles)
    loads = copies_of([(step_weight_in.at[side], step_weight)], sems)
    grad_in[...] = jnp.zeros_like(grad_in)
    grad_out[...] = jnp.zeros_like(grad_out)
    up = side == 0
    basis_b, basis_c = bases.at[0], bases.at[1]

    def some_tiles(first, keep):
        at_tiles = [first * group + g for g in range(group)]
        fill_rate_rows(rates, at_tiles, rate_rows)
        skips = [skip_rows[t] for t in at_tiles]
        sums = []
        for t in at_tiles:
            summed = step[t, cell_rows(0), :]
            for j in range(1, count):
                summed = summed + step[t, cell_rows(j), :]
            sums.append(summed)

        def start(kind, upward):
            spans = []
            for g in range(group):
                span = shifted(sums[g], 1, upward)
                by = 1
                while by < CHAINS:
                    span = span + shifted(span, by, upward)
                    by *= 2
                spans.append(span)
            first = []
            for n in range(states):
                at = side * states + n
                for g, t in enumerate(at_tiles):
                    decay = jnp.exp2(spans[g] * rate_rows[g, n])
                    value = incoming[0 if upward else 1, t, at : at + 1, :]
                    first.append(entering[kind, t, n] + decay * value)
            return tuple(first)

        def forward(i, state):
            j = order(i, count, up)
            at = cell_rows(j)
            acts = [act[t, at, :] for t in at_tiles]
            grads = [grad_gated[t, at, :] for t in at_tiles]
            drives = [step[t, at, :] * a for t, a in zip(at_tiles, acts)]
            outs = [[v * a, None] for v, a in zip(skips, acts)]
            new = []
            for n in range(states):
                lanes = lane_tile(n)
                b, c = basis_b[at, lanes], basis_c[at, lanes]
                read = grad_out[at, lanes]
                for g in range(group):
                    before = state[n * group + g]
                    decay = decays[at_tiles[g], at, lanes]
                    history[g, at, lanes] = before
                    current = decay * before + b * drives[g]
                    outs[g][n % 2] = plus(outs[g][n % 2], c * current)
                    read = read + current * grads[g]
                    new.append(current)
                grad_out[at, lanes] = read
            for g, t in enumerate(at_tiles):
                out = outs[g][0] + outs[g][1]
                if side == 0:
                    summed_out[t, at, :] = out
                else:
                    summed_out[t, at, :] = earlier[0][t, at, :] + out
            return tuple(new)

        unrolled(count, 4, forward, start(0, up))

        def retreat(i, state):
            j = order(i, count, not up)
            at = cell_rows(j)
            steps = [step[t, at, :] for t in at_tiles]
            acts = [act[t, at, :] for t in at_tiles]
            grads = [grad_gated[t, at, :] for t in at_tiles]
            drives = [v * a for v, a in zip(steps, acts)]
            step_terms = [[None, None] for _ in range(group)]
            drive_grads = [[None, None] for _ in range(group)]
            new = []
            for n in range(states):
                lanes = lane_tile(n)
                b, c = basis_b[at, lanes], basis_c[at, lanes]
                put = grad_in[at, lanes]
                for g in range(group):
                    adjoint = state[n * group + g] + c * grads[g]
                    carried = decays[at_tiles[g], at, lanes] * adjoint
                    new.append(carried)
                    term = carried * history[g, at, lanes] * rate_rows[g, n]
                    step_terms[g][n % 2] = plus(step_terms[g][n % 2], term)
                    drive_grads[g][n % 2] = plus(drive_grads[g][n % 2], adjoint * b)
                    put = put + adjoint * drives[g]
                grad_in[at, lanes] = put
            for g, t in enumerate(at_tiles):
                drive_grad = drive_grads[g][0] + drive_grads[g][1]
                step_term = step_terms[g][0] + step_terms[g][1]
                grad_step = step_term * LN2 + drive_grad * acts[g]
                grad_act[t, at, :] = grads[g] * skips[g] + drive_grad * steps[g]
                pre = step_pre[t, at, :]
                grad_pre[t, at, :] = grad_step * jax.nn.sigmoid(pre)
            return tuple(new)

        unrolled(count, 4, retreat, start(1, not up))
        return keep

    lax.fori_loop(0, tiles // group, some_tiles, 0)
    wide = full_width(grad_pre)
    weights[...] = jnp.zeros_like(weights)
    finish_all(loads)
    weights[:ranks] = step_weight[...]
    sums = jnp.zeros((length, LANES), jnp.float32)
    step_lanes = 4 * LANES
    for k, values in enumerate((grad_in, grad_out)):
        for at in range(0, states * LANES, step_lanes):
            rest = values[:, at : at + step_lanes]
            from_lane = k * states * LANES + at
            pick = spreader[:, from_lane : from_lane + step_lanes]
            for _ in range(2):
                piece = rest.astype(jnp.bfloat16)
                rest = rest - piece.astype(jnp.float32)
                sums = sums + lax.dot_general(
                    piece, pick, (((1,), (1,)), ((), ())), preferred_element_type=jnp.float32
                )
    lane = lax.broadcasted_iota(jnp.int32, (length, LANES), 1)
    partial[...] = dot(wide, weights[...], (1, 1)) + jnp.where(lane >= ranks, sums, 0.0)


def step_kernel(first_pre, second_pre, first, second, after_this, step_part):
    _, tiles, ranks, _ = step_part.shape
    for side, (grad_pre, projection) in enumerate(((first_pre, first), (second_pre, second))):
        wide = dot(projection[...], full_width(grad_pre), (0, 0))
        for t in range(tiles):
            step_part[side, t] = wide[:ranks, lane_tile(t)]


def gate_kernel(
    summed, gate, cot, after_this, block_out, gate_grad, plain
):
    for t in range(summed.shape[0]):
        lanes = lane_tile(t)
        values = gate[:, lanes]
        to_tokens(summed.at[t], plain)
        both = plain[...]
        block_out[:, lanes] = both * values * jax.nn.sigmoid(values)
        gate_grad[:, lanes] = cot[:, lanes] * both * silu_grad(values)


def weight_kernel(
    total, act, pre, grad_act, select, after_this, part, conv_grad, grad, plain, cells,
):
    weigh(
        0, (total,), act, pre, grad_act, select, conv_grad, grad, plain, cells, part,
    )


def second_weight_kernel(
    place, own, first, second, third, act, pre, grad_act, select, after_this,
    part, step_part, other_grad,
    keep, send, conv_grad, near, far, grad, plain, cells, mine,
):
    length, width = conv_grad.shape
    weigh(
        1, (own, first, second, third), act, pre, grad_act, select,
        conv_grad, grad, plain, cells, mine,
    )
    core = lax.rem(place[0], 2)
    for side, value in enumerate((part, mine)):
        for out, whose in ((keep, side), (send, 1 - side)):

            @pl.when(core == whose)
            def _():
                out[:width] = value[...]
                out[width:] = step_part[side].reshape(-1, LANES)
    head, tail = other_grad[:HALO], conv_grad[length - HALO :]
    near[...] = jnp.where(core == 0, tail, head)
    far[...] = jnp.where(core == 0, head, tail)


def weigh(side, terms, act, pre, grad_act, select, conv_grad, grad, plain, cells, part):
    total = terms[0][...]
    for term in terms[1:]:
        total = total + term[...]
    grad[...] = total
    part[...] = dot(full_width(act), grad[...], (0, 0))
    wide = dot(grad[...], select[side], (1, 1))
    for t in range(act.shape[0]):
        lanes = lane_tile(t)
        cells[...] = grad_act[t] + wide[:, lanes]
        to_tokens(cells, plain)
        conv_grad[:, lanes] = plain[...] * silu_grad(pre[t])


def halves_kernel(place, keep, got, mine, *refs):
    outs, (total,) = refs[:-1], refs[-1:]
    share = mine.shape[0]
    chips = len(outs) + 1
    for k in range(chips):
        at = slice(k * share, (k + 1) * share)
        total[k] = keep[at] + got[at]
    core, chip = lax.rem(place[0], 2), lax.div(place[0], 2)
    mine[...] = total[chip]
    for k, out in enumerate(outs, 1):
        out[...] = total[chip ^ turned(k, core, chips)]


def handover_kernel(value, *refs):
    terms, (total, out) = refs[:-2], refs[-2:]
    add_kernel(*terms, total)
    out[...] = value[...]


def add_after_kernel(near, far, *refs):
    add_kernel(*refs)


def add_kernel(*refs):
    total = refs[0][...]
    for ref in refs[1:-1]:
        total = total + ref[...]
    refs[-1][...] = total


def join_kernel(place, after_this, mine, *refs):
    parts, out = refs[:-1], refs[-1]
    core, chip = lax.rem(place[0], 2), lax.div(place[0], 2)
    out[chip] = mine[...]
    for k, part in enumerate(parts, 1):
        out[chip ^ turned(k, core, len(parts) + 1)] = part[...]


def outputs_kernel(place, mine, other, select_grad, step_grad, both):
    sides, width, _ = select_grad.shape
    ranks = step_grad.shape[1]
    chips = mine.shape[0]
    core = lax.rem(place[0], 2)
    size = mine.shape[1]
    for side in range(2):
        for k in range(chips):
            both[side, k * size : (k + 1) * size] = jnp.where(core == side, mine[k], other[k])
        select_grad[side] = both[side, :width]
        for t in range(width // LANES):
            at = width + t * ranks
            step_grad[side, :, lane_tile(t)] = both[side, at : at + ranks]


def exit_kernel(
    place, near, far, first, second, conv_weight, after_this, tokens_grad, up, down
):
    length, width = first.shape
    taps = conv_weight.shape[1]
    margin = taps - 1
    core = lax.rem(place[0], 2)
    up[:length] = first[...]
    up[length:] = jnp.where(core == 0, near[...], far[...])
    down[:HALO] = jnp.where(core == 0, far[...], near[...])
    down[HALO:] = second[...]
    for t in range(width // LANES):
        lanes = lane_tile(t)
        total = jnp.zeros((length, LANES), jnp.float32)
        for k in range(taps):
            at = margin - k
            total = total + conv_weight[0, k : k + 1, lanes] * up[at : at + length, lanes]
            at = HALO - margin + k
            total = total + conv_weight[1, k : k + 1, lanes] * down[at : at + length, lanes]
        tokens_grad[:, lanes] = total


def swapped_edges(near, far, axis):
    count = lax.axis_size(axis)
    pairs = [(i, i + 1) for i in range(1, count - 1, 2)]
    pairs = pairs + [(j, i) for i, j in pairs]
    return swapped(near, axis, 1), lax.ppermute(far, axis, pairs)


def swapped(value, axis, by):
    count = lax.axis_size(axis)
    return lax.ppermute(value, axis, [(i, i ^ by) for i in range(count)])


def swapped_chips(value, k):
    places = lax.axis_size("ctx")
    chips = places // 2
    pairs = [(i, i ^ (2 * ((k - 1 + i % 2) % (chips - 1) + 1))) for i in range(places)]
    return lax.ppermute(value, "ctx", pairs)


def call(kernel, name, out_shape, scratch, mib, args, kinds, outs=None, flops=2**28):
    spaces = {
        "v": pl.BlockSpec(memory_space=pltpu.VMEM),
        "m": pl.BlockSpec(memory_space=pltpu.VMEM),
        "b": pl.BlockSpec(memory_space=pltpu.VMEM),
        "h": pl.BlockSpec(memory_space=pltpu.HBM),
        "s": pl.BlockSpec(memory_space=pltpu.SMEM),
    }
    outs = outs or "v" * len(out_shape)
    pinned = {"m": pltpu.VMEM, "h": pltpu.HBM}
    args = [
        pltpu.with_memory_space_constraint(a, pinned[k]) if k in pinned else a
        for a, k in zip(args, kinds, strict=True)
    ]
    results = [
        pinned[k](shape, jnp.float32) if k in pinned else shape_of(*shape)
        for shape, k in zip(out_shape, outs, strict=True)
        if k != "b"
    ]
    at = outs.find("b")
    if at >= 0:
        results.insert(at, pltpu.VMEM(out_shape[at], jnp.bfloat16))
    return pl.pallas_call(
        kernel,
        in_specs=[spaces[k] for k in kinds],
        out_specs=[spaces[k] for k in outs],
        out_shape=results,
        scratch_shapes=scratch,
        compiler_params=params(mib),
        cost_estimate=pl.CostEstimate(flops=flops, bytes_accessed=flops // 64, transcendentals=0),
        name=name,
    )(*args)


def terms_of(partial):
    count = lax.axis_size("ch")
    if count != 4:
        zero = jnp.zeros_like(partial)
        return (lax.psum(partial, "ch"), zero, zero, zero)
    return (partial, *(swapped(partial, "ch", k) for k in range(1, count)))


def halved(place, keep, send, rows, chips, name):
    got = swapped(send, "ctx", 1)
    share = rows // chips
    mine, *sent = call(
        halves_kernel, name, ((share, LANES),) * chips, [pltpu.VMEM((chips, share, LANES), jnp.float32)],
        8, (place, keep, got), "svv",
    )
    return (mine, *(swapped_chips(part, k) for k, part in enumerate(sent, 1)))


def on_device(
    tokens, gate_input, cotangent, conv_weight, conv_bias, select_weight, step_weight,
    step_bias, decay_log, skip_gain,
):
    length, width = tokens.shape
    tiles = width // LANES
    states = decay_log.shape[1]
    ranks = step_weight.shape[1]
    places = lax.axis_size("ctx")
    place = lax.axis_index("ctx").astype(jnp.int32).reshape(1)
    group = tile_group(tiles)
    chips = places // 2
    near = places == 8
    narrow = (length, LANES)
    one = (tiles, length, LANES)
    flat = (length, width)
    chain_ends = (2, tiles, states, CHAINS, LANES)
    carry = (2, tiles, 2 * states + 8, LANES)
    row_rates = (tiles, 2 * states, LANES)
    packed = (tiles * 2 * states + -(-2 * tiles // 8) * 8, LANES)
    vmem = functools.partial(pltpu.VMEM, dtype=jnp.float32)
    dma = lambda n: pltpu.SemaphoreType.DMA((n,))
    bases = vmem((length, states * LANES))
    grouped = vmem((group, length, states * LANES))
    row_scratch = vmem((group, states, CHAINS, LANES))

    core = (place & 1)[:, None] == 0
    head, tail = tokens[:HALO], tokens[length - HALO :]
    edges = swapped_edges(jnp.where(core, tail, head), jnp.where(core, head, tail), "ctx")
    fetched = (
        tokens, select_weight, conv_weight, conv_bias, gate_input, cotangent, step_weight,
        decay_log, step_bias, skip_gain,
    )
    held, select, taps, taps_bias, gate, cot, *step_held = call(
        fetch_kernel, "fetch", tuple(a.shape for a in fetched), [dma(len(fetched))], 4, fetched,
        "h" * len(fetched), "m" * len(fetched),
    )
    first_partial, first_act, first_pre, extended = call(
        entry_kernel, "entry", (narrow, one, one, (length + 2 * HALO, width)), [vmem(narrow)],
        6, (place, *edges, held, taps, taps_bias, select), "svvmmmm", "vmmm",
    )
    first_terms = terms_of(first_partial)
    partial, act, pre, grad_gated, spreader = call(
        second_entry_kernel, "second_entry",
        (narrow, one, one, one, (LANES, 2 * states * LANES)),
        [vmem(narrow)],
        6, (extended, taps, taps_bias, select, gate, cot), "mmmmmm", "vmmmb",
    )
    projection_terms = (first_terms, terms_of(partial))
    acts, pres = (first_act, act), (first_pre, pre)
    earlier, locals_ = (), []
    for side in range(2):
        *found, carried, every_rate = call(
            functools.partial(local_kernel, side), ("first_local", "second_local")[side],
            (
                narrow, one, one, chain_ends, (*one[:-1], states * LANES),
                (2, length, states * LANES), (tiles, states, LANES), (tiles, 1, LANES),
                carry, row_rates,
            ),
            [row_scratch],
            10,
            (
                *projection_terms[side], acts[side], grad_gated, spreader, *earlier, *step_held,
            ),
            "vvvvmmm" + "v" * len(earlier) + "mmmm", "mmmmmmmmvv", 2**32,
        )
        earlier = (carried, every_rate)
        locals_.append(found)
    if near:
        other = swapped(carried, "ctx", 1)
        sent = call(
            pair_kernel, "pair", (packed,) * (chips - 1),
            [vmem(carry)], 8, (place, carried, other, every_rate), "svvv",
        )
        got = [swapped_chips(part, k) for k, part in enumerate(sent, 1)]
        (incoming,) = call(
            chain_kernel, "chain", ((2, *row_rates),), [vmem((chips, *carry[1:]))],
            8, (place, other, every_rate, *got), "svv" + "v" * len(got),
        )
    else:
        gathered = lax.all_gather(carried, "ctx")
        (incoming,) = call(
            long_chain_kernel, "chain", ((2, *row_rates),), [],
            48, (place, gathered, every_rate), "svv",
        )
    earlier, grad_terms, grad_acts, grad_pres = (), [], [], []
    for side in range(2):
        _, step, step_pre, entering, decays, spread_bases, rates, skip_rows = locals_[side]
        partial_grad, grad_act, grad_pre, summed = call(
            functools.partial(scan_kernel, side), ("first_scan", "second_scan")[side],
            (narrow, one, one, one),
            [
                vmem(step_weight.shape[1:]), row_scratch, grouped, bases, bases,
                vmem((LANES, width)), dma(1),
            ],
            10,
            (
                incoming, spread_bases, acts[side], step, step_pre, grad_gated, entering, decays,
                spreader, rates, skip_rows, *earlier, step_weight,
            ),
            "vmmmmmmmmmm" + "m" * side + "h", "vmmm", 2**33,
        )
        if side == 1:
            first_total, partial_grad = call(
                handover_kernel, "handover", (narrow, narrow), [], 4,
                (partial_grad, *grad_terms[0]), "vvvvv",
            )
        grad_terms.append(terms_of(partial_grad))
        earlier = (summed,)
        grad_acts.append(grad_act)
        grad_pres.append(grad_pre)
    arrived = grad_terms[1][1]
    (step_part,) = call(
        step_kernel, "step_grad", ((2, tiles, ranks, LANES),), [],
        8, (*grad_pres, locals_[0][0], locals_[1][0], arrived), "mmmmv", flops=0,
    )
    weight_scratch = [vmem(narrow), vmem(narrow), vmem(narrow)]
    part, first_grad = call(
        weight_kernel, "first_weights", ((width, LANES), flat), weight_scratch,
        8, (first_total, first_act, first_pre, grad_acts[0], select, arrived),
        "vmmmmv", "mm", 0,
    )
    block_out, gate_grad = call(
        gate_kernel, "gate", (flat, flat), [vmem(one[1:])],
        6, (summed, gate, cot, arrived), "mmmv", flops=0,
    )
    half = width + tiles * ranks
    keep, send, second_grad, *edges = call(
        second_weight_kernel, "weights",
        ((half, LANES), (half, LANES), flat, (HALO, width), (HALO, width)),
        [*weight_scratch, vmem((width, LANES))],
        10,
        (
            place, *grad_terms[1], act, pre, grad_acts[1], select, block_out, part, step_part,
            first_grad,
        ),
        "svvvvmmmmhmvm", "vvmvv",
    )
    edges = swapped_edges(*edges, "ctx")
    if near:
        shares = halved(place, keep, send, half, chips, "halves")
        rows = half // chips
        (mine,) = call(
            add_after_kernel, "share_sum", ((rows, LANES),), [], 4, (*edges, *shares),
            "v" * (2 + chips),
        )
        ahead = mine
    else:
        ahead = edges[0]
    (tokens_grad,) = call(
        exit_kernel, "exit", (flat,),
        [
            vmem((length + HALO, width)), vmem((length + HALO, width)),
        ],
        6, (place, *edges, first_grad, second_grad, taps, ahead), "svvmmmv",
    )
    if near:
        got = [swapped_chips(mine, k) for k in range(1, chips)]
        (joined,) = call(
            join_kernel, "joined", ((chips, rows, LANES),), [],
            8, (place, tokens_grad, mine, *got), "sh" + "v" * chips,
        )
        select_grad, step_grad = call(
            outputs_kernel, "weight_grads", ((2, width, LANES), (2, ranks, width)),
            [vmem((2, half, LANES))],
            12, (place, joined, swapped(joined, "ctx", 1)), "svv",
        )
    else:
        first = lax.rem(place[0], 2) == 0
        both = jnp.where(first, jnp.stack([keep, send]), jnp.stack([send, keep]))
        both = lax.psum(both, "ctx")
        select_grad = both[:, :width]
        step_grad = both[:, width:].reshape(2, tiles, ranks, LANES)
        step_grad = step_grad.transpose(0, 2, 1, 3).reshape(2, ranks, width)
    return (block_out, tokens_grad, gate_grad, select_grad, step_grad)


def solution(mesh):
    return jax.shard_map(
        on_device,
        mesh=mesh,
        in_specs=(
            P("ctx", "ch"),
            P("ctx", "ch"),
            P("ctx", "ch"),
            P(None, None, "ch"),
            P(None, "ch"),
            P(None, "ch", None),
            P(None, None, "ch"),
            P(None, "ch"),
            P(None, None, "ch"),
            P(None, "ch"),
        ),
        out_specs=(
            P("ctx", "ch"),
            P("ctx", "ch"),
            P("ctx", "ch"),
            P(None, "ch", None),
            P(None, None, "ch"),
        ),
        check_vma=False,
    )
```

```python
import functools

import jax
import jax.numpy as jnp
from jax import lax
from jax.experimental import pallas as pl
from jax.experimental.pallas import tpu as pltpu
from jax.sharding import PartitionSpec as P

FULL_PRECISION = lax.Precision.HIGHEST
LANES = 128
CHAINS = 8
HALO = 8
LOG2E = 1.4426950408889634
LN2 = 0.6931471805599453
MIB = 1024 * 1024


def params(mib):
    return pltpu.CompilerParams(vmem_limit_bytes=mib * MIB)


def shape_of(*dims):
    return jax.ShapeDtypeStruct(dims, jnp.float32)


def dot(a, b, contract):
    return lax.dot_general(
        a, b, ((contract[:1], contract[1:]), ((), ())), precision=FULL_PRECISION,
        preferred_element_type=jnp.float32,
    )


def silu_grad(values):
    sigmoid_values = jax.nn.sigmoid(values)
    return sigmoid_values * (1.0 + values * (1.0 - sigmoid_values))


def lane_tile(t):
    return slice(t * LANES, (t + 1) * LANES)


def full_width(ref, *lead):
    tiles = ref.shape[len(lead)]
    return jnp.concatenate([ref[(*lead, t)] for t in range(tiles)], axis=1)


def convolved(ext, at_row, side, lanes, rows, conv_weight, conv_bias):
    taps = conv_weight.shape[1]
    margin = taps - 1
    conv = jnp.broadcast_to(conv_bias[side : side + 1, lanes], (rows, LANES))
    for k in range(taps):
        at = at_row + (k - margin if side == 0 else margin - k)
        conv = conv + conv_weight[side, k : k + 1, lanes] * ext[at : at + rows, lanes]
    return conv


def copies_of(pairs, sems):
    copies = [pltpu.make_async_copy(a, b, sems.at[i]) for i, (a, b) in enumerate(pairs)]
    for copy in copies:
        copy.start()
    return copies


def to_cells(tokens, cells):
    count = tokens.shape[0] // CHAINS
    for j in range(count):
        cells[j * CHAINS : (j + 1) * CHAINS] = tokens[pl.ds(j, CHAINS, stride=count), :]


def to_tokens(cells, tokens):
    count = tokens.shape[0] // CHAINS
    for j in range(count):
        tokens[pl.ds(j, CHAINS, stride=count), :] = cells[j * CHAINS : (j + 1) * CHAINS]


def finish_all(copies):
    for copy in copies:
        copy.wait()


def fetch_kernel(*refs):
    count = (len(refs) - 1) // 2
    finish_all(copies_of(list(zip(refs[:count], refs[count : 2 * count])), refs[-1]))


def entry_kernel(
    place, near, far, tokens, conv_weight, conv_bias, select,
    partial, act, pre, ext, plain,
):
    length, width = tokens.shape
    core = lax.rem(place[0], 2)
    ext[:HALO] = jnp.where(core == 0, far[...], near[...])
    ext[HALO : HALO + length] = tokens[...]
    ext[HALO + length :] = jnp.where(core == 0, near[...], far[...])
    enter(0, ext, conv_weight, conv_bias, select, partial, act, pre, plain)


def second_entry_kernel(
    ext, conv_weight, conv_bias, select, gate, cot,
    partial, act, pre, grad_gated, spreader, plain,
):
    fill_spreader(spreader)
    enter(1, ext, conv_weight, conv_bias, select, partial, act, pre, plain)
    for t in range(grad_gated.shape[0]):
        lanes = lane_tile(t)
        values = gate[:, lanes]
        plain[...] = cot[:, lanes] * values * jax.nn.sigmoid(values)
        to_cells(plain, grad_gated.at[t])


def enter(side, ext, conv_weight, conv_bias, select, partial, act, pre, plain):
    tiles, length, _ = act.shape
    for t in range(tiles):
        conv = convolved(ext, HALO, side, lane_tile(t), length, conv_weight, conv_bias)
        pre[t] = conv
        plain[...] = conv * jax.nn.sigmoid(conv)
        to_cells(plain, act.at[t])
    partial[...] = dot(full_width(act), select[side], (1, 0))


def turned(k, by, count):
    return lax.rem(k - 1 + by, count - 1) + 1


def fill_spreader(spreader):
    rows, columns = spreader.shape
    bases = columns // LANES
    row = lax.broadcasted_iota(jnp.int32, (rows, LANES), 0)
    kind = jnp.where(row >= rows - 3 * bases, lax.rem(row + bases - rows % bases, bases), -1)
    for n in range(bases):
        spreader[:, lane_tile(n)] = jnp.where(kind == n, 1.0, 0.0).astype(jnp.bfloat16)


def fill_bases(projection, spreader, bases):
    states = bases.shape[2] // LANES
    first = LANES - 2 * states
    lane = lax.broadcasted_iota(jnp.int32, projection.shape, 1)
    rest = jnp.where(lane >= first, projection[...], 0.0)
    joined = jnp.zeros_like(rest)
    for k in range(3):
        part = rest.astype(jnp.bfloat16).astype(jnp.float32)
        rest = rest - part
        joined = joined + (pltpu.roll(part, LANES - 2 * states * k, 1) if k else part)
    joined = joined.astype(jnp.bfloat16)
    width = 4 * LANES
    for at in range(0, 2 * states * LANES, width):
        value = jnp.dot(
            joined, spreader[:, at : at + width], preferred_element_type=jnp.float32
        )
        kind, lanes = at // (states * LANES), at % (states * LANES)
        bases[kind, :, lanes : lanes + width] = value


def fill_rates(decay_log, rates):
    for t in range(rates.shape[0]):
        rates[t] = -LOG2E * jnp.exp(decay_log[:, lane_tile(t)])


def sublane():
    return lax.broadcasted_iota(jnp.int32, (CHAINS, LANES), 0)


def shifted(value, by, up):
    rolled = pltpu.roll(value, by if up else CHAINS - by, 0)
    place = sublane()
    keep = place >= by if up else place < CHAINS - by
    return jnp.where(keep, rolled, 0.0)


def over_chains(decays, ends, up):
    by = 1
    while by < CHAINS:
        ends = [d * shifted(f, by, up) + f for d, f in zip(decays, ends)]
        if 2 * by < CHAINS:
            turn = by if up else CHAINS - by
            decays = [d * pltpu.roll(d, turn, 0) for d in decays]
        by *= 2
    return ends


def order(i, count, up):
    return i if up else count - 1 - i


def tile_group(tiles):
    return 2 if tiles % 2 == 0 else 1


def unrolled(count, times, body, start):
    times = times if count % times == 0 else 1

    def several(i, state):
        for k in range(times):
            state = body(i * times + k, state)
        return state

    return lax.fori_loop(0, count // times, several, start)


def plus(total, term):
    return term if total is None else total + term


def fill_rate_rows(rates, tiles, rate_rows):
    for g, t in enumerate(tiles):
        for n in range(rate_rows.shape[1]):
            rate_rows[g, n] = jnp.broadcast_to(rates[t, n : n + 1], (CHAINS, LANES))


def cell_rows(j):
    return pl.ds(pl.multiple_of(j * CHAINS, CHAINS), CHAINS)


def local_kernel(side, *refs):
    own, first, second, third, act, grad_gated, spreader = refs[:7]
    earlier, refs = refs[7 : 7 + 2 * side], refs[7 + 2 * side :]
    step_weight, decay_log, step_bias, skip_gain, *refs = refs
    projection, step, step_pre, entering, decays, bases, rates, skip_rows, *refs = refs
    carry, row_rates, rate_rows = refs
    tiles, length, _ = act.shape
    states = decay_log.shape[1]
    ranks = step_weight.shape[1]
    count = length // CHAINS
    group = tile_group(tiles)
    projection[...] = (own[...] + first[...]) + (second[...] + third[...])
    fill_bases(projection, spreader, bases)
    fill_rates(decay_log.at[side], rates)
    for t in range(tiles):
        skip_rows[t] = skip_gain[side : side + 1, lane_tile(t)]
    wide = dot(projection[:, :ranks], step_weight[side], (1, 0)) + step_bias[side : side + 1]
    for t in range(tiles):
        part = wide[:, lane_tile(t)]
        step_pre[t] = part
        step[t] = jnp.maximum(part, 0.0) + jnp.log1p(jnp.exp(-jnp.abs(part)))
    zero = jnp.zeros((CHAINS, LANES), jnp.float32)
    if side:
        carry[...] = earlier[0][...]
        row_rates[...] = earlier[1][...]
    else:
        carry[...] = jnp.zeros_like(carry)
        row_rates[...] = jnp.zeros_like(row_rates)
    up = side == 0
    basis_b, basis_c = bases.at[0], bases.at[1]

    def some_tiles(first, keep):
        at_tiles = [first * group + g for g in range(group)]
        fill_rate_rows(rates, at_tiles, rate_rows)

        def forward(i, current):
            state, summed = current
            j = order(i, count, up)
            at = cell_rows(j)
            steps = [step[t, at, :] for t in at_tiles]
            drives = [v * act[t, at, :] for v, t in zip(steps, at_tiles)]
            new = []
            for n in range(states):
                lanes = lane_tile(n)
                b = basis_b[at, lanes]
                for g in range(group):
                    decay = jnp.exp2(steps[g] * rate_rows[g, n])
                    decays[at_tiles[g], at, lanes] = decay
                    new.append(decay * state[n * group + g] + b * drives[g])
            return (tuple(new), tuple(a + v for a, v in zip(summed, steps)))

        start = ((zero,) * (states * group), (zero,) * group)
        state, summed = unrolled(count, 4, forward, start)

        def retreat(i, state):
            j = order(i, count, not up)
            at = cell_rows(j)
            grads = [grad_gated[t, at, :] for t in at_tiles]
            new = []
            for n in range(states):
                lanes = lane_tile(n)
                c = basis_c[at, lanes]
                for g in range(group):
                    adjoint = state[n * group + g] + c * grads[g]
                    new.append(decays[at_tiles[g], at, lanes] * adjoint)
            return tuple(new)

        sent = unrolled(count, 4, retreat, (zero,) * (states * group))
        for g, t in enumerate(at_tiles):
            across = [jnp.exp2(summed[g] * rate_rows[g, n]) for n in range(states)]
            for kind, ends, upward in ((0, state, up), (1, sent, not up)):
                ends = over_chains(across, list(ends[g::group]), upward)
                last = CHAINS - 1 if upward else 0
                for n in range(states):
                    entering[kind, t, n] = shifted(ends[n], 1, upward)
                    at = side * states + n
                    carry[0 if upward else 1, t, at : at + 1] = ends[n][last : last + 1]
            whole = jnp.sum(summed[g], axis=0, keepdims=True)
            at = 2 * states + side
            for k in range(2):
                carry[k, t, at : at + 1] = whole
        return keep

    lax.fori_loop(0, tiles // group, some_tiles, 0)
    row_rates[:, side * states : (side + 1) * states] = rates[...]


def tile_decay(part, rates):
    rows = rates.shape[1]
    row = lax.broadcasted_iota(jnp.int32, rates.shape, 1)
    sums = jnp.where(row < rows // 2, part[:, rows : rows + 1], part[:, rows + 1 : rows + 2])
    return jnp.exp2(rates * sums)


def pair_kernel(place, mine, other, rates, *refs):
    outs, total = refs[:-1], refs[-1]
    rows = rates.shape[1]
    core, chip = lax.rem(place[0], 2), lax.div(place[0], 2)
    low = jnp.where(core == 0, mine[...], other[...])
    high = jnp.where(core == 0, other[...], mine[...])
    spread_rates = rates[...]
    decay_low = tile_decay(low[0], spread_rates)
    decay_high = tile_decay(high[0], spread_rates)
    total[...] = low + high
    total[0, :, :rows] = decay_high * low[0][:, :rows] + high[0][:, :rows]
    total[1, :, :rows] = decay_low * high[1][:, :rows] + low[1][:, :rows]
    tiles = rates.shape[0]
    for k, out in enumerate(outs, 1):
        to = chip ^ turned(k, core, len(outs) + 1)
        below = lax.convert_element_type(to < chip, jnp.int32)
        for t in range(tiles):
            out[t * rows : (t + 1) * rows] = total[below, t, :rows]
            for side in range(2):
                at = tiles * rows + side * tiles + t
                out[at : at + 1] = total[0, t, rows + side : rows + side + 1]


def chain_kernel(place, other, rates, *refs):
    gathered, (out, parts) = refs[:-2], refs[-2:]
    rows = rates.shape[1]
    chips = parts.shape[0]
    core, chip = lax.rem(place[0], 2), lax.div(place[0], 2)
    parts[chip] = jnp.zeros(parts.shape[1:], jnp.float32)
    tiles = rates.shape[0]
    for k, part in enumerate(gathered, 1):
        source = chip ^ turned(k, core, chips)
        for t in range(tiles):
            parts[source, t, :rows] = part[t * rows : (t + 1) * rows]
            for side in range(2):
                at = tiles * rows + side * tiles + t
                parts[source, t, rows + side : rows + side + 1] = part[at : at + 1]
    spread_rates = rates[...]
    for kind in range(2):
        state = jnp.zeros(rates.shape, jnp.float32)
        for k in range(chips) if kind == 0 else reversed(range(chips)):
            part = parts[k]
            new = tile_decay(part, spread_rates) * state + part[:, :rows]
            state = jnp.where(k < chip if kind == 0 else k > chip, new, state)
        part = other[kind]
        new = tile_decay(part, spread_rates) * state + part[:, :rows]
        out[kind] = jnp.where(core == 1 - kind, new, state)


def long_chain_kernel(place, gathered, rates, out):
    rows = rates.shape[1]
    shards = gathered.shape[0]
    for kind in range(2):

        def turn(i, state):
            part = gathered[order(i, shards, kind == 0), kind]
            return tile_decay(part, rates[...]) * state + part[:, :rows]

        turns = place[0] if kind == 0 else shards - 1 - place[0]
        out[kind] = lax.fori_loop(0, turns, turn, jnp.zeros(rates.shape, jnp.float32))


def scan_kernel(side, *refs):
    incoming, bases, act, step, step_pre, grad_gated, entering, decays, spreader, *refs = refs
    rates, skip_rows, *refs = refs
    earlier, refs = refs[:side], refs[side:]
    step_weight, *refs = refs
    partial, grad_act, grad_pre, summed_out, *refs = refs
    rate_rows, history, grad_in, grad_out, weights = refs
    tiles, length, _ = act.shape
    states = rates.shape[1]
    ranks = step_weight.shape[1]
    count = length // CHAINS
    group = tile_group(tiles)
    grad_in[...] = jnp.zeros_like(grad_in)
    grad_out[...] = jnp.zeros_like(grad_out)
    up = side == 0
    basis_b, basis_c = bases.at[0], bases.at[1]

    def some_tiles(first, keep):
        at_tiles = [first * group + g for g in range(group)]
        fill_rate_rows(rates, at_tiles, rate_rows)
        skips = [skip_rows[t] for t in at_tiles]
        sums = []
        for t in at_tiles:
            summed = step[t, cell_rows(0), :]
            for j in range(1, count):
                summed = summed + step[t, cell_rows(j), :]
            sums.append(summed)

        def start(kind, upward):
            spans = []
            for g in range(group):
                span = shifted(sums[g], 1, upward)
                by = 1
                while by < CHAINS:
                    span = span + shifted(span, by, upward)
                    by *= 2
                spans.append(span)
            first = []
            for n in range(states):
                at = side * states + n
                for g, t in enumerate(at_tiles):
                    decay = jnp.exp2(spans[g] * rate_rows[g, n])
                    value = incoming[0 if upward else 1, t, at : at + 1, :]
                    first.append(entering[kind, t, n] + decay * value)
            return tuple(first)

        def forward(i, state):
            j = order(i, count, up)
            at = cell_rows(j)
            acts = [act[t, at, :] for t in at_tiles]
            grads = [grad_gated[t, at, :] for t in at_tiles]
            drives = [step[t, at, :] * a for t, a in zip(at_tiles, acts)]
            outs = [[v * a, None] for v, a in zip(skips, acts)]
            new = []
            for n in range(states):
                lanes = lane_tile(n)
                b, c = basis_b[at, lanes], basis_c[at, lanes]
                read = grad_out[at, lanes]
                for g in range(group):
                    before = state[n * group + g]
                    decay = decays[at_tiles[g], at, lanes]
                    history[g, at, lanes] = before
                    current = decay * before + b * drives[g]
                    outs[g][n % 2] = plus(outs[g][n % 2], c * current)
                    read = read + current * grads[g]
                    new.append(current)
                grad_out[at, lanes] = read
            for g, t in enumerate(at_tiles):
                out = outs[g][0] + outs[g][1]
                if side == 0:
                    summed_out[t, at, :] = out
                else:
                    summed_out[t, at, :] = earlier[0][t, at, :] + out
            return tuple(new)

        unrolled(count, 2, forward, start(0, up))

        def retreat(i, state):
            j = order(i, count, not up)
            at = cell_rows(j)
            steps = [step[t, at, :] for t in at_tiles]
            acts = [act[t, at, :] for t in at_tiles]
            grads = [grad_gated[t, at, :] for t in at_tiles]
            drives = [v * a for v, a in zip(steps, acts)]
            step_terms = [[None, None] for _ in range(group)]
            drive_grads = [[None, None] for _ in range(group)]
            new = []
            for n in range(states):
                lanes = lane_tile(n)
                b, c = basis_b[at, lanes], basis_c[at, lanes]
                put = grad_in[at, lanes]
                for g in range(group):
                    adjoint = state[n * group + g] + c * grads[g]
                    carried = decays[at_tiles[g], at, lanes] * adjoint
                    new.append(carried)
                    term = carried * history[g, at, lanes] * rate_rows[g, n]
                    step_terms[g][n % 2] = plus(step_terms[g][n % 2], term)
                    drive_grads[g][n % 2] = plus(drive_grads[g][n % 2], adjoint * b)
                    put = put + adjoint * drives[g]
                grad_in[at, lanes] = put
            for g, t in enumerate(at_tiles):
                drive_grad = drive_grads[g][0] + drive_grads[g][1]
                step_term = step_terms[g][0] + step_terms[g][1]
                grad_step = step_term * LN2 + drive_grad * acts[g]
                grad_act[t, at, :] = grads[g] * skips[g] + drive_grad * steps[g]
                pre = step_pre[t, at, :]
                grad_pre[t, at, :] = grad_step * jax.nn.sigmoid(pre)
            return tuple(new)

        unrolled(count, 2, retreat, start(1, not up))
        return keep

    lax.fori_loop(0, tiles // group, some_tiles, 0)
    wide = full_width(grad_pre)
    weights[...] = jnp.zeros_like(weights)
    weights[:ranks] = step_weight[side]
    sums = jnp.zeros((length, LANES), jnp.float32)
    step_lanes = 4 * LANES
    for k, values in enumerate((grad_in, grad_out)):
        for at in range(0, states * LANES, step_lanes):
            rest = values[:, at : at + step_lanes]
            from_lane = k * states * LANES + at
            pick = spreader[:, from_lane : from_lane + step_lanes]
            for _ in range(2):
                piece = rest.astype(jnp.bfloat16)
                rest = rest - piece.astype(jnp.float32)
                sums = sums + lax.dot_general(
                    piece, pick, (((1,), (1,)), ((), ())), preferred_element_type=jnp.float32
                )
    lane = lax.broadcasted_iota(jnp.int32, (length, LANES), 1)
    partial[...] = dot(wide, weights[...], (1, 1)) + jnp.where(lane >= ranks, sums, 0.0)


def step_kernel(first_pre, second_pre, first, second, after_this, step_part):
    _, tiles, ranks, _ = step_part.shape
    for side, (grad_pre, projection) in enumerate(((first_pre, first), (second_pre, second))):
        wide = dot(projection[...], full_width(grad_pre), (0, 0))
        for t in range(tiles):
            step_part[side, t] = wide[:ranks, lane_tile(t)]


def gate_kernel(
    summed, gate, cot, after_this, block_out, gate_grad, plain
):
    for t in range(summed.shape[0]):
        lanes = lane_tile(t)
        values = gate[:, lanes]
        to_tokens(summed.at[t], plain)
        both = plain[...]
        block_out[:, lanes] = both * values * jax.nn.sigmoid(values)
        gate_grad[:, lanes] = cot[:, lanes] * both * silu_grad(values)


def weight_kernel(
    total, act, pre, grad_act, select, after_this, part, conv_grad, grad, plain, cells,
):
    weigh(
        0, (total,), act, pre, grad_act, select, conv_grad, grad, plain, cells, part,
    )


def second_weight_kernel(
    place, own, first, second, third, act, pre, grad_act, select, after_this,
    part, step_part, other_grad,
    keep, send, conv_grad, near, far, grad, plain, cells, mine,
):
    length, width = conv_grad.shape
    weigh(
        1, (own, first, second, third), act, pre, grad_act, select,
        conv_grad, grad, plain, cells, mine,
    )
    core = lax.rem(place[0], 2)
    for side, value in enumerate((part, mine)):
        for out, whose in ((keep, side), (send, 1 - side)):

            @pl.when(core == whose)
            def _():
                out[:width] = value[...]
                out[width:] = step_part[side].reshape(-1, LANES)
    head, tail = other_grad[:HALO], conv_grad[length - HALO :]
    near[...] = jnp.where(core == 0, tail, head)
    far[...] = jnp.where(core == 0, head, tail)


def weigh(side, terms, act, pre, grad_act, select, conv_grad, grad, plain, cells, part):
    total = terms[0][...]
    for term in terms[1:]:
        total = total + term[...]
    grad[...] = total
    part[...] = dot(full_width(act), grad[...], (0, 0))
    wide = dot(grad[...], select[side], (1, 1))
    for t in range(act.shape[0]):
        lanes = lane_tile(t)
        cells[...] = grad_act[t] + wide[:, lanes]
        to_tokens(cells, plain)
        conv_grad[:, lanes] = plain[...] * silu_grad(pre[t])


def halves_kernel(place, keep, got, mine, *refs):
    outs, (total,) = refs[:-1], refs[-1:]
    share = mine.shape[0]
    chips = len(outs) + 1
    for k in range(chips):
        at = slice(k * share, (k + 1) * share)
        total[k] = keep[at] + got[at]
    core, chip = lax.rem(place[0], 2), lax.div(place[0], 2)
    mine[...] = total[chip]
    for k, out in enumerate(outs, 1):
        out[...] = total[chip ^ turned(k, core, chips)]


def handover_kernel(value, *refs):
    terms, (total, out) = refs[:-2], refs[-2:]
    add_kernel(*terms, total)
    out[...] = value[...]


def add_kernel(*refs):
    total = refs[0][...]
    for ref in refs[1:-1]:
        total = total + ref[...]
    refs[-1][...] = total


def join_kernel(place, after_this, mine, *refs):
    parts, out = refs[:-1], refs[-1]
    core, chip = lax.rem(place[0], 2), lax.div(place[0], 2)
    out[chip] = mine[...]
    for k, part in enumerate(parts, 1):
        out[chip ^ turned(k, core, len(parts) + 1)] = part[...]


def outputs_kernel(place, mine, other, select_grad, step_grad, both):
    sides, width, _ = select_grad.shape
    ranks = step_grad.shape[1]
    chips = mine.shape[0]
    core = lax.rem(place[0], 2)
    size = mine.shape[1]
    for side in range(2):
        for k in range(chips):
            both[side, k * size : (k + 1) * size] = jnp.where(core == side, mine[k], other[k])
        select_grad[side] = both[side, :width]
        for t in range(width // LANES):
            at = width + t * ranks
            step_grad[side, :, lane_tile(t)] = both[side, at : at + ranks]


def exit_kernel(
    place, near, far, first, second, conv_weight, after_this, tokens_grad, up, down
):
    length, width = first.shape
    taps = conv_weight.shape[1]
    margin = taps - 1
    core = lax.rem(place[0], 2)
    up[:length] = first[...]
    up[length:] = jnp.where(core == 0, near[...], far[...])
    down[:HALO] = jnp.where(core == 0, far[...], near[...])
    down[HALO:] = second[...]
    for t in range(width // LANES):
        lanes = lane_tile(t)
        total = jnp.zeros((length, LANES), jnp.float32)
        for k in range(taps):
            at = margin - k
            total = total + conv_weight[0, k : k + 1, lanes] * up[at : at + length, lanes]
            at = HALO - margin + k
            total = total + conv_weight[1, k : k + 1, lanes] * down[at : at + length, lanes]
        tokens_grad[:, lanes] = total


def swapped_edges(near, far, axis):
    count = lax.axis_size(axis)
    pairs = [(i, i + 1) for i in range(1, count - 1, 2)]
    pairs = pairs + [(j, i) for i, j in pairs]
    return swapped(near, axis, 1), lax.ppermute(far, axis, pairs)


def swapped(value, axis, by):
    count = lax.axis_size(axis)
    return lax.ppermute(value, axis, [(i, i ^ by) for i in range(count)])


def swapped_chips(value, k):
    places = lax.axis_size("ctx")
    chips = places // 2
    pairs = [(i, i ^ (2 * ((k - 1 + i % 2) % (chips - 1) + 1))) for i in range(places)]
    return lax.ppermute(value, "ctx", pairs)


def call(kernel, name, out_shape, scratch, mib, args, kinds, outs=None, flops=2**28):
    spaces = {
        "v": pl.BlockSpec(memory_space=pltpu.VMEM),
        "m": pl.BlockSpec(memory_space=pltpu.VMEM),
        "b": pl.BlockSpec(memory_space=pltpu.VMEM),
        "h": pl.BlockSpec(memory_space=pltpu.HBM),
        "s": pl.BlockSpec(memory_space=pltpu.SMEM),
    }
    outs = outs or "v" * len(out_shape)
    pinned = {"m": pltpu.VMEM, "h": pltpu.HBM}
    args = [
        pltpu.with_memory_space_constraint(a, pinned[k]) if k in pinned else a
        for a, k in zip(args, kinds, strict=True)
    ]
    results = [
        pinned[k](shape, jnp.float32) if k in pinned else shape_of(*shape)
        for shape, k in zip(out_shape, outs, strict=True)
        if k != "b"
    ]
    at = outs.find("b")
    if at >= 0:
        results.insert(at, pltpu.VMEM(out_shape[at], jnp.bfloat16))
    return pl.pallas_call(
        kernel,
        in_specs=[spaces[k] for k in kinds],
        out_specs=[spaces[k] for k in outs],
        out_shape=results,
        scratch_shapes=scratch,
        compiler_params=params(mib),
        cost_estimate=pl.CostEstimate(flops=flops, bytes_accessed=flops // 64, transcendentals=0),
        name=name,
    )(*args)


def terms_of(partial):
    count = lax.axis_size("ch")
    if count != 4:
        zero = jnp.zeros_like(partial)
        return (lax.psum(partial, "ch"), zero, zero, zero)
    return (partial, *(swapped(partial, "ch", k) for k in range(1, count)))


def halved(place, keep, send, rows, chips, name):
    got = swapped(send, "ctx", 1)
    share = rows // chips
    mine, *sent = call(
        halves_kernel, name, ((share, LANES),) * chips, [pltpu.VMEM((chips, share, LANES), jnp.float32)],
        8, (place, keep, got), "svv",
    )
    return (mine, *(swapped_chips(part, k) for k, part in enumerate(sent, 1)))


def on_device(
    tokens, gate_input, cotangent, conv_weight, conv_bias, select_weight, step_weight,
    step_bias, decay_log, skip_gain,
):
    length, width = tokens.shape
    tiles = width // LANES
    states = decay_log.shape[1]
    ranks = step_weight.shape[1]
    places = lax.axis_size("ctx")
    place = lax.axis_index("ctx").astype(jnp.int32).reshape(1)
    group = tile_group(tiles)
    chips = places // 2
    near = places == 8
    narrow = (length, LANES)
    one = (tiles, length, LANES)
    flat = (length, width)
    chain_ends = (2, tiles, states, CHAINS, LANES)
    carry = (2, tiles, 2 * states + 8, LANES)
    row_rates = (tiles, 2 * states, LANES)
    packed = (tiles * 2 * states + -(-2 * tiles // 8) * 8, LANES)
    vmem = functools.partial(pltpu.VMEM, dtype=jnp.float32)
    dma = lambda n: pltpu.SemaphoreType.DMA((n,))
    bases = vmem((length, states * LANES))
    grouped = vmem((group, length, states * LANES))
    row_scratch = vmem((group, states, CHAINS, LANES))

    core = (place & 1)[:, None] == 0
    head, tail = tokens[:HALO], tokens[length - HALO :]
    edges = swapped_edges(jnp.where(core, tail, head), jnp.where(core, head, tail), "ctx")
    fetched = (
        tokens, select_weight, conv_weight, conv_bias, gate_input, cotangent, step_weight,
        decay_log, step_bias, skip_gain,
    )
    held, select, taps, taps_bias, gate, cot, *step_held = call(
        fetch_kernel, "fetch", tuple(a.shape for a in fetched), [dma(len(fetched))], 4, fetched,
        "h" * len(fetched), "m" * len(fetched),
    )
    first_partial, first_act, first_pre, extended = call(
        entry_kernel, "entry", (narrow, one, one, (length + 2 * HALO, width)), [vmem(narrow)],
        6, (place, *edges, held, taps, taps_bias, select), "svvmmmm", "vmmm",
    )
    first_terms = terms_of(first_partial)
    partial, act, pre, grad_gated, spreader = call(
        second_entry_kernel, "second_entry",
        (narrow, one, one, one, (LANES, 2 * states * LANES)),
        [vmem(narrow)],
        6, (extended, taps, taps_bias, select, gate, cot), "mmmmmm", "vmmmb",
    )
    projection_terms = (first_terms, terms_of(partial))
    acts, pres = (first_act, act), (first_pre, pre)
    earlier, locals_ = (), []
    for side in range(2):
        *found, carried, every_rate = call(
            functools.partial(local_kernel, side), ("first_local", "second_local")[side],
            (
                narrow, one, one, chain_ends, (*one[:-1], states * LANES),
                (2, length, states * LANES), (tiles, states, LANES), (tiles, 1, LANES),
                carry, row_rates,
            ),
            [row_scratch],
            10,
            (
                *projection_terms[side], acts[side], grad_gated, spreader, *earlier, *step_held,
            ),
            "vvvvmmm" + "v" * len(earlier) + "mmmm", "mmmmmmmmvv", 2**32,
        )
        earlier = (carried, every_rate)
        locals_.append(found)
    if near:
        other = swapped(carried, "ctx", 1)
        sent = call(
            pair_kernel, "pair", (packed,) * (chips - 1),
            [vmem(carry)], 8, (place, carried, other, every_rate), "svvv",
        )
        got = [swapped_chips(part, k) for k, part in enumerate(sent, 1)]
        (incoming,) = call(
            chain_kernel, "chain", ((2, *row_rates),), [vmem((chips, *carry[1:]))],
            8, (place, other, every_rate, *got), "svv" + "v" * len(got),
        )
    else:
        gathered = lax.all_gather(carried, "ctx")
        (incoming,) = call(
            long_chain_kernel, "chain", ((2, *row_rates),), [],
            48, (place, gathered, every_rate), "svv",
        )
    earlier, grad_terms, grad_acts, grad_pres = (), [], [], []
    for side in range(2):
        _, step, step_pre, entering, decays, spread_bases, rates, skip_rows = locals_[side]
        partial_grad, grad_act, grad_pre, summed = call(
            functools.partial(scan_kernel, side), ("first_scan", "second_scan")[side],
            (narrow, one, one, one),
            [
                row_scratch, grouped, bases, bases, vmem((LANES, width)),
            ],
            10,
            (
                incoming, spread_bases, acts[side], step, step_pre, grad_gated, entering, decays,
                spreader, rates, skip_rows, *earlier, step_held[0],
            ),
            "vmmmmmmmmmm" + "m" * side + "m", "vmmm", 2**33,
        )
        if side == 1:
            first_total, partial_grad = call(
                handover_kernel, "handover", (narrow, narrow), [], 4,
                (partial_grad, *grad_terms[0]), "vvvvv",
            )
        grad_terms.append(terms_of(partial_grad))
        earlier = (summed,)
        grad_acts.append(grad_act)
        grad_pres.append(grad_pre)
    arrived = grad_terms[1][1]
    (step_part,) = call(
        step_kernel, "step_grad", ((2, tiles, ranks, LANES),), [],
        8, (*grad_pres, locals_[0][0], locals_[1][0], arrived), "mmmmv", flops=0,
    )
    weight_scratch = [vmem(narrow), vmem(narrow), vmem(narrow)]
    part, first_grad = call(
        weight_kernel, "first_weights", ((width, LANES), flat), weight_scratch,
        8, (first_total, first_act, first_pre, grad_acts[0], select, arrived),
        "vmmmmv", "mm", 0,
    )
    block_out, gate_grad = call(
        gate_kernel, "gate", (flat, flat), [vmem(one[1:])],
        6, (summed, gate, cot, arrived), "mmmv", flops=0,
    )
    half = width + tiles * ranks
    keep, send, second_grad, *edges = call(
        second_weight_kernel, "weights",
        ((half, LANES), (half, LANES), flat, (HALO, width), (HALO, width)),
        [*weight_scratch, vmem((width, LANES))],
        10,
        (
            place, *grad_terms[1], act, pre, grad_acts[1], select, block_out, part, step_part,
            first_grad,
        ),
        "svvvvmmmmhmvm", "vvmvv",
    )
    edges = swapped_edges(*edges, "ctx")
    if near:
        shares = halved(place, keep, send, half, chips, "halves")
        rows = half // chips
        (mine,) = call(
            add_kernel, "share_sum", ((rows, LANES),), [], 4, shares, "v" * chips
        )
        ahead = mine
    else:
        ahead = edges[0]
    (tokens_grad,) = call(
        exit_kernel, "exit", (flat,),
        [
            vmem((length + HALO, width)), vmem((length + HALO, width)),
        ],
        6, (place, *edges, first_grad, second_grad, taps, ahead), "svvmmmv",
    )
    if near:
        got = [swapped_chips(mine, k) for k in range(1, chips)]
        (joined,) = call(
            join_kernel, "joined", ((chips, rows, LANES),), [],
            8, (place, tokens_grad, mine, *got), "sh" + "v" * chips,
        )
        select_grad, step_grad = call(
            outputs_kernel, "weight_grads", ((2, width, LANES), (2, ranks, width)),
            [vmem((2, half, LANES))],
            12, (place, joined, swapped(joined, "ctx", 1)), "svv",
        )
    else:
        first = lax.rem(place[0], 2) == 0
        both = jnp.where(first, jnp.stack([keep, send]), jnp.stack([send, keep]))
        both = lax.psum(both, "ctx")
        select_grad = both[:, :width]
        step_grad = both[:, width:].reshape(2, tiles, ranks, LANES)
        step_grad = step_grad.transpose(0, 2, 1, 3).reshape(2, ranks, width)
    return (block_out, tokens_grad, gate_grad, select_grad, step_grad)


def solution(mesh):
    return jax.shard_map(
        on_device,
        mesh=mesh,
        in_specs=(
            P("ctx", "ch"),
            P("ctx", "ch"),
            P("ctx", "ch"),
            P(None, None, "ch"),
            P(None, "ch"),
            P(None, "ch", None),
            P(None, None, "ch"),
            P(None, "ch"),
            P(None, None, "ch"),
            P(None, "ch"),
        ),
        out_specs=(
            P("ctx", "ch"),
            P("ctx", "ch"),
            P("ctx", "ch"),
            P(None, "ch", None),
            P(None, None, "ch"),
        ),
        check_vma=False,
    )
```
